32 devices in a mesh: dp: 8 (over z, y), ctx: 4 (over x, core).
Axes of the slice: x: 2, y: 2, z: 4, core: 2. Of those that a mesh axis runs over, the one named last changes fastest.
Arguments:
- tokens: bfloat16 [8192, 512], P(('dp', 'ctx')), may hold values from -6 to 6
- dest_owner: int32 [8192], P(('dp', 'ctx')), may hold values from 0 to 7, as said below
- dest_slot: int32 [8192], P(('dp', 'ctx')), may hold values from 0 to 255, as said below
- lengths: int32 [8, 3], P('dp'), may hold values from 1 to 768, 1024 in all within a row
- proj_weight: bfloat16 [512, 2048], replicated, may hold values from -0.25 to 0.25
- out_weight: bfloat16 [512, 512], replicated, may hold values from -0.25 to 0.25
- cotangent: bfloat16 [8192, 512], P(('dp', 'ctx')), may hold values from -6 to 6
Outputs:
- layer_out: bfloat16 [8192, 512], P(('dp', 'ctx'))
- grad_tokens: bfloat16 [8192, 512], P(('dp', 'ctx'))
- grad_proj: float32 [512, 2048], P('dp')
- grad_outw: float32 [512, 512], P('dp')
The draws below stay inside these ranges and needn't reach their ends.
Inputs may be any that keep to these rules, and one draw needn't show every extreme that they name: `dest_owner`: at every ctx index, the rows of one device name each owner at most 64 times, some owner exactly 64 times, and every owner receives exactly 256 rows from the devices of that ctx index. `dest_slot`: the rows that reach one owner device carry distinct slots that cover all of 0 to 255. Each group's lengths sum to 1024, the largest is exactly 768.
All inputs are finite; a program needn't handle non-finite values.
Results may differ from the reference program's by a relative error of at most 0.012.
Values may be sent and summed in bfloat16 or wider, within the bound.
No kernel may reach another device: no remote copies, remote signals or barrier semaphores. Data moves between devices by JAX's collectives and lax.ppermute only.
A program may use at most 64 MiB of HBM per device.

```python
import math
import jax
import jax.numpy as jnp
import numpy as np
from jax import lax

D = 512
HEADS = 8
TOK_DEV = 256
HIST = 3
SEG = 1024
CAP = 64
TOKENS = 8192
N_DP = 8
N_CTX = 4


def owner_tables(key):
    groups = N_DP
    half_cap = CAP // 2
    key_swing, key_order, key_rows, key_slots = jax.random.split(key, 4)
    swing = jax.random.randint(key_swing, (N_CTX, groups // 2), 0, half_cap + 1)
    swing = swing.at[:, 0].set(half_cap)
    paired = jnp.stack([half_cap + swing, half_cap - swing], axis=2).reshape(N_CTX, groups)

    def permute_groups(subkey):
        return jax.random.permutation(subkey, groups)

    def permute_rows(subkey):
        return jax.random.permutation(subkey, TOK_DEV)
    order = jax.vmap(permute_groups)(jax.random.split(key_order, N_CTX))
    share = jnp.take_along_axis(paired, order, axis=1).astype(jnp.int32)
    ends = jnp.cumsum(share, axis=1)
    rank = jax.vmap(permute_rows)(jax.random.split(key_rows, groups * N_CTX)).reshape(groups, N_CTX, TOK_DEV)
    passed = ends[None, :, None, :] <= rank[..., None]
    shift = jnp.sum(passed.astype(jnp.int32), axis=3)
    within = rank - jnp.sum(jnp.where(passed, share[None, :, None, :], 0), axis=3)
    source_ids = jnp.arange(groups, dtype=jnp.int32)[:, None, None]
    owner = (source_ids + shift) % groups
    owner_ids = jnp.arange(groups, dtype=jnp.int32)[:, None]
    sender_ids = jnp.arange(groups, dtype=jnp.int32)[None, :]
    incoming = share[:, (owner_ids - sender_ids) % groups]
    offsets = jnp.cumsum(incoming, axis=2) - incoming
    column_ids = jnp.arange(N_CTX, dtype=jnp.int32)[None, :, None]
    base = offsets[column_ids, owner, source_ids]
    slot_order = jax.vmap(permute_rows)(jax.random.split(key_slots, N_CTX * groups)).reshape(N_CTX, groups, TOK_DEV)
    slot = slot_order[column_ids, owner, base + within]
    return (owner.reshape(-1).astype(jnp.int32), slot.reshape(-1).astype(jnp.int32))


def draw_dest_owner(key, part):
    tables = owner_tables(key)
    return tables[0]


def draw_dest_slot(key, part):
    tables = owner_tables(key)
    return tables[1]


def block_scale(rng, extent, shards, least, top_value):
    def one(position, blocks):
        steps = jax.random.uniform(jax.random.fold_in(jax.random.fold_in(rng, 6), position), (blocks,), jnp.float32, least / len(shards), top_value / len(shards))
        return jnp.repeat(jnp.exp(steps), extent[position] // blocks).reshape((-1,) + (1,) * (len(extent) - position - 1))

    gain = one(*shards[0])
    for cut in shards[1:]:
        gain = gain * one(*cut)
    return gain


def length_profile(number_of, total, limit, skew):
    weights = [(1 << 20) // math.isqrt(standing ** skew) + 1 for standing in range(2, number_of + 1)]
    surplus, counts = total - limit - (number_of - 1), [1] * (number_of - 1)
    while surplus > 0:
        candidates = [i for i in range(number_of - 1) if counts[i] < limit]
        whole, remaining = sum([weights[i] for i in candidates]), surplus
        for i in candidates:
            extra = min(limit - counts[i], max(1, remaining * weights[i] // whole), surplus)
            counts[i] = counts[i] + extra
            surplus = surplus - extra
    return np.array([limit] + counts)


def ragged(rng, amount, total, limit, lean):
    if amount == 2:
        one = jax.random.randint(rng, (), max(1, total - limit), min(limit, total - 1) + 1)
        return jnp.stack([one, total - one])
    sizes = jnp.asarray(length_profile(amount, total, limit, lean), jnp.int32)
    pairs = (amount - 1) // 2
    source_of, taker = sizes[1:1 + 2 * pairs:2], sizes[2:2 + 2 * pairs:2]
    slack = jnp.minimum(source_of - 1, limit - taker)
    moved = jax.random.randint(jax.random.fold_in(rng, 1), (pairs,), 0, 1 << 20) % (slack + 1)
    sizes = sizes.at[1:1 + 2 * pairs:2].set(source_of - moved).at[2:2 + 2 * pairs:2].set(taker + moved)
    return sizes[jax.random.permutation(jax.random.fold_in(rng, 2), amount)]


def scatter_about(stream_key, dims, scale, bound, cuts=(), held_as=jnp.bfloat16):
    gain = block_scale(stream_key, dims, cuts, -0.22, 0.18) if cuts else 1.0
    values = jax.random.normal(stream_key, dims, jnp.float32) * scale * gain
    return jnp.minimum(jnp.maximum(values, -bound), bound).astype(held_as)


def setup_inputs(seed: int = 0) -> dict:
    seeds = jax.random.split(jax.random.key(seed), 8)
    tokens = scatter_about(seeds[0], (TOKENS, D), 1.0, 6.0, ((0, 32),))
    dest_owner = draw_dest_owner(jax.random.fold_in(seeds[7], 71), 0)
    dest_slot = draw_dest_slot(jax.random.fold_in(seeds[7], 71), 0)
    lengths = jax.vmap(lambda own: ragged(own, HIST, TOK_DEV * N_CTX, 3 * TOK_DEV * N_CTX // 4, 0))(jax.random.split(seeds[3], N_DP)).reshape((N_DP, HIST)).astype(jnp.int32)
    proj_weight = scatter_about(seeds[4], (D, 4 * D), D ** -0.5, 0.25)
    out_weight = scatter_about(seeds[5], (D, D), D ** -0.5, 0.25)
    cotangent = scatter_about(seeds[6], (TOKENS, D), 1.0, 6.0, ((0, 32),))
    return {"tokens": tokens, "dest_owner": dest_owner, "dest_slot": dest_slot, "lengths": lengths, "proj_weight": proj_weight, "out_weight": out_weight, "cotangent": cotangent}


epsilon = 1e-05

def normalize(value):
    middle = lax.optimization_barrier(jnp.mean(value, axis=-1, keepdims=True))
    centred = value - middle
    inv_dev = lax.rsqrt(lax.optimization_barrier(jnp.mean(centred * centred, axis=-1, keepdims=True)) + epsilon)
    return (centred * inv_dev, inv_dev)

def norm_back(grad, normed, inv_dev):
    return inv_dev * (grad - lax.optimization_barrier(jnp.mean(grad, axis=-1, keepdims=True)) - normed * lax.optimization_barrier(jnp.mean(grad * normed, axis=-1, keepdims=True)))

def silu_slope(value):
    squashed = jax.nn.sigmoid(value)
    return squashed * (1.0 + value * (1.0 - squashed))

def history_mask(query_pos, key_pos, hist_lengths):
    bounds = jnp.cumsum(hist_lengths)
    after_query = query_pos[:, None] >= bounds[None, :]
    query_hist = lax.optimization_barrier(jnp.sum(after_query.astype(jnp.int32), axis=1))
    query_start = lax.optimization_barrier(jnp.sum(jnp.where(after_query, hist_lengths[None, :], 0), axis=1))
    key_hist = lax.optimization_barrier(jnp.sum((key_pos[:, None] >= bounds[None, :]).astype(jnp.int32), axis=1))
    allowed = (query_hist[:, None] == key_hist[None, :]) & (key_pos[None, :] <= query_pos[:, None])
    count = (query_pos - query_start + 1).astype(jnp.float32)
    return (allowed, count)

def group_pass(owned, hist_lengths, proj_weight, out_weight, cotangent):
    rows, width = owned.shape
    head_dim = width // HEADS
    scale = head_dim ** (-0.5)
    owned_wide = owned.astype(jnp.float32)
    centred, inv_scale = normalize(owned_wide)
    normed_in = centred.astype(jnp.bfloat16)
    preact = jnp.dot(normed_in, proj_weight, preferred_element_type=jnp.float32)
    activated = jax.nn.silu(preact)
    blocks = [activated[:, i * width:(i + 1) * width].astype(jnp.bfloat16) for i in range(4)]
    gate_units, value_part, query_part, key_part = blocks

    def split(array):
        return array.astype(jnp.float32).reshape(rows, HEADS, head_dim)
    query_heads, key_heads, value_heads = (split(query_part), split(key_part), split(value_part))
    positions = jnp.arange(rows, dtype=jnp.int32)
    allowed, count = history_mask(positions, positions, hist_lengths)
    scores = jnp.einsum('qhe,khe->hqk', query_heads, key_heads) * scale
    weights = jnp.where(allowed[None], jax.nn.silu(scores) / count[None, :, None], 0.0).astype(jnp.bfloat16)
    attended = jnp.einsum('hqk,khe->qhe', weights.astype(jnp.float32), value_heads).reshape(rows, width)
    normed, inv_dev = normalize(attended)
    gated = (normed * gate_units.astype(jnp.float32)).astype(jnp.bfloat16)
    layer_out = (jnp.dot(gated, out_weight, preferred_element_type=jnp.float32) + owned_wide).astype(jnp.bfloat16)
    grad_gated = jnp.dot(cotangent, out_weight.T, preferred_element_type=jnp.float32)
    grad_units = grad_gated * normed
    grad_attended = norm_back(grad_gated * gate_units.astype(jnp.float32), normed, inv_dev).astype(jnp.bfloat16)
    grad_heads = split(grad_attended)
    grad_weights = jnp.einsum('qhe,khe->hqk', grad_heads, value_heads)
    grad_scores = (jnp.where(allowed[None], grad_weights * silu_slope(scores) / count[None, :, None], 0.0) * scale).astype(jnp.bfloat16)
    grad_values = jnp.einsum('hqk,qhe->khe', weights.astype(jnp.float32), grad_heads).reshape(rows, width)
    grad_queries = jnp.einsum('hqk,khe->qhe', grad_scores.astype(jnp.float32), key_heads).reshape(rows, width)
    grad_keys = jnp.einsum('hqk,qhe->khe', grad_scores.astype(jnp.float32), query_heads).reshape(rows, width)
    grad_act = jnp.concatenate([grad_units, grad_values, grad_queries, grad_keys], axis=1)
    grad_preact = (grad_act * silu_slope(preact)).astype(jnp.bfloat16)
    grad_proj = jnp.dot(normed_in.T, grad_preact, preferred_element_type=jnp.float32)
    grad_outw = jnp.dot(gated.T, cotangent, preferred_element_type=jnp.float32)
    grad_in = jnp.dot(grad_preact, proj_weight.T, preferred_element_type=jnp.float32)
    grad_owned = (norm_back(grad_in, centred, inv_scale) + cotangent.astype(jnp.float32)).astype(jnp.bfloat16)
    return (layer_out, grad_owned, grad_proj, grad_outw)

def reference(tokens, dest_owner, dest_slot, lengths, proj_weight, out_weight, cotangent):
    loader_rows = jnp.arange(TOKENS, dtype=jnp.int32)
    column = loader_rows // TOK_DEV % N_CTX
    target = ((dest_owner * N_CTX + column) * TOK_DEV + dest_slot).astype(jnp.int32)
    owned = jnp.zeros_like(tokens).at[target].set(tokens)
    owned_groups = owned.reshape(N_DP, SEG, D)
    cot_groups = cotangent.reshape(N_DP, SEG, D)

    def step(carry, item):
        block, hist_lengths, cot_block = item
        out_block, grad_block, proj_term, out_term = group_pass(block, hist_lengths, proj_weight, out_weight, cot_block)
        return ((carry[0] + proj_term, carry[1] + out_term), (out_block, grad_block))
    start = (jnp.zeros((D, 4 * D), jnp.float32), jnp.zeros((D, D), jnp.float32))
    sums, stacked = lax.scan(step, start, (owned_groups, lengths, cot_groups))
    layer_out = stacked[0].reshape(TOKENS, D)
    grad_owned = stacked[1].reshape(TOKENS, D)
    grad_tokens = grad_owned[target]
    return (layer_out, grad_tokens, sums[0], sums[1])
```

```python
import functools

import jax
import jax.numpy as jnp
from jax import lax
from jax.experimental import pallas as pl
from jax.experimental.pallas import tpu as pltpu
from jax.sharding import PartitionSpec as P

HEADS = 8
EPSILON = 1e-05
LANES = 128
F32 = jnp.float32
BF16 = jnp.bfloat16

WHOLE = pl.BlockSpec(memory_space=pltpu.VMEM)
SCALARS = pl.BlockSpec(memory_space=pltpu.SMEM)


def call(body, name, outs, scalars, arrays, scratch=(), flops=10**8, vmem=24):
    return pl.pallas_call(
        body,
        name=name,
        out_shape=[jax.ShapeDtypeStruct(s, d) for s, d in outs],
        in_specs=[SCALARS] * len(scalars) + [WHOLE] * len(arrays),
        out_specs=[WHOLE] * len(outs),
        scratch_shapes=list(scratch),
        compiler_params=pltpu.CompilerParams(vmem_limit_bytes=vmem * 2**20),
        cost_estimate=pl.CostEstimate(flops=flops, bytes_accessed=2**20, transcendentals=0),
    )(*scalars, *arrays)


def iota(shape, dim):
    return lax.broadcasted_iota(jnp.int32, shape, dim)


def mm(a, b):
    return jnp.dot(a, b, preferred_element_type=F32)


def mm_t(a, b):
    return lax.dot_general(a, b, (((1,), (1,)), ((), ())), preferred_element_type=F32)


def t_mm(a, b):
    return lax.dot_general(a, b, (((0,), (0,)), ((), ())), preferred_element_type=F32)


def hot(condition):
    return jnp.where(condition, 1.0, 0.0).astype(BF16)


def normalize(value):
    middle = jnp.mean(value, axis=-1, keepdims=True)
    centred = value - middle
    inv_dev = lax.rsqrt(jnp.mean(centred * centred, axis=-1, keepdims=True) + EPSILON)
    return centred * inv_dev, inv_dev


def norm_back(grad, normed, inv_dev):
    return inv_dev * (
        grad
        - jnp.mean(grad, axis=-1, keepdims=True)
        - normed * jnp.mean(grad * normed, axis=-1, keepdims=True)
    )


def silu_both(value):
    squashed = 0.5 * jnp.tanh(0.5 * value) + 0.5
    return value * squashed, squashed * (1.0 + value * (1.0 - squashed))


def rank_rows(owner):
    rows = owner.shape[1]
    down, across = iota((rows, rows), 0), iota((rows, rows), 1)
    spread = jnp.broadcast_to(owner, (rows, rows))
    owner_col = jnp.sum(jnp.where(down == across, spread, 0).astype(F32), axis=1, keepdims=True)
    same = owner_col.astype(jnp.int32) == spread
    rank_row = jnp.sum(jnp.where(same & (down < across), 1.0, 0.0), axis=0, keepdims=True)
    rank_col = jnp.sum(jnp.where(same & (across < down), 1.0, 0.0), axis=1, keepdims=True)
    return rank_row.astype(jnp.int32), rank_col.astype(jnp.int32)


def pack_body(capacity, stride, owner_ref, slot_ref, tokens_ref, out_ref):
    owner = owner_ref[...]
    rows = owner.shape[1]
    rank_row, rank_col = rank_rows(owner)
    total, width = out_ref.shape
    place = iota((total, rows), 0)
    chosen = hot(place == owner * stride + rank_row)
    slots = jnp.where(place == owner * stride + capacity, slot_ref[...] + 1, 0)
    by_rank = hot(rank_col == iota((rows, width), 1))
    out_ref[...] = (mm(chosen, tokens_ref[...]) + mm(slots.astype(F32).astype(BF16), by_rank)).astype(
        BF16
    )


def block_rem(owners, stride):
    col, first = iota((owners, owners * stride), 1), iota((owners, owners * stride), 0)
    above = jnp.sum(jnp.where(col >= stride * (first + 1), 1.0, 0.0), axis=0, keepdims=True)
    rem = iota((1, owners * stride), 1) - stride * above.astype(jnp.int32)
    inside = (col >= stride * first) & (col < stride * (first + 1))
    return rem, inside


def landing_row(table, owners, capacity, stride):
    rem, inside = block_rem(owners, stride)
    lanes = iota((table.shape[1], owners * stride), 0)
    spread = mm(table, hot((lanes == rem) & (lanes < capacity)))
    return jnp.sum(jnp.where(inside, spread, 0.0), axis=0, keepdims=True)


def place_body(owners, capacity, stride, arrived_ref, owned_ref, normed_ref, landing_ref):
    rows = owned_ref.shape[0]
    arrived = arrived_ref[...]
    total = arrived.shape[0]
    pick = hot(iota((owners, total), 1) == iota((owners, total), 0) * stride + capacity)
    table = mm(pick, arrived).astype(BF16)
    landing = landing_row(table, owners, capacity, stride).astype(jnp.int32)
    owned = mm(hot(iota((rows, total), 0) + 1 == landing), arrived)
    owned_ref[...] = owned.astype(BF16)
    normed_ref[...] = normalize(owned)[0].astype(BF16)
    landing_ref[...] = landing_row(table, owners, capacity, capacity).astype(jnp.int32)


def own_body(normed_ref, proj_ref, outw_ref, cot_ref, gate_ref, slope_ref, query_ref, kv_ref, grad_ref):
    width = normed_ref.shape[1]
    preact = mm(normed_ref[...], proj_ref[...])
    gate, slope = silu_both(preact[:, :width])
    gate_ref[...] = gate.astype(BF16)
    slope_ref[...] = slope
    kv_ref[:, :width] = silu_both(preact[:, width : 2 * width])[0].astype(BF16)
    query_ref[...] = silu_both(preact[:, 2 * width : 3 * width])[0].astype(BF16)
    kv_ref[:, width:] = silu_both(preact[:, 3 * width :])[0].astype(BF16)
    grad_ref[...] = mm_t(cot_ref[...], outw_ref[...])


def history_start(pos, lengths_ref):
    first = lengths_ref[0, 0]
    second = lengths_ref[0, 1]
    return jnp.where(pos >= first + second, first + second, jnp.where(pos >= first, first, 0))


def attend(query_ref, key, value, shared, acc_ref):
    width = query_ref.shape[1]
    left = iota((1, LANES), 1) < LANES // 2
    for pair in range(width // LANES):
        cols = slice(pair * LANES, (pair + 1) * LANES)
        query, key_pair, value_pair = query_ref[:, cols], key[:, cols], value[:, cols]
        total = acc_ref[:, cols]
        for mine in (left, ~left):
            half = mm_t(jnp.where(mine, query, 0).astype(BF16), key_pair) * 0.0625
            weights = (half * (1.0 + jnp.tanh(half)) * shared).astype(BF16)
            total += mm(weights, jnp.where(mine, value_pair, 0).astype(BF16))
        acc_ref[:, cols] = total


def forward_body(
    me_ref, lengths_ref, near_ref, far_ref, cross_ref, proj_ref, outw_ref, cot_ref, owned_ref,
    gate_ref, slope_ref, query_ref, kv_ref, grad_ref,
    out_ref, gated_ref, gate_grad_ref, *rest,
):
    grads, acc_ref = rest[:-1], rest[-1]
    rows, width = query_ref.shape
    me = me_ref[0]
    acc_ref[...] = jnp.zeros_like(acc_ref)
    query_pos = me * rows + iota((rows, 1), 0)
    start = history_start(query_pos, lengths_ref)
    inverse = 1.0 / (query_pos - start + 1).astype(F32)

    def shared_for(block):
        key_pos = block * rows + iota((1, rows), 1)
        return jnp.where((key_pos >= start) & (key_pos <= query_pos), inverse, 0.0)

    attend(query_ref, kv_ref[:, width:], kv_ref[:, :width], shared_for(me), acc_ref)
    for step, other_ref in ((1, near_ref), (2, far_ref), (3, cross_ref)):
        block = me ^ step
        reach = history_start(me * rows, lengths_ref)

        @pl.when((block < me) & ((block + 1) * rows > reach))
        def _():
            normed = other_ref[...]
            value = silu_both(mm(normed, proj_ref[:, width : 2 * width]))[0].astype(BF16)
            key = silu_both(mm(normed, proj_ref[:, 3 * width :]))[0].astype(BF16)
            attend(query_ref, key, value, shared_for(block), acc_ref)

    gate = gate_ref[...].astype(F32)
    normed, inv_dev = normalize(acc_ref[...])
    gated = (normed * gate).astype(BF16)
    gated_ref[...] = gated
    grad_gated = grad_ref[...]
    grad_attended = norm_back(grad_gated * gate, normed, inv_dev).astype(BF16)
    acc_ref[...] = grad_attended.astype(F32)
    piece = width // len(grads)
    for step, ref in enumerate(grads):
        ref[...] = acc_ref[:, pl.ds(pl.multiple_of((me ^ step) * piece, LANES), piece)].astype(BF16)
    out_ref[...] = (mm(gated, outw_ref[...]) + owned_ref[...].astype(F32)).astype(BF16)
    gate_grad_ref[...] = (grad_gated * normed * slope_ref[...]).astype(BF16)


def side_body(me_ref, gated_ref, cot_ref, gate_grad_ref, proj_ref, *rest):
    pieces, gate_in_ref, scratch_ref, narrow_ref = rest[:-3], rest[-3], rest[-2], rest[-1]
    rows, width = gated_ref.shape
    me = me_ref[0]
    piece = width // len(pieces)
    scratch_ref[...] = t_mm(gated_ref[...], cot_ref[...])
    narrow_ref[...] = gate_grad_ref[...].astype(F32)
    for step, ref in enumerate(pieces):
        cols = pl.ds(pl.multiple_of((me ^ step) * piece, LANES), piece)
        ref[:rows, :] = narrow_ref[:, cols].astype(BF16)
        ref[rows:, :] = scratch_ref[:, cols].astype(BF16)
    gate_in_ref[...] = mm_t(gate_grad_ref[...], proj_ref[:, :width])


def heads_body(me_ref, n0_ref, n1_ref, n2_ref, n3_ref, proj_ref, part_ref, slope_ref):
    rows, width = n0_ref.shape
    me = me_ref[0]
    piece = width // 4
    cols = [proj_ref[:, pl.ds(pl.multiple_of(b * width + me * piece, LANES), piece)] for b in (1, 2, 3)]
    weight = jnp.concatenate(cols, axis=1)
    for step, ref in enumerate((n0_ref, n1_ref, n2_ref, n3_ref)):
        act, slope = silu_both(mm(ref[...], weight))
        at = pl.ds(pl.multiple_of((me ^ step) * rows, rows), rows)
        part_ref[at, :] = act.astype(BF16)
        slope_ref[at, :] = slope


def backward_body(
    me_ref, lengths_ref, g0_ref, g1_ref, g2_ref, g3_ref, part_ref, slope_ref, *rest
):
    outs, grad_ref, total_ref = rest[:4], rest[4], rest[5]
    rows, piece = g0_ref.shape
    me = me_ref[0]
    for step, ref in enumerate((g0_ref, g1_ref, g2_ref, g3_ref)):
        grad_ref[pl.ds(pl.multiple_of((me ^ step) * rows, rows), rows), :] = ref[...]
    total_ref[...] = jnp.zeros_like(total_ref)
    left = iota((1, LANES), 1) < LANES // 2
    blocks = len(outs)

    def visit(q_block, k_block):
        q_at, k_at = slice(q_block * rows, (q_block + 1) * rows), slice(k_block * rows, (k_block + 1) * rows)
        query_pos = q_block * rows + iota((1, rows), 1)
        start = history_start(query_pos, lengths_ref)
        key_pos = k_block * rows + iota((rows, 1), 0)
        inverse = 1.0 / (query_pos - start + 1).astype(F32)
        shared = jnp.where((key_pos >= start) & (key_pos <= query_pos), inverse, 0.0)
        value = part_ref[k_at, :piece]
        query = part_ref[q_at, piece : 2 * piece]
        key = part_ref[k_at, 2 * piece :]
        grad = grad_ref[q_at, :]
        small = value * jnp.asarray(0.0625, BF16)
        d_value, d_query, d_key = 0.0, 0.0, 0.0
        for mine in (left, ~left):
            query_h = jnp.where(mine, query, 0).astype(BF16)
            key_h = jnp.where(mine, key, 0).astype(BF16)
            grad_h = jnp.where(mine, grad, 0).astype(BF16)
            half = mm_t(key_h, query) * 0.0625
            up = 1.0 + jnp.tanh(half)
            act = half * up
            weights = (act * shared).astype(BF16)
            slope = (up + act * (2.0 - up)) * shared
            d_scores = (mm_t(small, grad_h) * slope).astype(BF16)
            d_value += mm(weights, grad_h)
            d_key += mm(d_scores, query_h)
            d_query += t_mm(d_scores, key_h)
        total_ref[k_at, :piece] += d_value
        total_ref[q_at, piece : 2 * piece] += d_query
        total_ref[k_at, 2 * piece :] += d_key

    for q_block in range(blocks):
        visit(q_block, q_block)
        for k_block in range(q_block):
            reach = history_start(q_block * rows, lengths_ref)

            @pl.when((k_block + 1) * rows > reach)
            def _():
                visit(q_block, k_block)

    for step, ref in enumerate(outs):
        at = pl.ds(pl.multiple_of((me ^ step) * rows, rows), rows)
        ref[...] = (total_ref[at, :] * slope_ref[at, :]).astype(BF16)


def weight_body(*refs):
    normed, grads, sides, out_ref = refs[:4], refs[4:8], refs[8:12], refs[12]
    rows, piece = normed[0].shape[0], sides[0].shape[1]
    qkv, gate, outw = 0.0, 0.0, 0.0
    for n_ref, g_ref, s_ref in zip(normed, grads, sides):
        qkv += t_mm(n_ref[...], g_ref[...])
        gate += t_mm(n_ref[...], s_ref[:rows, :])
        outw += s_ref[rows:, :].astype(F32)
    out_ref[:, :piece] = gate.astype(BF16)
    out_ref[:, piece : 4 * piece] = qkv.astype(BF16)
    out_ref[:, 4 * piece :] = outw.astype(BF16)


def input_body(
    me_ref, g0_ref, g1_ref, g2_ref, g3_ref, gate_in_ref, owned_ref, cot_ref, landing_ref, proj_ref, out_ref
):
    rows, width = owned_ref.shape
    me = me_ref[0]
    piece = width // 4
    total = gate_in_ref[...]
    for step, ref in enumerate((g0_ref, g1_ref, g2_ref, g3_ref)):
        cols = [
            proj_ref[:, pl.ds(pl.multiple_of(b * width + (me ^ step) * piece, LANES), piece)] for b in (1, 2, 3)
        ]
        total += mm_t(ref[...], jnp.concatenate(cols, axis=1))
    centred, inv_scale = normalize(owned_ref[...].astype(F32))
    grad = (norm_back(total, centred, inv_scale) + cot_ref[...].astype(F32)).astype(BF16)
    select = hot(iota((rows, out_ref.shape[0]), 0) + 1 == landing_ref[...])
    out_ref[...] = t_mm(select, grad).astype(BF16)


def return_body(capacity, owner_ref, back_ref, out_ref):
    owner = owner_ref[...]
    rank_row, _ = rank_rows(owner)
    total = back_ref.shape[0]
    chosen = hot(iota((total, owner.shape[1]), 0) == owner * capacity + rank_row)
    out_ref[...] = t_mm(chosen, back_ref[...]).astype(BF16)


def sum_body(parts_ref, out_ref):
    total = parts_ref[0].astype(F32)
    for i in range(1, parts_ref.shape[0]):
        total += parts_ref[i].astype(F32)
    out_ref[...] = total.astype(BF16)


def finish_body(me_ref, w0_ref, w1_ref, w2_ref, w3_ref, proj_ref, outw_ref):
    me = me_ref[0]
    width = outw_ref.shape[1]
    piece = width // 4
    for step, ref in enumerate((w0_ref, w1_ref, w2_ref, w3_ref)):
        for b in range(4):
            at = pl.ds(pl.multiple_of(b * width + (me ^ step) * piece, LANES), piece)
            proj_ref[:, at] = ref[:, b * piece : (b + 1) * piece].astype(F32)
        at = pl.ds(pl.multiple_of((me ^ step) * piece, LANES), piece)
        outw_ref[:, at] = ref[:, 4 * piece :].astype(F32)


def on_device(tokens, dest_owner, dest_slot, lengths, proj_weight, out_weight, cotangent):
    rows, width = tokens.shape
    owners = lax.axis_size("dp")
    cycle = lax.axis_size("ctx")
    assert cycle == 4 and width == cycle * LANES
    capacity = 2 * rows // owners
    stride = capacity + 8
    piece = width // cycle
    me = lax.axis_index("ctx").astype(jnp.int32).reshape(1)
    owner_row = dest_owner.reshape(1, rows)
    slot_row = dest_slot.reshape(1, rows)
    square = ((rows, width), BF16)

    def hop(value, step):
        return lax.ppermute(value, "ctx", [(i, i ^ step) for i in range(cycle)])

    def gather(value):
        near, far = hop(value, 1), hop(value, 2)
        return near, far, hop(far, 1)

    def exchange(values):
        return [values[0]] + [hop(values[step], step) for step in (2, 3, 1)]

    def swap(value):
        return lax.all_to_all(value, "dp", split_axis=0, concat_axis=0, tiled=True)

    (outgoing,) = call(
        functools.partial(pack_body, capacity, stride),
        "pack", [((owners * stride, width), BF16)], [], [owner_row, slot_row, tokens],
    )
    arrived = swap(outgoing.reshape(owners, stride, width)).reshape(owners * stride, width)
    owned, normed, landing = call(
        functools.partial(place_body, owners, capacity, stride),
        "place", [square, square, ((1, owners * capacity), jnp.int32)], [], [arrived],
    )
    near, far, cross = gather(normed)
    gate, slope, query, keys_values, grad_gated = call(
        own_body, "own_rows",
        [square, ((rows, width), F32), square, ((rows, 2 * width), BF16), ((rows, width), F32)],
        [], [normed, proj_weight, out_weight, cotangent], flops=10**9,
    )
    layer_out, gated, gate_grad, *grad_pieces = call(
        forward_body, "forward",
        [square, square, square] + [((rows, piece), BF16)] * cycle,
        [me, lengths],
        [near, far, cross, proj_weight, out_weight, cotangent, owned, gate, slope, query, keys_values, grad_gated],
        scratch=[pltpu.VMEM((rows, width), F32)], flops=4 * 10**9, vmem=32,
    )
    r0, r2, r3, r1 = exchange(grad_pieces)
    *sides, gate_in = call(
        side_body, "side", [((rows + width, piece), BF16)] * cycle + [((rows, width), F32)],
        [me], [gated, cotangent, gate_grad, proj_weight],
        scratch=[pltpu.VMEM((width, width), F32), pltpu.VMEM((rows, width), F32)], flops=10**9,
    )
    parts, slopes = call(
        heads_body, "heads",
        [((rows * cycle, 3 * piece), BF16), ((rows * cycle, 3 * piece), F32)],
        [me], [normed, near, far, cross, proj_weight], flops=10**9,
    )
    s0, s2, s3, s1 = exchange(sides)
    grads = call(
        backward_body, "backward", [((rows, 3 * piece), BF16)] * cycle,
        [me, lengths], [r0, r1, r2, r3, parts, slopes],
        scratch=[pltpu.VMEM((rows * cycle, piece), BF16), pltpu.VMEM((rows * cycle, 3 * piece), F32)],
        flops=4 * 10**9, vmem=32,
    )
    p0, p2, p3, p1 = exchange(grads)
    (weight_part,) = call(
        weight_body, "weights", [((width, 5 * piece), BF16)], [],
        [normed, near, far, cross, *grads, s0, s1, s2, s3], flops=10**9,
    )
    share = width // owners
    summed_parts = swap(weight_part.reshape(owners, share, 5 * piece))
    (back,) = call(
        input_body, "input_grad", [((owners * capacity, width), BF16)], [me],
        [p0, p1, p2, p3, gate_in, owned, cotangent, landing, proj_weight], flops=10**9,
    )
    returned = swap(back.reshape(owners, capacity, width)).reshape(owners * capacity, width)
    (mine,) = call(sum_body, "sum", [((share, 5 * piece), BF16)], [], [summed_parts])
    w1, w2, w3 = gather(mine)
    (grad_tokens,) = call(
        functools.partial(return_body, capacity), "give_back", [square], [], [owner_row, returned]
    )
    grad_proj, grad_outw = call(
        finish_body, "finish", [((share, 4 * width), F32), ((share, width), F32)],
        [me], [mine, w1, w2, w3],
    )
    return layer_out, grad_tokens, grad_proj, grad_outw


def solution(mesh):
    placed = (
        P(("dp", "ctx"), None),
        P(("dp", "ctx")),
        P(("dp", "ctx")),
        P("dp", None),
        P(),
        P(),
        P(("dp", "ctx"), None),
    )
    return jax.shard_map(
        on_device,
        mesh=mesh,
        in_specs=placed,
        out_specs=(P(("dp", "ctx"), None), P(("dp", "ctx"), None), P("dp", None), P("dp", None)),
        check_vma=False,
    )
```

```python
import functools

import jax
import jax.numpy as jnp
from jax import lax
from jax.experimental import pallas as pl
from jax.experimental.pallas import tpu as pltpu
from jax.sharding import PartitionSpec as P

HEADS = 8
EPSILON = 1e-05
LANES = 128
F32 = jnp.float32
BF16 = jnp.bfloat16

WHOLE = pl.BlockSpec(memory_space=pltpu.VMEM)
SCALARS = pl.BlockSpec(memory_space=pltpu.SMEM)
ANYWHERE = pl.BlockSpec(memory_space=pltpu.HBM)


def call(body, name, outs, scalars, arrays, scratch=(), flops=10**8, vmem=8, far=()):
    return pl.pallas_call(
        body,
        name=name,
        out_shape=[jax.ShapeDtypeStruct(s, d) for s, d in outs],
        in_specs=[SCALARS] * len(scalars) + [WHOLE] * len(arrays) + [ANYWHERE] * len(far),
        out_specs=[WHOLE] * len(outs),
        scratch_shapes=list(scratch),
        compiler_params=pltpu.CompilerParams(vmem_limit_bytes=vmem * 2**20),
        cost_estimate=pl.CostEstimate(flops=flops, bytes_accessed=2**20, transcendentals=0),
    )(*scalars, *arrays, *far)


def iota(shape, dim):
    return lax.broadcasted_iota(jnp.int32, shape, dim)


def mm(a, b):
    return jnp.dot(a, b, preferred_element_type=F32)


def mm_t(a, b):
    return lax.dot_general(a, b, (((1,), (1,)), ((), ())), preferred_element_type=F32)


def t_mm(a, b):
    return lax.dot_general(a, b, (((0,), (0,)), ((), ())), preferred_element_type=F32)


def hot(condition):
    return jnp.where(condition, 1.0, 0.0).astype(BF16)


def normalize(value):
    middle = jnp.mean(value, axis=-1, keepdims=True)
    centred = value - middle
    inv_dev = lax.rsqrt(jnp.mean(centred * centred, axis=-1, keepdims=True) + EPSILON)
    return centred * inv_dev, inv_dev


def norm_back(grad, normed, inv_dev):
    return inv_dev * (
        grad
        - jnp.mean(grad, axis=-1, keepdims=True)
        - normed * jnp.mean(grad * normed, axis=-1, keepdims=True)
    )


def silu_both(value):
    squashed = 0.5 * jnp.tanh(0.5 * value) + 0.5
    return value * squashed, squashed * (1.0 + value * (1.0 - squashed))


def rank_rows(owner):
    rows = owner.shape[1]
    down, across = iota((rows, rows), 0), iota((rows, rows), 1)
    spread = jnp.broadcast_to(owner, (rows, rows))
    owner_col = jnp.sum(jnp.where(down == across, spread, 0).astype(F32), axis=1, keepdims=True)
    same = owner_col.astype(jnp.int32) == spread
    rank_row = jnp.sum(jnp.where(same & (down < across), 1.0, 0.0), axis=0, keepdims=True)
    rank_col = jnp.sum(jnp.where(same & (across < down), 1.0, 0.0), axis=1, keepdims=True)
    return rank_row.astype(jnp.int32), rank_col.astype(jnp.int32)


def fetch(sources, targets, sems):
    copies = [pltpu.make_async_copy(a, b, sems.at[i]) for i, (a, b) in enumerate(zip(sources, targets))]
    for copy in copies:
        copy.start()
    for copy in copies:
        copy.wait()


def pack_body(
    capacity, stride, owner_hbm, slot_hbm, tokens_hbm, out_ref, owner_ref, slot_ref, tokens_ref, sems
):
    fetch((owner_hbm, slot_hbm, tokens_hbm), (owner_ref, slot_ref, tokens_ref), sems)
    owner = owner_ref[...]
    rows = owner.shape[1]
    rank_row, rank_col = rank_rows(owner)
    total, width = out_ref.shape
    place = iota((total, rows), 0)
    chosen = hot(place == owner * stride + rank_row)
    slots = jnp.where(place == owner * stride + capacity, slot_ref[...] + 1, 0)
    by_rank = hot(rank_col == iota((rows, width), 1))
    out_ref[...] = (mm(chosen, tokens_ref[...]) + mm(slots.astype(F32).astype(BF16), by_rank)).astype(
        BF16
    )


def block_rem(owners, stride):
    col, first = iota((owners, owners * stride), 1), iota((owners, owners * stride), 0)
    above = jnp.sum(jnp.where(col >= stride * (first + 1), 1.0, 0.0), axis=0, keepdims=True)
    rem = iota((1, owners * stride), 1) - stride * above.astype(jnp.int32)
    inside = (col >= stride * first) & (col < stride * (first + 1))
    return rem, inside


def landing_row(table, owners, capacity, stride):
    rem, inside = block_rem(owners, stride)
    lanes = iota((table.shape[1], owners * stride), 0)
    spread = mm(table, hot((lanes == rem) & (lanes < capacity)))
    return jnp.sum(jnp.where(inside, spread, 0.0), axis=0, keepdims=True)


def place_body(owners, capacity, stride, arrived_ref, owned_ref, normed_ref, landing_ref):
    rows = owned_ref.shape[0]
    arrived = arrived_ref[...]
    total = arrived.shape[0]
    pick = hot(iota((owners, total), 1) == iota((owners, total), 0) * stride + capacity)
    table = mm(pick, arrived).astype(BF16)
    landing = landing_row(table, owners, capacity, stride).astype(jnp.int32)
    owned = mm(hot(iota((rows, total), 0) + 1 == landing), arrived)
    owned_ref[...] = owned.astype(BF16)
    normed_ref[...] = normalize(owned)[0].astype(BF16)
    landing_ref[...] = landing_row(table, owners, capacity, capacity).astype(jnp.int32)


def early_body(cot_ref, outw_ref, grad_ref):
    grad_ref[...] = mm_t(cot_ref[...], outw_ref[...])


def history_start(pos, lengths_ref):
    first = lengths_ref[0, 0]
    second = lengths_ref[0, 1]
    return jnp.where(pos >= first + second, first + second, jnp.where(pos >= first, first, 0))


def attend(query_ref, key, value, shared, acc_ref):
    width = query_ref.shape[1]
    left = iota((1, LANES), 1) < LANES // 2
    for pair in range(width // LANES):
        cols = slice(pair * LANES, (pair + 1) * LANES)
        query, key_pair, value_pair = query_ref[:, cols], key[:, cols], value[:, cols]
        total = acc_ref[:, cols]
        for mine in (left, ~left):
            half = mm_t(jnp.where(mine, query, 0).astype(BF16), key_pair) * 0.0625
            weights = (half * (1.0 + jnp.tanh(half)) * shared).astype(BF16)
            total += mm(weights, jnp.where(mine, value_pair, 0).astype(BF16))
        acc_ref[:, cols] = total


def shared_factor(block, me, rows, lengths_ref):
    query_pos = me * rows + iota((rows, 1), 0)
    start = history_start(query_pos, lengths_ref)
    inverse = 1.0 / (query_pos - start + 1).astype(F32)
    key_pos = block * rows + iota((1, rows), 1)
    return jnp.where((key_pos >= start) & (key_pos <= query_pos), inverse, 0.0)


def attend_other(step, me, lengths_ref, other_ref, proj_ref, query_ref, acc_ref):
    rows, width = query_ref.shape
    block = me ^ step
    reach = history_start(me * rows, lengths_ref)

    @pl.when((block < me) & ((block + 1) * rows > reach))
    def _():
        normed = other_ref[...]
        value = silu_both(mm(normed, proj_ref[:, width : 2 * width]))[0].astype(BF16)
        key = silu_both(mm(normed, proj_ref[:, 3 * width :]))[0].astype(BF16)
        attend(query_ref, key, value, shared_factor(block, me, rows, lengths_ref), acc_ref)


def own_body(me_ref, lengths_ref, normed_ref, proj_ref, gate_ref, slope_ref, query_ref, acc_ref):
    rows, width = normed_ref.shape
    me = me_ref[0]
    preact = mm(normed_ref[...], proj_ref[...])
    gate, slope = silu_both(preact[:, :width])
    gate_ref[...] = gate.astype(BF16)
    slope_ref[...] = slope
    value = silu_both(preact[:, width : 2 * width])[0].astype(BF16)
    query_ref[...] = silu_both(preact[:, 2 * width : 3 * width])[0].astype(BF16)
    key = silu_both(preact[:, 3 * width :])[0].astype(BF16)
    acc_ref[...] = jnp.zeros_like(acc_ref)
    attend(query_ref, key, value, shared_factor(me, me, rows, lengths_ref), acc_ref)


def middle_body(me_ref, lengths_ref, near_ref, far_ref, proj_ref, query_ref, partial_ref, acc_ref):
    me = me_ref[0]
    acc_ref[...] = partial_ref[...]
    attend_other(1, me, lengths_ref, near_ref, proj_ref, query_ref, acc_ref)
    attend_other(2, me, lengths_ref, far_ref, proj_ref, query_ref, acc_ref)


def forward_body(
    me_ref, lengths_ref, cross_ref, proj_ref, outw_ref, owned_ref,
    gate_ref, slope_ref, query_ref, partial_ref, grad_ref,
    out_ref, gated_ref, gate_grad_ref, *rest,
):
    grads, acc_ref = rest[:-1], rest[-1]
    rows, width = query_ref.shape
    me = me_ref[0]
    acc_ref[...] = partial_ref[...]
    attend_other(3, me, lengths_ref, cross_ref, proj_ref, query_ref, acc_ref)
    gate = gate_ref[...].astype(F32)
    normed, inv_dev = normalize(acc_ref[...])
    gated = (normed * gate).astype(BF16)
    gated_ref[...] = gated
    grad_gated = grad_ref[...]
    grad_attended = norm_back(grad_gated * gate, normed, inv_dev).astype(BF16)
    acc_ref[...] = grad_attended.astype(F32)
    piece = width // len(grads)
    for step, ref in enumerate(grads):
        ref[...] = acc_ref[:, pl.ds(pl.multiple_of((me ^ step) * piece, LANES), piece)].astype(BF16)
    out_ref[...] = (mm(gated, outw_ref[...]) + owned_ref[...].astype(F32)).astype(BF16)
    gate_grad_ref[...] = (grad_gated * normed * slope_ref[...]).astype(BF16)


def side_body(me_ref, gated_ref, cot_ref, gate_grad_ref, proj_ref, *rest):
    pieces, gate_in_ref, scratch_ref, narrow_ref = rest[:-3], rest[-3], rest[-2], rest[-1]
    rows, width = gated_ref.shape
    me = me_ref[0]
    piece = width // len(pieces)
    scratch_ref[...] = t_mm(gated_ref[...], cot_ref[...])
    narrow_ref[...] = gate_grad_ref[...].astype(F32)
    for step, ref in enumerate(pieces):
        cols = pl.ds(pl.multiple_of((me ^ step) * piece, LANES), piece)
        ref[:rows, :] = narrow_ref[:, cols].astype(BF16)
        ref[rows:, :] = scratch_ref[:, cols].astype(BF16)
    gate_in_ref[...] = mm_t(gate_grad_ref[...], proj_ref[:, :width])


def heads_body(me_ref, n0_ref, n1_ref, n2_ref, n3_ref, proj_ref, part_ref, slope_ref):
    rows, width = n0_ref.shape
    me = me_ref[0]
    piece = width // 4
    cols = [proj_ref[:, pl.ds(pl.multiple_of(b * width + me * piece, LANES), piece)] for b in (1, 2, 3)]
    weight = jnp.concatenate(cols, axis=1)
    for step, ref in enumerate((n0_ref, n1_ref, n2_ref, n3_ref)):
        act, slope = silu_both(mm(ref[...], weight))
        at = pl.ds(pl.multiple_of((me ^ step) * rows, rows), rows)
        part_ref[at, :] = act.astype(BF16)
        slope_ref[at, :] = slope


def backward_body(
    me_ref, lengths_ref, g0_ref, g1_ref, g2_ref, g3_ref, part_ref, slope_ref, *rest
):
    outs, grad_ref, total_ref = rest[:4], rest[4], rest[5]
    rows, piece = g0_ref.shape
    me = me_ref[0]
    for step, ref in enumerate((g0_ref, g1_ref, g2_ref, g3_ref)):
        grad_ref[pl.ds(pl.multiple_of((me ^ step) * rows, rows), rows), :] = ref[...]
    total_ref[...] = jnp.zeros_like(total_ref)
    left = iota((1, LANES), 1) < LANES // 2
    blocks = len(outs)

    def visit(q_block, k_block):
        q_at, k_at = slice(q_block * rows, (q_block + 1) * rows), slice(k_block * rows, (k_block + 1) * rows)
        query_pos = q_block * rows + iota((1, rows), 1)
        start = history_start(query_pos, lengths_ref)
        key_pos = k_block * rows + iota((rows, 1), 0)
        inverse = 1.0 / (query_pos - start + 1).astype(F32)
        shared = jnp.where((key_pos >= start) & (key_pos <= query_pos), inverse, 0.0)
        value = part_ref[k_at, :piece]
        query = part_ref[q_at, piece : 2 * piece]
        key = part_ref[k_at, 2 * piece :]
        grad = grad_ref[q_at, :]
        small = value * jnp.asarray(0.0625, BF16)
        d_value, d_query, d_key = 0.0, 0.0, 0.0
        for mine in (left, ~left):
            query_h = jnp.where(mine, query, 0).astype(BF16)
            key_h = jnp.where(mine, key, 0).astype(BF16)
            grad_h = jnp.where(mine, grad, 0).astype(BF16)
            half = mm_t(key_h, query) * 0.0625
            up = 1.0 + jnp.tanh(half)
            act = half * up
            weights = (act * shared).astype(BF16)
            slope = (up + act * (2.0 - up)) * shared
            d_scores = (mm_t(small, grad_h) * slope).astype(BF16)
            d_value += mm(weights, grad_h)
            d_key += mm(d_scores, query_h)
            d_query += t_mm(d_scores, key_h)
        total_ref[k_at, :piece] += d_value
        total_ref[q_at, piece : 2 * piece] += d_query
        total_ref[k_at, 2 * piece :] += d_key

    for q_block in range(blocks):
        visit(q_block, q_block)
        for k_block in range(q_block):
            reach = history_start(q_block * rows, lengths_ref)

            @pl.when((k_block + 1) * rows > reach)
            def _():
                visit(q_block, k_block)

    for step, ref in enumerate(outs):
        at = pl.ds(pl.multiple_of((me ^ step) * rows, rows), rows)
        ref[...] = (total_ref[at, :] * slope_ref[at, :]).astype(BF16)


def weight_body(*refs):
    normed, grads, sides, out_ref = refs[:4], refs[4:8], refs[8:12], refs[-1]
    rows, piece = normed[0].shape[0], sides[0].shape[1]
    qkv, gate, outw = 0.0, 0.0, 0.0
    for n_ref, g_ref, s_ref in zip(normed, grads, sides):
        qkv += t_mm(n_ref[...], g_ref[...])
        gate += t_mm(n_ref[...], s_ref[:rows, :])
        outw += s_ref[rows:, :].astype(F32)
    out_ref[:, :piece] = gate.astype(BF16)
    out_ref[:, piece : 4 * piece] = qkv.astype(BF16)
    out_ref[:, 4 * piece :] = outw.astype(BF16)


def input_body(
    me_ref, g0_ref, g1_ref, g2_ref, g3_ref, gate_in_ref, owned_ref, cot_ref, landing_ref, proj_ref, out_ref
):
    rows, width = owned_ref.shape
    me = me_ref[0]
    piece = width // 4
    total = gate_in_ref[...]
    for step, ref in enumerate((g0_ref, g1_ref, g2_ref, g3_ref)):
        cols = [
            proj_ref[:, pl.ds(pl.multiple_of(b * width + (me ^ step) * piece, LANES), piece)] for b in (1, 2, 3)
        ]
        total += mm_t(ref[...], jnp.concatenate(cols, axis=1))
    centred, inv_scale = normalize(owned_ref[...].astype(F32))
    grad = (norm_back(total, centred, inv_scale) + cot_ref[...].astype(F32)).astype(BF16)
    select = hot(iota((rows, out_ref.shape[0]), 0) + 1 == landing_ref[...])
    out_ref[...] = t_mm(select, grad).astype(BF16)


def return_body(capacity, owner_ref, back_ref, out_ref):
    owner = owner_ref[...]
    rank_row, _ = rank_rows(owner)
    total = back_ref.shape[0]
    chosen = hot(iota((total, owner.shape[1]), 0) == owner * capacity + rank_row)
    out_ref[...] = t_mm(chosen, back_ref[...]).astype(BF16)


def sum_body(parts_ref, out_ref):
    total = parts_ref[0].astype(F32)
    for i in range(1, parts_ref.shape[0]):
        total += parts_ref[i].astype(F32)
    out_ref[...] = total.astype(BF16)


def finish_body(me_ref, w0_ref, w1_ref, w2_ref, w3_ref, proj_ref, outw_ref):
    me = me_ref[0]
    width = outw_ref.shape[1]
    piece = width // 4
    for step, ref in enumerate((w0_ref, w1_ref, w2_ref, w3_ref)):
        for b in range(4):
            at = pl.ds(pl.multiple_of(b * width + (me ^ step) * piece, LANES), piece)
            proj_ref[:, at] = ref[:, b * piece : (b + 1) * piece].astype(F32)
        at = pl.ds(pl.multiple_of((me ^ step) * piece, LANES), piece)
        outw_ref[:, at] = ref[:, 4 * piece :].astype(F32)


def on_device(tokens, dest_owner, dest_slot, lengths, proj_weight, out_weight, cotangent):
    rows, width = tokens.shape
    owners = lax.axis_size("dp")
    cycle = lax.axis_size("ctx")
    assert cycle == 4 and width == cycle * LANES
    capacity = 2 * rows // owners
    stride = capacity + 8
    piece = width // cycle
    me = lax.axis_index("ctx").astype(jnp.int32).reshape(1)
    owner_row = dest_owner.reshape(1, rows)
    slot_row = dest_slot.reshape(1, rows)
    square = ((rows, width), BF16)

    def hop(value, step):
        return lax.ppermute(value, "ctx", [(i, i ^ step) for i in range(cycle)])

    def gather(value):
        near, far = hop(value, 1), hop(value, 2)
        return near, far, hop(far, 1)

    def exchange(values):
        return [values[0]] + [hop(values[step], step) for step in (2, 3, 1)]

    def swap(value):
        return lax.all_to_all(value, "dp", split_axis=0, concat_axis=0, tiled=True)

    (outgoing,) = call(
        functools.partial(pack_body, capacity, stride),
        "pack", [((owners * stride, width), BF16)], [], [], far=[owner_row, slot_row, tokens],
        scratch=[
            pltpu.VMEM((1, rows), jnp.int32),
            pltpu.VMEM((1, rows), jnp.int32),
            pltpu.VMEM((rows, width), BF16),
            pltpu.SemaphoreType.DMA((3,)),
        ],
    )
    arrived = swap(outgoing.reshape(owners, stride, width)).reshape(owners * stride, width)
    owned, normed, landing = call(
        functools.partial(place_body, owners, capacity, stride),
        "place", [square, square, ((1, owners * capacity), jnp.int32)], [], [arrived],
    )
    near, far, cross = gather(normed)
    wide = ((rows, width), F32)
    (grad_gated,) = call(early_body, "early", [wide], [], [cotangent, out_weight], flops=10**8)
    gate, slope, query, partial = call(
        own_body, "own_rows", [square, wide, square, wide],
        [me, lengths], [normed, proj_weight], flops=10**9, vmem=16,
    )
    (partial,) = call(
        middle_body, "middle", [wide], [me, lengths], [near, far, proj_weight, query, partial],
        flops=10**9, vmem=16,
    )
    layer_out, gated, gate_grad, *grad_pieces = call(
        forward_body, "forward",
        [square, square, square] + [((rows, piece), BF16)] * cycle,
        [me, lengths],
        [cross, proj_weight, out_weight, owned, gate, slope, query, partial, grad_gated],
        scratch=[pltpu.VMEM((rows, width), F32)], flops=10**9, vmem=16,
    )
    r0, r2, r3, r1 = exchange(grad_pieces)
    *sides, gate_in = call(
        side_body, "side", [((rows + width, piece), BF16)] * cycle + [((rows, width), F32)],
        [me], [gated, cotangent, gate_grad, proj_weight],
        scratch=[pltpu.VMEM((width, width), F32), pltpu.VMEM((rows, width), F32)], flops=10**9,
    )
    parts, slopes = call(
        heads_body, "heads",
        [((rows * cycle, 3 * piece), BF16), ((rows * cycle, 3 * piece), F32)],
        [me], [normed, near, far, cross, proj_weight], flops=10**9, vmem=16,
    )
    s0, s2, s3, s1 = exchange(sides)
    grads = call(
        backward_body, "backward", [((rows, 3 * piece), BF16)] * cycle,
        [me, lengths], [r0, r1, r2, r3, parts, slopes],
        scratch=[pltpu.VMEM((rows * cycle, piece), BF16), pltpu.VMEM((rows * cycle, 3 * piece), F32)],
        flops=4 * 10**9, vmem=16,
    )
    p0, p2, p3, p1 = exchange(grads)
    (weight_part,) = call(
        weight_body, "weights", [((width, 5 * piece), BF16)], [],
        [normed, near, far, cross, *grads, s0, s1, s2, s3], flops=10**9, vmem=16, far=[p1],
    )
    share = width // owners
    summed_parts = swap(weight_part.reshape(owners, share, 5 * piece))
    (back,) = call(
        input_body, "input_grad", [((owners * capacity, width), BF16)], [me],
        [p0, p1, p2, p3, gate_in, owned, cotangent, landing, proj_weight], flops=10**9, vmem=16,
    )
    returned = swap(back.reshape(owners, capacity, width)).reshape(owners * capacity, width)
    (mine,) = call(sum_body, "sum", [((share, 5 * piece), BF16)], [], [summed_parts])
    w1, w2, w3 = gather(mine)
    (grad_tokens,) = call(
        functools.partial(return_body, capacity), "give_back", [square], [], [owner_row, returned]
    )
    grad_proj, grad_outw = call(
        finish_body, "finish", [((share, 4 * width), F32), ((share, width), F32)],
        [me], [mine, w1, w2, w3],
    )
    return layer_out, grad_tokens, grad_proj, grad_outw


def solution(mesh):
    placed = (
        P(("dp", "ctx"), None),
        P(("dp", "ctx")),
        P(("dp", "ctx")),
        P("dp", None),
        P(),
        P(),
        P(("dp", "ctx"), None),
    )
    return jax.shard_map(
        on_device,
        mesh=mesh,
        in_specs=placed,
        out_specs=(P(("dp", "ctx"), None), P(("dp", "ctx"), None), P("dp", None), P("dp", None)),
        check_vma=False,
    )
```

```python
import functools

import jax
import jax.numpy as jnp
from jax import lax
from jax.experimental import pallas as pl
from jax.experimental.pallas import tpu as pltpu
from jax.sharding import PartitionSpec as P

HEADS = 8
EPSILON = 1e-05
LANES = 128
F32 = jnp.float32
BF16 = jnp.bfloat16

WHOLE = pl.BlockSpec(memory_space=pltpu.VMEM)
SCALARS = pl.BlockSpec(memory_space=pltpu.SMEM)
ANYWHERE = pl.BlockSpec(memory_space=pltpu.HBM)


def call(body, name, outs, scalars, arrays, scratch=(), flops=10**8, vmem=8, far=()):
    return pl.pallas_call(
        body,
        name=name,
        out_shape=[jax.ShapeDtypeStruct(s, d) for s, d in outs],
        in_specs=[SCALARS] * len(scalars) + [WHOLE] * len(arrays) + [ANYWHERE] * len(far),
        out_specs=[WHOLE] * len(outs),
        scratch_shapes=list(scratch),
        compiler_params=pltpu.CompilerParams(vmem_limit_bytes=vmem * 2**20),
        cost_estimate=pl.CostEstimate(flops=flops, bytes_accessed=2**20, transcendentals=0),
    )(*scalars, *arrays, *far)


def iota(shape, dim):
    return lax.broadcasted_iota(jnp.int32, shape, dim)


def mm(a, b):
    return jnp.dot(a, b, preferred_element_type=F32)


def mm_t(a, b):
    return lax.dot_general(a, b, (((1,), (1,)), ((), ())), preferred_element_type=F32)


def t_mm(a, b):
    return lax.dot_general(a, b, (((0,), (0,)), ((), ())), preferred_element_type=F32)


def hot(condition):
    return jnp.where(condition, 1.0, 0.0).astype(BF16)


def normalize(value):
    middle = jnp.mean(value, axis=-1, keepdims=True)
    centred = value - middle
    inv_dev = lax.rsqrt(jnp.mean(centred * centred, axis=-1, keepdims=True) + EPSILON)
    return centred * inv_dev, inv_dev


def norm_back(grad, normed, inv_dev):
    return inv_dev * (
        grad
        - jnp.mean(grad, axis=-1, keepdims=True)
        - normed * jnp.mean(grad * normed, axis=-1, keepdims=True)
    )


def silu_both(value):
    squashed = 0.5 * jnp.tanh(0.5 * value) + 0.5
    return value * squashed, squashed * (1.0 + value * (1.0 - squashed))


def rank_rows(owner):
    rows = owner.shape[1]
    down, across = iota((rows, rows), 0), iota((rows, rows), 1)
    spread = jnp.broadcast_to(owner, (rows, rows))
    owner_col = jnp.sum(jnp.where(down == across, spread, 0).astype(F32), axis=1, keepdims=True)
    same = owner_col.astype(jnp.int32) == spread
    rank_row = jnp.sum(jnp.where(same & (down < across), 1.0, 0.0), axis=0, keepdims=True)
    rank_col = jnp.sum(jnp.where(same & (across < down), 1.0, 0.0), axis=1, keepdims=True)
    return rank_row.astype(jnp.int32), rank_col.astype(jnp.int32)


def fetch(sources, targets, sems):
    copies = [pltpu.make_async_copy(a, b, sems.at[i]) for i, (a, b) in enumerate(zip(sources, targets))]
    for copy in copies:
        copy.start()
    for copy in copies:
        copy.wait()


def store_blocks(refs, value):
    size = refs[0].shape[0]
    for i, ref in enumerate(refs):
        ref[...] = value[i * size : (i + 1) * size].astype(ref.dtype)


def load_blocks(refs):
    return jnp.concatenate([ref[...].astype(F32) for ref in refs], axis=0).astype(BF16)


def pack_body(capacity, stride, outs, mask_ref, owner_hbm, slot_hbm, tokens_hbm, *rest):
    out_refs, (owner_ref, slot_ref, tokens_ref, sems) = rest[:outs], rest[outs:]
    fetch((owner_hbm, slot_hbm, tokens_hbm), (owner_ref, slot_ref, tokens_ref), sems)
    owner = owner_ref[...] ^ mask_ref[0]
    rows = owner.shape[1]
    rank_row, rank_col = rank_rows(owner)
    total, width = outs * out_refs[0].shape[0], out_refs[0].shape[1]
    place = iota((total, rows), 0)
    chosen = hot(place == owner * stride + rank_row)
    slots = jnp.where(place == owner * stride + capacity, slot_ref[...] + 1, 0)
    by_rank = hot(rank_col == iota((rows, width), 1))
    store_blocks(out_refs, mm(chosen, tokens_ref[...]) + mm(slots.astype(F32).astype(BF16), by_rank))


def block_rem(owners, stride):
    col, first = iota((owners, owners * stride), 1), iota((owners, owners * stride), 0)
    above = jnp.sum(jnp.where(col >= stride * (first + 1), 1.0, 0.0), axis=0, keepdims=True)
    rem = iota((1, owners * stride), 1) - stride * above.astype(jnp.int32)
    inside = (col >= stride * first) & (col < stride * (first + 1))
    return rem, inside


def landing_row(table, owners, capacity, stride):
    rem, inside = block_rem(owners, stride)
    lanes = iota((table.shape[1], owners * stride), 0)
    spread = mm(table, hot((lanes == rem) & (lanes < capacity)))
    return jnp.sum(jnp.where(inside, spread, 0.0), axis=0, keepdims=True)


def place_body(owners, capacity, stride, *refs):
    owned_ref, normed_ref, landing_ref = refs[-3:]
    rows = owned_ref.shape[0]
    arrived = load_blocks(refs[:-3])
    total = arrived.shape[0]
    pick = hot(iota((owners, total), 1) == iota((owners, total), 0) * stride + capacity)
    table = mm(pick, arrived).astype(BF16)
    landing = landing_row(table, owners, capacity, stride).astype(jnp.int32)
    owned = mm(hot(iota((rows, total), 0) + 1 == landing), arrived)
    owned_ref[...] = owned.astype(BF16)
    normed_ref[...] = normalize(owned)[0].astype(BF16)
    landing_ref[...] = landing_row(table, owners, capacity, capacity).astype(jnp.int32)


def early_body(cot_ref, outw_ref, grad_ref):
    grad_ref[...] = mm_t(cot_ref[...], outw_ref[...])


def history_start(pos, lengths_ref):
    first = lengths_ref[0, 0]
    second = lengths_ref[0, 1]
    return jnp.where(pos >= first + second, first + second, jnp.where(pos >= first, first, 0))


def attend(query_ref, key, value, shared, acc_ref):
    width = query_ref.shape[1]
    left = iota((1, LANES), 1) < LANES // 2
    for pair in range(width // LANES):
        cols = slice(pair * LANES, (pair + 1) * LANES)
        query, key_pair, value_pair = query_ref[:, cols], key[:, cols], value[:, cols]
        total = acc_ref[:, cols]
        for mine in (left, ~left):
            half = mm_t(jnp.where(mine, query, 0).astype(BF16), key_pair) * 0.0625
            weights = (half * (1.0 + jnp.tanh(half)) * shared).astype(BF16)
            total += mm(weights, jnp.where(mine, value_pair, 0).astype(BF16))
        acc_ref[:, cols] = total


def shared_factor(block, me, rows, lengths_ref):
    query_pos = me * rows + iota((rows, 1), 0)
    start = history_start(query_pos, lengths_ref)
    inverse = 1.0 / (query_pos - start + 1).astype(F32)
    key_pos = block * rows + iota((1, rows), 1)
    return jnp.where((key_pos >= start) & (key_pos <= query_pos), inverse, 0.0)


def attend_other(step, me, lengths_ref, other_ref, proj_ref, query_ref, acc_ref):
    rows, width = query_ref.shape
    block = me ^ step
    reach = history_start(me * rows, lengths_ref)

    @pl.when((block < me) & ((block + 1) * rows > reach))
    def _():
        normed = other_ref[...]
        value = silu_both(mm(normed, proj_ref[:, width : 2 * width]))[0].astype(BF16)
        key = silu_both(mm(normed, proj_ref[:, 3 * width :]))[0].astype(BF16)
        attend(query_ref, key, value, shared_factor(block, me, rows, lengths_ref), acc_ref)


def own_body(me_ref, lengths_ref, normed_ref, proj_ref, gate_ref, slope_ref, query_ref, acc_ref):
    rows, width = normed_ref.shape
    me = me_ref[0]
    preact = mm(normed_ref[...], proj_ref[...])
    gate, slope = silu_both(preact[:, :width])
    gate_ref[...] = gate.astype(BF16)
    slope_ref[...] = slope
    value = silu_both(preact[:, width : 2 * width])[0].astype(BF16)
    query_ref[...] = silu_both(preact[:, 2 * width : 3 * width])[0].astype(BF16)
    key = silu_both(preact[:, 3 * width :])[0].astype(BF16)
    acc_ref[...] = jnp.zeros_like(acc_ref)
    attend(query_ref, key, value, shared_factor(me, me, rows, lengths_ref), acc_ref)


def middle_body(me_ref, lengths_ref, near_ref, far_ref, proj_ref, query_ref, partial_ref, acc_ref):
    me = me_ref[0]
    acc_ref[...] = partial_ref[...]
    attend_other(1, me, lengths_ref, near_ref, proj_ref, query_ref, acc_ref)
    attend_other(2, me, lengths_ref, far_ref, proj_ref, query_ref, acc_ref)


def forward_body(
    me_ref, lengths_ref, cross_ref, proj_ref, outw_ref, owned_ref,
    gate_ref, slope_ref, query_ref, partial_ref, grad_ref,
    out_ref, gated_ref, gate_grad_ref, *rest,
):
    grads, acc_ref = rest[:-1], rest[-1]
    rows, width = query_ref.shape
    me = me_ref[0]
    acc_ref[...] = partial_ref[...]
    attend_other(3, me, lengths_ref, cross_ref, proj_ref, query_ref, acc_ref)
    gate = gate_ref[...].astype(F32)
    normed, inv_dev = normalize(acc_ref[...])
    gated = (normed * gate).astype(BF16)
    gated_ref[...] = gated
    grad_gated = grad_ref[...]
    grad_attended = norm_back(grad_gated * gate, normed, inv_dev).astype(BF16)
    acc_ref[...] = grad_attended.astype(F32)
    piece = width // len(grads)
    for step, ref in enumerate(grads):
        ref[...] = acc_ref[:, pl.ds(pl.multiple_of((me ^ step) * piece, LANES), piece)].astype(BF16)
    out_ref[...] = (mm(gated, outw_ref[...]) + owned_ref[...].astype(F32)).astype(BF16)
    gate_grad_ref[...] = (grad_gated * normed * slope_ref[...]).astype(BF16)


def side_body(me_ref, gated_ref, cot_ref, gate_grad_ref, proj_ref, *rest):
    pieces, gate_in_ref, scratch_ref, narrow_ref = rest[:-3], rest[-3], rest[-2], rest[-1]
    rows, width = gated_ref.shape
    me = me_ref[0]
    piece = width // len(pieces)
    scratch_ref[...] = t_mm(gated_ref[...], cot_ref[...])
    narrow_ref[...] = gate_grad_ref[...].astype(F32)
    for step, ref in enumerate(pieces):
        cols = pl.ds(pl.multiple_of((me ^ step) * piece, LANES), piece)
        ref[:rows, :] = narrow_ref[:, cols].astype(BF16)
        ref[rows:, :] = scratch_ref[:, cols].astype(BF16)
    gate_in_ref[...] = mm_t(gate_grad_ref[...], proj_ref[:, :width])


def heads_body(me_ref, n0_ref, n1_ref, n2_ref, n3_ref, proj_ref, part_ref, slope_ref):
    rows, width = n0_ref.shape
    me = me_ref[0]
    piece = width // 4
    cols = [proj_ref[:, pl.ds(pl.multiple_of(b * width + me * piece, LANES), piece)] for b in (1, 2, 3)]
    weight = jnp.concatenate(cols, axis=1)
    for step, ref in enumerate((n0_ref, n1_ref, n2_ref, n3_ref)):
        act, slope = silu_both(mm(ref[...], weight))
        at = pl.ds(pl.multiple_of((me ^ step) * rows, rows), rows)
        part_ref[at, :] = act.astype(BF16)
        slope_ref[at, :] = slope


def backward_body(
    me_ref, lengths_ref, g0_ref, g1_ref, g2_ref, g3_ref, part_ref, slope_ref, *rest
):
    outs, grad_ref, total_ref = rest[:4], rest[4], rest[5]
    rows, piece = g0_ref.shape
    me = me_ref[0]
    for step, ref in enumerate((g0_ref, g1_ref, g2_ref, g3_ref)):
        grad_ref[pl.ds(pl.multiple_of((me ^ step) * rows, rows), rows), :] = ref[...]
    total_ref[...] = jnp.zeros_like(total_ref)
    left = iota((1, LANES), 1) < LANES // 2
    blocks = len(outs)

    def visit(q_block, k_block):
        q_at, k_at = slice(q_block * rows, (q_block + 1) * rows), slice(k_block * rows, (k_block + 1) * rows)
        query_pos = q_block * rows + iota((1, rows), 1)
        start = history_start(query_pos, lengths_ref)
        key_pos = k_block * rows + iota((rows, 1), 0)
        inverse = 1.0 / (query_pos - start + 1).astype(F32)
        shared = jnp.where((key_pos >= start) & (key_pos <= query_pos), inverse, 0.0)
        value = part_ref[k_at, :piece]
        query = part_ref[q_at, piece : 2 * piece]
        key = part_ref[k_at, 2 * piece :]
        grad = grad_ref[q_at, :]
        small = value * jnp.asarray(0.0625, BF16)
        d_value, d_query, d_key = 0.0, 0.0, 0.0
        for mine in (left, ~left):
            query_h = jnp.where(mine, query, 0).astype(BF16)
            key_h = jnp.where(mine, key, 0).astype(BF16)
            grad_h = jnp.where(mine, grad, 0).astype(BF16)
            half = mm_t(key_h, query) * 0.0625
            up = 1.0 + jnp.tanh(half)
            act = half * up
            weights = (act * shared).astype(BF16)
            slope = (up + act * (2.0 - up)) * shared
            d_scores = (mm_t(small, grad_h) * slope).astype(BF16)
            d_value += mm(weights, grad_h)
            d_key += mm(d_scores, query_h)
            d_query += t_mm(d_scores, key_h)
        total_ref[k_at, :piece] += d_value
        total_ref[q_at, piece : 2 * piece] += d_query
        total_ref[k_at, 2 * piece :] += d_key

    for q_block in range(blocks):
        visit(q_block, q_block)
        for k_block in range(q_block):
            reach = history_start(q_block * rows, lengths_ref)

            @pl.when((k_block + 1) * rows > reach)
            def _():
                visit(q_block, k_block)

    for step, ref in enumerate(outs):
        at = pl.ds(pl.multiple_of((me ^ step) * rows, rows), rows)
        ref[...] = (total_ref[at, :] * slope_ref[at, :]).astype(BF16)


def weight_body(sources, pairs, dp_ref, *refs):
    normed, grads, sides = refs[:sources], refs[sources : 2 * sources], refs[2 * sources : 3 * sources]
    outs, total_ref = refs[3 * sources : -1], refs[-1]
    rows, piece = normed[0].shape[0], sides[0].shape[1]
    qkv, gate, outw = 0.0, 0.0, 0.0
    for n_ref, g_ref, s_ref in zip(normed, grads, sides):
        qkv += t_mm(n_ref[...], g_ref[...])
        gate += t_mm(n_ref[...], s_ref[:rows, :])
        outw += s_ref[rows:, :].astype(F32)
    total_ref[:, :piece] = gate
    total_ref[:, piece : 4 * piece] = qkv
    total_ref[:, 4 * piece :] = outw
    if len(outs) == 1:
        outs[0][...] = total_ref[...].astype(BF16)
        return
    kept_ref, sent_ref = outs
    half = kept_ref.shape[0]
    share = half // pairs
    for j in range(pairs):
        at = slice(j * share, (j + 1) * share)
        for ref, k in ((kept_ref, 2 * j), (sent_ref, 2 * j + 1)):
            source = pl.ds(pl.multiple_of((dp_ref[0] ^ k) * share, share), share)
            ref[at, :] = total_ref[source, :].astype(BF16)


def halve_body(pairs, kept_ref, came_ref, *refs):
    keep_ref, send_ref = refs[-2:]
    share = kept_ref.shape[0] // pairs
    for j in range(pairs):
        at = slice(j * share, (j + 1) * share)
        to = slice(j // 2 * share, (j // 2 + 1) * share)
        total = kept_ref[at, :].astype(F32) + came_ref[at, :].astype(F32)
        (send_ref if j % 2 else keep_ref)[to, :] = total.astype(BF16)


def input_body(
    blocks, me_ref, mask_ref, g0_ref, g1_ref, g2_ref, g3_ref,
    gate_in_ref, owned_ref, cot_ref, landing_ref, proj_ref, out_ref,
):
    rows, width = owned_ref.shape
    me = me_ref[0]
    piece = width // 4
    total = gate_in_ref[...]
    for step, ref in enumerate((g0_ref, g1_ref, g2_ref, g3_ref)):
        cols = [
            proj_ref[:, pl.ds(pl.multiple_of(b * width + (me ^ step) * piece, LANES), piece)] for b in (1, 2, 3)
        ]
        total += mm_t(ref[...], jnp.concatenate(cols, axis=1))
    centred, inv_scale = normalize(owned_ref[...].astype(F32))
    grad = (norm_back(total, centred, inv_scale) + cot_ref[...].astype(F32)).astype(BF16)
    select = hot(iota((rows, landing_ref.shape[1]), 0) + 1 == landing_ref[...])
    value = t_mm(select, grad)
    size = value.shape[0] // blocks
    for k in range(blocks):
        at = pl.ds(pl.multiple_of((mask_ref[0] ^ k) * size, size), size)
        out_ref[at, :] = value[k * size : (k + 1) * size].astype(BF16)


def return_body(capacity, owner_ref, back_ref, out_ref):
    owner = owner_ref[...]
    rank_row, _ = rank_rows(owner)
    chosen = hot(iota((back_ref.shape[0], owner.shape[1]), 0) == owner * capacity + rank_row)
    out_ref[...] = t_mm(chosen, back_ref[...]).astype(BF16)


def sum_body(*refs):
    total = 0.0
    for ref in refs[:-1]:
        parts = ref[...].astype(F32)
        total += parts if ref.ndim == 2 else jnp.sum(parts, axis=0)
    refs[-1][...] = total.astype(BF16)


def finish_body(me_ref, w0_ref, w1_ref, w2_ref, w3_ref, proj_ref, outw_ref):
    me = me_ref[0]
    width = outw_ref.shape[1]
    piece = width // 4
    for step, ref in enumerate((w0_ref, w1_ref, w2_ref, w3_ref)):
        for b in range(4):
            at = pl.ds(pl.multiple_of(b * width + (me ^ step) * piece, LANES), piece)
            proj_ref[:, at] = ref[:, b * piece : (b + 1) * piece].astype(F32)
        at = pl.ds(pl.multiple_of((me ^ step) * piece, LANES), piece)
        outw_ref[:, at] = ref[:, 4 * piece :].astype(F32)


def on_device(tokens, dest_owner, dest_slot, lengths, proj_weight, out_weight, cotangent):
    rows, width = tokens.shape
    owners = lax.axis_size("dp")
    cycle = lax.axis_size("ctx")
    assert cycle == 4 and width == cycle * LANES
    capacity = 2 * rows // owners
    stride = capacity + 8
    piece = width // cycle
    me = lax.axis_index("ctx").astype(jnp.int32).reshape(1)
    owner_row = dest_owner.reshape(1, rows)
    slot_row = dest_slot.reshape(1, rows)
    square = ((rows, width), BF16)

    def hop(value, step):
        return lax.ppermute(value, "ctx", [(i, i ^ step) for i in range(cycle)])

    def gather(value):
        near, far = hop(value, 1), hop(value, 2)
        return near, far, hop(far, 1)

    def exchange(values):
        return [values[0]] + [hop(values[step], step) for step in (2, 3, 1)]

    by_hops = owners <= 8
    blocks = owners if by_hops else 1
    dp = lax.axis_index("dp").astype(jnp.int32).reshape(1)
    mask = dp if by_hops else jnp.zeros_like(dp)

    def dp_hop(value, step):
        return lax.ppermute(value, "dp", [(i, i ^ step) for i in range(owners)])

    def swap_whole(value):
        split = value.reshape(owners, value.shape[0] // owners, value.shape[1])
        return lax.all_to_all(split, "dp", split_axis=0, concat_axis=0, tiled=True).reshape(value.shape)

    def swap(values):
        if by_hops:
            order = sorted(range(1, owners), key=lambda k: -k)
            moved = {k: dp_hop(values[k], k) for k in order}
            return [values[0]] + [moved[k] for k in range(1, owners)]
        return [swap_whole(values[0])]

    def block_shapes(height, columns, dtype):
        return [((owners * height // blocks, columns), dtype)] * blocks

    outgoing = call(
        functools.partial(pack_body, capacity, stride, blocks),
        "pack", block_shapes(stride, width, BF16), [mask], [], far=[owner_row, slot_row, tokens],
        scratch=[
            pltpu.VMEM((1, rows), jnp.int32),
            pltpu.VMEM((1, rows), jnp.int32),
            pltpu.VMEM((rows, width), BF16),
            pltpu.SemaphoreType.DMA((3,)),
        ],
    )
    arrived = swap(outgoing)
    owned, normed, landing = call(
        functools.partial(place_body, owners, capacity, stride),
        "place", [square, square, ((1, owners * capacity), jnp.int32)], [], arrived,
    )
    near, far, cross = gather(normed)
    wide = ((rows, width), F32)
    (grad_gated,) = call(early_body, "early", [wide], [], [cotangent, out_weight], flops=10**8)
    gate, slope, query, partial = call(
        own_body, "own_rows", [square, wide, square, wide],
        [me, lengths], [normed, proj_weight], flops=10**10, vmem=16,
    )
    (partial,) = call(
        middle_body, "middle", [wide], [me, lengths], [near, far, proj_weight, query, partial],
        flops=10**10, vmem=16,
    )
    layer_out, gated, gate_grad, *grad_pieces = call(
        forward_body, "forward",
        [square, square, square] + [((rows, piece), BF16)] * cycle,
        [me, lengths],
        [cross, proj_weight, out_weight, owned, gate, slope, query, partial, grad_gated],
        scratch=[pltpu.VMEM((rows, width), F32)], flops=10**10, vmem=16,
    )
    r0, r2, r3, r1 = exchange(grad_pieces)
    *sides, gate_in = call(
        side_body, "side", [((rows + width, piece), BF16)] * cycle + [((rows, width), F32)],
        [me], [gated, cotangent, gate_grad, proj_weight],
        scratch=[pltpu.VMEM((width, width), F32), pltpu.VMEM((rows, width), F32)], flops=10**10,
    )
    parts, slopes = call(
        heads_body, "heads",
        [((rows * cycle, 3 * piece), BF16), ((rows * cycle, 3 * piece), F32)],
        [me], [normed, near, far, cross, proj_weight], flops=10**10, vmem=16,
    )
    s0, s2, s3, s1 = exchange(sides)
    grads = call(
        backward_body, "backward", [((rows, 3 * piece), BF16)] * cycle,
        [me, lengths], [r0, r1, r2, r3, parts, slopes],
        scratch=[pltpu.VMEM((rows * cycle, piece), BF16), pltpu.VMEM((rows * cycle, 3 * piece), F32)],
        flops=4 * 10**10, vmem=16,
    )
    p0, p2, p3, p1 = exchange(grads)
    share = width // owners
    pairs = owners // 2
    half = ((pairs * share, 5 * piece), BF16)
    weight_parts = call(
        functools.partial(weight_body, cycle, pairs), "weights",
        [half, half] if by_hops else [((width, 5 * piece), BF16)], [dp],
        [normed, near, far, cross, *grads, s0, s1, s2, s3], flops=10**10, vmem=16,
        scratch=[pltpu.VMEM((width, 5 * piece), F32)],
    )
    if by_hops:
        kept, sent = weight_parts
        came = dp_hop(sent, 1)
    else:
        summed_parts = swap_whole(weight_parts[0])
        summed_parts = [summed_parts.reshape(owners, share, 5 * piece)]
    (back,) = call(
        functools.partial(input_body, blocks), "input_grad", [((owners * capacity, width), BF16)], [me, mask],
        [p0, p1, p2, p3, gate_in, owned, cotangent, landing, proj_weight], flops=2 * 10**10, vmem=16,
    )
    returned = swap_whole(back)
    if by_hops:
        behind, bit = [back], 2
        while bit < owners:
            kept, sent = call(
                functools.partial(halve_body, pairs), "halve",
                [((pairs * share // 2, 5 * piece), BF16)] * 2, [], [kept, came], far=behind,
            )
            came = dp_hop(sent, bit)
            behind, bit, pairs = [], 2 * bit, pairs // 2
        summed_parts = [kept, came]
    (mine,) = call(sum_body, "sum", [((share, 5 * piece), BF16)], [], summed_parts)
    w1, w2, w3 = (hop(mine, step) for step in range(1, cycle))
    (grad_tokens,) = call(
        functools.partial(return_body, capacity), "give_back", [square], [], [owner_row, returned]
    )
    grad_proj, grad_outw = call(
        finish_body, "finish", [((share, 4 * width), F32), ((share, width), F32)],
        [me], [mine, w1, w2, w3],
    )
    return layer_out, grad_tokens, grad_proj, grad_outw


def solution(mesh):
    placed = (
        P(("dp", "ctx"), None),
        P(("dp", "ctx")),
        P(("dp", "ctx")),
        P("dp", None),
        P(),
        P(),
        P(("dp", "ctx"), None),
    )
    return jax.shard_map(
        on_device,
        mesh=mesh,
        in_specs=placed,
        out_specs=(P(("dp", "ctx"), None), P(("dp", "ctx"), None), P("dp", None), P("dp", None)),
        check_vma=False,
    )
```

```python
import functools

import jax
import jax.numpy as jnp
from jax import lax
from jax.experimental import pallas as pl
from jax.experimental.pallas import tpu as pltpu
from jax.sharding import PartitionSpec as P

HEADS = 8
EPSILON = 1e-05
LANES = 128
F32 = jnp.float32
BF16 = jnp.bfloat16

WHOLE = pl.BlockSpec(memory_space=pltpu.VMEM)
SCALARS = pl.BlockSpec(memory_space=pltpu.SMEM)
ANYWHERE = pl.BlockSpec(memory_space=pltpu.HBM)


def call(body, name, outs, scalars, arrays, scratch=(), flops=10**8, vmem=8, far=()):
    return pl.pallas_call(
        body,
        name=name,
        out_shape=[jax.ShapeDtypeStruct(s, d) for s, d in outs],
        in_specs=[SCALARS] * len(scalars) + [WHOLE] * len(arrays) + [ANYWHERE] * len(far),
        out_specs=[WHOLE] * len(outs),
        scratch_shapes=list(scratch),
        compiler_params=pltpu.CompilerParams(vmem_limit_bytes=vmem * 2**20),
        cost_estimate=pl.CostEstimate(flops=flops, bytes_accessed=2**20, transcendentals=0),
    )(*scalars, *arrays, *far)


def iota(shape, dim):
    return lax.broadcasted_iota(jnp.int32, shape, dim)


def mm(a, b):
    return jnp.dot(a, b, preferred_element_type=F32)


def mm_t(a, b):
    return lax.dot_general(a, b, (((1,), (1,)), ((), ())), preferred_element_type=F32)


def t_mm(a, b):
    return lax.dot_general(a, b, (((0,), (0,)), ((), ())), preferred_element_type=F32)


def hot(condition):
    return jnp.where(condition, 1.0, 0.0).astype(BF16)


def normalize(value):
    middle = jnp.mean(value, axis=-1, keepdims=True)
    centred = value - middle
    inv_dev = lax.rsqrt(jnp.mean(centred * centred, axis=-1, keepdims=True) + EPSILON)
    return centred * inv_dev, inv_dev


def norm_back(grad, normed, inv_dev):
    return inv_dev * (
        grad
        - jnp.mean(grad, axis=-1, keepdims=True)
        - normed * jnp.mean(grad * normed, axis=-1, keepdims=True)
    )


def silu_both(value):
    squashed = 0.5 * jnp.tanh(0.5 * value) + 0.5
    return value * squashed, squashed * (1.0 + value * (1.0 - squashed))


def rank_rows(owner):
    rows = owner.shape[1]
    down, across = iota((rows, rows), 0), iota((rows, rows), 1)
    spread = jnp.broadcast_to(owner, (rows, rows))
    owner_col = jnp.sum(jnp.where(down == across, spread, 0).astype(F32), axis=1, keepdims=True)
    same = owner_col.astype(jnp.int32) == spread
    rank_row = jnp.sum(jnp.where(same & (down < across), 1.0, 0.0), axis=0, keepdims=True)
    rank_col = jnp.sum(jnp.where(same & (across < down), 1.0, 0.0), axis=1, keepdims=True)
    return rank_row.astype(jnp.int32), rank_col.astype(jnp.int32)


def fetch(sources, targets, sems):
    copies = [pltpu.make_async_copy(a, b, sems.at[i]) for i, (a, b) in enumerate(zip(sources, targets))]
    for copy in copies:
        copy.start()
    for copy in copies:
        copy.wait()


def store_blocks(refs, value):
    size = refs[0].shape[0]
    for i, ref in enumerate(refs):
        ref[...] = value[i * size : (i + 1) * size].astype(ref.dtype)


def load_blocks(refs):
    return jnp.concatenate([ref[...].astype(F32) for ref in refs], axis=0).astype(BF16)


def pack_body(capacity, stride, outs, mask_ref, owner_hbm, slot_hbm, tokens_hbm, *rest):
    out_refs, (owner_ref, slot_ref, tokens_ref, sems) = rest[:outs], rest[outs:]
    fetch((owner_hbm, slot_hbm, tokens_hbm), (owner_ref, slot_ref, tokens_ref), sems)
    owner = owner_ref[...] ^ mask_ref[0]
    rows = owner.shape[1]
    rank_row, rank_col = rank_rows(owner)
    total, width = outs * out_refs[0].shape[0], out_refs[0].shape[1]
    place = iota((total, rows), 0)
    chosen = hot(place == owner * stride + rank_row)
    slots = jnp.where(place == owner * stride + capacity, slot_ref[...] + 1, 0)
    by_rank = hot(rank_col == iota((rows, width), 1))
    store_blocks(out_refs, mm(chosen, tokens_ref[...]) + mm(slots.astype(F32).astype(BF16), by_rank))


def block_rem(owners, stride):
    col, first = iota((owners, owners * stride), 1), iota((owners, owners * stride), 0)
    above = jnp.sum(jnp.where(col >= stride * (first + 1), 1.0, 0.0), axis=0, keepdims=True)
    rem = iota((1, owners * stride), 1) - stride * above.astype(jnp.int32)
    inside = (col >= stride * first) & (col < stride * (first + 1))
    return rem, inside


def landing_row(table, owners, capacity, stride):
    rem, inside = block_rem(owners, stride)
    lanes = iota((table.shape[1], owners * stride), 0)
    spread = mm(table, hot((lanes == rem) & (lanes < capacity)))
    return jnp.sum(jnp.where(inside, spread, 0.0), axis=0, keepdims=True)


def place_body(owners, capacity, stride, *refs):
    owned_ref, normed_ref, landing_ref = refs[-3:]
    rows = owned_ref.shape[0]
    arrived = load_blocks(refs[:-3])
    total = arrived.shape[0]
    pick = hot(iota((owners, total), 1) == iota((owners, total), 0) * stride + capacity)
    table = mm(pick, arrived).astype(BF16)
    landing = landing_row(table, owners, capacity, stride).astype(jnp.int32)
    owned = mm(hot(iota((rows, total), 0) + 1 == landing), arrived)
    owned_ref[...] = owned.astype(BF16)
    normed_ref[...] = normalize(owned)[0].astype(BF16)
    landing_ref[...] = landing_row(table, owners, capacity, capacity).astype(jnp.int32)


def early_body(cot_ref, outw_ref, grad_ref):
    grad_ref[...] = mm_t(cot_ref[...], outw_ref[...])


def history_start(pos, lengths_ref):
    first = lengths_ref[0, 0]
    second = lengths_ref[0, 1]
    return jnp.where(pos >= first + second, first + second, jnp.where(pos >= first, first, 0))


def attend(query_ref, key, value, shared, acc_ref):
    width = query_ref.shape[1]
    left = iota((1, LANES), 1) < LANES // 2
    for pair in range(width // LANES):
        cols = slice(pair * LANES, (pair + 1) * LANES)
        query, key_pair, value_pair = query_ref[:, cols], key[:, cols], value[:, cols]
        total = acc_ref[:, cols]
        for mine in (left, ~left):
            half = mm_t(jnp.where(mine, query, 0).astype(BF16), key_pair) * 0.0625
            weights = (half * (1.0 + jnp.tanh(half)) * shared).astype(BF16)
            total += mm(weights, jnp.where(mine, value_pair, 0).astype(BF16))
        acc_ref[:, cols] = total


def shared_factor(block, me, rows, lengths_ref):
    query_pos = me * rows + iota((rows, 1), 0)
    start = history_start(query_pos, lengths_ref)
    inverse = 1.0 / (query_pos - start + 1).astype(F32)
    key_pos = block * rows + iota((1, rows), 1)
    return jnp.where((key_pos >= start) & (key_pos <= query_pos), inverse, 0.0)


def attend_other(step, me, lengths_ref, other_ref, proj_ref, query_ref, acc_ref):
    rows, width = query_ref.shape
    block = me ^ step
    reach = history_start(me * rows, lengths_ref)

    @pl.when((block < me) & ((block + 1) * rows > reach))
    def _():
        normed = other_ref[...]
        value = silu_both(mm(normed, proj_ref[:, width : 2 * width]))[0].astype(BF16)
        key = silu_both(mm(normed, proj_ref[:, 3 * width :]))[0].astype(BF16)
        attend(query_ref, key, value, shared_factor(block, me, rows, lengths_ref), acc_ref)


def own_body(me_ref, lengths_ref, normed_ref, proj_ref, gate_ref, slope_ref, query_ref, acc_ref):
    rows, width = normed_ref.shape
    me = me_ref[0]
    preact = mm(normed_ref[...], proj_ref[...])
    gate, slope = silu_both(preact[:, :width])
    gate_ref[...] = gate.astype(BF16)
    slope_ref[...] = slope
    value = silu_both(preact[:, width : 2 * width])[0].astype(BF16)
    query_ref[...] = silu_both(preact[:, 2 * width : 3 * width])[0].astype(BF16)
    key = silu_both(preact[:, 3 * width :])[0].astype(BF16)
    acc_ref[...] = jnp.zeros_like(acc_ref)
    attend(query_ref, key, value, shared_factor(me, me, rows, lengths_ref), acc_ref)


def middle_body(me_ref, lengths_ref, near_ref, far_ref, proj_ref, query_ref, partial_ref, acc_ref):
    me = me_ref[0]
    acc_ref[...] = partial_ref[...]
    attend_other(1, me, lengths_ref, near_ref, proj_ref, query_ref, acc_ref)
    attend_other(2, me, lengths_ref, far_ref, proj_ref, query_ref, acc_ref)


def forward_body(
    me_ref, lengths_ref, cross_ref, proj_ref, outw_ref, owned_ref,
    gate_ref, slope_ref, query_ref, partial_ref, grad_ref,
    out_ref, gated_ref, gate_grad_ref, *rest,
):
    grads, acc_ref = rest[:-1], rest[-1]
    rows, width = query_ref.shape
    me = me_ref[0]
    acc_ref[...] = partial_ref[...]
    attend_other(3, me, lengths_ref, cross_ref, proj_ref, query_ref, acc_ref)
    gate = gate_ref[...].astype(F32)
    normed, inv_dev = normalize(acc_ref[...])
    gated = (normed * gate).astype(BF16)
    gated_ref[...] = gated
    grad_gated = grad_ref[...]
    grad_attended = norm_back(grad_gated * gate, normed, inv_dev).astype(BF16)
    acc_ref[...] = grad_attended.astype(F32)
    piece = width // len(grads)
    for step, ref in enumerate(grads):
        ref[...] = acc_ref[:, pl.ds(pl.multiple_of((me ^ step) * piece, LANES), piece)].astype(BF16)
    out_ref[...] = (mm(gated, outw_ref[...]) + owned_ref[...].astype(F32)).astype(BF16)
    gate_grad_ref[...] = (grad_gated * normed * slope_ref[...]).astype(BF16)


def side_body(normed_ref, gated_ref, cot_ref, gate_grad_ref, proj_ref, part_ref, gate_in_ref):
    width = gated_ref.shape[1]
    gate_grad = gate_grad_ref[...]
    part_ref[:, :width] = t_mm(normed_ref[...], gate_grad).astype(BF16)
    part_ref[:, width:] = t_mm(gated_ref[...], cot_ref[...]).astype(BF16)
    gate_in_ref[...] = mm_t(gate_grad, proj_ref[:, :width])


def heads_body(me_ref, n0_ref, n1_ref, n2_ref, n3_ref, proj_ref, part_ref, slope_ref):
    rows, width = n0_ref.shape
    me = me_ref[0]
    piece = width // 4
    cols = [proj_ref[:, pl.ds(pl.multiple_of(b * width + me * piece, LANES), piece)] for b in (1, 2, 3)]
    weight = jnp.concatenate(cols, axis=1)
    for step, ref in enumerate((n0_ref, n1_ref, n2_ref, n3_ref)):
        act, slope = silu_both(mm(ref[...], weight))
        at = pl.ds(pl.multiple_of((me ^ step) * rows, rows), rows)
        part_ref[at, :] = act.astype(BF16)
        slope_ref[at, :] = slope


def backward_body(
    me_ref, lengths_ref, g0_ref, g1_ref, g2_ref, g3_ref, part_ref, slope_ref, *rest
):
    outs, (grad_ref, total_ref) = rest[-6:-2], rest[-2:]
    rows, piece = g0_ref.shape
    me = me_ref[0]
    for step, ref in enumerate((g0_ref, g1_ref, g2_ref, g3_ref)):
        grad_ref[pl.ds(pl.multiple_of((me ^ step) * rows, rows), rows), :] = ref[...]
    total_ref[...] = jnp.zeros_like(total_ref)
    left = iota((1, LANES), 1) < LANES // 2
    blocks = len(outs)

    def visit(q_block, k_block):
        q_at, k_at = slice(q_block * rows, (q_block + 1) * rows), slice(k_block * rows, (k_block + 1) * rows)
        query_pos = q_block * rows + iota((1, rows), 1)
        start = history_start(query_pos, lengths_ref)
        key_pos = k_block * rows + iota((rows, 1), 0)
        inverse = 1.0 / (query_pos - start + 1).astype(F32)
        shared = jnp.where((key_pos >= start) & (key_pos <= query_pos), inverse, 0.0)
        value = part_ref[k_at, :piece]
        query = part_ref[q_at, piece : 2 * piece]
        key = part_ref[k_at, 2 * piece :]
        grad = grad_ref[q_at, :]
        small = value * jnp.asarray(0.0625, BF16)
        d_value, d_query, d_key = 0.0, 0.0, 0.0
        for mine in (left, ~left):
            query_h = jnp.where(mine, query, 0).astype(BF16)
            key_h = jnp.where(mine, key, 0).astype(BF16)
            grad_h = jnp.where(mine, grad, 0).astype(BF16)
            half = mm_t(key_h, query) * 0.0625
            up = 1.0 + jnp.tanh(half)
            act = half * up
            weights = (act * shared).astype(BF16)
            slope = (up + act * (2.0 - up)) * shared
            d_scores = (mm_t(small, grad_h) * slope).astype(BF16)
            d_value += mm(weights, grad_h)
            d_key += mm(d_scores, query_h)
            d_query += t_mm(d_scores, key_h)
        total_ref[k_at, :piece] += d_value
        total_ref[q_at, piece : 2 * piece] += d_query
        total_ref[k_at, 2 * piece :] += d_key

    for q_block in range(blocks):
        visit(q_block, q_block)
        for k_block in range(q_block):
            reach = history_start(q_block * rows, lengths_ref)

            @pl.when((k_block + 1) * rows > reach)
            def _():
                visit(q_block, k_block)

    for step, ref in enumerate(outs):
        at = pl.ds(pl.multiple_of((me ^ step) * rows, rows), rows)
        ref[...] = (total_ref[at, :] * slope_ref[at, :]).astype(BF16)


def weight_body(sources, pairs, dp_ref, *refs):
    normed, grads = refs[:sources], refs[sources : 2 * sources]
    outs, total_ref = refs[2 * sources : -1], refs[-1]
    total = 0.0
    for n_ref, g_ref in zip(normed, grads):
        total += t_mm(n_ref[...], g_ref[...])
    if len(outs) == 1:
        outs[0][...] = total.astype(BF16)
        return
    total_ref[...] = total
    kept_ref, sent_ref = outs
    share = kept_ref.shape[0] // pairs
    for j in range(pairs):
        at = slice(j * share, (j + 1) * share)
        for ref, k in ((kept_ref, 2 * j), (sent_ref, 2 * j + 1)):
            source = pl.ds(pl.multiple_of((dp_ref[0] ^ k) * share, share), share)
            ref[at, :] = total_ref[source, :].astype(BF16)


def pair_body(kept_ref, came_ref, *outs):
    store_blocks(outs, kept_ref[...].astype(F32) + came_ref[...].astype(F32))


def input_body(
    blocks, me_ref, mask_ref, g0_ref, g1_ref, g2_ref, g3_ref,
    gate_in_ref, owned_ref, cot_ref, landing_ref, proj_ref, *rest,
):
    out_ref = rest[-1]
    rows, width = owned_ref.shape
    me = me_ref[0]
    piece = width // 4
    total = gate_in_ref[...]
    for step, ref in enumerate((g0_ref, g1_ref, g2_ref, g3_ref)):
        cols = [
            proj_ref[:, pl.ds(pl.multiple_of(b * width + (me ^ step) * piece, LANES), piece)] for b in (1, 2, 3)
        ]
        total += mm_t(ref[...], jnp.concatenate(cols, axis=1))
    centred, inv_scale = normalize(owned_ref[...].astype(F32))
    grad = (norm_back(total, centred, inv_scale) + cot_ref[...].astype(F32)).astype(BF16)
    select = hot(iota((rows, landing_ref.shape[1]), 0) + 1 == landing_ref[...])
    value = t_mm(select, grad)
    size = value.shape[0] // blocks
    for k in range(blocks):
        at = pl.ds(pl.multiple_of((mask_ref[0] ^ k) * size, size), size)
        out_ref[at, :] = value[k * size : (k + 1) * size].astype(BF16)


def return_body(capacity, owner_ref, back_ref, out_ref):
    owner = owner_ref[...]
    rank_row, _ = rank_rows(owner)
    chosen = hot(iota((back_ref.shape[0], owner.shape[1]), 0) == owner * capacity + rank_row)
    out_ref[...] = t_mm(chosen, back_ref[...]).astype(BF16)


def sum_body(*refs):
    total = 0.0
    for ref in refs[:-1]:
        parts = ref[...].astype(F32)
        total += parts if ref.ndim == 2 else jnp.sum(parts, axis=0)
    refs[-1][...] = total.astype(BF16)


def finish_body(me_ref, w0_ref, w1_ref, w2_ref, w3_ref, rest_ref, proj_ref, outw_ref):
    me = me_ref[0]
    width = outw_ref.shape[1]
    piece = width // 4
    proj_ref[:, :width] = rest_ref[:, :width].astype(F32)
    outw_ref[...] = rest_ref[:, width:].astype(F32)
    for step, ref in enumerate((w0_ref, w1_ref, w2_ref, w3_ref)):
        for b in range(3):
            at = pl.ds(pl.multiple_of((b + 1) * width + (me ^ step) * piece, LANES), piece)
            proj_ref[:, at] = ref[:, b * piece : (b + 1) * piece].astype(F32)


def on_device(tokens, dest_owner, dest_slot, lengths, proj_weight, out_weight, cotangent):
    rows, width = tokens.shape
    owners = lax.axis_size("dp")
    cycle = lax.axis_size("ctx")
    assert cycle == 4 and width == cycle * LANES
    capacity = 2 * rows // owners
    stride = capacity + 8
    piece = width // cycle
    me = lax.axis_index("ctx").astype(jnp.int32).reshape(1)
    owner_row = dest_owner.reshape(1, rows)
    slot_row = dest_slot.reshape(1, rows)
    square = ((rows, width), BF16)

    def hop(value, step):
        return lax.ppermute(value, "ctx", [(i, i ^ step) for i in range(cycle)])

    def gather(value):
        near, far = hop(value, 1), hop(value, 2)
        return near, far, hop(far, 1)

    def exchange(values):
        return [values[0]] + [hop(values[step], step) for step in (2, 3, 1)]

    by_hops = owners <= 8
    blocks = owners if by_hops else 1
    dp = lax.axis_index("dp").astype(jnp.int32).reshape(1)
    mask = dp if by_hops else jnp.zeros_like(dp)

    def dp_hop(value, step):
        return lax.ppermute(value, "dp", [(i, i ^ step) for i in range(owners)])

    def swap_whole(value):
        split = value.reshape(owners, value.shape[0] // owners, value.shape[1])
        return lax.all_to_all(split, "dp", split_axis=0, concat_axis=0, tiled=True).reshape(value.shape)

    def swap(values):
        if by_hops:
            order = sorted(range(1, owners), key=lambda k: -k)
            moved = {k: dp_hop(values[k], k) for k in order}
            return [values[0]] + [moved[k] for k in range(1, owners)]
        return [swap_whole(values[0])]

    def block_shapes(height, columns, dtype):
        return [((owners * height // blocks, columns), dtype)] * blocks

    outgoing = call(
        functools.partial(pack_body, capacity, stride, blocks),
        "pack", block_shapes(stride, width, BF16), [mask], [], far=[owner_row, slot_row, tokens],
        scratch=[
            pltpu.VMEM((1, rows), jnp.int32),
            pltpu.VMEM((1, rows), jnp.int32),
            pltpu.VMEM((rows, width), BF16),
            pltpu.SemaphoreType.DMA((3,)),
        ],
    )
    arrived = swap(outgoing)
    owned, normed, landing = call(
        functools.partial(place_body, owners, capacity, stride),
        "place", [square, square, ((1, owners * capacity), jnp.int32)], [], arrived,
    )
    near, far, cross = gather(normed)
    wide = ((rows, width), F32)
    (grad_gated,) = call(early_body, "early", [wide], [], [cotangent, out_weight], flops=10**8)
    gate, slope, query, partial = call(
        own_body, "own_rows", [square, wide, square, wide],
        [me, lengths], [normed, proj_weight], flops=10**10, vmem=16,
    )
    (partial,) = call(
        middle_body, "middle", [wide], [me, lengths], [near, far, proj_weight, query, partial],
        flops=10**10, vmem=16,
    )
    layer_out, gated, gate_grad, *grad_pieces = call(
        forward_body, "forward",
        [square, square, square] + [((rows, piece), BF16)] * cycle,
        [me, lengths],
        [cross, proj_weight, out_weight, owned, gate, slope, query, partial, grad_gated],
        scratch=[pltpu.VMEM((rows, width), F32)], flops=10**10, vmem=16,
    )
    r0, r2, r3, r1 = exchange(grad_pieces)
    side_part, gate_in = call(
        side_body, "side", [((width, 2 * width), BF16), wide],
        [], [normed, gated, cotangent, gate_grad, proj_weight], flops=10**10,
    )
    side_sum = lax.psum(lax.psum_scatter(side_part, "dp", scatter_dimension=0, tiled=True), "ctx")
    parts, slopes = call(
        heads_body, "heads",
        [((rows * cycle, 3 * piece), BF16), ((rows * cycle, 3 * piece), F32)],
        [me], [normed, near, far, cross, proj_weight], flops=10**10, vmem=16,
    )
    grads = call(
        backward_body, "backward", [((rows, 3 * piece), BF16)] * cycle,
        [me, lengths], [r0, r1, r2, r3, parts, slopes],
        scratch=[pltpu.VMEM((rows * cycle, piece), BF16), pltpu.VMEM((rows * cycle, 3 * piece), F32)],
        flops=4 * 10**10, vmem=16, far=[side_part],
    )
    p0, p2, p3, p1 = exchange(grads)
    share = width // owners
    pairs = owners // 2
    columns = 3 * piece
    weight_parts = call(
        functools.partial(weight_body, cycle, pairs), "weights",
        [((pairs * share, columns), BF16)] * 2 if by_hops else [((width, columns), BF16)], [dp],
        [normed, near, far, cross, *grads], flops=10**10, vmem=16,
        scratch=[pltpu.VMEM((width, columns), F32)],
    )
    if by_hops:
        kept, sent = weight_parts
        halves = call(
            pair_body, "pair_sum", [((share, columns), BF16)] * pairs, [], [kept, dp_hop(sent, 1)]
        )
        summed_parts = [halves[0]] + [dp_hop(halves[j], 2 * j) for j in range(1, pairs)]
    else:
        halves = weight_parts
        summed_parts = [swap_whole(weight_parts[0]).reshape(owners, share, columns)]
    (back,) = call(
        functools.partial(input_body, blocks), "input_grad", [((owners * capacity, width), BF16)], [me, mask],
        [p0, p1, p2, p3, gate_in, owned, cotangent, landing, proj_weight], flops=2 * 10**10, vmem=16,
        far=[halves[0]],
    )
    returned = swap_whole(back)
    (mine,) = call(sum_body, "sum", [((share, columns), BF16)], [], summed_parts)
    w1, w2, w3 = (hop(mine, step) for step in range(1, cycle))
    (grad_tokens,) = call(
        functools.partial(return_body, capacity), "give_back", [square], [], [owner_row, returned]
    )
    grad_proj, grad_outw = call(
        finish_body, "finish", [((share, 4 * width), F32), ((share, width), F32)],
        [me], [mine, w1, w2, w3, side_sum],
    )
    return layer_out, grad_tokens, grad_proj, grad_outw


def solution(mesh):
    placed = (
        P(("dp", "ctx"), None),
        P(("dp", "ctx")),
        P(("dp", "ctx")),
        P("dp", None),
        P(),
        P(),
        P(("dp", "ctx"), None),
    )
    return jax.shard_map(
        on_device,
        mesh=mesh,
        in_specs=placed,
        out_specs=(P(("dp", "ctx"), None), P(("dp", "ctx"), None), P("dp", None), P("dp", None)),
        check_vma=False,
    )
```

```python
import functools

import jax
import jax.numpy as jnp
from jax import lax
from jax.experimental import pallas as pl
from jax.experimental.pallas import tpu as pltpu
from jax.sharding import PartitionSpec as P

HEADS = 8
EPSILON = 1e-05
LANES = 128
F32 = jnp.float32
BF16 = jnp.bfloat16

WHOLE = pl.BlockSpec(memory_space=pltpu.VMEM)
SCALARS = pl.BlockSpec(memory_space=pltpu.SMEM)
ANYWHERE = pl.BlockSpec(memory_space=pltpu.HBM)


def call(body, name, outs, scalars, arrays, scratch=(), flops=10**8, vmem=8, far=()):
    return pl.pallas_call(
        body,
        name=name,
        out_shape=[jax.ShapeDtypeStruct(s, d) for s, d in outs],
        in_specs=[SCALARS] * len(scalars) + [WHOLE] * len(arrays) + [ANYWHERE] * len(far),
        out_specs=[WHOLE] * len(outs),
        scratch_shapes=list(scratch),
        compiler_params=pltpu.CompilerParams(vmem_limit_bytes=vmem * 2**20),
        cost_estimate=pl.CostEstimate(flops=flops, bytes_accessed=2**20, transcendentals=0),
    )(*scalars, *arrays, *far)


def iota(shape, dim):
    return lax.broadcasted_iota(jnp.int32, shape, dim)


def mm(a, b):
    return jnp.dot(a, b, preferred_element_type=F32)


def mm_t(a, b):
    return lax.dot_general(a, b, (((1,), (1,)), ((), ())), preferred_element_type=F32)


def t_mm(a, b):
    return lax.dot_general(a, b, (((0,), (0,)), ((), ())), preferred_element_type=F32)


def hot(condition):
    return jnp.where(condition, 1.0, 0.0).astype(BF16)


def normalize(value):
    middle = jnp.mean(value, axis=-1, keepdims=True)
    centred = value - middle
    inv_dev = lax.rsqrt(jnp.mean(centred * centred, axis=-1, keepdims=True) + EPSILON)
    return centred * inv_dev, inv_dev


def norm_back(grad, normed, inv_dev):
    return inv_dev * (
        grad
        - jnp.mean(grad, axis=-1, keepdims=True)
        - normed * jnp.mean(grad * normed, axis=-1, keepdims=True)
    )


def silu_both(value):
    squashed = 0.5 * jnp.tanh(0.5 * value) + 0.5
    return value * squashed, squashed * (1.0 + value * (1.0 - squashed))


def rank_rows(owner):
    rows = owner.shape[1]
    down, across = iota((rows, rows), 0), iota((rows, rows), 1)
    spread = jnp.broadcast_to(owner, (rows, rows))
    owner_col = jnp.sum(jnp.where(down == across, spread, 0).astype(F32), axis=1, keepdims=True)
    same = owner_col.astype(jnp.int32) == spread
    rank_row = jnp.sum(jnp.where(same & (down < across), 1.0, 0.0), axis=0, keepdims=True)
    rank_col = jnp.sum(jnp.where(same & (across < down), 1.0, 0.0), axis=1, keepdims=True)
    return rank_row.astype(jnp.int32), rank_col.astype(jnp.int32)


def fetch(sources, targets, sems):
    copies = [pltpu.make_async_copy(a, b, sems.at[i]) for i, (a, b) in enumerate(zip(sources, targets))]
    for copy in copies:
        copy.start()
    for copy in copies:
        copy.wait()


def store_blocks(refs, value):
    size = refs[0].shape[0]
    for i, ref in enumerate(refs):
        ref[...] = value[i * size : (i + 1) * size].astype(ref.dtype)


def load_blocks(refs):
    return jnp.concatenate([ref[...].astype(F32) for ref in refs], axis=0).astype(BF16)


def pack_body(capacity, stride, outs, mask_ref, owner_hbm, slot_hbm, tokens_hbm, *rest):
    out_refs, (owner_ref, slot_ref, tokens_ref, sems) = rest[:outs], rest[outs:]
    fetch((owner_hbm, slot_hbm, tokens_hbm), (owner_ref, slot_ref, tokens_ref), sems)
    owner = owner_ref[...] ^ mask_ref[0]
    rows = owner.shape[1]
    rank_row, rank_col = rank_rows(owner)
    total, width = outs * out_refs[0].shape[0], out_refs[0].shape[1]
    place = iota((total, rows), 0)
    chosen = hot(place == owner * stride + rank_row)
    slots = jnp.where(place == owner * stride + capacity, slot_ref[...] + 1, 0)
    by_rank = hot(rank_col == iota((rows, width), 1))
    store_blocks(out_refs, mm(chosen, tokens_ref[...]) + mm(slots.astype(F32).astype(BF16), by_rank))


def block_rem(owners, stride):
    col, first = iota((owners, owners * stride), 1), iota((owners, owners * stride), 0)
    above = jnp.sum(jnp.where(col >= stride * (first + 1), 1.0, 0.0), axis=0, keepdims=True)
    rem = iota((1, owners * stride), 1) - stride * above.astype(jnp.int32)
    inside = (col >= stride * first) & (col < stride * (first + 1))
    return rem, inside


def landing_row(table, owners, capacity, stride):
    rem, inside = block_rem(owners, stride)
    lanes = iota((table.shape[1], owners * stride), 0)
    spread = mm(table, hot((lanes == rem) & (lanes < capacity)))
    return jnp.sum(jnp.where(inside, spread, 0.0), axis=0, keepdims=True)


def place_body(owners, capacity, stride, *refs):
    owned_ref, normed_ref, landing_ref = refs[-3:]
    rows = owned_ref.shape[0]
    arrived = load_blocks(refs[:-3])
    total = arrived.shape[0]
    pick = hot(iota((owners, total), 1) == iota((owners, total), 0) * stride + capacity)
    table = mm(pick, arrived).astype(BF16)
    landing = landing_row(table, owners, capacity, stride).astype(jnp.int32)
    owned = mm(hot(iota((rows, total), 0) + 1 == landing), arrived)
    owned_ref[...] = owned.astype(BF16)
    normed_ref[...] = normalize(owned)[0].astype(BF16)
    landing_ref[...] = landing_row(table, owners, capacity, capacity).astype(jnp.int32)


def early_body(cot_ref, outw_ref, grad_ref):
    grad_ref[...] = mm_t(cot_ref[...], outw_ref[...])


def history_start(pos, lengths_ref):
    first = lengths_ref[0, 0]
    second = lengths_ref[0, 1]
    return jnp.where(pos >= first + second, first + second, jnp.where(pos >= first, first, 0))


def attend(query_ref, key, value, shared, acc_ref):
    width = query_ref.shape[1]
    left = iota((1, LANES), 1) < LANES // 2
    for pair in range(width // LANES):
        cols = slice(pair * LANES, (pair + 1) * LANES)
        query, key_pair, value_pair = query_ref[:, cols], key[:, cols], value[:, cols]
        total = acc_ref[:, cols]
        for mine in (left, ~left):
            half = mm_t(jnp.where(mine, query, 0).astype(BF16), key_pair) * 0.0625
            weights = (half * (1.0 + jnp.tanh(half)) * shared).astype(BF16)
            total += mm(weights, jnp.where(mine, value_pair, 0).astype(BF16))
        acc_ref[:, cols] = total


def shared_factor(block, me, rows, lengths_ref):
    query_pos = me * rows + iota((rows, 1), 0)
    start = history_start(query_pos, lengths_ref)
    inverse = 1.0 / (query_pos - start + 1).astype(F32)
    key_pos = block * rows + iota((1, rows), 1)
    return jnp.where((key_pos >= start) & (key_pos <= query_pos), inverse, 0.0)


def attend_other(step, me, lengths_ref, other_ref, proj_ref, query_ref, acc_ref):
    rows, width = query_ref.shape
    block = me ^ step
    reach = history_start(me * rows, lengths_ref)

    @pl.when((block < me) & ((block + 1) * rows > reach))
    def _():
        normed = other_ref[...]
        value = silu_both(mm(normed, proj_ref[:, width : 2 * width]))[0].astype(BF16)
        key = silu_both(mm(normed, proj_ref[:, 3 * width :]))[0].astype(BF16)
        attend(query_ref, key, value, shared_factor(block, me, rows, lengths_ref), acc_ref)


def own_body(me_ref, lengths_ref, normed_ref, proj_ref, gate_ref, slope_ref, query_ref, acc_ref):
    rows, width = normed_ref.shape
    me = me_ref[0]
    preact = mm(normed_ref[...], proj_ref[...])
    gate, slope = silu_both(preact[:, :width])
    gate_ref[...] = gate.astype(BF16)
    slope_ref[...] = slope
    value = silu_both(preact[:, width : 2 * width])[0].astype(BF16)
    query_ref[...] = silu_both(preact[:, 2 * width : 3 * width])[0].astype(BF16)
    key = silu_both(preact[:, 3 * width :])[0].astype(BF16)
    acc_ref[...] = jnp.zeros_like(acc_ref)
    attend(query_ref, key, value, shared_factor(me, me, rows, lengths_ref), acc_ref)


def middle_body(me_ref, lengths_ref, near_ref, far_ref, proj_ref, query_ref, partial_ref, acc_ref):
    me = me_ref[0]
    acc_ref[...] = partial_ref[...]
    attend_other(1, me, lengths_ref, near_ref, proj_ref, query_ref, acc_ref)
    attend_other(2, me, lengths_ref, far_ref, proj_ref, query_ref, acc_ref)


def forward_body(
    me_ref, lengths_ref, cross_ref, proj_ref, outw_ref, owned_ref,
    gate_ref, slope_ref, query_ref, partial_ref, grad_ref,
    out_ref, gated_ref, gate_grad_ref, *rest,
):
    grads, acc_ref = rest[:-1], rest[-1]
    rows, width = query_ref.shape
    me = me_ref[0]
    acc_ref[...] = partial_ref[...]
    attend_other(3, me, lengths_ref, cross_ref, proj_ref, query_ref, acc_ref)
    gate = gate_ref[...].astype(F32)
    normed, inv_dev = normalize(acc_ref[...])
    gated = (normed * gate).astype(BF16)
    gated_ref[...] = gated
    grad_gated = grad_ref[...]
    grad_attended = norm_back(grad_gated * gate, normed, inv_dev).astype(BF16)
    acc_ref[...] = grad_attended.astype(F32)
    piece = width // len(grads)
    for step, ref in enumerate(grads):
        ref[...] = acc_ref[:, pl.ds(pl.multiple_of((me ^ step) * piece, LANES), piece)].astype(BF16)
    out_ref[...] = (mm(gated, outw_ref[...]) + owned_ref[...].astype(F32)).astype(BF16)
    gate_grad_ref[...] = (grad_gated * normed * slope_ref[...]).astype(BF16)


def side_body(me_ref, normed_ref, gated_ref, cot_ref, gate_grad_ref, proj_ref, kept_ref, sent_ref, gate_in_ref, part_ref):
    width = gated_ref.shape[1]
    me = me_ref[0]
    gate_grad = gate_grad_ref[...]
    part_ref[:, :width] = t_mm(normed_ref[...], gate_grad)
    part_ref[:, width:] = t_mm(gated_ref[...], cot_ref[...])
    gate_in_ref[...] = mm_t(gate_grad, proj_ref[:, :width])
    for ref, steps in ((kept_ref, (0, 2)), (sent_ref, (1, 3))):
        place = 0
        for step in steps:
            for base in (0, width):
                source = pl.ds(pl.multiple_of(base + (me ^ step) * LANES, LANES), LANES)
                ref[:, place : place + LANES] = part_ref[:, source].astype(BF16)
                place += LANES


def side_sum_body(kept_ref, came_ref, keep_ref, send_ref):
    total = kept_ref[...].astype(F32) + came_ref[...].astype(F32)
    half = total.shape[1] // 2
    keep_ref[...] = total[:, :half].astype(BF16)
    send_ref[...] = total[:, half:].astype(BF16)


def heads_body(me_ref, n0_ref, n1_ref, n2_ref, n3_ref, proj_ref, part_ref, slope_ref):
    rows, width = n0_ref.shape
    me = me_ref[0]
    piece = width // 4
    cols = [proj_ref[:, pl.ds(pl.multiple_of(b * width + me * piece, LANES), piece)] for b in (1, 2, 3)]
    weight = jnp.concatenate(cols, axis=1)
    for step, ref in enumerate((n0_ref, n1_ref, n2_ref, n3_ref)):
        act, slope = silu_both(mm(ref[...], weight))
        at = pl.ds(pl.multiple_of((me ^ step) * rows, rows), rows)
        part_ref[at, :] = act.astype(BF16)
        slope_ref[at, :] = slope


def block_at(block, rows):
    return pl.ds(pl.multiple_of(block * rows, rows), rows)


def visit(first, second, same, lengths_ref, part_ref, grad_ref, total_ref):
    rows, piece = grad_ref.shape[0] // 4, grad_ref.shape[1]
    q_block, k_block = jnp.maximum(first, second), jnp.minimum(first, second)

    def work():
        q_at, k_at = block_at(q_block, rows), block_at(k_block, rows)
        left = iota((1, LANES), 1) < LANES // 2
        query_pos = q_block * rows + iota((1, rows), 1)
        start = history_start(query_pos, lengths_ref)
        key_pos = k_block * rows + iota((rows, 1), 0)
        inverse = 1.0 / (query_pos - start + 1).astype(F32)
        shared = jnp.where((key_pos >= start) & (key_pos <= query_pos), inverse, 0.0)
        value = part_ref[k_at, :piece]
        query = part_ref[q_at, piece : 2 * piece]
        key = part_ref[k_at, 2 * piece :]
        grad = grad_ref[q_at, :]
        small = value * jnp.asarray(0.0625, BF16)
        d_value, d_query, d_key = 0.0, 0.0, 0.0
        for mine in (left, ~left):
            query_h = jnp.where(mine, query, 0).astype(BF16)
            key_h = jnp.where(mine, key, 0).astype(BF16)
            grad_h = jnp.where(mine, grad, 0).astype(BF16)
            half = mm_t(key_h, query) * 0.0625
            up = 1.0 + jnp.tanh(half)
            act = half * up
            weights = (act * shared).astype(BF16)
            slope = (up + act * (2.0 - up)) * shared
            d_scores = (mm_t(small, grad_h) * slope).astype(BF16)
            d_value += mm(weights, grad_h)
            d_key += mm(d_scores, query_h)
            d_query += t_mm(d_scores, key_h)
        total_ref[k_at, :piece] += d_value
        total_ref[q_at, piece : 2 * piece] += d_query
        total_ref[k_at, 2 * piece :] += d_key

    if same:
        work()
    else:
        pl.when((k_block + 1) * rows > history_start(q_block * rows, lengths_ref))(work)


def backward_rows(steps, finished, me, lengths_ref, part_ref, slope_ref, grad_ref, total_ref, refs):
    done = list(finished)
    for step, ref in zip(steps, refs):
        for other in range(4):
            if other not in done:
                visit(me ^ step, me ^ other, other == step, lengths_ref, part_ref, grad_ref, total_ref)
        done.append(step)
        at = block_at(me ^ step, ref.shape[0])
        ref[...] = (total_ref[at, :] * slope_ref[at, :]).astype(BF16)


def backward_far_body(
    me_ref, lengths_ref, g0_ref, g1_ref, g2_ref, g3_ref, part_ref, slope_ref, *rest
):
    o2_ref, o3_ref, total_ref, grad_ref = rest[-4:]
    rows = g0_ref.shape[0]
    me = me_ref[0]
    for step, ref in enumerate((g0_ref, g1_ref, g2_ref, g3_ref)):
        grad_ref[block_at(me ^ step, rows), :] = ref[...]
    total_ref[...] = jnp.zeros_like(total_ref)
    backward_rows(
        (2, 3), (), me, lengths_ref, part_ref, slope_ref, grad_ref, total_ref, (o2_ref, o3_ref)
    )


def backward_rest_body(
    me_ref, lengths_ref, part_ref, slope_ref, grad_ref, sums_ref, o0_ref, o1_ref, total_ref
):
    total_ref[...] = sums_ref[...]
    backward_rows(
        (1, 0), (2, 3), me_ref[0], lengths_ref, part_ref, slope_ref, grad_ref, total_ref, (o1_ref, o0_ref)
    )


def relay(value, after):
    return pl.pallas_call(
        lambda *refs: None,
        name="relay",
        out_shape=jax.ShapeDtypeStruct(value.shape, value.dtype),
        in_specs=[ANYWHERE] * (1 + len(after)),
        out_specs=ANYWHERE,
        input_output_aliases={0: 0},
    )(value, *after)


def weight_body(sources, pairs, dp_ref, kept_side_ref, came_side_ref, *refs):
    normed, grads = refs[:sources], refs[sources : 2 * sources]
    outs, total_ref = refs[2 * sources : -1], refs[-1]
    side = kept_side_ref.shape[1]
    total = 0.0
    for n_ref, g_ref in zip(normed, grads):
        total += t_mm(n_ref[...], g_ref[...])
    total_ref[:, :side] = kept_side_ref[...].astype(F32) + came_side_ref[...].astype(F32)
    total_ref[:, side:] = total
    if len(outs) == 1:
        outs[0][...] = total_ref[...].astype(BF16)
        return
    kept_ref, sent_ref = outs
    share = kept_ref.shape[0] // pairs
    for j in range(pairs):
        at = slice(j * share, (j + 1) * share)
        for ref, k in ((kept_ref, 2 * j), (sent_ref, 2 * j + 1)):
            source = pl.ds(pl.multiple_of((dp_ref[0] ^ k) * share, share), share)
            ref[at, :] = total_ref[source, :].astype(BF16)


def pair_body(kept_ref, came_ref, *outs):
    store_blocks(outs, kept_ref[...].astype(F32) + came_ref[...].astype(F32))


def input_body(
    blocks, me_ref, mask_ref, g0_ref, g1_ref, g2_ref, g3_ref,
    gate_in_ref, owned_ref, cot_ref, landing_ref, proj_ref, *rest,
):
    out_ref = rest[-1]
    rows, width = owned_ref.shape
    me = me_ref[0]
    piece = width // 4
    total = gate_in_ref[...]
    for step, ref in enumerate((g0_ref, g1_ref, g2_ref, g3_ref)):
        cols = [
            proj_ref[:, pl.ds(pl.multiple_of(b * width + (me ^ step) * piece, LANES), piece)] for b in (1, 2, 3)
        ]
        total += mm_t(ref[...], jnp.concatenate(cols, axis=1))
    centred, inv_scale = normalize(owned_ref[...].astype(F32))
    grad = (norm_back(total, centred, inv_scale) + cot_ref[...].astype(F32)).astype(BF16)
    select = hot(iota((rows, landing_ref.shape[1]), 0) + 1 == landing_ref[...])
    value = t_mm(select, grad)
    size = value.shape[0] // blocks
    for k in range(blocks):
        at = pl.ds(pl.multiple_of((mask_ref[0] ^ k) * size, size), size)
        out_ref[at, :] = value[k * size : (k + 1) * size].astype(BF16)


def return_body(capacity, owner_ref, back_ref, out_ref):
    owner = owner_ref[...]
    rank_row, _ = rank_rows(owner)
    chosen = hot(iota((back_ref.shape[0], owner.shape[1]), 0) == owner * capacity + rank_row)
    out_ref[...] = t_mm(chosen, back_ref[...]).astype(BF16)


def sum_body(*refs):
    total = 0.0
    for ref in refs[:-1]:
        parts = ref[...].astype(F32)
        total += parts if ref.ndim == 2 else jnp.sum(parts, axis=0)
    refs[-1][...] = total.astype(BF16)


def finish_body(me_ref, w0_ref, w1_ref, w2_ref, w3_ref, proj_ref, outw_ref):
    me = me_ref[0]
    width = outw_ref.shape[1]
    for step, ref in enumerate((w0_ref, w1_ref, w2_ref, w3_ref)):
        at = pl.ds(pl.multiple_of((me ^ step) * LANES, LANES), LANES)
        outw_ref[:, at] = ref[:, LANES : 2 * LANES].astype(F32)
        for b, source in enumerate((0, 2, 3, 4)):
            at = pl.ds(pl.multiple_of(b * width + (me ^ step) * LANES, LANES), LANES)
            proj_ref[:, at] = ref[:, source * LANES : (source + 1) * LANES].astype(F32)


def on_device(tokens, dest_owner, dest_slot, lengths, proj_weight, out_weight, cotangent):
    rows, width = tokens.shape
    owners = lax.axis_size("dp")
    cycle = lax.axis_size("ctx")
    assert cycle == 4 and width == cycle * LANES
    capacity = 2 * rows // owners
    stride = capacity + 8
    piece = width // cycle
    me = lax.axis_index("ctx").astype(jnp.int32).reshape(1)
    owner_row = dest_owner.reshape(1, rows)
    slot_row = dest_slot.reshape(1, rows)
    square = ((rows, width), BF16)

    def hop(value, step):
        return lax.ppermute(value, "ctx", [(i, i ^ step) for i in range(cycle)])

    def gather(value):
        near, far = hop(value, 1), hop(value, 2)
        return near, far, hop(far, 1)

    def exchange(values):
        return [values[0]] + [hop(values[step], step) for step in (2, 3, 1)]

    by_hops = owners <= 8
    blocks = owners if by_hops else 1
    dp = lax.axis_index("dp").astype(jnp.int32).reshape(1)
    mask = dp if by_hops else jnp.zeros_like(dp)

    def dp_hop(value, step):
        return lax.ppermute(value, "dp", [(i, i ^ step) for i in range(owners)])

    def swap_whole(value):
        split = value.reshape(owners, value.shape[0] // owners, value.shape[1])
        return lax.all_to_all(split, "dp", split_axis=0, concat_axis=0, tiled=True).reshape(value.shape)

    def swap(values):
        if by_hops:
            order = sorted(range(1, owners), key=lambda k: -k)
            moved = {k: dp_hop(values[k], k) for k in order}
            return [values[0]] + [moved[k] for k in range(1, owners)]
        return [swap_whole(values[0])]

    def block_shapes(height, columns, dtype):
        return [((owners * height // blocks, columns), dtype)] * blocks

    outgoing = call(
        functools.partial(pack_body, capacity, stride, blocks),
        "pack", block_shapes(stride, width, BF16), [mask], [], far=[owner_row, slot_row, tokens],
        scratch=[
            pltpu.VMEM((1, rows), jnp.int32),
            pltpu.VMEM((1, rows), jnp.int32),
            pltpu.VMEM((rows, width), BF16),
            pltpu.SemaphoreType.DMA((3,)),
        ],
    )
    arrived = swap(outgoing)
    owned, normed, landing = call(
        functools.partial(place_body, owners, capacity, stride),
        "place", [square, square, ((1, owners * capacity), jnp.int32)], [], arrived,
    )
    near, far, cross = gather(normed)
    wide = ((rows, width), F32)
    (grad_gated,) = call(early_body, "early", [wide], [], [cotangent, out_weight], flops=10**8)
    gate, slope, query, partial = call(
        own_body, "own_rows", [square, wide, square, wide],
        [me, lengths], [normed, proj_weight], flops=10**10, vmem=16,
    )
    (partial,) = call(
        middle_body, "middle", [wide], [me, lengths], [near, far, proj_weight, query, partial],
        vmem=16,
    )
    layer_out, gated, gate_grad, *grad_pieces = call(
        forward_body, "forward",
        [square, square, square] + [((rows, piece), BF16)] * cycle,
        [me, lengths],
        [cross, proj_weight, out_weight, owned, gate, slope, query, partial, grad_gated],
        scratch=[pltpu.VMEM((rows, width), F32)], vmem=16,
    )
    r0, r2, r3, r1 = exchange(grad_pieces)
    side_half = ((width, 4 * piece), BF16)
    side_piece = ((width, 2 * piece), BF16)
    side_kept, side_sent, gate_in = call(
        side_body, "side", [side_half, side_half, wide],
        [me], [normed, gated, cotangent, gate_grad, proj_weight],
        scratch=[pltpu.VMEM((width, 2 * width), F32)], vmem=16,
    )
    side_came = hop(side_sent, 1)
    parts, slopes = call(
        heads_body, "heads",
        [((rows * cycle, 3 * piece), BF16), ((rows * cycle, 3 * piece), F32)],
        [me], [normed, near, far, cross, proj_weight], vmem=16,
    )
    side_keep, side_send = call(
        side_sum_body, "side_sum", [side_piece, side_piece], [], [side_kept, side_came]
    )
    side_last = hop(side_send, 2)
    grad_block = ((rows, 3 * piece), BF16)
    sums = ((rows * cycle, 3 * piece), F32)
    grad_rows = ((rows * cycle, piece), BF16)
    far_block, cross_block, totals, grad_all = call(
        backward_far_body, "backward_far", [grad_block, grad_block, sums, grad_rows],
        [me, lengths], [r0, r1, r2, r3, parts, slopes], vmem=16, far=[side_send],
    )
    p2, p3 = hop(far_block, 2), hop(cross_block, 3)
    own_block, near_block = call(
        backward_rest_body, "backward_rest", [grad_block] * 2,
        [me, lengths], [parts, slopes, grad_all, totals], vmem=16,
        scratch=[pltpu.VMEM(*sums)],
    )
    p1 = hop(near_block, 1)
    p0, grads = own_block, [own_block, near_block, far_block, cross_block]
    share = width // owners
    pairs = owners // 2
    columns = 5 * piece
    weight_parts = call(
        functools.partial(weight_body, cycle, pairs), "weights",
        [((pairs * share, columns), BF16)] * 2 if by_hops else [((width, columns), BF16)], [dp],
        [side_keep, side_last, normed, near, far, cross, *grads], vmem=16,
        scratch=[pltpu.VMEM((width, columns), F32)],
    )
    if by_hops:
        kept, sent = weight_parts
        halves = call(
            pair_body, "pair_sum", [((share, columns), BF16)] * pairs, [], [kept, dp_hop(relay(sent, [p2, p3]), 1)]
        )
        summed_parts = [halves[0]] + [dp_hop(halves[j], 2 * j) for j in range(1, pairs)]
    else:
        halves = weight_parts
        summed_parts = [swap_whole(weight_parts[0]).reshape(owners, share, columns)]
    (back,) = call(
        functools.partial(input_body, blocks), "input_grad", [((owners * capacity, width), BF16)], [me, mask],
        [p0, p1, p2, p3, gate_in, owned, cotangent, landing, proj_weight], vmem=16,
    )
    returned = swap_whole(back)
    (mine,) = call(sum_body, "sum", [((share, columns), BF16)], [], summed_parts)
    w1, w2, w3 = (hop(mine, step) for step in range(1, cycle))
    (grad_tokens,) = call(
        functools.partial(return_body, capacity), "give_back", [square], [], [owner_row, returned]
    )
    grad_proj, grad_outw = call(
        finish_body, "finish", [((share, 4 * width), F32), ((share, width), F32)],
        [me], [mine, w1, w2, w3],
    )
    return layer_out, grad_tokens, grad_proj, grad_outw


def solution(mesh):
    placed = (
        P(("dp", "ctx"), None),
        P(("dp", "ctx")),
        P(("dp", "ctx")),
        P("dp", None),
        P(),
        P(),
        P(("dp", "ctx"), None),
    )
    return jax.shard_map(
        on_device,
        mesh=mesh,
        in_specs=placed,
        out_specs=(P(("dp", "ctx"), None), P(("dp", "ctx"), None), P("dp", None), P("dp", None)),
        check_vma=False,
    )
```

```python
import functools

import jax
import jax.numpy as jnp
from jax import lax
from jax.experimental import pallas as pl
from jax.experimental.pallas import tpu as pltpu
from jax.sharding import PartitionSpec as P

HEADS = 8
EPSILON = 1e-05
LANES = 128
F32 = jnp.float32
BF16 = jnp.bfloat16

WHOLE = pl.BlockSpec(memory_space=pltpu.VMEM)
SCALARS = pl.BlockSpec(memory_space=pltpu.SMEM)
ANYWHERE = pl.BlockSpec(memory_space=pltpu.HBM)


def call(body, name, outs, scalars, arrays, scratch=(), flops=10**8, vmem=8, far=()):
    return pl.pallas_call(
        body,
        name=name,
        out_shape=[jax.ShapeDtypeStruct(s, d) for s, d in outs],
        in_specs=[SCALARS] * len(scalars) + [WHOLE] * len(arrays) + [ANYWHERE] * len(far),
        out_specs=[WHOLE] * len(outs),
        scratch_shapes=list(scratch),
        compiler_params=pltpu.CompilerParams(vmem_limit_bytes=vmem * 2**20),
        cost_estimate=pl.CostEstimate(flops=flops, bytes_accessed=2**20, transcendentals=0),
    )(*scalars, *arrays, *far)


def iota(shape, dim):
    return lax.broadcasted_iota(jnp.int32, shape, dim)


def mm(a, b):
    return jnp.dot(a, b, preferred_element_type=F32)


def mm_t(a, b):
    return lax.dot_general(a, b, (((1,), (1,)), ((), ())), preferred_element_type=F32)


def t_mm(a, b):
    return lax.dot_general(a, b, (((0,), (0,)), ((), ())), preferred_element_type=F32)


def hot(condition):
    return jnp.where(condition, 1.0, 0.0).astype(BF16)


def normalize(value):
    middle = jnp.mean(value, axis=-1, keepdims=True)
    centred = value - middle
    inv_dev = lax.rsqrt(jnp.mean(centred * centred, axis=-1, keepdims=True) + EPSILON)
    return centred * inv_dev, inv_dev


def norm_back(grad, normed, inv_dev):
    return inv_dev * (
        grad
        - jnp.mean(grad, axis=-1, keepdims=True)
        - normed * jnp.mean(grad * normed, axis=-1, keepdims=True)
    )


def silu_both(value):
    squashed = 0.5 * jnp.tanh(0.5 * value) + 0.5
    return value * squashed, squashed * (1.0 + value * (1.0 - squashed))


def rank_rows(owner):
    rows = owner.shape[1]
    down, across = iota((rows, rows), 0), iota((rows, rows), 1)
    spread = jnp.broadcast_to(owner, (rows, rows))
    owner_col = jnp.sum(jnp.where(down == across, spread, 0).astype(F32), axis=1, keepdims=True)
    same = owner_col.astype(jnp.int32) == spread
    rank_row = jnp.sum(jnp.where(same & (down < across), 1.0, 0.0), axis=0, keepdims=True)
    rank_col = jnp.sum(jnp.where(same & (across < down), 1.0, 0.0), axis=1, keepdims=True)
    return rank_row.astype(jnp.int32), rank_col.astype(jnp.int32)


def fetch(sources, targets, sems):
    copies = [pltpu.make_async_copy(a, b, sems.at[i]) for i, (a, b) in enumerate(zip(sources, targets))]
    for copy in copies:
        copy.start()
    for copy in copies:
        copy.wait()


def store_blocks(refs, value):
    size = refs[0].shape[0]
    for i, ref in enumerate(refs):
        ref[...] = value[i * size : (i + 1) * size].astype(ref.dtype)


def load_blocks(refs):
    return jnp.concatenate([ref[...].astype(F32) for ref in refs], axis=0).astype(BF16)


def pack_body(capacity, stride, outs, mask_ref, owner_hbm, slot_hbm, tokens_hbm, *rest):
    out_refs, (owner_ref, slot_ref, tokens_ref, sems) = rest[:outs], rest[outs:]
    fetch((owner_hbm, slot_hbm, tokens_hbm), (owner_ref, slot_ref, tokens_ref), sems)
    owner = owner_ref[...] ^ mask_ref[0]
    rows = owner.shape[1]
    rank_row, rank_col = rank_rows(owner)
    total, width = outs * out_refs[0].shape[0], out_refs[0].shape[1]
    place = iota((total, rows), 0)
    chosen = hot(place == owner * stride + rank_row)
    slots = jnp.where(place == owner * stride + capacity, slot_ref[...] + 1, 0)
    by_rank = hot(rank_col == iota((rows, width), 1))
    store_blocks(out_refs, mm(chosen, tokens_ref[...]) + mm(slots.astype(F32).astype(BF16), by_rank))


def block_rem(owners, stride):
    col, first = iota((owners, owners * stride), 1), iota((owners, owners * stride), 0)
    above = jnp.sum(jnp.where(col >= stride * (first + 1), 1.0, 0.0), axis=0, keepdims=True)
    rem = iota((1, owners * stride), 1) - stride * above.astype(jnp.int32)
    inside = (col >= stride * first) & (col < stride * (first + 1))
    return rem, inside


def landing_row(table, owners, capacity, stride):
    rem, inside = block_rem(owners, stride)
    lanes = iota((table.shape[1], owners * stride), 0)
    spread = mm(table, hot((lanes == rem) & (lanes < capacity)))
    return jnp.sum(jnp.where(inside, spread, 0.0), axis=0, keepdims=True)


def place_body(owners, capacity, stride, *refs):
    owned_ref, normed_ref, landing_ref = refs[-3:]
    rows = owned_ref.shape[0]
    arrived = load_blocks(refs[:-4])
    total = arrived.shape[0]
    pick = hot(iota((owners, total), 1) == iota((owners, total), 0) * stride + capacity)
    table = mm(pick, arrived).astype(BF16)
    landing = landing_row(table, owners, capacity, stride).astype(jnp.int32)
    owned = mm(hot(iota((rows, total), 0) + 1 == landing), arrived)
    owned_ref[...] = owned.astype(BF16)
    normed_ref[...] = normalize(owned)[0].astype(BF16)
    landing_ref[...] = landing_row(table, owners, capacity, capacity).astype(jnp.int32)


def early_body(cot_ref, outw_ref, proj_ref, grad_ref):
    grad_ref[...] = mm_t(cot_ref[...], outw_ref[...])


def history_start(pos, lengths_ref):
    first = lengths_ref[0, 0]
    second = lengths_ref[0, 1]
    return jnp.where(pos >= first + second, first + second, jnp.where(pos >= first, first, 0))


def attend(query_ref, key, value, shared, acc_ref):
    width = query_ref.shape[1]
    left = iota((1, LANES), 1) < LANES // 2
    for pair in range(width // LANES):
        cols = slice(pair * LANES, (pair + 1) * LANES)
        query, key_pair, value_pair = query_ref[:, cols], key[:, cols], value[:, cols]
        total = acc_ref[:, cols]
        for mine in (left, ~left):
            half = mm_t(jnp.where(mine, query, 0).astype(BF16), key_pair) * 0.0625
            weights = (half * (1.0 + jnp.tanh(half)) * shared).astype(BF16)
            total += mm(weights, jnp.where(mine, value_pair, 0).astype(BF16))
        acc_ref[:, cols] = total


def shared_factor(block, me, rows, lengths_ref):
    query_pos = me * rows + iota((rows, 1), 0)
    start = history_start(query_pos, lengths_ref)
    inverse = 1.0 / (query_pos - start + 1).astype(F32)
    key_pos = block * rows + iota((1, rows), 1)
    return jnp.where((key_pos >= start) & (key_pos <= query_pos), inverse, 0.0)


def attend_other(step, me, lengths_ref, other_ref, proj_ref, query_ref, acc_ref):
    rows, width = query_ref.shape
    block = me ^ step
    reach = history_start(me * rows, lengths_ref)

    @pl.when((block < me) & ((block + 1) * rows > reach))
    def _():
        normed = other_ref[...]
        value = silu_both(mm(normed, proj_ref[:, width : 2 * width]))[0].astype(BF16)
        key = silu_both(mm(normed, proj_ref[:, 3 * width :]))[0].astype(BF16)
        attend(query_ref, key, value, shared_factor(block, me, rows, lengths_ref), acc_ref)


def own_body(me_ref, lengths_ref, normed_ref, proj_ref, gate_ref, slope_ref, query_ref, acc_ref):
    rows, width = normed_ref.shape
    me = me_ref[0]
    preact = mm(normed_ref[...], proj_ref[...])
    gate, slope = silu_both(preact[:, :width])
    gate_ref[...] = gate.astype(BF16)
    slope_ref[...] = slope
    value = silu_both(preact[:, width : 2 * width])[0].astype(BF16)
    query_ref[...] = silu_both(preact[:, 2 * width : 3 * width])[0].astype(BF16)
    key = silu_both(preact[:, 3 * width :])[0].astype(BF16)
    acc_ref[...] = jnp.zeros_like(acc_ref)
    attend(query_ref, key, value, shared_factor(me, me, rows, lengths_ref), acc_ref)


def middle_body(me_ref, lengths_ref, near_ref, far_ref, proj_ref, query_ref, partial_ref, acc_ref):
    me = me_ref[0]
    acc_ref[...] = partial_ref[...]
    attend_other(1, me, lengths_ref, near_ref, proj_ref, query_ref, acc_ref)
    attend_other(2, me, lengths_ref, far_ref, proj_ref, query_ref, acc_ref)


def forward_body(
    me_ref, lengths_ref, cross_ref, proj_ref, outw_ref, owned_ref,
    gate_ref, slope_ref, query_ref, partial_ref, grad_ref,
    out_ref, gated_ref, gate_grad_ref, *rest,
):
    pieces_ref, acc_ref = rest
    rows, width = query_ref.shape
    me = me_ref[0]
    acc_ref[...] = partial_ref[...]
    attend_other(3, me, lengths_ref, cross_ref, proj_ref, query_ref, acc_ref)
    gate = gate_ref[...].astype(F32)
    normed, inv_dev = normalize(acc_ref[...])
    gated = (normed * gate).astype(BF16)
    gated_ref[...] = gated
    grad_gated = grad_ref[...]
    grad_attended = norm_back(grad_gated * gate, normed, inv_dev).astype(BF16)
    piece = pieces_ref.shape[2]
    for i in range(pieces_ref.shape[0]):
        pieces_ref[i] = grad_attended[:, i * piece : (i + 1) * piece]
    out_ref[...] = (mm(gated, outw_ref[...]) + owned_ref[...].astype(F32)).astype(BF16)
    gate_grad_ref[...] = (grad_gated * normed * slope_ref[...]).astype(BF16)


def side_body(
    me_ref, normed_ref, gated_ref, cot_ref, gate_grad_ref, proj_ref, kept_ref, sent_ref, gate_in_ref, part_ref
):
    width = gated_ref.shape[1]
    me = me_ref[0]
    gate_grad = gate_grad_ref[...]
    part_ref[:, :width] = t_mm(normed_ref[...], gate_grad)
    part_ref[:, width:] = t_mm(gated_ref[...], cot_ref[...])
    gate_in_ref[...] = mm_t(gate_grad, proj_ref[:, :width])
    for ref, steps in ((kept_ref, (0, 2)), (sent_ref, (1, 3))):
        place = 0
        for step in steps:
            for base in (0, width):
                source = pl.ds(pl.multiple_of(base + (me ^ step) * LANES, LANES), LANES)
                ref[:, place : place + LANES] = part_ref[:, source].astype(BF16)
                place += LANES


def side_sum_body(kept_ref, came_ref, keep_ref, send_ref):
    total = kept_ref[...].astype(F32) + came_ref[...].astype(F32)
    half = total.shape[1] // 2
    keep_ref[...] = total[:, :half].astype(BF16)
    send_ref[...] = total[:, half:].astype(BF16)


def heads_body(me_ref, n0_ref, n1_ref, n2_ref, n3_ref, proj_ref, part_ref, slope_ref):
    rows, width = n0_ref.shape
    me = me_ref[0]
    piece = width // 4
    cols = [proj_ref[:, pl.ds(pl.multiple_of(b * width + me * piece, LANES), piece)] for b in (1, 2, 3)]
    weight = jnp.concatenate(cols, axis=1)
    for step, ref in enumerate((n0_ref, n1_ref, n2_ref, n3_ref)):
        act, slope = silu_both(mm(ref[...], weight))
        at = pl.ds(pl.multiple_of((me ^ step) * rows, rows), rows)
        part_ref[at, :] = act.astype(BF16)
        slope_ref[at, :] = slope


def block_at(block, rows):
    return pl.ds(pl.multiple_of(block * rows, rows), rows)


def visit(first, second, same, lengths_ref, part_ref, grad_ref, total_ref):
    rows, piece = grad_ref.shape[0] // 4, grad_ref.shape[1]
    q_block, k_block = jnp.maximum(first, second), jnp.minimum(first, second)

    def work():
        q_at, k_at = block_at(q_block, rows), block_at(k_block, rows)
        left = iota((1, LANES), 1) < LANES // 2
        query_pos = q_block * rows + iota((1, rows), 1)
        start = history_start(query_pos, lengths_ref)
        key_pos = k_block * rows + iota((rows, 1), 0)
        inverse = 1.0 / (query_pos - start + 1).astype(F32)
        shared = jnp.where((key_pos >= start) & (key_pos <= query_pos), inverse, 0.0)
        value = part_ref[k_at, :piece]
        query = part_ref[q_at, piece : 2 * piece]
        key = part_ref[k_at, 2 * piece :]
        grad = grad_ref[q_at, :]
        small = value * jnp.asarray(0.0625, BF16)
        d_value, d_query, d_key = 0.0, 0.0, 0.0
        for mine in (left, ~left):
            query_h = jnp.where(mine, query, 0).astype(BF16)
            key_h = jnp.where(mine, key, 0).astype(BF16)
            grad_h = jnp.where(mine, grad, 0).astype(BF16)
            half = mm_t(key_h, query) * 0.0625
            up = 1.0 + jnp.tanh(half)
            act = half * up
            weights = (act * shared).astype(BF16)
            slope = (up + act * (2.0 - up)) * shared
            d_scores = (mm_t(small, grad_h) * slope).astype(BF16)
            d_value += mm(weights, grad_h)
            d_key += mm(d_scores, query_h)
            d_query += t_mm(d_scores, key_h)
        total_ref[k_at, :piece] += d_value
        total_ref[q_at, piece : 2 * piece] += d_query
        total_ref[k_at, 2 * piece :] += d_key

    if same:
        work()
    else:
        pl.when((k_block + 1) * rows > history_start(q_block * rows, lengths_ref))(work)


def backward_rows(steps, finished, me, lengths_ref, part_ref, slope_ref, grad_ref, total_ref, refs):
    done = list(finished)
    for step, ref in zip(steps, refs):
        for other in range(4):
            if other not in done:
                visit(me ^ step, me ^ other, other == step, lengths_ref, part_ref, grad_ref, total_ref)
        done.append(step)
        at = block_at(me ^ step, ref.shape[0])
        ref[...] = (total_ref[at, :] * slope_ref[at, :]).astype(BF16)


def backward_far_body(me_ref, lengths_ref, grad_ref, part_ref, slope_ref, *rest):
    sent_ref, o2_ref, o3_ref, total_ref = rest[-4:]
    me = me_ref[0]
    total_ref[...] = jnp.zeros_like(total_ref)
    backward_rows(
        (2, 3), (), me, lengths_ref, part_ref, slope_ref, grad_ref, total_ref, (o2_ref, o3_ref)
    )
    for step, ref in ((0, None), (1, None), (2, o2_ref), (3, o3_ref)):
        sent_ref[me ^ step] = jnp.zeros_like(o2_ref) if ref is None else ref[...]


def backward_rest_body(
    me_ref, lengths_ref, grad_ref, part_ref, slope_ref, sums_ref, *rest
):
    o0_ref, o1_ref, total_ref = rest[-3:]
    total_ref[...] = sums_ref[...]
    backward_rows(
        (1, 0), (2, 3), me_ref[0], lengths_ref, part_ref, slope_ref, grad_ref, total_ref, (o1_ref, o0_ref)
    )


def weight_body(sources, pairs, dp_ref, kept_side_ref, came_side_ref, *refs):
    normed, grads = refs[:sources], refs[sources : 2 * sources]
    outs, total_ref = refs[2 * sources : -1], refs[-1]
    side = kept_side_ref.shape[1]
    total = 0.0
    for n_ref, g_ref in zip(normed, grads):
        total += t_mm(n_ref[...], g_ref[...])
    total_ref[:, :side] = kept_side_ref[...].astype(F32) + came_side_ref[...].astype(F32)
    total_ref[:, side:] = total
    if len(outs) == 1:
        outs[0][...] = total_ref[...].astype(BF16)
        return
    kept_ref, sent_ref = outs
    share = kept_ref.shape[0] // pairs
    for j in range(pairs):
        at = slice(j * share, (j + 1) * share)
        for ref, k in ((kept_ref, 2 * j), (sent_ref, 2 * j + 1)):
            source = pl.ds(pl.multiple_of((dp_ref[0] ^ k) * share, share), share)
            ref[at, :] = total_ref[source, :].astype(BF16)


def pair_body(kept_ref, came_ref, *outs):
    store_blocks(outs, kept_ref[...].astype(F32) + came_ref[...].astype(F32))


def input_body(
    blocks, me_ref, mask_ref, own_ref, near_ref, far_ref,
    gate_in_ref, owned_ref, cot_ref, landing_ref, proj_ref, *rest,
):
    out_ref = rest[-1]
    rows, width = owned_ref.shape
    me = me_ref[0]
    piece = width // 4
    total = gate_in_ref[...]
    came = (own_ref[...], near_ref[...], far_ref[me ^ 2], far_ref[me ^ 3])
    for step, value in enumerate(came):
        cols = [
            proj_ref[:, pl.ds(pl.multiple_of(b * width + (me ^ step) * piece, LANES), piece)] for b in (1, 2, 3)
        ]
        total += mm_t(value, jnp.concatenate(cols, axis=1))
    centred, inv_scale = normalize(owned_ref[...].astype(F32))
    grad = (norm_back(total, centred, inv_scale) + cot_ref[...].astype(F32)).astype(BF16)
    select = hot(iota((rows, landing_ref.shape[1]), 0) + 1 == landing_ref[...])
    value = t_mm(select, grad)
    size = value.shape[0] // blocks
    for k in range(blocks):
        at = pl.ds(pl.multiple_of((mask_ref[0] ^ k) * size, size), size)
        out_ref[at, :] = value[k * size : (k + 1) * size].astype(BF16)


def return_body(capacity, owner_ref, back_ref, out_ref):
    owner = owner_ref[...]
    rank_row, _ = rank_rows(owner)
    chosen = hot(iota((back_ref.shape[0], owner.shape[1]), 0) == owner * capacity + rank_row)
    out_ref[...] = t_mm(chosen, back_ref[...]).astype(BF16)


def sum_body(*refs):
    total = 0.0
    for ref in refs[:-1]:
        parts = ref[...].astype(F32)
        total += parts if ref.ndim == 2 else jnp.sum(parts, axis=0)
    refs[-1][...] = total.astype(BF16)


def finish_body(me_ref, w0_ref, w1_ref, w2_ref, w3_ref, proj_ref, outw_ref):
    me = me_ref[0]
    width = outw_ref.shape[1]
    for step, ref in enumerate((w0_ref, w1_ref, w2_ref, w3_ref)):
        at = pl.ds(pl.multiple_of((me ^ step) * LANES, LANES), LANES)
        outw_ref[:, at] = ref[:, LANES : 2 * LANES].astype(F32)
        for b, source in enumerate((0, 2, 3, 4)):
            at = pl.ds(pl.multiple_of(b * width + (me ^ step) * LANES, LANES), LANES)
            proj_ref[:, at] = ref[:, source * LANES : (source + 1) * LANES].astype(F32)


def on_device(tokens, dest_owner, dest_slot, lengths, proj_weight, out_weight, cotangent):
    rows, width = tokens.shape
    owners = lax.axis_size("dp")
    cycle = lax.axis_size("ctx")
    assert cycle == 4 and width == cycle * LANES
    capacity = 2 * rows // owners
    stride = capacity + 8
    piece = width // cycle
    me = lax.axis_index("ctx").astype(jnp.int32).reshape(1)
    owner_row = dest_owner.reshape(1, rows)
    slot_row = dest_slot.reshape(1, rows)
    square = ((rows, width), BF16)

    def hop(value, step):
        return lax.ppermute(value, "ctx", [(i, i ^ step) for i in range(cycle)])

    def gather(value):
        near, far = hop(value, 1), hop(value, 2)
        return near, far, hop(far, 1)

    def trade(value):
        return lax.all_to_all(value, "ctx", split_axis=0, concat_axis=0, tiled=True)

    by_hops = owners <= 8
    blocks = owners if by_hops else 1
    dp = lax.axis_index("dp").astype(jnp.int32).reshape(1)
    mask = dp if by_hops else jnp.zeros_like(dp)

    def dp_hop(value, step):
        return lax.ppermute(value, "dp", [(i, i ^ step) for i in range(owners)])

    def swap_whole(value):
        split = value.reshape(owners, value.shape[0] // owners, value.shape[1])
        return lax.all_to_all(split, "dp", split_axis=0, concat_axis=0, tiled=True).reshape(value.shape)

    def swap(values):
        if by_hops:
            order = sorted(range(1, owners), key=lambda k: -k)
            moved = {k: dp_hop(values[k], k) for k in order}
            return [values[0]] + [moved[k] for k in range(1, owners)]
        return [swap_whole(values[0])]

    def block_shapes(height, columns, dtype):
        return [((owners * height // blocks, columns), dtype)] * blocks

    outgoing = call(
        functools.partial(pack_body, capacity, stride, blocks),
        "pack", block_shapes(stride, width, BF16), [mask], [], far=[owner_row, slot_row, tokens],
        scratch=[
            pltpu.VMEM((1, rows), jnp.int32),
            pltpu.VMEM((1, rows), jnp.int32),
            pltpu.VMEM((rows, width), BF16),
            pltpu.SemaphoreType.DMA((3,)),
        ],
    )
    arrived = swap(outgoing)
    wide = ((rows, width), F32)
    (grad_gated,) = call(early_body, "early", [wide], [], [cotangent, out_weight, proj_weight])
    owned, normed, landing = call(
        functools.partial(place_body, owners, capacity, stride),
        "place", [square, square, ((1, owners * capacity), jnp.int32)], [], arrived, far=[grad_gated],
    )
    near, far, cross = gather(normed)
    gate, slope, query, partial = call(
        own_body, "own_rows", [square, wide, square, wide],
        [me, lengths], [normed, proj_weight], flops=10**10, vmem=16,
    )
    (partial,) = call(
        middle_body, "middle", [wide], [me, lengths], [near, far, proj_weight, query, partial],
        flops=10**10, vmem=16,
    )
    layer_out, gated, gate_grad, grad_pieces = call(
        forward_body, "forward",
        [square, square, square, ((cycle, rows, piece), BF16)],
        [me, lengths],
        [cross, proj_weight, out_weight, owned, gate, slope, query, partial, grad_gated],
        scratch=[pltpu.VMEM((rows, width), F32)], vmem=16,
    )
    grad_all = trade(grad_pieces).reshape(cycle * rows, piece)
    side_half = ((width, 4 * piece), BF16)
    side_piece = ((width, 2 * piece), BF16)
    side_kept, side_sent, gate_in = call(
        side_body, "side", [side_half, side_half, wide],
        [me], [normed, gated, cotangent, gate_grad, proj_weight],
        scratch=[pltpu.VMEM((width, 2 * width), F32)], vmem=16,
    )
    side_came = hop(side_sent, 1)
    parts, slopes = call(
        heads_body, "heads",
        [((rows * cycle, 3 * piece), BF16), ((rows * cycle, 3 * piece), F32)],
        [me], [normed, near, far, cross, proj_weight], vmem=16,
    )
    side_keep, side_send = call(
        side_sum_body, "side_sum", [side_piece, side_piece], [], [side_kept, side_came]
    )
    side_last = hop(side_send, 2)
    grad_block = ((rows, 3 * piece), BF16)
    sums = ((rows * cycle, 3 * piece), F32)
    sent_blocks, far_block, cross_block, totals = call(
        backward_far_body, "backward_far",
        [((cycle, rows, 3 * piece), BF16), grad_block, grad_block, sums],
        [me, lengths], [grad_all, parts, slopes], vmem=16,
    )
    far_came = trade(sent_blocks)
    own_block, near_block = call(
        backward_rest_body, "backward_rest", [grad_block] * 2,
        [me, lengths], [grad_all, parts, slopes, totals], vmem=16, far=[side_last],
        scratch=[pltpu.VMEM(*sums)],
    )
    p1 = hop(near_block, 1)
    grads = [own_block, near_block, far_block, cross_block]
    share = width // owners
    pairs = owners // 2
    columns = 5 * piece
    weight_parts = call(
        functools.partial(weight_body, cycle, pairs), "weights",
        [((pairs * share, columns), BF16)] * 2 if by_hops else [((width, columns), BF16)], [dp],
        [side_keep, side_last, normed, near, far, cross, *grads], vmem=16,
        scratch=[pltpu.VMEM((width, columns), F32)],
    )
    if by_hops:
        kept, sent = weight_parts
        halves = call(
            pair_body, "pair_sum", [((share, columns), BF16)] * pairs, [], [kept, dp_hop(sent, 1)]
        )
        summed_parts = [halves[0]] + [dp_hop(halves[j], 2 * j) for j in range(1, pairs)]
    else:
        halves = weight_parts
        summed_parts = [swap_whole(weight_parts[0]).reshape(owners, share, columns)]
    (back,) = call(
        functools.partial(input_body, blocks), "input_grad", [((owners * capacity, width), BF16)], [me, mask],
        [own_block, p1, far_came, gate_in, owned, cotangent, landing, proj_weight], vmem=16,
        far=[halves[0]],
    )
    returned = swap_whole(back)
    (mine,) = call(sum_body, "sum", [((share, columns), BF16)], [], summed_parts)
    w1, w2, w3 = (hop(mine, step) for step in range(1, cycle))
    (grad_tokens,) = call(
        functools.partial(return_body, capacity), "give_back", [square], [], [owner_row, returned]
    )
    grad_proj, grad_outw = call(
        finish_body, "finish", [((share, 4 * width), F32), ((share, width), F32)],
        [me], [mine, w1, w2, w3],
    )
    return layer_out, grad_tokens, grad_proj, grad_outw


def solution(mesh):
    placed = (
        P(("dp", "ctx"), None),
        P(("dp", "ctx")),
        P(("dp", "ctx")),
        P("dp", None),
        P(),
        P(),
        P(("dp", "ctx"), None),
    )
    return jax.shard_map(
        on_device,
        mesh=mesh,
        in_specs=placed,
        out_specs=(P(("dp", "ctx"), None), P(("dp", "ctx"), None), P("dp", None), P("dp", None)),
        check_vma=False,
    )
```

```python
import functools

import jax
import jax.numpy as jnp
from jax import lax
from jax.experimental import pallas as pl
from jax.experimental.pallas import tpu as pltpu
from jax.sharding import PartitionSpec as P

HEADS = 8
EPSILON = 1e-05
LANES = 128
F32 = jnp.float32
BF16 = jnp.bfloat16

WHOLE = pl.BlockSpec(memory_space=pltpu.VMEM)
SCALARS = pl.BlockSpec(memory_space=pltpu.SMEM)
ANYWHERE = pl.BlockSpec(memory_space=pltpu.HBM)


def call(body, name, outs, scalars, arrays, scratch=(), flops=10**8, vmem=8, far=()):
    return pl.pallas_call(
        body,
        name=name,
        out_shape=[jax.ShapeDtypeStruct(s, d) for s, d in outs],
        in_specs=[SCALARS] * len(scalars) + [WHOLE] * len(arrays) + [ANYWHERE] * len(far),
        out_specs=[WHOLE] * len(outs),
        scratch_shapes=list(scratch),
        compiler_params=pltpu.CompilerParams(vmem_limit_bytes=vmem * 2**20),
        cost_estimate=pl.CostEstimate(flops=flops, bytes_accessed=2**20, transcendentals=0),
    )(*scalars, *arrays, *far)


def iota(shape, dim):
    return lax.broadcasted_iota(jnp.int32, shape, dim)


def mm(a, b):
    return jnp.dot(a, b, preferred_element_type=F32)


def mm_t(a, b):
    return lax.dot_general(a, b, (((1,), (1,)), ((), ())), preferred_element_type=F32)


def t_mm(a, b):
    return lax.dot_general(a, b, (((0,), (0,)), ((), ())), preferred_element_type=F32)


def hot(condition):
    return jnp.where(condition, 1.0, 0.0).astype(BF16)


def normalize(value):
    middle = jnp.mean(value, axis=-1, keepdims=True)
    centred = value - middle
    inv_dev = lax.rsqrt(jnp.mean(centred * centred, axis=-1, keepdims=True) + EPSILON)
    return centred * inv_dev, inv_dev


def norm_back(grad, normed, inv_dev):
    return inv_dev * (
        grad
        - jnp.mean(grad, axis=-1, keepdims=True)
        - normed * jnp.mean(grad * normed, axis=-1, keepdims=True)
    )


def silu_both(value):
    squashed = 0.5 * jnp.tanh(0.5 * value) + 0.5
    return value * squashed, squashed * (1.0 + value * (1.0 - squashed))


def rank_rows(owner):
    rows = owner.shape[1]
    down, across = iota((rows, rows), 0), iota((rows, rows), 1)
    spread = jnp.broadcast_to(owner, (rows, rows))
    owner_col = jnp.sum(jnp.where(down == across, spread, 0).astype(F32), axis=1, keepdims=True)
    same = owner_col.astype(jnp.int32) == spread
    rank_row = jnp.sum(jnp.where(same & (down < across), 1.0, 0.0), axis=0, keepdims=True)
    rank_col = jnp.sum(jnp.where(same & (across < down), 1.0, 0.0), axis=1, keepdims=True)
    return rank_row.astype(jnp.int32), rank_col.astype(jnp.int32)


def fetch(sources, targets, sems):
    copies = [pltpu.make_async_copy(a, b, sems.at[i]) for i, (a, b) in enumerate(zip(sources, targets))]
    for copy in copies:
        copy.start()
    for copy in copies:
        copy.wait()


def store_blocks(refs, value):
    size = refs[0].shape[0]
    for i, ref in enumerate(refs):
        ref[...] = value[i * size : (i + 1) * size].astype(ref.dtype)


def hop_order(count):
    return sorted(range(count), key=lambda k: (0 < k < count // 2, k))


def load_blocks(refs):
    order = hop_order(len(refs))
    return jnp.concatenate(
        [refs[order.index(k)][...].astype(F32) for k in range(len(refs))], axis=0
    ).astype(BF16)


def pack_body(capacity, stride, outs, mask_ref, owner_hbm, slot_hbm, tokens_hbm, *rest):
    out_refs, (owner_ref, slot_ref, tokens_ref, sems) = rest[:outs], rest[outs:]
    fetch((owner_hbm, slot_hbm, tokens_hbm), (owner_ref, slot_ref, tokens_ref), sems)
    owner = owner_ref[...] ^ mask_ref[0]
    rows = owner.shape[1]
    rank_row, rank_col = rank_rows(owner)
    total, width = outs * out_refs[0].shape[0], out_refs[0].shape[1]
    place = iota((total, rows), 0)
    chosen = hot(place == owner * stride + rank_row)
    slots = jnp.where(place == owner * stride + capacity, slot_ref[...] + 1, 0)
    by_rank = hot(rank_col == iota((rows, width), 1))
    store_blocks(out_refs, mm(chosen, tokens_ref[...]) + mm(slots.astype(F32).astype(BF16), by_rank))


def block_rem(owners, stride):
    col, first = iota((owners, owners * stride), 1), iota((owners, owners * stride), 0)
    above = jnp.sum(jnp.where(col >= stride * (first + 1), 1.0, 0.0), axis=0, keepdims=True)
    rem = iota((1, owners * stride), 1) - stride * above.astype(jnp.int32)
    inside = (col >= stride * first) & (col < stride * (first + 1))
    return rem, inside


def landing_row(table, owners, capacity, stride):
    rem, inside = block_rem(owners, stride)
    lanes = iota((table.shape[1], owners * stride), 0)
    spread = mm(table, hot((lanes == rem) & (lanes < capacity)))
    return jnp.sum(jnp.where(inside, spread, 0.0), axis=0, keepdims=True)


def place_body(owners, capacity, stride, *refs):
    owned_ref, normed_ref, landing_ref = refs[-3:]
    rows = owned_ref.shape[0]
    arrived = load_blocks(refs[:-4])
    total = arrived.shape[0]
    pick = hot(iota((owners, total), 1) == iota((owners, total), 0) * stride + capacity)
    table = mm(pick, arrived).astype(BF16)
    landing = landing_row(table, owners, capacity, stride).astype(jnp.int32)
    owned = mm(hot(iota((rows, total), 0) + 1 == landing), arrived)
    owned_ref[...] = owned.astype(BF16)
    normed_ref[...] = normalize(owned)[0].astype(BF16)
    landing_ref[...] = landing_row(table, owners, capacity, capacity).astype(jnp.int32)


def early_body(cot_ref, outw_ref, proj_ref, grad_ref):
    grad_ref[...] = mm_t(cot_ref[...], outw_ref[...])


def history_start(pos, lengths_ref):
    first = lengths_ref[0, 0]
    second = lengths_ref[0, 1]
    return jnp.where(pos >= first + second, first + second, jnp.where(pos >= first, first, 0))


def attend(query_ref, key, value, shared, acc_ref):
    width = query_ref.shape[1]
    left = iota((1, LANES), 1) < LANES // 2
    for pair in range(width // LANES):
        cols = slice(pair * LANES, (pair + 1) * LANES)
        query, key_pair, value_pair = query_ref[:, cols], key[:, cols], value[:, cols]
        total = acc_ref[:, cols]
        for mine in (left, ~left):
            half = mm_t(jnp.where(mine, query, 0).astype(BF16), key_pair) * 0.0625
            weights = (half * (1.0 + jnp.tanh(half)) * shared).astype(BF16)
            total += mm(weights, jnp.where(mine, value_pair, 0).astype(BF16))
        acc_ref[:, cols] = total


def shared_factor(block, me, rows, lengths_ref):
    query_pos = me * rows + iota((rows, 1), 0)
    start = history_start(query_pos, lengths_ref)
    inverse = 1.0 / (query_pos - start + 1).astype(F32)
    key_pos = block * rows + iota((1, rows), 1)
    return jnp.where((key_pos >= start) & (key_pos <= query_pos), inverse, 0.0)


def attend_other(step, me, lengths_ref, other_ref, proj_ref, query_ref, acc_ref):
    rows, width = query_ref.shape
    block = me ^ step
    reach = history_start(me * rows, lengths_ref)

    @pl.when((block < me) & ((block + 1) * rows > reach))
    def _():
        normed = other_ref[...]
        value = silu_both(mm(normed, proj_ref[:, width : 2 * width]))[0].astype(BF16)
        key = silu_both(mm(normed, proj_ref[:, 3 * width :]))[0].astype(BF16)
        attend(query_ref, key, value, shared_factor(block, me, rows, lengths_ref), acc_ref)


def own_body(me_ref, lengths_ref, normed_ref, proj_ref, gate_ref, slope_ref, query_ref, acc_ref):
    rows, width = normed_ref.shape
    me = me_ref[0]
    preact = mm(normed_ref[...], proj_ref[...])
    gate, slope = silu_both(preact[:, :width])
    gate_ref[...] = gate.astype(BF16)
    slope_ref[...] = slope
    value = silu_both(preact[:, width : 2 * width])[0].astype(BF16)
    query_ref[...] = silu_both(preact[:, 2 * width : 3 * width])[0].astype(BF16)
    key = silu_both(preact[:, 3 * width :])[0].astype(BF16)
    acc_ref[...] = jnp.zeros_like(acc_ref)
    attend(query_ref, key, value, shared_factor(me, me, rows, lengths_ref), acc_ref)


def middle_body(me_ref, lengths_ref, near_ref, far_ref, proj_ref, query_ref, partial_ref, acc_ref):
    me = me_ref[0]
    acc_ref[...] = partial_ref[...]
    attend_other(1, me, lengths_ref, near_ref, proj_ref, query_ref, acc_ref)
    attend_other(2, me, lengths_ref, far_ref, proj_ref, query_ref, acc_ref)


def forward_body(
    me_ref, lengths_ref, cross_ref, proj_ref, outw_ref, owned_ref,
    gate_ref, slope_ref, query_ref, partial_ref, grad_ref,
    out_ref, gated_ref, gate_grad_ref, *rest,
):
    grads, acc_ref = rest[:-1], rest[-1]
    rows, width = query_ref.shape
    me = me_ref[0]
    acc_ref[...] = partial_ref[...]
    attend_other(3, me, lengths_ref, cross_ref, proj_ref, query_ref, acc_ref)
    gate = gate_ref[...].astype(F32)
    normed, inv_dev = normalize(acc_ref[...])
    gated = (normed * gate).astype(BF16)
    gated_ref[...] = gated
    grad_gated = grad_ref[...]
    grad_attended = norm_back(grad_gated * gate, normed, inv_dev).astype(BF16)
    acc_ref[...] = grad_attended.astype(F32)
    piece = width // len(grads)
    for step, ref in enumerate(grads):
        ref[...] = acc_ref[:, pl.ds(pl.multiple_of((me ^ step) * piece, LANES), piece)].astype(BF16)
    out_ref[...] = (mm(gated, outw_ref[...]) + owned_ref[...].astype(F32)).astype(BF16)
    gate_grad_ref[...] = (grad_gated * normed * slope_ref[...]).astype(BF16)


def side_body(me_ref, normed_ref, gated_ref, cot_ref, gate_grad_ref, proj_ref, kept_ref, sent_ref, gate_in_ref, part_ref):
    width = gated_ref.shape[1]
    me = me_ref[0]
    gate_grad = gate_grad_ref[...]
    part_ref[:, :width] = t_mm(normed_ref[...], gate_grad)
    part_ref[:, width:] = t_mm(gated_ref[...], cot_ref[...])
    gate_in_ref[...] = mm_t(gate_grad, proj_ref[:, :width])
    for ref, steps in ((kept_ref, (0, 2)), (sent_ref, (1, 3))):
        place = 0
        for step in steps:
            for base in (0, width):
                source = pl.ds(pl.multiple_of(base + (me ^ step) * LANES, LANES), LANES)
                ref[:, place : place + LANES] = part_ref[:, source].astype(BF16)
                place += LANES


def side_sum_body(kept_ref, came_ref, keep_ref, send_ref):
    total = kept_ref[...].astype(F32) + came_ref[...].astype(F32)
    half = total.shape[1] // 2
    keep_ref[...] = total[:, :half].astype(BF16)
    send_ref[...] = total[:, half:].astype(BF16)


def heads_body(me_ref, n0_ref, n1_ref, n2_ref, n3_ref, proj_ref, part_ref, slope_ref):
    rows, width = n0_ref.shape
    me = me_ref[0]
    piece = width // 4
    cols = [proj_ref[:, pl.ds(pl.multiple_of(b * width + me * piece, LANES), piece)] for b in (1, 2, 3)]
    weight = jnp.concatenate(cols, axis=1)
    for step, ref in enumerate((n0_ref, n1_ref, n2_ref, n3_ref)):
        act, slope = silu_both(mm(ref[...], weight))
        at = pl.ds(pl.multiple_of((me ^ step) * rows, rows), rows)
        part_ref[at, :] = act.astype(BF16)
        slope_ref[at, :] = slope


def block_at(block, rows):
    return pl.ds(pl.multiple_of(block * rows, rows), rows)


def visit(first, second, same, lengths_ref, part_ref, grad_ref, total_ref):
    rows, piece = grad_ref.shape[0] // 4, grad_ref.shape[1]
    q_block, k_block = jnp.maximum(first, second), jnp.minimum(first, second)

    def work():
        q_at, k_at = block_at(q_block, rows), block_at(k_block, rows)
        left = iota((1, LANES), 1) < LANES // 2
        query_pos = q_block * rows + iota((1, rows), 1)
        start = history_start(query_pos, lengths_ref)
        key_pos = k_block * rows + iota((rows, 1), 0)
        inverse = 1.0 / (query_pos - start + 1).astype(F32)
        shared = jnp.where((key_pos >= start) & (key_pos <= query_pos), inverse, 0.0)
        value = part_ref[k_at, :piece]
        query = part_ref[q_at, piece : 2 * piece]
        key = part_ref[k_at, 2 * piece :]
        grad = grad_ref[q_at, :]
        small = value * jnp.asarray(0.0625, BF16)
        d_value, d_query, d_key = 0.0, 0.0, 0.0
        for mine in (left, ~left):
            query_h = jnp.where(mine, query, 0).astype(BF16)
            key_h = jnp.where(mine, key, 0).astype(BF16)
            grad_h = jnp.where(mine, grad, 0).astype(BF16)
            half = mm_t(key_h, query) * 0.0625
            up = 1.0 + jnp.tanh(half)
            act = half * up
            weights = (act * shared).astype(BF16)
            slope = (up + act * (2.0 - up)) * shared
            d_scores = (mm_t(small, grad_h) * slope).astype(BF16)
            d_value += mm(weights, grad_h)
            d_key += mm(d_scores, query_h)
            d_query += t_mm(d_scores, key_h)
        total_ref[k_at, :piece] += d_value
        total_ref[q_at, piece : 2 * piece] += d_query
        total_ref[k_at, 2 * piece :] += d_key

    if same:
        work()
    else:
        pl.when((k_block + 1) * rows > history_start(q_block * rows, lengths_ref))(work)


def backward_rows(steps, finished, me, lengths_ref, part_ref, slope_ref, grad_ref, total_ref, refs):
    done = list(finished)
    for step, ref in zip(steps, refs):
        for other in range(4):
            if other not in done:
                visit(me ^ step, me ^ other, other == step, lengths_ref, part_ref, grad_ref, total_ref)
        done.append(step)
        at = block_at(me ^ step, ref.shape[0])
        ref[...] = (total_ref[at, :] * slope_ref[at, :]).astype(BF16)


def backward_far_body(
    me_ref, lengths_ref, g0_ref, g1_ref, g2_ref, g3_ref, part_ref, slope_ref, *rest
):
    o2_ref, o3_ref, total_ref, grad_ref = rest[-4:]
    rows = g0_ref.shape[0]
    me = me_ref[0]
    for step, ref in enumerate((g0_ref, g1_ref, g2_ref, g3_ref)):
        grad_ref[block_at(me ^ step, rows), :] = ref[...]
    total_ref[...] = jnp.zeros_like(total_ref)
    backward_rows(
        (2, 3), (), me, lengths_ref, part_ref, slope_ref, grad_ref, total_ref, (o2_ref, o3_ref)
    )


def backward_rest_body(
    me_ref, lengths_ref, part_ref, slope_ref, grad_ref, sums_ref, o0_ref, o1_ref, total_ref
):
    total_ref[...] = sums_ref[...]
    backward_rows(
        (1, 0), (2, 3), me_ref[0], lengths_ref, part_ref, slope_ref, grad_ref, total_ref, (o1_ref, o0_ref)
    )


def weight_body(sources, pairs, dp_ref, kept_side_ref, came_side_ref, *refs):
    normed, grads = refs[:sources], refs[sources : 2 * sources]
    outs, total_ref = refs[2 * sources : -1], refs[-1]
    side = kept_side_ref.shape[1]
    total = 0.0
    for n_ref, g_ref in zip(normed, grads):
        total += t_mm(n_ref[...], g_ref[...])
    total_ref[:, :side] = kept_side_ref[...].astype(F32) + came_side_ref[...].astype(F32)
    total_ref[:, side:] = total
    if len(outs) == 1:
        outs[0][...] = total_ref[...].astype(BF16)
        return
    kept_ref, sent_ref = outs
    share = kept_ref.shape[0] // pairs
    for j in range(pairs):
        at = slice(j * share, (j + 1) * share)
        for ref, k in ((kept_ref, 2 * j), (sent_ref, 2 * j + 1)):
            source = pl.ds(pl.multiple_of((dp_ref[0] ^ k) * share, share), share)
            ref[at, :] = total_ref[source, :].astype(BF16)


def pair_body(kept_ref, came_ref, _, *outs):
    store_blocks(outs, kept_ref[...].astype(F32) + came_ref[...].astype(F32))


def head_columns(owner, proj_ref):
    width = proj_ref.shape[0]
    cols = [proj_ref[:, pl.ds(pl.multiple_of(b * width + owner * LANES, LANES), LANES)] for b in (1, 2, 3)]
    return jnp.concatenate(cols, axis=1)


def input_far_body(me_ref, far_ref, cross_ref, gate_in_ref, proj_ref, out_ref):
    me = me_ref[0]
    total = gate_in_ref[...] + mm_t(far_ref[...], head_columns(me ^ 2, proj_ref))
    out_ref[...] = total + mm_t(cross_ref[...], head_columns(me ^ 3, proj_ref))


def input_body(
    blocks, me_ref, own_ref, near_ref, partial_ref, owned_ref, cot_ref, landing_ref, proj_ref, *rest
):
    rows = owned_ref.shape[0]
    me = me_ref[0]
    total = partial_ref[...] + mm_t(own_ref[...], head_columns(me, proj_ref))
    total += mm_t(near_ref[...], head_columns(me ^ 1, proj_ref))
    centred, inv_scale = normalize(owned_ref[...].astype(F32))
    grad = (norm_back(total, centred, inv_scale) + cot_ref[...].astype(F32)).astype(BF16)
    select = hot(iota((rows, landing_ref.shape[1]), 0) + 1 == landing_ref[...])
    store_blocks(rest[-blocks:], t_mm(select, grad))


def return_body(capacity, mask_ref, owner_ref, *refs):
    owner = owner_ref[...] ^ mask_ref[0]
    rank_row, _ = rank_rows(owner)
    back = load_blocks(refs[:-1])
    chosen = hot(iota((back.shape[0], owner.shape[1]), 0) == owner * capacity + rank_row)
    refs[-1][...] = t_mm(chosen, back).astype(BF16)


def sum_body(*refs):
    total = 0.0
    for ref in refs[:-1]:
        parts = ref[...].astype(F32)
        total += parts if ref.ndim == 2 else jnp.sum(parts, axis=0)
    refs[-1][...] = total.astype(BF16)


def finish_body(me_ref, w0_ref, w1_ref, w2_ref, w3_ref, proj_ref, outw_ref):
    me = me_ref[0]
    width = outw_ref.shape[1]
    for step, ref in enumerate((w0_ref, w1_ref, w2_ref, w3_ref)):
        at = pl.ds(pl.multiple_of((me ^ step) * LANES, LANES), LANES)
        outw_ref[:, at] = ref[:, LANES : 2 * LANES].astype(F32)
        for b, source in enumerate((0, 2, 3, 4)):
            at = pl.ds(pl.multiple_of(b * width + (me ^ step) * LANES, LANES), LANES)
            proj_ref[:, at] = ref[:, source * LANES : (source + 1) * LANES].astype(F32)


def on_device(tokens, dest_owner, dest_slot, lengths, proj_weight, out_weight, cotangent):
    rows, width = tokens.shape
    owners = lax.axis_size("dp")
    cycle = lax.axis_size("ctx")
    assert cycle == 4 and width == cycle * LANES
    capacity = 2 * rows // owners
    stride = capacity + 8
    piece = width // cycle
    me = lax.axis_index("ctx").astype(jnp.int32).reshape(1)
    owner_row = dest_owner.reshape(1, rows)
    slot_row = dest_slot.reshape(1, rows)
    square = ((rows, width), BF16)

    def hop(value, step):
        return lax.ppermute(value, "ctx", [(i, i ^ step) for i in range(cycle)])

    def gather(value):
        near, far = hop(value, 1), hop(value, 2)
        return near, far, hop(far, 1)

    def exchange(values):
        return [values[0]] + [hop(values[step], step) for step in (2, 3, 1)]

    by_hops = owners <= 8
    blocks = owners if by_hops else 1
    dp = lax.axis_index("dp").astype(jnp.int32).reshape(1)
    mask = dp if by_hops else jnp.zeros_like(dp)

    def dp_hop(value, step):
        return lax.ppermute(value, "dp", [(i, i ^ step) for i in range(owners)])

    def swap_whole(value):
        split = value.reshape(owners, value.shape[0] // owners, value.shape[1])
        return lax.all_to_all(split, "dp", split_axis=0, concat_axis=0, tiled=True).reshape(value.shape)

    def swap(values):
        if by_hops:
            return [dp_hop(values[k], k) if k else values[k] for k in hop_order(owners)]
        return [swap_whole(values[0])]

    def block_shapes(height, columns, dtype):
        return [((owners * height // blocks, columns), dtype)] * blocks

    outgoing = call(
        functools.partial(pack_body, capacity, stride, blocks),
        "pack", block_shapes(stride, width, BF16), [mask], [], far=[owner_row, slot_row, tokens],
        scratch=[
            pltpu.VMEM((1, rows), jnp.int32),
            pltpu.VMEM((1, rows), jnp.int32),
            pltpu.VMEM((rows, width), BF16),
            pltpu.SemaphoreType.DMA((3,)),
        ],
    )
    arrived = swap(outgoing)
    wide = ((rows, width), F32)
    (grad_gated,) = call(early_body, "early", [wide], [], [cotangent, out_weight, proj_weight])
    owned, normed, landing = call(
        functools.partial(place_body, owners, capacity, stride),
        "place", [square, square, ((1, owners * capacity), jnp.int32)], [], arrived, far=[grad_gated],
    )
    near, far, cross = gather(normed)
    gate, slope, query, partial = call(
        own_body, "own_rows", [square, wide, square, wide],
        [me, lengths], [normed, proj_weight], flops=10**10, vmem=16,
    )
    (partial,) = call(
        middle_body, "middle", [wide], [me, lengths], [near, far, proj_weight, query, partial],
        flops=10**10, vmem=16,
    )
    layer_out, gated, gate_grad, *grad_pieces = call(
        forward_body, "forward",
        [square, square, square] + [((rows, piece), BF16)] * cycle,
        [me, lengths],
        [cross, proj_weight, out_weight, owned, gate, slope, query, partial, grad_gated],
        scratch=[pltpu.VMEM((rows, width), F32)], vmem=16,
    )
    r0, r2, r3, r1 = exchange(grad_pieces)
    side_half = ((width, 4 * piece), BF16)
    side_piece = ((width, 2 * piece), BF16)
    side_kept, side_sent, gate_in = call(
        side_body, "side", [side_half, side_half, wide],
        [me], [normed, gated, cotangent, gate_grad, proj_weight],
        scratch=[pltpu.VMEM((width, 2 * width), F32)], vmem=16,
    )
    side_came = hop(side_sent, 1)
    parts, slopes = call(
        heads_body, "heads",
        [((rows * cycle, 3 * piece), BF16), ((rows * cycle, 3 * piece), F32)],
        [me], [normed, near, far, cross, proj_weight], vmem=16,
    )
    side_keep, side_send = call(
        side_sum_body, "side_sum", [side_piece, side_piece], [], [side_kept, side_came]
    )
    side_last = hop(side_send, 2)
    grad_block = ((rows, 3 * piece), BF16)
    sums = ((rows * cycle, 3 * piece), F32)
    grad_rows = ((rows * cycle, piece), BF16)
    far_block, cross_block, totals, grad_all = call(
        backward_far_body, "backward_far", [grad_block, grad_block, sums, grad_rows],
        [me, lengths], [r0, r1, r2, r3, parts, slopes], flops=10**10, vmem=16,
    )
    p2, p3 = hop(far_block, 2), hop(cross_block, 3)
    own_block, near_block = call(
        backward_rest_body, "backward_rest", [grad_block] * 2,
        [me, lengths], [parts, slopes, grad_all, totals], vmem=16,
        scratch=[pltpu.VMEM(*sums)],
    )
    p1 = hop(near_block, 1)
    grads = [own_block, near_block, far_block, cross_block]
    share = width // owners
    pairs = owners // 2
    columns = 5 * piece
    weight_parts = call(
        functools.partial(weight_body, cycle, pairs), "weights",
        [((pairs * share, columns), BF16)] * 2 if by_hops else [((width, columns), BF16)], [dp],
        [side_keep, side_last, normed, near, far, cross, *grads], vmem=16,
        scratch=[pltpu.VMEM((width, columns), F32)],
    )
    (partial_in,) = call(
        input_far_body, "input_far", [wide], [me], [p2, p3, gate_in, proj_weight], flops=6 * 10**9,
    )
    if by_hops:
        kept, sent = weight_parts
        halves = call(
            pair_body, "pair_sum", [((share, columns), BF16)] * pairs, [], [kept, dp_hop(sent, 1)],
            far=[partial_in],
        )
        summed_parts = [halves[0]] + [dp_hop(halves[j], 2 * j) for j in range(1, pairs)]
    else:
        halves = weight_parts
        summed_parts = [swap_whole(weight_parts[0]).reshape(owners, share, columns)]
    back = call(
        functools.partial(input_body, blocks), "input_grad", block_shapes(capacity, width, BF16), [me],
        [own_block, p1, partial_in, owned, cotangent, landing, proj_weight], vmem=16,
        far=[halves[0]],
    )
    returned = swap(back)
    (mine,) = call(sum_body, "sum", [((share, columns), BF16)], [], summed_parts)
    w1, w2, w3 = (hop(mine, step) for step in range(1, cycle))
    (grad_tokens,) = call(
        functools.partial(return_body, capacity), "give_back", [square], [mask], [owner_row, *returned]
    )
    grad_proj, grad_outw = call(
        finish_body, "finish", [((share, 4 * width), F32), ((share, width), F32)],
        [me], [mine, w1, w2, w3],
    )
    return layer_out, grad_tokens, grad_proj, grad_outw


def solution(mesh):
    placed = (
        P(("dp", "ctx"), None),
        P(("dp", "ctx")),
        P(("dp", "ctx")),
        P("dp", None),
        P(),
        P(),
        P(("dp", "ctx"), None),
    )
    return jax.shard_map(
        on_device,
        mesh=mesh,
        in_specs=placed,
        out_specs=(P(("dp", "ctx"), None), P(("dp", "ctx"), None), P("dp", None), P("dp", None)),
        check_vma=False,
    )
```

```python
import functools

import jax
import jax.numpy as jnp
from jax import lax
from jax.experimental import pallas as pl
from jax.experimental.pallas import tpu as pltpu
from jax.sharding import PartitionSpec as P

HEADS = 8
EPSILON = 1e-05
LANES = 128
F32 = jnp.float32
BF16 = jnp.bfloat16

WHOLE = pl.BlockSpec(memory_space=pltpu.VMEM)
SCALARS = pl.BlockSpec(memory_space=pltpu.SMEM)
ANYWHERE = pl.BlockSpec(memory_space=pltpu.HBM)


def call(body, name, outs, scalars, arrays, scratch=(), flops=10**8, vmem=8, far=()):
    return pl.pallas_call(
        body,
        name=name,
        out_shape=[jax.ShapeDtypeStruct(s, d) for s, d in outs],
        in_specs=[SCALARS] * len(scalars) + [WHOLE] * len(arrays) + [ANYWHERE] * len(far),
        out_specs=[WHOLE] * len(outs),
        scratch_shapes=list(scratch),
        compiler_params=pltpu.CompilerParams(vmem_limit_bytes=vmem * 2**20),
        cost_estimate=pl.CostEstimate(flops=flops, bytes_accessed=2**20, transcendentals=0),
    )(*scalars, *arrays, *far)


def iota(shape, dim):
    return lax.broadcasted_iota(jnp.int32, shape, dim)


def mm(a, b):
    return jnp.dot(a, b, preferred_element_type=F32)


def mm_t(a, b):
    return lax.dot_general(a, b, (((1,), (1,)), ((), ())), preferred_element_type=F32)


def t_mm(a, b):
    return lax.dot_general(a, b, (((0,), (0,)), ((), ())), preferred_element_type=F32)


def hot(condition):
    return jnp.where(condition, 1.0, 0.0).astype(BF16)


def normalize(value):
    middle = jnp.mean(value, axis=-1, keepdims=True)
    centred = value - middle
    inv_dev = lax.rsqrt(jnp.mean(centred * centred, axis=-1, keepdims=True) + EPSILON)
    return centred * inv_dev, inv_dev


def norm_back(grad, normed, inv_dev):
    return inv_dev * (
        grad
        - jnp.mean(grad, axis=-1, keepdims=True)
        - normed * jnp.mean(grad * normed, axis=-1, keepdims=True)
    )


def silu_both(value):
    squashed = 0.5 * jnp.tanh(0.5 * value) + 0.5
    return value * squashed, squashed * (1.0 + value * (1.0 - squashed))


def rank_rows(owner):
    rows = owner.shape[1]
    down, across = iota((rows, rows), 0), iota((rows, rows), 1)
    spread = jnp.broadcast_to(owner, (rows, rows))
    owner_col = jnp.sum(jnp.where(down == across, spread, 0).astype(F32), axis=1, keepdims=True)
    same = owner_col.astype(jnp.int32) == spread
    rank_row = jnp.sum(jnp.where(same & (down < across), 1.0, 0.0), axis=0, keepdims=True)
    rank_col = jnp.sum(jnp.where(same & (across < down), 1.0, 0.0), axis=1, keepdims=True)
    return rank_row.astype(jnp.int32), rank_col.astype(jnp.int32)


def fetch(sources, targets, sems):
    copies = [pltpu.make_async_copy(a, b, sems.at[i]) for i, (a, b) in enumerate(zip(sources, targets))]
    for copy in copies:
        copy.start()
    for copy in copies:
        copy.wait()


def store_blocks(refs, value):
    size = refs[0].shape[0]
    for i, ref in enumerate(refs):
        ref[...] = value[i * size : (i + 1) * size].astype(ref.dtype)


def hop_order(count):
    return sorted(range(count), key=lambda k: (0 < k < count // 2, k))


def load_blocks(refs):
    order = hop_order(len(refs))
    return jnp.concatenate(
        [refs[order.index(k)][...].astype(F32) for k in range(len(refs))], axis=0
    ).astype(BF16)


def pack_body(capacity, stride, first, owner_ref, slot_ref, tokens_ref, out_refs):
    owner = owner_ref[...]
    rows = owner.shape[1]
    rank_row, rank_col = rank_rows(owner)
    total, width = len(out_refs) * out_refs[0].shape[0], out_refs[0].shape[1]
    place = iota((total, rows), 0) + first * stride
    chosen = hot(place == owner * stride + rank_row)
    slots = jnp.where(place == owner * stride + capacity, slot_ref[...] + 1, 0)
    by_rank = hot(rank_col == iota((rows, width), 1))
    store_blocks(out_refs, mm(chosen, tokens_ref[...]) + mm(slots.astype(F32).astype(BF16), by_rank))


def pack_far_body(capacity, stride, first, outs, mask_ref, owner_hbm, slot_hbm, tokens_hbm, *refs):
    out_refs, kept_refs, sems = refs[:outs], refs[outs:-1], refs[-1]
    owner_ref, slot_ref, tokens_ref = kept_refs
    fetch((owner_hbm, slot_hbm, tokens_hbm), (owner_ref, slot_ref, tokens_ref), sems)
    owner_ref[...] = owner_ref[...] ^ mask_ref[0]
    pack_body(capacity, stride, first, owner_ref, slot_ref, tokens_ref, out_refs)


def pack_near_body(capacity, stride, outs, owner_ref, slot_ref, tokens_ref, *refs):
    pack_body(capacity, stride, 0, owner_ref, slot_ref, tokens_ref, refs[-outs:])


def block_rem(owners, stride):
    col, first = iota((owners, owners * stride), 1), iota((owners, owners * stride), 0)
    above = jnp.sum(jnp.where(col >= stride * (first + 1), 1.0, 0.0), axis=0, keepdims=True)
    rem = iota((1, owners * stride), 1) - stride * above.astype(jnp.int32)
    inside = (col >= stride * first) & (col < stride * (first + 1))
    return rem, inside


def landing_row(table, owners, capacity, stride):
    rem, inside = block_rem(owners, stride)
    lanes = iota((table.shape[1], owners * stride), 0)
    spread = mm(table, hot((lanes == rem) & (lanes < capacity)))
    return jnp.sum(jnp.where(inside, spread, 0.0), axis=0, keepdims=True)


def place_body(owners, capacity, stride, *refs):
    owned_ref, normed_ref, landing_ref = refs[-3:]
    rows = owned_ref.shape[0]
    arrived = load_blocks(refs[:-3])
    total = arrived.shape[0]
    pick = hot(iota((owners, total), 1) == iota((owners, total), 0) * stride + capacity)
    table = mm(pick, arrived).astype(BF16)
    landing = landing_row(table, owners, capacity, stride).astype(jnp.int32)
    owned = mm(hot(iota((rows, total), 0) + 1 == landing), arrived)
    owned_ref[...] = owned.astype(BF16)
    normed_ref[...] = normalize(owned)[0].astype(BF16)
    landing_ref[...] = landing_row(table, owners, capacity, capacity).astype(jnp.int32)


def early_body(cot_ref, outw_ref, proj_ref, grad_ref):
    grad_ref[...] = mm_t(cot_ref[...], outw_ref[...])


def history_start(pos, lengths_ref):
    first = lengths_ref[0, 0]
    second = lengths_ref[0, 1]
    return jnp.where(pos >= first + second, first + second, jnp.where(pos >= first, first, 0))


def attend(query_ref, key, value, shared, acc_ref):
    width = query_ref.shape[1]
    left = iota((1, LANES), 1) < LANES // 2
    for pair in range(width // LANES):
        cols = slice(pair * LANES, (pair + 1) * LANES)
        query, key_pair, value_pair = query_ref[:, cols], key[:, cols], value[:, cols]
        total = acc_ref[:, cols]
        for mine in (left, ~left):
            half = mm_t(jnp.where(mine, query, 0).astype(BF16), key_pair) * 0.0625
            weights = (half * (1.0 + jnp.tanh(half)) * shared).astype(BF16)
            total += mm(weights, jnp.where(mine, value_pair, 0).astype(BF16))
        acc_ref[:, cols] = total


def shared_factor(block, me, rows, lengths_ref):
    query_pos = me * rows + iota((rows, 1), 0)
    start = history_start(query_pos, lengths_ref)
    inverse = 1.0 / (query_pos - start + 1).astype(F32)
    key_pos = block * rows + iota((1, rows), 1)
    return jnp.where((key_pos >= start) & (key_pos <= query_pos), inverse, 0.0)


def attend_other(step, me, lengths_ref, other_ref, proj_ref, query_ref, acc_ref):
    rows, width = query_ref.shape
    block = me ^ step
    reach = history_start(me * rows, lengths_ref)

    @pl.when((block < me) & ((block + 1) * rows > reach))
    def _():
        normed = other_ref[...]
        value = silu_both(mm(normed, proj_ref[:, width : 2 * width]))[0].astype(BF16)
        key = silu_both(mm(normed, proj_ref[:, 3 * width :]))[0].astype(BF16)
        attend(query_ref, key, value, shared_factor(block, me, rows, lengths_ref), acc_ref)


def own_body(me_ref, lengths_ref, normed_ref, proj_ref, gate_ref, slope_ref, query_ref, acc_ref):
    rows, width = normed_ref.shape
    me = me_ref[0]
    preact = mm(normed_ref[...], proj_ref[...])
    gate, slope = silu_both(preact[:, :width])
    gate_ref[...] = gate.astype(BF16)
    slope_ref[...] = slope
    value = silu_both(preact[:, width : 2 * width])[0].astype(BF16)
    query_ref[...] = silu_both(preact[:, 2 * width : 3 * width])[0].astype(BF16)
    key = silu_both(preact[:, 3 * width :])[0].astype(BF16)
    acc_ref[...] = jnp.zeros_like(acc_ref)
    attend(query_ref, key, value, shared_factor(me, me, rows, lengths_ref), acc_ref)


def middle_body(me_ref, lengths_ref, near_ref, far_ref, proj_ref, query_ref, partial_ref, acc_ref):
    me = me_ref[0]
    acc_ref[...] = partial_ref[...]
    attend_other(1, me, lengths_ref, near_ref, proj_ref, query_ref, acc_ref)
    attend_other(2, me, lengths_ref, far_ref, proj_ref, query_ref, acc_ref)


def forward_body(
    me_ref, lengths_ref, cross_ref, proj_ref, outw_ref, owned_ref,
    gate_ref, slope_ref, query_ref, partial_ref, grad_ref,
    out_ref, gated_ref, gate_grad_ref, *rest,
):
    grads, acc_ref = rest[:-1], rest[-1]
    rows, width = query_ref.shape
    me = me_ref[0]
    acc_ref[...] = partial_ref[...]
    attend_other(3, me, lengths_ref, cross_ref, proj_ref, query_ref, acc_ref)
    gate = gate_ref[...].astype(F32)
    normed, inv_dev = normalize(acc_ref[...])
    gated = (normed * gate).astype(BF16)
    gated_ref[...] = gated
    grad_gated = grad_ref[...]
    grad_attended = norm_back(grad_gated * gate, normed, inv_dev).astype(BF16)
    acc_ref[...] = grad_attended.astype(F32)
    piece = width // len(grads)
    for step, ref in enumerate(grads):
        ref[...] = acc_ref[:, pl.ds(pl.multiple_of((me ^ step) * piece, LANES), piece)].astype(BF16)
    out_ref[...] = (mm(gated, outw_ref[...]) + owned_ref[...].astype(F32)).astype(BF16)
    gate_grad_ref[...] = (grad_gated * normed * slope_ref[...]).astype(BF16)


def side_body(me_ref, normed_ref, gated_ref, cot_ref, gate_grad_ref, proj_ref, kept_ref, sent_ref, gate_in_ref, part_ref):
    width = gated_ref.shape[1]
    me = me_ref[0]
    gate_grad = gate_grad_ref[...]
    part_ref[:, :width] = t_mm(normed_ref[...], gate_grad)
    part_ref[:, width:] = t_mm(gated_ref[...], cot_ref[...])
    gate_in_ref[...] = mm_t(gate_grad, proj_ref[:, :width])
    for ref, steps in ((kept_ref, (0, 2)), (sent_ref, (1, 3))):
        place = 0
        for step in steps:
            for base in (0, width):
                source = pl.ds(pl.multiple_of(base + (me ^ step) * LANES, LANES), LANES)
                ref[:, place : place + LANES] = part_ref[:, source].astype(BF16)
                place += LANES


def side_sum_body(kept_ref, came_ref, keep_ref, send_ref):
    total = kept_ref[...].astype(F32) + came_ref[...].astype(F32)
    half = total.shape[1] // 2
    keep_ref[...] = total[:, :half].astype(BF16)
    send_ref[...] = total[:, half:].astype(BF16)


def heads_body(me_ref, n0_ref, n1_ref, n2_ref, n3_ref, proj_ref, part_ref, slope_ref):
    rows, width = n0_ref.shape
    me = me_ref[0]
    piece = width // 4
    cols = [proj_ref[:, pl.ds(pl.multiple_of(b * width + me * piece, LANES), piece)] for b in (1, 2, 3)]
    weight = jnp.concatenate(cols, axis=1)
    for step, ref in enumerate((n0_ref, n1_ref, n2_ref, n3_ref)):
        act, slope = silu_both(mm(ref[...], weight))
        at = pl.ds(pl.multiple_of((me ^ step) * rows, rows), rows)
        part_ref[at, :] = act.astype(BF16)
        slope_ref[at, :] = slope


def block_at(block, rows):
    return pl.ds(pl.multiple_of(block * rows, rows), rows)


def visit(first, second, same, lengths_ref, part_ref, grad_ref, total_ref):
    rows, piece = grad_ref.shape[0] // 4, grad_ref.shape[1]
    q_block, k_block = jnp.maximum(first, second), jnp.minimum(first, second)

    def work():
        q_at, k_at = block_at(q_block, rows), block_at(k_block, rows)
        left = iota((1, LANES), 1) < LANES // 2
        query_pos = q_block * rows + iota((1, rows), 1)
        start = history_start(query_pos, lengths_ref)
        key_pos = k_block * rows + iota((rows, 1), 0)
        inverse = 1.0 / (query_pos - start + 1).astype(F32)
        allowed = key_pos >= start
        if same:
            allowed &= key_pos <= query_pos
        shared = jnp.where(allowed, inverse, 0.0)
        value = part_ref[k_at, :piece]
        query = part_ref[q_at, piece : 2 * piece]
        key = part_ref[k_at, 2 * piece :]
        grad = grad_ref[q_at, :]
        small = value * jnp.asarray(0.0625, BF16)
        d_value, d_query, d_key = 0.0, 0.0, 0.0
        for mine in (left, ~left):
            query_h = jnp.where(mine, query, 0).astype(BF16)
            key_h = jnp.where(mine, key, 0).astype(BF16)
            grad_h = jnp.where(mine, grad, 0).astype(BF16)
            half = mm_t(key_h, query) * 0.0625
            up = 1.0 + jnp.tanh(half)
            act = half * up
            weights = (act * shared).astype(BF16)
            slope = (up + act * (2.0 - up)) * shared
            d_scores = (mm_t(small, grad_h) * slope).astype(BF16)
            d_value += mm(weights, grad_h)
            d_key += mm(d_scores, query_h)
            d_query += t_mm(d_scores, key_h)
        total_ref[k_at, :piece] += d_value
        total_ref[q_at, piece : 2 * piece] += d_query
        total_ref[k_at, 2 * piece :] += d_key

    if same:
        work()
    else:
        pl.when((k_block + 1) * rows > history_start(q_block * rows, lengths_ref))(work)


def backward_rows(steps, finished, me, lengths_ref, part_ref, slope_ref, grad_ref, total_ref, refs):
    done = list(finished)
    for step, ref in zip(steps, refs):
        for other in range(4):
            if other not in done:
                visit(me ^ step, me ^ other, other == step, lengths_ref, part_ref, grad_ref, total_ref)
        done.append(step)
        at = block_at(me ^ step, ref.shape[0])
        ref[...] = (total_ref[at, :] * slope_ref[at, :]).astype(BF16)


def backward_far_body(
    me_ref, lengths_ref, g0_ref, g1_ref, g2_ref, g3_ref, part_ref, slope_ref, *rest
):
    o2_ref, o3_ref, total_ref, grad_ref = rest[-4:]
    rows = g0_ref.shape[0]
    me = me_ref[0]
    for step, ref in enumerate((g0_ref, g1_ref, g2_ref, g3_ref)):
        grad_ref[block_at(me ^ step, rows), :] = ref[...]
    total_ref[...] = jnp.zeros_like(total_ref)
    backward_rows(
        (2, 3), (), me, lengths_ref, part_ref, slope_ref, grad_ref, total_ref, (o2_ref, o3_ref)
    )


def backward_rest_body(
    me_ref, lengths_ref, part_ref, slope_ref, grad_ref, sums_ref, o0_ref, o1_ref, total_ref
):
    total_ref[...] = sums_ref[...]
    backward_rows(
        (1, 0), (2, 3), me_ref[0], lengths_ref, part_ref, slope_ref, grad_ref, total_ref, (o1_ref, o0_ref)
    )


def weight_body(sources, pairs, dp_ref, kept_side_ref, came_side_ref, *refs):
    normed, grads = refs[:sources], refs[sources : 2 * sources]
    outs, total_ref = refs[2 * sources : -1], refs[-1]
    side = kept_side_ref.shape[1]
    total = 0.0
    for n_ref, g_ref in zip(normed, grads):
        total += t_mm(n_ref[...], g_ref[...])
    total_ref[:, :side] = kept_side_ref[...].astype(F32) + came_side_ref[...].astype(F32)
    total_ref[:, side:] = total
    if len(outs) == 1:
        outs[0][...] = total_ref[...].astype(BF16)
        return
    kept_ref, sent_ref = outs
    share = kept_ref.shape[0] // pairs
    for j in range(pairs):
        at = slice(j * share, (j + 1) * share)
        for ref, k in ((kept_ref, 2 * j), (sent_ref, 2 * j + 1)):
            source = pl.ds(pl.multiple_of((dp_ref[0] ^ k) * share, share), share)
            ref[at, :] = total_ref[source, :].astype(BF16)


def halve_body(pairs, kept_ref, came_ref, *refs):
    keep_ref, send_ref = refs[-2:]
    share = kept_ref.shape[0] // pairs
    total = kept_ref[...].astype(F32) + came_ref[...].astype(F32)
    for j in range(pairs):
        at = slice(j // 2 * share, (j // 2 + 1) * share)
        (send_ref if j % 2 else keep_ref)[at, :] = total[j * share : (j + 1) * share].astype(BF16)


def head_columns(owner, proj_ref):
    width = proj_ref.shape[0]
    cols = [proj_ref[:, pl.ds(pl.multiple_of(b * width + owner * LANES, LANES), LANES)] for b in (1, 2, 3)]
    return jnp.concatenate(cols, axis=1)


def input_far_body(me_ref, far_ref, cross_ref, gate_in_ref, proj_ref, out_ref):
    me = me_ref[0]
    total = gate_in_ref[...] + mm_t(far_ref[...], head_columns(me ^ 2, proj_ref))
    out_ref[...] = total + mm_t(cross_ref[...], head_columns(me ^ 3, proj_ref))


def input_body(
    blocks, me_ref, mask_ref, own_ref, near_ref, partial_ref,
    owned_ref, cot_ref, landing_ref, proj_ref, out_ref,
):
    rows = owned_ref.shape[0]
    me = me_ref[0]
    total = partial_ref[...] + mm_t(own_ref[...], head_columns(me, proj_ref))
    total += mm_t(near_ref[...], head_columns(me ^ 1, proj_ref))
    centred, inv_scale = normalize(owned_ref[...].astype(F32))
    grad = (norm_back(total, centred, inv_scale) + cot_ref[...].astype(F32)).astype(BF16)
    select = hot(iota((rows, landing_ref.shape[1]), 0) + 1 == landing_ref[...])
    value = t_mm(select, grad)
    size = value.shape[0] // blocks
    for k in range(blocks):
        at = pl.ds(pl.multiple_of((mask_ref[0] ^ k) * size, size), size)
        out_ref[at, :] = value[k * size : (k + 1) * size].astype(BF16)


def return_body(capacity, mask_ref, owner_ref, back_ref, out_ref):
    owner = owner_ref[...] ^ mask_ref[0]
    rank_row, _ = rank_rows(owner)
    chosen = hot(iota((back_ref.shape[0], owner.shape[1]), 0) == owner * capacity + rank_row)
    out_ref[...] = t_mm(chosen, back_ref[...]).astype(BF16)


def sum_body(*refs):
    total = 0.0
    for ref in refs[:-1]:
        parts = ref[...].astype(F32)
        total += parts if ref.ndim == 2 else jnp.sum(parts, axis=0)
    refs[-1][...] = total.astype(BF16)


def finish_body(me_ref, w0_ref, w1_ref, w2_ref, w3_ref, proj_ref, outw_ref):
    me = me_ref[0]
    width = outw_ref.shape[1]
    for step, ref in enumerate((w0_ref, w1_ref, w2_ref, w3_ref)):
        at = pl.ds(pl.multiple_of((me ^ step) * LANES, LANES), LANES)
        outw_ref[:, at] = ref[:, LANES : 2 * LANES].astype(F32)
        for b, source in enumerate((0, 2, 3, 4)):
            at = pl.ds(pl.multiple_of(b * width + (me ^ step) * LANES, LANES), LANES)
            proj_ref[:, at] = ref[:, source * LANES : (source + 1) * LANES].astype(F32)


def on_device(tokens, dest_owner, dest_slot, lengths, proj_weight, out_weight, cotangent):
    rows, width = tokens.shape
    owners = lax.axis_size("dp")
    cycle = lax.axis_size("ctx")
    assert cycle == 4 and width == cycle * LANES
    capacity = 2 * rows // owners
    stride = capacity + 8
    piece = width // cycle
    me = lax.axis_index("ctx").astype(jnp.int32).reshape(1)
    owner_row = dest_owner.reshape(1, rows)
    slot_row = dest_slot.reshape(1, rows)
    square = ((rows, width), BF16)

    def hop(value, step):
        return lax.ppermute(value, "ctx", [(i, i ^ step) for i in range(cycle)])

    def gather(value):
        near, far = hop(value, 1), hop(value, 2)
        return near, far, hop(far, 1)

    def exchange(values):
        return [values[0]] + [hop(values[step], step) for step in (2, 3, 1)]

    by_hops = owners <= 8
    blocks = owners if by_hops else 1
    dp = lax.axis_index("dp").astype(jnp.int32).reshape(1)
    mask = dp if by_hops else jnp.zeros_like(dp)

    def dp_hop(value, step):
        return lax.ppermute(value, "dp", [(i, i ^ step) for i in range(owners)])

    def swap_whole(value):
        split = value.reshape(owners, value.shape[0] // owners, value.shape[1])
        return lax.all_to_all(split, "dp", split_axis=0, concat_axis=0, tiled=True).reshape(value.shape)

    def swap(values):
        if by_hops:
            return [dp_hop(values[k], k) if k else values[k] for k in hop_order(owners)]
        return [swap_whole(values[0])]

    def block_shapes(height, columns, dtype):
        return [((owners * height // blocks, columns), dtype)] * blocks

    wide = ((rows, width), F32)
    late = blocks // 2
    far_blocks = call(
        functools.partial(pack_far_body, capacity, stride, late, blocks - late),
        "pack_far",
        block_shapes(stride, width, BF16)[late:] + [((1, rows), jnp.int32)] * 2 + [square],
        [mask], [], far=[owner_row, slot_row, tokens], scratch=[pltpu.SemaphoreType.DMA((3,))],
    )
    *far_blocks, owner_here, slot_here, tokens_here = far_blocks
    (grad_gated,) = call(early_body, "early", [wide], [], [cotangent, out_weight, proj_weight])
    near_blocks = call(
        functools.partial(pack_near_body, capacity, stride, late),
        "pack_near", block_shapes(stride, width, BF16)[:late], [],
        [owner_here, slot_here, tokens_here], far=[grad_gated],
    ) if late else []
    arrived = swap([*near_blocks, *far_blocks])
    owned, normed, landing = call(
        functools.partial(place_body, owners, capacity, stride),
        "place", [square, square, ((1, owners * capacity), jnp.int32)], [], arrived,
    )
    near, far, cross = gather(normed)
    gate, slope, query, partial = call(
        own_body, "own_rows", [square, wide, square, wide],
        [me, lengths], [normed, proj_weight], flops=10**10, vmem=16,
    )
    (partial,) = call(
        middle_body, "middle", [wide], [me, lengths], [near, far, proj_weight, query, partial],
        flops=10**10, vmem=16,
    )
    layer_out, gated, gate_grad, *grad_pieces = call(
        forward_body, "forward",
        [square, square, square] + [((rows, piece), BF16)] * cycle,
        [me, lengths],
        [cross, proj_weight, out_weight, owned, gate, slope, query, partial, grad_gated],
        scratch=[pltpu.VMEM((rows, width), F32)], vmem=16,
    )
    r0, r2, r3, r1 = exchange(grad_pieces)
    side_half = ((width, 4 * piece), BF16)
    side_piece = ((width, 2 * piece), BF16)
    side_kept, side_sent, gate_in = call(
        side_body, "side", [side_half, side_half, wide],
        [me], [normed, gated, cotangent, gate_grad, proj_weight],
        scratch=[pltpu.VMEM((width, 2 * width), F32)], vmem=16,
    )
    side_came = hop(side_sent, 1)
    parts, slopes = call(
        heads_body, "heads",
        [((rows * cycle, 3 * piece), BF16), ((rows * cycle, 3 * piece), F32)],
        [me], [normed, near, far, cross, proj_weight], vmem=16,
    )
    side_keep, side_send = call(
        side_sum_body, "side_sum", [side_piece, side_piece], [], [side_kept, side_came]
    )
    side_last = hop(side_send, 2)
    grad_block = ((rows, 3 * piece), BF16)
    sums = ((rows * cycle, 3 * piece), F32)
    grad_rows = ((rows * cycle, piece), BF16)
    far_block, cross_block, totals, grad_all = call(
        backward_far_body, "backward_far", [grad_block, grad_block, sums, grad_rows],
        [me, lengths], [r0, r1, r2, r3, parts, slopes], flops=10**10, vmem=16,
    )
    p2, p3 = hop(far_block, 2), hop(cross_block, 3)
    own_block, near_block = call(
        backward_rest_body, "backward_rest", [grad_block] * 2,
        [me, lengths], [parts, slopes, grad_all, totals], vmem=16,
        scratch=[pltpu.VMEM(*sums)],
    )
    p1 = hop(near_block, 1)
    grads = [own_block, near_block, far_block, cross_block]
    share = width // owners
    pairs = owners // 2
    columns = 5 * piece
    weight_parts = call(
        functools.partial(weight_body, cycle, pairs), "weights",
        [((pairs * share, columns), BF16)] * 2 if by_hops else [((width, columns), BF16)], [dp],
        [side_keep, side_last, normed, near, far, cross, *grads], vmem=16,
        scratch=[pltpu.VMEM((width, columns), F32)],
    )
    (partial_in,) = call(
        input_far_body, "input_far", [wide], [me], [p2, p3, gate_in, proj_weight], flops=6 * 10**9,
    )
    (back,) = call(
        functools.partial(input_body, blocks), "input_grad", [((owners * capacity, width), BF16)], [me, mask],
        [own_block, p1, partial_in, owned, cotangent, landing, proj_weight], vmem=16,
    )
    returned = swap_whole(back)
    if by_hops:
        kept, sent = weight_parts
        came, behind, bit = dp_hop(sent, 1), [back], 2
        while bit < owners:
            kept, sent = call(
                functools.partial(halve_body, pairs), "halve",
                [((pairs * share // 2, columns), BF16)] * 2, [], [kept, came], far=behind,
            )
            came, behind, bit, pairs = dp_hop(sent, bit), [], 2 * bit, pairs // 2
        summed_parts = [kept, came]
    else:
        summed_parts = [swap_whole(weight_parts[0]).reshape(owners, share, columns)]
    (mine,) = call(sum_body, "sum", [((share, columns), BF16)], [], summed_parts)
    w1, w2, w3 = (hop(mine, step) for step in range(1, cycle))
    (grad_tokens,) = call(
        functools.partial(return_body, capacity), "give_back", [square], [mask], [owner_here, returned]
    )
    grad_proj, grad_outw = call(
        finish_body, "finish", [((share, 4 * width), F32), ((share, width), F32)],
        [me], [mine, w1, w2, w3],
    )
    return layer_out, grad_tokens, grad_proj, grad_outw


def solution(mesh):
    placed = (
        P(("dp", "ctx"), None),
        P(("dp", "ctx")),
        P(("dp", "ctx")),
        P("dp", None),
        P(),
        P(),
        P(("dp", "ctx"), None),
    )
    return jax.shard_map(
        on_device,
        mesh=mesh,
        in_specs=placed,
        out_specs=(P(("dp", "ctx"), None), P(("dp", "ctx"), None), P("dp", None), P("dp", None)),
        check_vma=False,
    )
```

```python
import functools

import jax
import jax.numpy as jnp
from jax import lax
from jax.experimental import pallas as pl
from jax.experimental.pallas import tpu as pltpu
from jax.sharding import PartitionSpec as P

HEADS = 8
EPSILON = 1e-05
LANES = 128
F32 = jnp.float32
BF16 = jnp.bfloat16

WHOLE = pl.BlockSpec(memory_space=pltpu.VMEM)
SCALARS = pl.BlockSpec(memory_space=pltpu.SMEM)
ANYWHERE = pl.BlockSpec(memory_space=pltpu.HBM)


def call(body, name, outs, scalars, arrays, scratch=(), flops=10**8, vmem=8, far=()):
    return pl.pallas_call(
        body,
        name=name,
        out_shape=[jax.ShapeDtypeStruct(s, d) for s, d in outs],
        in_specs=[SCALARS] * len(scalars) + [WHOLE] * len(arrays) + [ANYWHERE] * len(far),
        out_specs=[WHOLE] * len(outs),
        scratch_shapes=list(scratch),
        compiler_params=pltpu.CompilerParams(vmem_limit_bytes=vmem * 2**20),
        cost_estimate=pl.CostEstimate(flops=flops, bytes_accessed=2**20, transcendentals=0),
    )(*scalars, *arrays, *far)


def iota(shape, dim):
    return lax.broadcasted_iota(jnp.int32, shape, dim)


def mm(a, b):
    return jnp.dot(a, b, preferred_element_type=F32)


def mm_t(a, b):
    return lax.dot_general(a, b, (((1,), (1,)), ((), ())), preferred_element_type=F32)


def t_mm(a, b):
    return lax.dot_general(a, b, (((0,), (0,)), ((), ())), preferred_element_type=F32)


def hot(condition):
    return jnp.where(condition, 1.0, 0.0).astype(BF16)


def normalize(value):
    middle = jnp.mean(value, axis=-1, keepdims=True)
    centred = value - middle
    inv_dev = lax.rsqrt(jnp.mean(centred * centred, axis=-1, keepdims=True) + EPSILON)
    return centred * inv_dev, inv_dev


def norm_back(grad, normed, inv_dev):
    return inv_dev * (
        grad
        - jnp.mean(grad, axis=-1, keepdims=True)
        - normed * jnp.mean(grad * normed, axis=-1, keepdims=True)
    )


def silu_both(value):
    squashed = 0.5 * jnp.tanh(0.5 * value) + 0.5
    return value * squashed, squashed * (1.0 + value * (1.0 - squashed))


def rank_rows(owner):
    rows = owner.shape[1]
    down, across = iota((rows, rows), 0), iota((rows, rows), 1)
    spread = jnp.broadcast_to(owner, (rows, rows))
    owner_col = jnp.sum(jnp.where(down == across, spread, 0).astype(F32), axis=1, keepdims=True)
    same = owner_col.astype(jnp.int32) == spread
    rank_row = jnp.sum(jnp.where(same & (down < across), 1.0, 0.0), axis=0, keepdims=True)
    rank_col = jnp.sum(jnp.where(same & (across < down), 1.0, 0.0), axis=1, keepdims=True)
    return rank_row.astype(jnp.int32), rank_col.astype(jnp.int32)


def fetch(sources, targets, sems):
    copies = [pltpu.make_async_copy(a, b, sems.at[i]) for i, (a, b) in enumerate(zip(sources, targets))]
    for copy in copies:
        copy.start()
    for copy in copies:
        copy.wait()


def store_blocks(refs, value):
    size = refs[0].shape[0]
    for i, ref in enumerate(refs):
        ref[...] = value[i * size : (i + 1) * size].astype(ref.dtype)


def hop_order(count):
    return sorted(range(count), key=lambda k: (0 < k < count // 2, k))


def load_blocks(refs):
    order = hop_order(len(refs))
    return jnp.concatenate(
        [refs[order.index(k)][...].astype(F32) for k in range(len(refs))], axis=0
    ).astype(BF16)


def pack_body(capacity, stride, outs, mask_ref, owner_hbm, slot_hbm, tokens_hbm, *refs):
    out_refs, (owner_ref, slot_ref, tokens_ref, sems) = refs[:outs], refs[outs:]
    fetch((owner_hbm, slot_hbm, tokens_hbm), (owner_ref, slot_ref, tokens_ref), sems)
    owner = owner_ref[...] ^ mask_ref[0]
    owner_ref[...] = owner
    rows = owner.shape[1]
    rank_row, rank_col = rank_rows(owner)
    total, width = outs * out_refs[0].shape[0], out_refs[0].shape[1]
    place = iota((total, rows), 0)
    chosen = hot(place == owner * stride + rank_row)
    slots = jnp.where(place == owner * stride + capacity, slot_ref[...] + 1, 0)
    by_rank = hot(rank_col == iota((rows, width), 1))
    store_blocks(out_refs, mm(chosen, tokens_ref[...]) + mm(slots.astype(F32).astype(BF16), by_rank))


def relay(value, after):
    return pl.pallas_call(
        lambda *refs: None,
        name="relay",
        out_shape=jax.ShapeDtypeStruct(value.shape, value.dtype),
        in_specs=[ANYWHERE] * (1 + len(after)),
        out_specs=ANYWHERE,
        input_output_aliases={0: 0},
    )(value, *after)


def block_rem(owners, stride):
    col, first = iota((owners, owners * stride), 1), iota((owners, owners * stride), 0)
    above = jnp.sum(jnp.where(col >= stride * (first + 1), 1.0, 0.0), axis=0, keepdims=True)
    rem = iota((1, owners * stride), 1) - stride * above.astype(jnp.int32)
    inside = (col >= stride * first) & (col < stride * (first + 1))
    return rem, inside


def landing_row(table, owners, capacity, stride):
    rem, inside = block_rem(owners, stride)
    lanes = iota((table.shape[1], owners * stride), 0)
    spread = mm(table, hot((lanes == rem) & (lanes < capacity)))
    return jnp.sum(jnp.where(inside, spread, 0.0), axis=0, keepdims=True)


def place_body(owners, capacity, stride, *refs):
    owned_ref, normed_ref, landing_ref = refs[-3:]
    rows = owned_ref.shape[0]
    arrived = load_blocks(refs[:-3])
    total = arrived.shape[0]
    pick = hot(iota((owners, total), 1) == iota((owners, total), 0) * stride + capacity)
    table = mm(pick, arrived).astype(BF16)
    landing = landing_row(table, owners, capacity, stride).astype(jnp.int32)
    owned = mm(hot(iota((rows, total), 0) + 1 == landing), arrived)
    owned_ref[...] = owned.astype(BF16)
    normed_ref[...] = normalize(owned)[0].astype(BF16)
    landing_ref[...] = landing_row(table, owners, capacity, capacity).astype(jnp.int32)


def early_body(cot_ref, outw_ref, proj_ref, grad_ref):
    grad_ref[...] = mm_t(cot_ref[...], outw_ref[...])


def history_start(pos, lengths_ref):
    first = lengths_ref[0, 0]
    second = lengths_ref[0, 1]
    return jnp.where(pos >= first + second, first + second, jnp.where(pos >= first, first, 0))


def attend(query_ref, key, value, shared, acc_ref):
    width = query_ref.shape[1]
    left = iota((1, LANES), 1) < LANES // 2
    for pair in range(width // LANES):
        cols = slice(pair * LANES, (pair + 1) * LANES)
        query, key_pair, value_pair = query_ref[:, cols], key[:, cols], value[:, cols]
        total = acc_ref[:, cols]
        for mine in (left, ~left):
            half = mm_t(jnp.where(mine, query, 0).astype(BF16), key_pair) * 0.0625
            weights = (half * (1.0 + jnp.tanh(half)) * shared).astype(BF16)
            total += mm(weights, jnp.where(mine, value_pair, 0).astype(BF16))
        acc_ref[:, cols] = total


def shared_factor(block, me, rows, lengths_ref):
    query_pos = me * rows + iota((rows, 1), 0)
    start = history_start(query_pos, lengths_ref)
    inverse = 1.0 / (query_pos - start + 1).astype(F32)
    key_pos = block * rows + iota((1, rows), 1)
    return jnp.where((key_pos >= start) & (key_pos <= query_pos), inverse, 0.0)


def attend_other(step, me, lengths_ref, other_ref, proj_ref, query_ref, acc_ref):
    rows, width = query_ref.shape
    block = me ^ step
    reach = history_start(me * rows, lengths_ref)

    @pl.when((block < me) & ((block + 1) * rows > reach))
    def _():
        normed = other_ref[...]
        value = silu_both(mm(normed, proj_ref[:, width : 2 * width]))[0].astype(BF16)
        key = silu_both(mm(normed, proj_ref[:, 3 * width :]))[0].astype(BF16)
        attend(query_ref, key, value, shared_factor(block, me, rows, lengths_ref), acc_ref)


def own_body(me_ref, lengths_ref, normed_ref, proj_ref, gate_ref, slope_ref, query_ref, acc_ref):
    rows, width = normed_ref.shape
    me = me_ref[0]
    preact = mm(normed_ref[...], proj_ref[...])
    gate, slope = silu_both(preact[:, :width])
    gate_ref[...] = gate.astype(BF16)
    slope_ref[...] = slope
    value = silu_both(preact[:, width : 2 * width])[0].astype(BF16)
    query_ref[...] = silu_both(preact[:, 2 * width : 3 * width])[0].astype(BF16)
    key = silu_both(preact[:, 3 * width :])[0].astype(BF16)
    acc_ref[...] = jnp.zeros_like(acc_ref)
    attend(query_ref, key, value, shared_factor(me, me, rows, lengths_ref), acc_ref)


def middle_body(me_ref, lengths_ref, near_ref, far_ref, proj_ref, query_ref, partial_ref, acc_ref):
    me = me_ref[0]
    acc_ref[...] = partial_ref[...]
    attend_other(1, me, lengths_ref, near_ref, proj_ref, query_ref, acc_ref)
    attend_other(2, me, lengths_ref, far_ref, proj_ref, query_ref, acc_ref)


def forward_body(
    me_ref, lengths_ref, cross_ref, proj_ref, outw_ref, owned_ref,
    gate_ref, slope_ref, query_ref, partial_ref, grad_ref,
    out_ref, gated_ref, gate_grad_ref, *rest,
):
    grads, acc_ref = rest[:-1], rest[-1]
    rows, width = query_ref.shape
    me = me_ref[0]
    acc_ref[...] = partial_ref[...]
    attend_other(3, me, lengths_ref, cross_ref, proj_ref, query_ref, acc_ref)
    gate = gate_ref[...].astype(F32)
    normed, inv_dev = normalize(acc_ref[...])
    gated = (normed * gate).astype(BF16)
    gated_ref[...] = gated
    grad_gated = grad_ref[...]
    grad_attended = norm_back(grad_gated * gate, normed, inv_dev).astype(BF16)
    acc_ref[...] = grad_attended.astype(F32)
    piece = width // len(grads)
    for step, ref in enumerate(grads):
        ref[...] = acc_ref[:, pl.ds(pl.multiple_of((me ^ step) * piece, LANES), piece)].astype(BF16)
    out_ref[...] = (mm(gated, outw_ref[...]) + owned_ref[...].astype(F32)).astype(BF16)
    gate_grad_ref[...] = (grad_gated * normed * slope_ref[...]).astype(BF16)


def side_body(me_ref, normed_ref, gated_ref, cot_ref, gate_grad_ref, proj_ref, kept_ref, sent_ref, gate_in_ref, part_ref):
    width = gated_ref.shape[1]
    me = me_ref[0]
    gate_grad = gate_grad_ref[...]
    part_ref[:, :width] = t_mm(normed_ref[...], gate_grad)
    part_ref[:, width:] = t_mm(gated_ref[...], cot_ref[...])
    gate_in_ref[...] = mm_t(gate_grad, proj_ref[:, :width])
    for ref, steps in ((kept_ref, (0, 2)), (sent_ref, (1, 3))):
        place = 0
        for step in steps:
            for base in (0, width):
                source = pl.ds(pl.multiple_of(base + (me ^ step) * LANES, LANES), LANES)
                ref[:, place : place + LANES] = part_ref[:, source].astype(BF16)
                place += LANES


def side_sum_body(kept_ref, came_ref, keep_ref, send_ref):
    total = kept_ref[...].astype(F32) + came_ref[...].astype(F32)
    half = total.shape[1] // 2
    keep_ref[...] = total[:, :half].astype(BF16)
    send_ref[...] = total[:, half:].astype(BF16)


def heads_body(me_ref, n0_ref, n1_ref, n2_ref, n3_ref, proj_ref, part_ref, slope_ref):
    rows, width = n0_ref.shape
    me = me_ref[0]
    piece = width // 4
    cols = [proj_ref[:, pl.ds(pl.multiple_of(b * width + me * piece, LANES), piece)] for b in (1, 2, 3)]
    weight = jnp.concatenate(cols, axis=1)
    for step, ref in enumerate((n0_ref, n1_ref, n2_ref, n3_ref)):
        act, slope = silu_both(mm(ref[...], weight))
        at = pl.ds(pl.multiple_of((me ^ step) * rows, rows), rows)
        part_ref[at, :] = act.astype(BF16)
        slope_ref[at, :] = slope


def block_at(block, rows):
    return pl.ds(pl.multiple_of(block * rows, rows), rows)


def visit(first, second, same, lengths_ref, part_ref, grad_ref, total_ref):
    rows, piece = grad_ref.shape[0] // 4, grad_ref.shape[1]
    q_block, k_block = jnp.maximum(first, second), jnp.minimum(first, second)

    def work():
        q_at, k_at = block_at(q_block, rows), block_at(k_block, rows)
        left = iota((1, LANES), 1) < LANES // 2
        query_pos = q_block * rows + iota((1, rows), 1)
        start = history_start(query_pos, lengths_ref)
        key_pos = k_block * rows + iota((rows, 1), 0)
        inverse = 1.0 / (query_pos - start + 1).astype(F32)
        allowed = key_pos >= start
        if same:
            allowed &= key_pos <= query_pos
        shared = jnp.where(allowed, inverse, 0.0)
        value = part_ref[k_at, :piece]
        query = part_ref[q_at, piece : 2 * piece]
        key = part_ref[k_at, 2 * piece :]
        grad = grad_ref[q_at, :]
        small = value * jnp.asarray(0.0625, BF16)
        d_value, d_query, d_key = 0.0, 0.0, 0.0
        for mine in (left, ~left):
            query_h = jnp.where(mine, query, 0).astype(BF16)
            key_h = jnp.where(mine, key, 0).astype(BF16)
            grad_h = jnp.where(mine, grad, 0).astype(BF16)
            half = mm_t(key_h, query) * 0.0625
            up = 1.0 + jnp.tanh(half)
            act = half * up
            weights = (act * shared).astype(BF16)
            slope = (up + act * (2.0 - up)) * shared
            d_scores = (mm_t(small, grad_h) * slope).astype(BF16)
            d_value += mm(weights, grad_h)
            d_key += mm(d_scores, query_h)
            d_query += t_mm(d_scores, key_h)
        total_ref[k_at, :piece] += d_value
        total_ref[q_at, piece : 2 * piece] += d_query
        total_ref[k_at, 2 * piece :] += d_key

    if same:
        work()
    else:
        pl.when((k_block + 1) * rows > history_start(q_block * rows, lengths_ref))(work)


def backward_rows(steps, finished, me, lengths_ref, part_ref, slope_ref, grad_ref, total_ref, refs):
    done = list(finished)
    for step, ref in zip(steps, refs):
        for other in range(4):
            if other not in done:
                visit(me ^ step, me ^ other, other == step, lengths_ref, part_ref, grad_ref, total_ref)
        done.append(step)
        at = block_at(me ^ step, ref.shape[0])
        ref[...] = (total_ref[at, :] * slope_ref[at, :]).astype(BF16)


def backward_far_body(
    me_ref, lengths_ref, g0_ref, g1_ref, g2_ref, g3_ref, part_ref, slope_ref, *rest
):
    o2_ref, o3_ref, total_ref, grad_ref = rest[-4:]
    rows = g0_ref.shape[0]
    me = me_ref[0]
    for step, ref in enumerate((g0_ref, g1_ref, g2_ref, g3_ref)):
        grad_ref[block_at(me ^ step, rows), :] = ref[...]
    total_ref[...] = jnp.zeros_like(total_ref)
    backward_rows(
        (2, 3), (), me, lengths_ref, part_ref, slope_ref, grad_ref, total_ref, (o2_ref, o3_ref)
    )


def backward_rest_body(
    me_ref, lengths_ref, part_ref, slope_ref, grad_ref, sums_ref, o0_ref, o1_ref, total_ref
):
    total_ref[...] = sums_ref[...]
    backward_rows(
        (1, 0), (2, 3), me_ref[0], lengths_ref, part_ref, slope_ref, grad_ref, total_ref, (o1_ref, o0_ref)
    )


def weight_body(sources, pairs, dp_ref, kept_side_ref, came_side_ref, *refs):
    normed, grads = refs[:sources], refs[sources : 2 * sources]
    outs, total_ref = refs[2 * sources : -1], refs[-1]
    side = kept_side_ref.shape[1]
    total = 0.0
    for n_ref, g_ref in zip(normed, grads):
        total += t_mm(n_ref[...], g_ref[...])
    total_ref[:, :side] = kept_side_ref[...].astype(F32) + came_side_ref[...].astype(F32)
    total_ref[:, side:] = total
    if len(outs) == 1:
        outs[0][...] = total_ref[...].astype(BF16)
        return
    kept_ref, sent_ref = outs
    share = kept_ref.shape[0] // pairs
    for j in range(pairs):
        at = slice(j * share, (j + 1) * share)
        for ref, k in ((kept_ref, 2 * j), (sent_ref, 2 * j + 1)):
            source = pl.ds(pl.multiple_of((dp_ref[0] ^ k) * share, share), share)
            ref[at, :] = total_ref[source, :].astype(BF16)


def halve_body(pairs, kept_ref, came_ref, *refs):
    keep_ref, send_ref = refs[-2:]
    share = kept_ref.shape[0] // pairs
    total = kept_ref[...].astype(F32) + came_ref[...].astype(F32)
    for j in range(pairs):
        at = slice(j // 2 * share, (j // 2 + 1) * share)
        (send_ref if j % 2 else keep_ref)[at, :] = total[j * share : (j + 1) * share].astype(BF16)


def head_columns(owner, proj_ref):
    width = proj_ref.shape[0]
    cols = [proj_ref[:, pl.ds(pl.multiple_of(b * width + owner * LANES, LANES), LANES)] for b in (1, 2, 3)]
    return jnp.concatenate(cols, axis=1)


def input_far_body(me_ref, far_ref, cross_ref, gate_in_ref, proj_ref, out_ref):
    me = me_ref[0]
    total = gate_in_ref[...] + mm_t(far_ref[...], head_columns(me ^ 2, proj_ref))
    out_ref[...] = total + mm_t(cross_ref[...], head_columns(me ^ 3, proj_ref))


def input_body(
    blocks, me_ref, mask_ref, own_ref, near_ref, partial_ref,
    owned_ref, cot_ref, landing_ref, proj_ref, *rest,
):
    out_ref = rest[-1]
    rows = owned_ref.shape[0]
    me = me_ref[0]
    total = partial_ref[...] + mm_t(own_ref[...], head_columns(me, proj_ref))
    total += mm_t(near_ref[...], head_columns(me ^ 1, proj_ref))
    centred, inv_scale = normalize(owned_ref[...].astype(F32))
    grad = (norm_back(total, centred, inv_scale) + cot_ref[...].astype(F32)).astype(BF16)
    select = hot(iota((rows, landing_ref.shape[1]), 0) + 1 == landing_ref[...])
    value = t_mm(select, grad)
    size = value.shape[0] // blocks
    for k in range(blocks):
        at = pl.ds(pl.multiple_of((mask_ref[0] ^ k) * size, size), size)
        out_ref[at, :] = value[k * size : (k + 1) * size].astype(BF16)


def return_body(capacity, mask_ref, owner_ref, back_ref, out_ref):
    owner = owner_ref[...] ^ mask_ref[0]
    rank_row, _ = rank_rows(owner)
    chosen = hot(iota((back_ref.shape[0], owner.shape[1]), 0) == owner * capacity + rank_row)
    out_ref[...] = t_mm(chosen, back_ref[...]).astype(BF16)


def sum_body(*refs):
    total = 0.0
    for ref in refs[:-1]:
        parts = ref[...].astype(F32)
        total += parts if ref.ndim == 2 else jnp.sum(parts, axis=0)
    refs[-1][...] = total.astype(BF16)


def finish_body(me_ref, w0_ref, w1_ref, w2_ref, w3_ref, proj_ref, outw_ref):
    me = me_ref[0]
    width = outw_ref.shape[1]
    for step, ref in enumerate((w0_ref, w1_ref, w2_ref, w3_ref)):
        at = pl.ds(pl.multiple_of((me ^ step) * LANES, LANES), LANES)
        outw_ref[:, at] = ref[:, LANES : 2 * LANES].astype(F32)
        for b, source in enumerate((0, 2, 3, 4)):
            at = pl.ds(pl.multiple_of(b * width + (me ^ step) * LANES, LANES), LANES)
            proj_ref[:, at] = ref[:, source * LANES : (source + 1) * LANES].astype(F32)


def on_device(tokens, dest_owner, dest_slot, lengths, proj_weight, out_weight, cotangent):
    rows, width = tokens.shape
    owners = lax.axis_size("dp")
    cycle = lax.axis_size("ctx")
    assert cycle == 4 and width == cycle * LANES
    capacity = 2 * rows // owners
    stride = capacity + 8
    piece = width // cycle
    me = lax.axis_index("ctx").astype(jnp.int32).reshape(1)
    owner_row = dest_owner.reshape(1, rows)
    slot_row = dest_slot.reshape(1, rows)
    square = ((rows, width), BF16)

    def hop(value, step):
        return lax.ppermute(value, "ctx", [(i, i ^ step) for i in range(cycle)])

    def gather(value):
        near, far = hop(value, 1), hop(value, 2)
        return near, far, hop(far, 1)

    def exchange(values):
        return [values[0]] + [hop(values[step], step) for step in (2, 3, 1)]

    by_hops = owners <= 8
    blocks = owners if by_hops else 1
    dp = lax.axis_index("dp").astype(jnp.int32).reshape(1)
    mask = dp if by_hops else jnp.zeros_like(dp)

    def dp_hop(value, step):
        return lax.ppermute(value, "dp", [(i, i ^ step) for i in range(owners)])

    def swap_whole(value):
        split = value.reshape(owners, value.shape[0] // owners, value.shape[1])
        return lax.all_to_all(split, "dp", split_axis=0, concat_axis=0, tiled=True).reshape(value.shape)

    def swap(values):
        if by_hops:
            return [dp_hop(values[k], k) if k else values[k] for k in hop_order(owners)]
        return [swap_whole(values[0])]

    def block_shapes(height, columns, dtype):
        return [((owners * height // blocks, columns), dtype)] * blocks

    wide = ((rows, width), F32)
    *outgoing, owner_here = call(
        functools.partial(pack_body, capacity, stride, blocks),
        "pack", block_shapes(stride, width, BF16) + [((1, rows), jnp.int32)],
        [mask], [], far=[owner_row, slot_row, tokens],
        scratch=[
            pltpu.VMEM((1, rows), jnp.int32),
            pltpu.VMEM((rows, width), BF16),
            pltpu.SemaphoreType.DMA((3,)),
        ],
    )
    (grad_gated,) = call(early_body, "early", [wide], [], [cotangent, out_weight, proj_weight])
    if by_hops:
        outgoing[owners // 4] = relay(outgoing[owners // 4], [grad_gated])
    arrived = swap(outgoing)
    owned, normed, landing = call(
        functools.partial(place_body, owners, capacity, stride),
        "place", [square, square, ((1, owners * capacity), jnp.int32)], [], arrived,
    )
    near, far, cross = gather(normed)
    gate, slope, query, partial = call(
        own_body, "own_rows", [square, wide, square, wide],
        [me, lengths], [normed, proj_weight], flops=10**10, vmem=16,
    )
    (partial,) = call(
        middle_body, "middle", [wide], [me, lengths], [near, far, proj_weight, query, partial],
        flops=10**10, vmem=16,
    )
    layer_out, gated, gate_grad, *grad_pieces = call(
        forward_body, "forward",
        [square, square, square] + [((rows, piece), BF16)] * cycle,
        [me, lengths],
        [cross, proj_weight, out_weight, owned, gate, slope, query, partial, grad_gated],
        scratch=[pltpu.VMEM((rows, width), F32)], vmem=16,
    )
    r0, r2, r3, r1 = exchange(grad_pieces)
    side_half = ((width, 4 * piece), BF16)
    side_piece = ((width, 2 * piece), BF16)
    side_kept, side_sent, gate_in = call(
        side_body, "side", [side_half, side_half, wide],
        [me], [normed, gated, cotangent, gate_grad, proj_weight],
        scratch=[pltpu.VMEM((width, 2 * width), F32)], vmem=16,
    )
    side_came = hop(side_sent, 1)
    parts, slopes = call(
        heads_body, "heads",
        [((rows * cycle, 3 * piece), BF16), ((rows * cycle, 3 * piece), F32)],
        [me], [normed, near, far, cross, proj_weight], vmem=16,
    )
    side_keep, side_send = call(
        side_sum_body, "side_sum", [side_piece, side_piece], [], [side_kept, side_came]
    )
    side_last = hop(side_send, 2)
    grad_block = ((rows, 3 * piece), BF16)
    sums = ((rows * cycle, 3 * piece), F32)
    grad_rows = ((rows * cycle, piece), BF16)
    far_block, cross_block, totals, grad_all = call(
        backward_far_body, "backward_far", [grad_block, grad_block, sums, grad_rows],
        [me, lengths], [r0, r1, r2, r3, parts, slopes], flops=10**10, vmem=16,
    )
    p2, p3 = hop(far_block, 2), hop(cross_block, 3)
    own_block, near_block = call(
        backward_rest_body, "backward_rest", [grad_block] * 2,
        [me, lengths], [parts, slopes, grad_all, totals], vmem=16,
        scratch=[pltpu.VMEM(*sums)],
    )
    p1 = hop(near_block, 1)
    grads = [own_block, near_block, far_block, cross_block]
    share = width // owners
    pairs = owners // 2
    columns = 5 * piece
    weight_parts = call(
        functools.partial(weight_body, cycle, pairs), "weights",
        [((pairs * share, columns), BF16)] * 2 if by_hops else [((width, columns), BF16)], [dp],
        [side_keep, side_last, normed, near, far, cross, *grads], vmem=16,
        scratch=[pltpu.VMEM((width, columns), F32)],
    )
    (partial_in,) = call(
        input_far_body, "input_far", [wide], [me], [p2, p3, gate_in, proj_weight], flops=6 * 10**9,
    )
    came = dp_hop(weight_parts[1], 1) if by_hops else weight_parts[0]
    (back,) = call(
        functools.partial(input_body, blocks), "input_grad", [((owners * capacity, width), BF16)], [me, mask],
        [own_block, p1, partial_in, owned, cotangent, landing, proj_weight], vmem=16,
        far=[came],
    )
    returned = swap_whole(back)
    if by_hops:
        kept, sent = weight_parts
        bit, behind = 2, [back]
        while bit < owners:
            kept, sent = call(
                functools.partial(halve_body, pairs), "halve",
                [((pairs * share // 2, columns), BF16)] * 2, [], [kept, came], far=behind,
            )
            came, bit, pairs, behind = dp_hop(sent, bit), 2 * bit, pairs // 2, []
        summed_parts = [kept, came]
    else:
        summed_parts = [swap_whole(weight_parts[0]).reshape(owners, share, columns)]
    (mine,) = call(sum_body, "sum", [((share, columns), BF16)], [], summed_parts)
    w1, w2, w3 = (hop(mine, step) for step in range(1, cycle))
    (grad_tokens,) = call(
        functools.partial(return_body, capacity), "give_back", [square], [mask], [owner_here, returned]
    )
    grad_proj, grad_outw = call(
        finish_body, "finish", [((share, 4 * width), F32), ((share, width), F32)],
        [me], [mine, w1, w2, w3],
    )
    return layer_out, grad_tokens, grad_proj, grad_outw


def solution(mesh):
    placed = (
        P(("dp", "ctx"), None),
        P(("dp", "ctx")),
        P(("dp", "ctx")),
        P("dp", None),
        P(),
        P(),
        P(("dp", "ctx"), None),
    )
    return jax.shard_map(
        on_device,
        mesh=mesh,
        in_specs=placed,
        out_specs=(P(("dp", "ctx"), None), P(("dp", "ctx"), None), P("dp", None), P("dp", None)),
        check_vma=False,
    )
```

```python
import functools

import jax
import jax.numpy as jnp
from jax import lax
from jax.experimental import pallas as pl
from jax.experimental.pallas import tpu as pltpu
from jax.sharding import PartitionSpec as P

HEADS = 8
EPSILON = 1e-05
LANES = 128
F32 = jnp.float32
BF16 = jnp.bfloat16

WHOLE = pl.BlockSpec(memory_space=pltpu.VMEM)
SCALARS = pl.BlockSpec(memory_space=pltpu.SMEM)
ANYWHERE = pl.BlockSpec(memory_space=pl.ANY)


def call(body, name, outs, scalars, arrays, scratch=(), flops=10**8, vmem=8, far=()):
    return pl.pallas_call(
        body,
        name=name,
        out_shape=[jax.ShapeDtypeStruct(s, d) for s, d in outs],
        in_specs=[SCALARS] * len(scalars) + [WHOLE] * len(arrays) + [ANYWHERE] * len(far),
        out_specs=[WHOLE] * len(outs),
        scratch_shapes=list(scratch),
        compiler_params=pltpu.CompilerParams(vmem_limit_bytes=vmem * 2**20),
        cost_estimate=pl.CostEstimate(flops=flops, bytes_accessed=2**20, transcendentals=0),
    )(*scalars, *arrays, *far)


def iota(shape, dim):
    return lax.broadcasted_iota(jnp.int32, shape, dim)


def mm(a, b):
    return jnp.dot(a, b, preferred_element_type=F32)


def mm_t(a, b):
    return lax.dot_general(a, b, (((1,), (1,)), ((), ())), preferred_element_type=F32)


def t_mm(a, b):
    return lax.dot_general(a, b, (((0,), (0,)), ((), ())), preferred_element_type=F32)


def hot(condition):
    return jnp.where(condition, 1.0, 0.0).astype(BF16)


def normalize(value):
    middle = jnp.mean(value, axis=-1, keepdims=True)
    centred = value - middle
    inv_dev = lax.rsqrt(jnp.mean(centred * centred, axis=-1, keepdims=True) + EPSILON)
    return centred * inv_dev, inv_dev


def norm_back(grad, normed, inv_dev):
    return inv_dev * (
        grad
        - jnp.mean(grad, axis=-1, keepdims=True)
        - normed * jnp.mean(grad * normed, axis=-1, keepdims=True)
    )


def silu_both(value):
    squashed = 0.5 * jnp.tanh(0.5 * value) + 0.5
    return value * squashed, squashed * (1.0 + value * (1.0 - squashed))


def rank_rows(owner):
    rows = owner.shape[1]
    down, across = iota((rows, rows), 0), iota((rows, rows), 1)
    spread = jnp.broadcast_to(owner, (rows, rows))
    owner_col = jnp.sum(jnp.where(down == across, spread, 0).astype(F32), axis=1, keepdims=True)
    same = owner_col.astype(jnp.int32) == spread
    rank_row = jnp.sum(jnp.where(same & (down < across), 1.0, 0.0), axis=0, keepdims=True)
    rank_col = jnp.sum(jnp.where(same & (across < down), 1.0, 0.0), axis=1, keepdims=True)
    return rank_row.astype(jnp.int32), rank_col.astype(jnp.int32)


def fetch(sources, targets, sems):
    copies = [pltpu.make_async_copy(a, b, sems.at[i]) for i, (a, b) in enumerate(zip(sources, targets))]
    for copy in copies:
        copy.start()
    for copy in copies:
        copy.wait()


def store_blocks(refs, value):
    size = refs[0].shape[0]
    for i, ref in enumerate(refs):
        ref[...] = value[i * size : (i + 1) * size].astype(ref.dtype)


def hop_order(count):
    return sorted(range(count), key=lambda k: (0 < k < count // 2, k))


def load_blocks(refs):
    order = hop_order(len(refs))
    return jnp.concatenate(
        [refs[order.index(k)][...].astype(F32) for k in range(len(refs))], axis=0
    ).astype(BF16)


def pack_body(capacity, stride, outs, mask_ref, owner_hbm, slot_hbm, tokens_hbm, *refs):
    out_refs, (owner_ref, slot_ref, tokens_ref, sems) = refs[:outs], refs[outs:]
    fetch((owner_hbm, slot_hbm, tokens_hbm), (owner_ref, slot_ref, tokens_ref), sems)
    owner = owner_ref[...] ^ mask_ref[0]
    owner_ref[...] = owner
    rows = owner.shape[1]
    rank_row, rank_col = rank_rows(owner)
    total, width = outs * out_refs[0].shape[0], out_refs[0].shape[1]
    place = iota((total, rows), 0)
    chosen = hot(place == owner * stride + rank_row)
    slots = jnp.where(place == owner * stride + capacity, slot_ref[...] + 1, 0)
    by_rank = hot(rank_col == iota((rows, width), 1))
    store_blocks(out_refs, mm(chosen, tokens_ref[...]) + mm(slots.astype(F32).astype(BF16), by_rank))


def relay(value, after):
    return pl.pallas_call(
        lambda *refs: None,
        name="relay",
        out_shape=jax.ShapeDtypeStruct(value.shape, value.dtype),
        in_specs=[ANYWHERE] * (1 + len(after)),
        out_specs=ANYWHERE,
        input_output_aliases={0: 0},
    )(value, *after)


def block_rem(owners, stride):
    col, first = iota((owners, owners * stride), 1), iota((owners, owners * stride), 0)
    above = jnp.sum(jnp.where(col >= stride * (first + 1), 1.0, 0.0), axis=0, keepdims=True)
    rem = iota((1, owners * stride), 1) - stride * above.astype(jnp.int32)
    inside = (col >= stride * first) & (col < stride * (first + 1))
    return rem, inside


def landing_row(table, owners, capacity, stride):
    rem, inside = block_rem(owners, stride)
    lanes = iota((table.shape[1], owners * stride), 0)
    spread = mm(table, hot((lanes == rem) & (lanes < capacity)))
    return jnp.sum(jnp.where(inside, spread, 0.0), axis=0, keepdims=True)


def place_body(owners, capacity, stride, *refs):
    owned_ref, normed_ref, landing_ref = refs[-3:]
    rows = owned_ref.shape[0]
    arrived = load_blocks(refs[:-3])
    total = arrived.shape[0]
    pick = hot(iota((owners, total), 1) == iota((owners, total), 0) * stride + capacity)
    table = mm(pick, arrived).astype(BF16)
    landing = landing_row(table, owners, capacity, stride).astype(jnp.int32)
    owned = mm(hot(iota((rows, total), 0) + 1 == landing), arrived)
    owned_ref[...] = owned.astype(BF16)
    normed_ref[...] = normalize(owned)[0].astype(BF16)
    landing_ref[...] = landing_row(table, owners, capacity, capacity).astype(jnp.int32)


def early_body(cot_ref, outw_ref, proj_ref, grad_ref):
    grad_ref[...] = mm_t(cot_ref[...], outw_ref[...])


def history_start(pos, lengths_ref):
    first = lengths_ref[0, 0]
    second = lengths_ref[0, 1]
    return jnp.where(pos >= first + second, first + second, jnp.where(pos >= first, first, 0))


def attend(query_ref, key, value, shared, acc_ref):
    width = query_ref.shape[1]
    left = iota((1, LANES), 1) < LANES // 2
    for pair in range(width // LANES):
        cols = slice(pair * LANES, (pair + 1) * LANES)
        query, key_pair, value_pair = query_ref[:, cols], key[:, cols], value[:, cols]
        total = acc_ref[:, cols]
        for mine in (left, ~left):
            half = mm_t(jnp.where(mine, query, 0).astype(BF16), key_pair) * 0.0625
            weights = (half * (1.0 + jnp.tanh(half)) * shared).astype(BF16)
            total += mm(weights, jnp.where(mine, value_pair, 0).astype(BF16))
        acc_ref[:, cols] = total


def shared_factor(block, me, rows, lengths_ref):
    query_pos = me * rows + iota((rows, 1), 0)
    start = history_start(query_pos, lengths_ref)
    inverse = 1.0 / (query_pos - start + 1).astype(F32)
    key_pos = block * rows + iota((1, rows), 1)
    return jnp.where((key_pos >= start) & (key_pos <= query_pos), inverse, 0.0)


def attend_other(step, me, lengths_ref, other_ref, proj_ref, query_ref, acc_ref):
    rows, width = query_ref.shape
    block = me ^ step
    reach = history_start(me * rows, lengths_ref)

    @pl.when((block < me) & ((block + 1) * rows > reach))
    def _():
        normed = other_ref[...]
        value = silu_both(mm(normed, proj_ref[:, width : 2 * width]))[0].astype(BF16)
        key = silu_both(mm(normed, proj_ref[:, 3 * width :]))[0].astype(BF16)
        attend(query_ref, key, value, shared_factor(block, me, rows, lengths_ref), acc_ref)


def own_body(me_ref, lengths_ref, normed_ref, proj_ref, gate_ref, slope_ref, query_ref, acc_ref):
    rows, width = normed_ref.shape
    me = me_ref[0]
    preact = mm(normed_ref[...], proj_ref[...])
    gate, slope = silu_both(preact[:, :width])
    gate_ref[...] = gate.astype(BF16)
    slope_ref[...] = slope
    value = silu_both(preact[:, width : 2 * width])[0].astype(BF16)
    query_ref[...] = silu_both(preact[:, 2 * width : 3 * width])[0].astype(BF16)
    key = silu_both(preact[:, 3 * width :])[0].astype(BF16)
    acc_ref[...] = jnp.zeros_like(acc_ref)
    attend(query_ref, key, value, shared_factor(me, me, rows, lengths_ref), acc_ref)


def middle_body(me_ref, lengths_ref, near_ref, far_ref, proj_ref, query_ref, partial_ref, acc_ref):
    me = me_ref[0]
    acc_ref[...] = partial_ref[...]
    attend_other(1, me, lengths_ref, near_ref, proj_ref, query_ref, acc_ref)
    attend_other(2, me, lengths_ref, far_ref, proj_ref, query_ref, acc_ref)


def forward_body(
    me_ref, lengths_ref, cross_ref, proj_ref, outw_ref, owned_ref,
    gate_ref, slope_ref, query_ref, partial_ref, grad_ref,
    out_ref, gated_ref, gate_grad_ref, *rest,
):
    grads, acc_ref = rest[:-1], rest[-1]
    rows, width = query_ref.shape
    me = me_ref[0]
    acc_ref[...] = partial_ref[...]
    attend_other(3, me, lengths_ref, cross_ref, proj_ref, query_ref, acc_ref)
    gate = gate_ref[...].astype(F32)
    normed, inv_dev = normalize(acc_ref[...])
    gated = (normed * gate).astype(BF16)
    gated_ref[...] = gated
    grad_gated = grad_ref[...]
    grad_attended = norm_back(grad_gated * gate, normed, inv_dev).astype(BF16)
    acc_ref[...] = grad_attended.astype(F32)
    piece = width // len(grads)
    for step, ref in enumerate(grads):
        ref[...] = acc_ref[:, pl.ds(pl.multiple_of((me ^ step) * piece, LANES), piece)].astype(BF16)
    out_ref[...] = (mm(gated, outw_ref[...]) + owned_ref[...].astype(F32)).astype(BF16)
    gate_grad_ref[...] = (grad_gated * normed * slope_ref[...]).astype(BF16)


def side_body(me_ref, normed_ref, gated_ref, cot_ref, gate_grad_ref, proj_ref, kept_ref, sent_ref, gate_in_ref, part_ref):
    width = gated_ref.shape[1]
    me = me_ref[0]
    gate_grad = gate_grad_ref[...]
    part_ref[:, :width] = t_mm(normed_ref[...], gate_grad)
    part_ref[:, width:] = t_mm(gated_ref[...], cot_ref[...])
    gate_in_ref[...] = mm_t(gate_grad, proj_ref[:, :width])
    for ref, steps in ((kept_ref, (0, 2)), (sent_ref, (1, 3))):
        place = 0
        for step in steps:
            for base in (0, width):
                source = pl.ds(pl.multiple_of(base + (me ^ step) * LANES, LANES), LANES)
                ref[:, place : place + LANES] = part_ref[:, source].astype(BF16)
                place += LANES


def side_sum_body(kept_ref, came_ref, keep_ref, send_ref):
    total = kept_ref[...].astype(F32) + came_ref[...].astype(F32)
    half = total.shape[1] // 2
    keep_ref[...] = total[:, :half].astype(BF16)
    send_ref[...] = total[:, half:].astype(BF16)


def heads_body(me_ref, n0_ref, n1_ref, n2_ref, n3_ref, proj_ref, part_ref, slope_ref):
    rows, width = n0_ref.shape
    me = me_ref[0]
    piece = width // 4
    cols = [proj_ref[:, pl.ds(pl.multiple_of(b * width + me * piece, LANES), piece)] for b in (1, 2, 3)]
    weight = jnp.concatenate(cols, axis=1)
    for step, ref in enumerate((n0_ref, n1_ref, n2_ref, n3_ref)):
        act, slope = silu_both(mm(ref[...], weight))
        at = pl.ds(pl.multiple_of((me ^ step) * rows, rows), rows)
        part_ref[at, :] = act.astype(BF16)
        slope_ref[at, :] = slope


def block_at(block, rows):
    return pl.ds(pl.multiple_of(block * rows, rows), rows)


def visit(first, second, same, lengths_ref, part_ref, grad_ref, total_ref):
    rows, piece = grad_ref.shape[0] // 4, grad_ref.shape[1]
    q_block, k_block = jnp.maximum(first, second), jnp.minimum(first, second)

    def work():
        q_at, k_at = block_at(q_block, rows), block_at(k_block, rows)
        left = iota((1, LANES), 1) < LANES // 2
        query_pos = q_block * rows + iota((1, rows), 1)
        start = history_start(query_pos, lengths_ref)
        key_pos = k_block * rows + iota((rows, 1), 0)
        inverse = 1.0 / (query_pos - start + 1).astype(F32)
        allowed = key_pos >= start
        if same:
            allowed &= key_pos <= query_pos
        shared = jnp.where(allowed, inverse, 0.0)
        value = part_ref[k_at, :piece]
        query = part_ref[q_at, piece : 2 * piece]
        key = part_ref[k_at, 2 * piece :]
        grad = grad_ref[q_at, :]
        small = value * jnp.asarray(0.0625, BF16)
        d_value, d_query, d_key = 0.0, 0.0, 0.0
        for mine in (left, ~left):
            query_h = jnp.where(mine, query, 0).astype(BF16)
            key_h = jnp.where(mine, key, 0).astype(BF16)
            grad_h = jnp.where(mine, grad, 0).astype(BF16)
            half = mm_t(key_h, query) * 0.0625
            up = 1.0 + jnp.tanh(half)
            act = half * up
            weights = (act * shared).astype(BF16)
            slope = (up + act * (2.0 - up)) * shared
            d_scores = (mm_t(small, grad_h) * slope).astype(BF16)
            d_value += mm(weights, grad_h)
            d_key += mm(d_scores, query_h)
            d_query += t_mm(d_scores, key_h)
        total_ref[k_at, :piece] += d_value
        total_ref[q_at, piece : 2 * piece] += d_query
        total_ref[k_at, 2 * piece :] += d_key

    if same:
        work()
    else:
        pl.when((k_block + 1) * rows > history_start(q_block * rows, lengths_ref))(work)


def backward_rows(steps, finished, me, lengths_ref, part_ref, slope_ref, grad_ref, total_ref, refs):
    done = list(finished)
    for step, ref in zip(steps, refs):
        for other in range(4):
            if other not in done:
                visit(me ^ step, me ^ other, other == step, lengths_ref, part_ref, grad_ref, total_ref)
        done.append(step)
        at = block_at(me ^ step, ref.shape[0])
        ref[...] = (total_ref[at, :] * slope_ref[at, :]).astype(BF16)


def backward_far_body(
    me_ref, lengths_ref, g0_ref, g1_ref, g2_ref, g3_ref, part_ref, slope_ref, *rest
):
    o2_ref, o3_ref, total_ref, grad_ref = rest[-4:]
    rows = g0_ref.shape[0]
    me = me_ref[0]
    for step, ref in enumerate((g0_ref, g1_ref, g2_ref, g3_ref)):
        grad_ref[block_at(me ^ step, rows), :] = ref[...]
    total_ref[...] = jnp.zeros_like(total_ref)
    backward_rows(
        (2, 3), (), me, lengths_ref, part_ref, slope_ref, grad_ref, total_ref, (o2_ref, o3_ref)
    )


def backward_rest_body(
    me_ref, lengths_ref, part_ref, slope_ref, grad_ref, sums_ref, o0_ref, o1_ref, total_ref
):
    total_ref[...] = sums_ref[...]
    backward_rows(
        (1, 0), (2, 3), me_ref[0], lengths_ref, part_ref, slope_ref, grad_ref, total_ref, (o1_ref, o0_ref)
    )


def weight_body(sources, pairs, dp_ref, kept_side_ref, came_side_ref, *refs):
    normed, grads = refs[:sources], refs[sources : 2 * sources]
    outs, total_ref = refs[2 * sources : -1], refs[-1]
    side = kept_side_ref.shape[1]
    total = 0.0
    for n_ref, g_ref in zip(normed, grads):
        total += t_mm(n_ref[...], g_ref[...])
    total_ref[:, :side] = kept_side_ref[...].astype(F32) + came_side_ref[...].astype(F32)
    total_ref[:, side:] = total
    if len(outs) == 1:
        outs[0][...] = total_ref[...].astype(BF16)
        return
    kept_ref, sent_ref = outs
    share = kept_ref.shape[0] // pairs
    for j in range(pairs):
        at = slice(j * share, (j + 1) * share)
        for ref, k in ((kept_ref, 2 * j), (sent_ref, 2 * j + 1)):
            source = pl.ds(pl.multiple_of((dp_ref[0] ^ k) * share, share), share)
            ref[at, :] = total_ref[source, :].astype(BF16)


def pair_body(kept_ref, came_ref, _, *outs):
    store_blocks(outs, kept_ref[...].astype(F32) + came_ref[...].astype(F32))


def head_columns(owner, proj_ref):
    width = proj_ref.shape[0]
    cols = [proj_ref[:, pl.ds(pl.multiple_of(b * width + owner * LANES, LANES), LANES)] for b in (1, 2, 3)]
    return jnp.concatenate(cols, axis=1)


def input_far_body(me_ref, far_ref, cross_ref, gate_in_ref, proj_ref, out_ref):
    me = me_ref[0]
    total = gate_in_ref[...] + mm_t(far_ref[...], head_columns(me ^ 2, proj_ref))
    out_ref[...] = total + mm_t(cross_ref[...], head_columns(me ^ 3, proj_ref))


def input_body(
    blocks, me_ref, mask_ref, own_ref, near_ref, partial_ref,
    owned_ref, cot_ref, landing_ref, proj_ref, *rest,
):
    out_ref = rest[-1]
    rows = owned_ref.shape[0]
    me = me_ref[0]
    total = partial_ref[...] + mm_t(own_ref[...], head_columns(me, proj_ref))
    total += mm_t(near_ref[...], head_columns(me ^ 1, proj_ref))
    centred, inv_scale = normalize(owned_ref[...].astype(F32))
    grad = (norm_back(total, centred, inv_scale) + cot_ref[...].astype(F32)).astype(BF16)
    select = hot(iota((rows, landing_ref.shape[1]), 0) + 1 == landing_ref[...])
    value = t_mm(select, grad)
    size = value.shape[0] // blocks
    for k in range(blocks):
        at = pl.ds(pl.multiple_of((mask_ref[0] ^ k) * size, size), size)
        out_ref[at, :] = value[k * size : (k + 1) * size].astype(BF16)


def return_body(capacity, mask_ref, owner_ref, back_ref, out_ref):
    owner = owner_ref[...] ^ mask_ref[0]
    rank_row, _ = rank_rows(owner)
    chosen = hot(iota((back_ref.shape[0], owner.shape[1]), 0) == owner * capacity + rank_row)
    out_ref[...] = t_mm(chosen, back_ref[...]).astype(BF16)


def sum_body(*refs):
    total = 0.0
    for ref in refs[:-1]:
        parts = ref[...].astype(F32)
        total += parts if ref.ndim == 2 else jnp.sum(parts, axis=0)
    refs[-1][...] = total.astype(BF16)


def finish_body(me_ref, w0_ref, w1_ref, w2_ref, w3_ref, proj_ref, outw_ref):
    me = me_ref[0]
    width = outw_ref.shape[1]
    for step, ref in enumerate((w0_ref, w1_ref, w2_ref, w3_ref)):
        at = pl.ds(pl.multiple_of((me ^ step) * LANES, LANES), LANES)
        outw_ref[:, at] = ref[:, LANES : 2 * LANES].astype(F32)
        for b, source in enumerate((0, 2, 3, 4)):
            at = pl.ds(pl.multiple_of(b * width + (me ^ step) * LANES, LANES), LANES)
            proj_ref[:, at] = ref[:, source * LANES : (source + 1) * LANES].astype(F32)


def on_device(tokens, dest_owner, dest_slot, lengths, proj_weight, out_weight, cotangent):
    rows, width = tokens.shape
    owners = lax.axis_size("dp")
    cycle = lax.axis_size("ctx")
    assert cycle == 4 and width == cycle * LANES
    capacity = 2 * rows // owners
    stride = capacity + 8
    piece = width // cycle
    me = lax.axis_index("ctx").astype(jnp.int32).reshape(1)
    owner_row = dest_owner.reshape(1, rows)
    slot_row = dest_slot.reshape(1, rows)
    square = ((rows, width), BF16)

    def hop(value, step):
        return lax.ppermute(value, "ctx", [(i, i ^ step) for i in range(cycle)])

    def gather(value):
        near, far = hop(value, 1), hop(value, 2)
        return near, far, hop(far, 1)

    def exchange(values):
        return [values[0]] + [hop(values[step], step) for step in (2, 3, 1)]

    by_hops = owners <= 8
    blocks = owners if by_hops else 1
    dp = lax.axis_index("dp").astype(jnp.int32).reshape(1)
    mask = dp if by_hops else jnp.zeros_like(dp)

    def dp_hop(value, step):
        return lax.ppermute(value, "dp", [(i, i ^ step) for i in range(owners)])

    def swap_whole(value):
        split = value.reshape(owners, value.shape[0] // owners, value.shape[1])
        return lax.all_to_all(split, "dp", split_axis=0, concat_axis=0, tiled=True).reshape(value.shape)

    def swap(values):
        if by_hops:
            return [dp_hop(values[k], k) if k else values[k] for k in hop_order(owners)]
        return [swap_whole(values[0])]

    def block_shapes(height, columns, dtype):
        return [((owners * height // blocks, columns), dtype)] * blocks

    wide = ((rows, width), F32)
    *outgoing, owner_here = call(
        functools.partial(pack_body, capacity, stride, blocks),
        "pack", block_shapes(stride, width, BF16) + [((1, rows), jnp.int32)],
        [mask], [], far=[owner_row, slot_row, tokens],
        scratch=[
            pltpu.VMEM((1, rows), jnp.int32),
            pltpu.VMEM((rows, width), BF16),
            pltpu.SemaphoreType.DMA((3,)),
        ],
    )
    (grad_gated,) = call(early_body, "early", [wide], [], [cotangent, out_weight, proj_weight])
    if by_hops:
        outgoing[owners // 4] = relay(outgoing[owners // 4], [grad_gated])
    arrived = swap(outgoing)
    owned, normed, landing = call(
        functools.partial(place_body, owners, capacity, stride),
        "place", [square, square, ((1, owners * capacity), jnp.int32)], [], arrived,
    )
    near, far, cross = gather(normed)
    gate, slope, query, partial = call(
        own_body, "own_rows", [square, wide, square, wide],
        [me, lengths], [normed, proj_weight], flops=10**10, vmem=16,
    )
    (partial,) = call(
        middle_body, "middle", [wide], [me, lengths], [near, far, proj_weight, query, partial],
        flops=10**10, vmem=16,
    )
    layer_out, gated, gate_grad, *grad_pieces = call(
        forward_body, "forward",
        [square, square, square] + [((rows, piece), BF16)] * cycle,
        [me, lengths],
        [cross, proj_weight, out_weight, owned, gate, slope, query, partial, grad_gated],
        scratch=[pltpu.VMEM((rows, width), F32)], vmem=16,
    )
    r0, r2, r3, r1 = exchange(grad_pieces)
    side_half = ((width, 4 * piece), BF16)
    side_piece = ((width, 2 * piece), BF16)
    side_kept, side_sent, gate_in = call(
        side_body, "side", [side_half, side_half, wide],
        [me], [normed, gated, cotangent, gate_grad, proj_weight],
        scratch=[pltpu.VMEM((width, 2 * width), F32)], vmem=16,
    )
    side_came = hop(side_sent, 1)
    parts, slopes = call(
        heads_body, "heads",
        [((rows * cycle, 3 * piece), BF16), ((rows * cycle, 3 * piece), F32)],
        [me], [normed, near, far, cross, proj_weight], vmem=16,
    )
    side_keep, side_send = call(
        side_sum_body, "side_sum", [side_piece, side_piece], [], [side_kept, side_came]
    )
    side_last = hop(side_send, 2)
    grad_block = ((rows, 3 * piece), BF16)
    sums = ((rows * cycle, 3 * piece), F32)
    grad_rows = ((rows * cycle, piece), BF16)
    far_block, cross_block, totals, grad_all = call(
        backward_far_body, "backward_far", [grad_block, grad_block, sums, grad_rows],
        [me, lengths], [r0, r1, r2, r3, parts, slopes], flops=10**10, vmem=16,
    )
    p2, p3 = hop(far_block, 2), hop(cross_block, 3)
    own_block, near_block = call(
        backward_rest_body, "backward_rest", [grad_block] * 2,
        [me, lengths], [parts, slopes, grad_all, totals], vmem=16,
        scratch=[pltpu.VMEM(*sums)],
    )
    p1 = hop(near_block, 1)
    grads = [own_block, near_block, far_block, cross_block]
    share = width // owners
    pairs = owners // 2
    columns = 5 * piece
    weight_parts = call(
        functools.partial(weight_body, cycle, pairs), "weights",
        [((pairs * share, columns), BF16)] * 2 if by_hops else [((width, columns), BF16)], [dp],
        [side_keep, side_last, normed, near, far, cross, *grads], vmem=16,
        scratch=[pltpu.VMEM((width, columns), F32)],
    )
    (partial_in,) = call(
        input_far_body, "input_far", [wide], [me], [p2, p3, gate_in, proj_weight], flops=6 * 10**9,
    )
    (back,) = call(
        functools.partial(input_body, blocks), "input_grad", [((owners * capacity, width), BF16)], [me, mask],
        [own_block, p1, partial_in, owned, cotangent, landing, proj_weight], vmem=16,
    )
    if by_hops:
        kept, sent = weight_parts
        halves = call(
            pair_body, "pair_sum", [((share, columns), BF16)] * pairs, [], [kept, dp_hop(sent, 1)],
            far=[partial_in],
        )
        summed_parts = [halves[0]] + [dp_hop(halves[j], 2 * j) for j in range(1, pairs)]
    else:
        summed_parts = [swap_whole(weight_parts[0]).reshape(owners, share, columns)]
    (mine,) = call(sum_body, "sum", [((share, columns), BF16)], [], summed_parts)
    returned = swap_whole(relay(back, [mine]))
    w1, w2, w3 = (hop(mine, step) for step in range(1, cycle))
    (grad_tokens,) = call(
        functools.partial(return_body, capacity), "give_back", [square], [mask], [owner_here, returned]
    )
    grad_proj, grad_outw = call(
        finish_body, "finish", [((share, 4 * width), F32), ((share, width), F32)],
        [me], [mine, w1, w2, w3],
    )
    return layer_out, grad_tokens, grad_proj, grad_outw


def solution(mesh):
    placed = (
        P(("dp", "ctx"), None),
        P(("dp", "ctx")),
        P(("dp", "ctx")),
        P("dp", None),
        P(),
        P(),
        P(("dp", "ctx"), None),
    )
    return jax.shard_map(
        on_device,
        mesh=mesh,
        in_specs=placed,
        out_specs=(P(("dp", "ctx"), None), P(("dp", "ctx"), None), P("dp", None), P("dp", None)),
        check_vma=False,
    )
```

```python
import functools

import jax
import jax.numpy as jnp
from jax import lax
from jax.experimental import pallas as pl
from jax.experimental.pallas import tpu as pltpu
from jax.sharding import PartitionSpec as P

HEADS = 8
EPSILON = 1e-05
LANES = 128
F32 = jnp.float32
BF16 = jnp.bfloat16

WHOLE = pl.BlockSpec(memory_space=pltpu.VMEM)
SCALARS = pl.BlockSpec(memory_space=pltpu.SMEM)
ANYWHERE = pl.BlockSpec(memory_space=pl.ANY)


def call(body, name, outs, scalars, arrays, scratch=(), flops=10**8, vmem=8, far=()):
    return pl.pallas_call(
        body,
        name=name,
        out_shape=[jax.ShapeDtypeStruct(s, d) for s, d in outs],
        in_specs=[SCALARS] * len(scalars) + [WHOLE] * len(arrays) + [ANYWHERE] * len(far),
        out_specs=[WHOLE] * len(outs),
        scratch_shapes=list(scratch),
        compiler_params=pltpu.CompilerParams(vmem_limit_bytes=vmem * 2**20),
        cost_estimate=pl.CostEstimate(flops=flops, bytes_accessed=2**20, transcendentals=0),
    )(*scalars, *arrays, *far)


def iota(shape, dim):
    return lax.broadcasted_iota(jnp.int32, shape, dim)


def mm(a, b):
    return jnp.dot(a, b, preferred_element_type=F32)


def mm_t(a, b):
    return lax.dot_general(a, b, (((1,), (1,)), ((), ())), preferred_element_type=F32)


def t_mm(a, b):
    return lax.dot_general(a, b, (((0,), (0,)), ((), ())), preferred_element_type=F32)


def hot(condition):
    return jnp.where(condition, 1.0, 0.0).astype(BF16)


def normalize(value):
    middle = jnp.mean(value, axis=-1, keepdims=True)
    centred = value - middle
    inv_dev = lax.rsqrt(jnp.mean(centred * centred, axis=-1, keepdims=True) + EPSILON)
    return centred * inv_dev, inv_dev


def norm_back(grad, normed, inv_dev):
    return inv_dev * (
        grad
        - jnp.mean(grad, axis=-1, keepdims=True)
        - normed * jnp.mean(grad * normed, axis=-1, keepdims=True)
    )


def silu_both(value):
    squashed = 0.5 * jnp.tanh(0.5 * value) + 0.5
    return value * squashed, squashed * (1.0 + value * (1.0 - squashed))


def rank_rows(owner):
    rows = owner.shape[1]
    down, across = iota((rows, rows), 0), iota((rows, rows), 1)
    spread = jnp.broadcast_to(owner, (rows, rows))
    owner_col = jnp.sum(jnp.where(down == across, spread, 0).astype(F32), axis=1, keepdims=True)
    same = owner_col.astype(jnp.int32) == spread
    rank_row = jnp.sum(jnp.where(same & (down < across), 1.0, 0.0), axis=0, keepdims=True)
    rank_col = jnp.sum(jnp.where(same & (across < down), 1.0, 0.0), axis=1, keepdims=True)
    return rank_row.astype(jnp.int32), rank_col.astype(jnp.int32)


def fetch(sources, targets, sems):
    copies = [pltpu.make_async_copy(a, b, sems.at[i]) for i, (a, b) in enumerate(zip(sources, targets))]
    for copy in copies:
        copy.start()
    for copy in copies:
        copy.wait()


def store_blocks(refs, value):
    size = refs[0].shape[0]
    for i, ref in enumerate(refs):
        ref[...] = value[i * size : (i + 1) * size].astype(ref.dtype)


def hop_order(count):
    return sorted(range(count), key=lambda k: (0 < k < count // 2, k))


def load_blocks(refs):
    order = hop_order(len(refs))
    return jnp.concatenate(
        [refs[order.index(k)][...].astype(F32) for k in range(len(refs))], axis=0
    ).astype(BF16)


def pack_blocks(steps, capacity, stride, owner, slot, tokens, out_refs):
    rows, width = tokens.shape
    rank_row, rank_col = rank_rows(owner)
    place = iota((len(steps) * stride, rows), 0)
    for i, (before, k) in enumerate(zip((-1, *steps), steps)):
        if k != before + 1:
            place = jnp.where(iota(place.shape, 0) >= i * stride, place + (k - before - 1) * stride, place)
    chosen = hot(place == owner * stride + rank_row)
    slots = jnp.where(place == owner * stride + capacity, slot + 1, 0)
    by_rank = hot(rank_col == iota((rows, width), 1))
    store_blocks(out_refs, mm(chosen, tokens) + mm(slots.astype(F32).astype(BF16), by_rank))


def pack_body(steps, capacity, stride, mask_ref, owner_hbm, slot_hbm, tokens_hbm, *refs):
    *out_refs, owner_ref, slot_ref, tokens_ref, sems = refs
    fetch((owner_hbm, slot_hbm, tokens_hbm), (owner_ref, slot_ref, tokens_ref), sems)
    owner = owner_ref[...] ^ mask_ref[0]
    owner_ref[...] = owner
    if len(steps) == 1:
        steps = range(out_refs[0].shape[0] // stride)
    pack_blocks(tuple(steps), capacity, stride, owner, slot_ref[...], tokens_ref[...], out_refs)


def pack_rest_body(steps, capacity, stride, owner_ref, slot_ref, tokens_ref, _, *out_refs):
    pack_blocks(steps, capacity, stride, owner_ref[...], slot_ref[...], tokens_ref[...], out_refs)


def block_rem(owners, stride):
    col, first = iota((owners, owners * stride), 1), iota((owners, owners * stride), 0)
    above = jnp.sum(jnp.where(col >= stride * (first + 1), 1.0, 0.0), axis=0, keepdims=True)
    rem = iota((1, owners * stride), 1) - stride * above.astype(jnp.int32)
    inside = (col >= stride * first) & (col < stride * (first + 1))
    return rem, inside


def landing_row(table, owners, capacity, stride):
    rem, inside = block_rem(owners, stride)
    lanes = iota((table.shape[1], owners * stride), 0)
    spread = mm(table, hot((lanes == rem) & (lanes < capacity)))
    return jnp.sum(jnp.where(inside, spread, 0.0), axis=0, keepdims=True)


def place_body(owners, capacity, stride, *refs):
    owned_ref, normed_ref, landing_ref = refs[-3:]
    rows = owned_ref.shape[0]
    arrived = load_blocks(refs[:-3])
    total = arrived.shape[0]
    pick = hot(iota((owners, total), 1) == iota((owners, total), 0) * stride + capacity)
    table = mm(pick, arrived).astype(BF16)
    landing = landing_row(table, owners, capacity, stride).astype(jnp.int32)
    owned = mm(hot(iota((rows, total), 0) + 1 == landing), arrived)
    owned_ref[...] = owned.astype(BF16)
    normed_ref[...] = normalize(owned)[0].astype(BF16)
    landing_ref[...] = landing_row(table, owners, capacity, capacity).astype(jnp.int32)


def early_body(cot_ref, outw_ref, proj_ref, grad_ref):
    grad_ref[...] = mm_t(cot_ref[...], outw_ref[...])


def history_start(pos, lengths_ref):
    first = lengths_ref[0, 0]
    second = lengths_ref[0, 1]
    return jnp.where(pos >= first + second, first + second, jnp.where(pos >= first, first, 0))


def attend(query_ref, key, value, shared, acc_ref):
    width = query_ref.shape[1]
    left = iota((1, LANES), 1) < LANES // 2
    for pair in range(width // LANES):
        cols = slice(pair * LANES, (pair + 1) * LANES)
        query, key_pair, value_pair = query_ref[:, cols], key[:, cols], value[:, cols]
        total = acc_ref[:, cols]
        for mine in (left, ~left):
            half = mm_t(jnp.where(mine, query, 0).astype(BF16), key_pair) * 0.0625
            weights = (half * (1.0 + jnp.tanh(half)) * shared).astype(BF16)
            total += mm(weights, jnp.where(mine, value_pair, 0).astype(BF16))
        acc_ref[:, cols] = total


def shared_factor(block, me, rows, lengths_ref):
    query_pos = me * rows + iota((rows, 1), 0)
    start = history_start(query_pos, lengths_ref)
    inverse = 1.0 / (query_pos - start + 1).astype(F32)
    key_pos = block * rows + iota((1, rows), 1)
    return jnp.where((key_pos >= start) & (key_pos <= query_pos), inverse, 0.0)


def attend_other(step, me, lengths_ref, other_ref, proj_ref, query_ref, acc_ref):
    rows, width = query_ref.shape
    block = me ^ step
    reach = history_start(me * rows, lengths_ref)

    @pl.when((block < me) & ((block + 1) * rows > reach))
    def _():
        normed = other_ref[...]
        value = silu_both(mm(normed, proj_ref[:, width : 2 * width]))[0].astype(BF16)
        key = silu_both(mm(normed, proj_ref[:, 3 * width :]))[0].astype(BF16)
        attend(query_ref, key, value, shared_factor(block, me, rows, lengths_ref), acc_ref)


def own_body(me_ref, lengths_ref, normed_ref, proj_ref, gate_ref, slope_ref, query_ref, acc_ref):
    rows, width = normed_ref.shape
    me = me_ref[0]
    preact = mm(normed_ref[...], proj_ref[...])
    gate, slope = silu_both(preact[:, :width])
    gate_ref[...] = gate.astype(BF16)
    slope_ref[...] = slope
    value = silu_both(preact[:, width : 2 * width])[0].astype(BF16)
    query_ref[...] = silu_both(preact[:, 2 * width : 3 * width])[0].astype(BF16)
    key = silu_both(preact[:, 3 * width :])[0].astype(BF16)
    acc_ref[...] = jnp.zeros_like(acc_ref)
    attend(query_ref, key, value, shared_factor(me, me, rows, lengths_ref), acc_ref)


def middle_body(me_ref, lengths_ref, near_ref, far_ref, proj_ref, query_ref, partial_ref, acc_ref):
    me = me_ref[0]
    acc_ref[...] = partial_ref[...]
    attend_other(1, me, lengths_ref, near_ref, proj_ref, query_ref, acc_ref)
    attend_other(2, me, lengths_ref, far_ref, proj_ref, query_ref, acc_ref)


def forward_body(
    me_ref, lengths_ref, cross_ref, proj_ref, gate_ref, query_ref, partial_ref, grad_ref,
    normed_ref, *rest,
):
    grads, acc_ref = rest[:-1], rest[-1]
    width = query_ref.shape[1]
    me = me_ref[0]
    acc_ref[...] = partial_ref[...]
    attend_other(3, me, lengths_ref, cross_ref, proj_ref, query_ref, acc_ref)
    normed, inv_dev = normalize(acc_ref[...])
    normed_ref[...] = normed
    acc_ref[...] = norm_back(grad_ref[...] * gate_ref[...].astype(F32), normed, inv_dev)
    piece = width // len(grads)
    for step, ref in enumerate(grads):
        ref[...] = acc_ref[:, pl.ds(pl.multiple_of((me ^ step) * piece, LANES), piece)].astype(BF16)


def side_body(
    me_ref, own_ref, normed_ref, gate_ref, slope_ref, grad_ref, cot_ref, proj_ref, outw_ref, owned_ref,
    kept_ref, sent_ref, gate_in_ref, out_ref, part_ref,
):
    width = own_ref.shape[1]
    me = me_ref[0]
    normed = normed_ref[...]
    gated = (normed * gate_ref[...].astype(F32)).astype(BF16)
    gate_grad = (grad_ref[...] * normed * slope_ref[...]).astype(BF16)
    out_ref[...] = (mm(gated, outw_ref[...]) + owned_ref[...].astype(F32)).astype(BF16)
    part_ref[:, :width] = t_mm(own_ref[...], gate_grad)
    part_ref[:, width:] = t_mm(gated, cot_ref[...])
    gate_in_ref[...] = mm_t(gate_grad, proj_ref[:, :width])
    for ref, steps in ((kept_ref, (0, 2)), (sent_ref, (1, 3))):
        place = 0
        for step in steps:
            for base in (0, width):
                source = pl.ds(pl.multiple_of(base + (me ^ step) * LANES, LANES), LANES)
                ref[:, place : place + LANES] = part_ref[:, source].astype(BF16)
                place += LANES


def side_sum_body(kept_ref, came_ref, keep_ref, send_ref):
    total = kept_ref[...].astype(F32) + came_ref[...].astype(F32)
    half = total.shape[1] // 2
    keep_ref[...] = total[:, :half].astype(BF16)
    send_ref[...] = total[:, half:].astype(BF16)


def heads_body(me_ref, n0_ref, n1_ref, n2_ref, n3_ref, proj_ref, part_ref, slope_ref):
    rows, width = n0_ref.shape
    me = me_ref[0]
    piece = width // 4
    cols = [proj_ref[:, pl.ds(pl.multiple_of(b * width + me * piece, LANES), piece)] for b in (1, 2, 3)]
    weight = jnp.concatenate(cols, axis=1)
    for step, ref in enumerate((n0_ref, n1_ref, n2_ref, n3_ref)):
        act, slope = silu_both(mm(ref[...], weight))
        at = pl.ds(pl.multiple_of((me ^ step) * rows, rows), rows)
        part_ref[at, :] = act.astype(BF16)
        slope_ref[at, :] = slope


def block_at(block, rows):
    return pl.ds(pl.multiple_of(block * rows, rows), rows)


def visit(first, second, same, lengths_ref, part_ref, grad_ref, total_ref):
    rows, piece = grad_ref.shape[0] // 4, grad_ref.shape[1]
    q_block, k_block = jnp.maximum(first, second), jnp.minimum(first, second)

    def work():
        q_at, k_at = block_at(q_block, rows), block_at(k_block, rows)
        left = iota((1, LANES), 1) < LANES // 2
        query_pos = q_block * rows + iota((1, rows), 1)
        start = history_start(query_pos, lengths_ref)
        key_pos = k_block * rows + iota((rows, 1), 0)
        inverse = 1.0 / (query_pos - start + 1).astype(F32)
        allowed = key_pos >= start
        if same:
            allowed &= key_pos <= query_pos
        shared = jnp.where(allowed, inverse, 0.0)
        value = part_ref[k_at, :piece]
        query = part_ref[q_at, piece : 2 * piece]
        key = part_ref[k_at, 2 * piece :]
        grad = grad_ref[q_at, :]
        small = value * jnp.asarray(0.0625, BF16)
        d_value, d_query, d_key = 0.0, 0.0, 0.0
        for mine in (left, ~left):
            query_h = jnp.where(mine, query, 0).astype(BF16)
            key_h = jnp.where(mine, key, 0).astype(BF16)
            grad_h = jnp.where(mine, grad, 0).astype(BF16)
            half = mm_t(key_h, query) * 0.0625
            up = 1.0 + jnp.tanh(half)
            act = half * up
            weights = (act * shared).astype(BF16)
            slope = (up + act * (2.0 - up)) * shared
            d_scores = (mm_t(small, grad_h) * slope).astype(BF16)
            d_value += mm(weights, grad_h)
            d_key += mm(d_scores, query_h)
            d_query += t_mm(d_scores, key_h)
        total_ref[k_at, :piece] += d_value
        total_ref[q_at, piece : 2 * piece] += d_query
        total_ref[k_at, 2 * piece :] += d_key

    if same:
        work()
    else:
        pl.when((k_block + 1) * rows > history_start(q_block * rows, lengths_ref))(work)


def backward_rows(steps, finished, me, lengths_ref, part_ref, slope_ref, grad_ref, total_ref, refs):
    done = list(finished)
    for step, ref in zip(steps, refs):
        for other in range(4):
            if other not in done:
                visit(me ^ step, me ^ other, other == step, lengths_ref, part_ref, grad_ref, total_ref)
        done.append(step)
        at = block_at(me ^ step, ref.shape[0])
        ref[...] = (total_ref[at, :] * slope_ref[at, :]).astype(BF16)


def collect_body(me_ref, g0_ref, g1_ref, g2_ref, g3_ref, grad_ref):
    rows = g0_ref.shape[0]
    for step, ref in enumerate((g0_ref, g1_ref, g2_ref, g3_ref)):
        grad_ref[block_at(me_ref[0] ^ step, rows), :] = ref[...]


def backward_far_body(me_ref, lengths_ref, part_ref, slope_ref, grad_ref, o2_ref, o3_ref, total_ref):
    total_ref[...] = jnp.zeros_like(total_ref)
    backward_rows(
        (2, 3), (), me_ref[0], lengths_ref, part_ref, slope_ref, grad_ref, total_ref, (o2_ref, o3_ref)
    )


def backward_rest_body(
    me_ref, lengths_ref, part_ref, slope_ref, grad_ref, sums_ref, o0_ref, o1_ref, total_ref
):
    total_ref[...] = sums_ref[...]
    backward_rows(
        (1, 0), (2, 3), me_ref[0], lengths_ref, part_ref, slope_ref, grad_ref, total_ref, (o1_ref, o0_ref)
    )


def weight_body(sources, pairs, dp_ref, kept_side_ref, came_side_ref, *refs):
    normed, grads = refs[:sources], refs[sources : 2 * sources]
    outs, total_ref = refs[2 * sources : -1], refs[-1]
    side = kept_side_ref.shape[1]
    total = 0.0
    for n_ref, g_ref in zip(normed, grads):
        total += t_mm(n_ref[...], g_ref[...])
    total_ref[:, :side] = kept_side_ref[...].astype(F32) + came_side_ref[...].astype(F32)
    total_ref[:, side:] = total
    if len(outs) == 1:
        outs[0][...] = total_ref[...].astype(BF16)
        return
    kept_ref, sent_ref = outs
    share = kept_ref.shape[0] // pairs
    for j in range(pairs):
        at = slice(j * share, (j + 1) * share)
        for ref, k in ((kept_ref, 2 * j), (sent_ref, 2 * j + 1)):
            source = pl.ds(pl.multiple_of((dp_ref[0] ^ k) * share, share), share)
            ref[at, :] = total_ref[source, :].astype(BF16)


def pair_body(kept_ref, came_ref, _, *outs):
    store_blocks(outs, kept_ref[...].astype(F32) + came_ref[...].astype(F32))


def head_columns(owner, proj_ref):
    width = proj_ref.shape[0]
    cols = [proj_ref[:, pl.ds(pl.multiple_of(b * width + owner * LANES, LANES), LANES)] for b in (1, 2, 3)]
    return jnp.concatenate(cols, axis=1)


def input_far_body(me_ref, far_ref, cross_ref, gate_in_ref, proj_ref, out_ref):
    me = me_ref[0]
    total = gate_in_ref[...] + mm_t(far_ref[...], head_columns(me ^ 2, proj_ref))
    out_ref[...] = total + mm_t(cross_ref[...], head_columns(me ^ 3, proj_ref))


def input_body(me_ref, own_ref, near_ref, partial_ref, owned_ref, cot_ref, proj_ref, out_ref):
    me = me_ref[0]
    total = partial_ref[...] + mm_t(own_ref[...], head_columns(me, proj_ref))
    total += mm_t(near_ref[...], head_columns(me ^ 1, proj_ref))
    centred, inv_scale = normalize(owned_ref[...].astype(F32))
    grad = (norm_back(total, centred, inv_scale) + cot_ref[...].astype(F32)).astype(BF16)
    out_ref[...] = grad


def spread_body(blocks, mask_ref, grad_ref, landing_ref, _, out_ref):
    select = hot(iota((grad_ref.shape[0], landing_ref.shape[1]), 0) + 1 == landing_ref[...])
    value = t_mm(select, grad_ref[...])
    size = value.shape[0] // blocks
    for k in range(blocks):
        at = pl.ds(pl.multiple_of((mask_ref[0] ^ k) * size, size), size)
        out_ref[at, :] = value[k * size : (k + 1) * size].astype(BF16)


def return_body(capacity, mask_ref, owner_ref, back_ref, out_ref):
    owner = owner_ref[...] ^ mask_ref[0]
    rank_row, _ = rank_rows(owner)
    chosen = hot(iota((back_ref.shape[0], owner.shape[1]), 0) == owner * capacity + rank_row)
    out_ref[...] = t_mm(chosen, back_ref[...]).astype(BF16)


def sum_body(*refs):
    total = 0.0
    for ref in refs[:-1]:
        parts = ref[...].astype(F32)
        total += parts if ref.ndim == 2 else jnp.sum(parts, axis=0)
    refs[-1][...] = total.astype(BF16)


def finish_body(me_ref, w0_ref, w1_ref, w2_ref, w3_ref, proj_ref, outw_ref):
    me = me_ref[0]
    width = outw_ref.shape[1]
    for step, ref in enumerate((w0_ref, w1_ref, w2_ref, w3_ref)):
        at = pl.ds(pl.multiple_of((me ^ step) * LANES, LANES), LANES)
        outw_ref[:, at] = ref[:, LANES : 2 * LANES].astype(F32)
        for b, source in enumerate((0, 2, 3, 4)):
            at = pl.ds(pl.multiple_of(b * width + (me ^ step) * LANES, LANES), LANES)
            proj_ref[:, at] = ref[:, source * LANES : (source + 1) * LANES].astype(F32)


def on_device(tokens, dest_owner, dest_slot, lengths, proj_weight, out_weight, cotangent):
    rows, width = tokens.shape
    owners = lax.axis_size("dp")
    cycle = lax.axis_size("ctx")
    assert cycle == 4 and width == cycle * LANES
    capacity = 2 * rows // owners
    stride = capacity + 8
    piece = width // cycle
    me = lax.axis_index("ctx").astype(jnp.int32).reshape(1)
    owner_row = dest_owner.reshape(1, rows)
    slot_row = dest_slot.reshape(1, rows)
    square = ((rows, width), BF16)

    def hop(value, step):
        return lax.ppermute(value, "ctx", [(i, i ^ step) for i in range(cycle)])

    def gather(value):
        near, far = hop(value, 1), hop(value, 2)
        return near, far, hop(far, 1)

    def exchange(values):
        return [values[0]] + [hop(values[step], step) for step in (2, 3, 1)]

    by_hops = owners <= 8
    blocks = owners if by_hops else 1
    dp = lax.axis_index("dp").astype(jnp.int32).reshape(1)
    mask = dp if by_hops else jnp.zeros_like(dp)

    def dp_hop(value, step):
        return lax.ppermute(value, "dp", [(i, i ^ step) for i in range(owners)])

    def swap_whole(value):
        split = value.reshape(owners, value.shape[0] // owners, value.shape[1])
        return lax.all_to_all(split, "dp", split_axis=0, concat_axis=0, tiled=True).reshape(value.shape)

    def swap(values):
        if by_hops:
            return [dp_hop(values[k], k) if k else values[k] for k in hop_order(owners)]
        return [swap_whole(values[0])]

    def block_shapes(height, columns, dtype):
        return [((owners * height // blocks, columns), dtype)] * blocks

    wide = ((rows, width), F32)
    steps = tuple(range(blocks))
    later = steps[owners // 4 : owners // 2] if by_hops else ()
    first = tuple(k for k in steps if k not in later)
    *outgoing, owner_here, slot_here, tokens_here = call(
        functools.partial(pack_body, first, capacity, stride),
        "pack",
        block_shapes(stride, width, BF16)[: len(first)] + [((1, rows), jnp.int32)] * 2 + [square],
        [mask], [], far=[owner_row, slot_row, tokens], scratch=[pltpu.SemaphoreType.DMA((3,))],
    )
    (grad_gated,) = call(early_body, "early", [wide], [], [cotangent, out_weight, proj_weight])
    outgoing = dict(zip(first, outgoing))
    if later:
        rest = call(
            functools.partial(pack_rest_body, later, capacity, stride),
            "pack_rest", block_shapes(stride, width, BF16)[: len(later)], [],
            [owner_here, slot_here, tokens_here], far=[grad_gated],
        )
        outgoing.update(zip(later, rest))
    arrived = swap([outgoing[k] for k in steps])
    owned, normed, landing = call(
        functools.partial(place_body, owners, capacity, stride),
        "place", [square, square, ((1, owners * capacity), jnp.int32)], [], arrived,
    )
    near, far, cross = gather(normed)
    gate, slope, query, partial = call(
        own_body, "own_rows", [square, wide, square, wide],
        [me, lengths], [normed, proj_weight], flops=10**10, vmem=16,
    )
    (partial,) = call(
        middle_body, "middle", [wide], [me, lengths], [near, far, proj_weight, query, partial],
        flops=10**10, vmem=16,
    )
    normed_out, *grad_pieces = call(
        forward_body, "forward", [wide] + [((rows, piece), BF16)] * cycle,
        [me, lengths], [cross, proj_weight, gate, query, partial, grad_gated],
        scratch=[pltpu.VMEM((rows, width), F32)], vmem=16,
    )
    r0, r2, r3, r1 = exchange(grad_pieces)
    side_half = ((width, 4 * piece), BF16)
    side_piece = ((width, 2 * piece), BF16)
    side_kept, side_sent, gate_in, layer_out = call(
        side_body, "side", [side_half, side_half, wide, square],
        [me], [normed, normed_out, gate, slope, grad_gated, cotangent, proj_weight, out_weight, owned],
        scratch=[pltpu.VMEM((width, 2 * width), F32)], vmem=16,
    )
    side_came = hop(side_sent, 1)
    parts, slopes = call(
        heads_body, "heads",
        [((rows * cycle, 3 * piece), BF16), ((rows * cycle, 3 * piece), F32)],
        [me], [normed, near, far, cross, proj_weight], vmem=16,
    )
    side_keep, side_send = call(
        side_sum_body, "side_sum", [side_piece, side_piece], [], [side_kept, side_came]
    )
    side_last = hop(side_send, 2)
    grad_block = ((rows, 3 * piece), BF16)
    sums = ((rows * cycle, 3 * piece), F32)
    grad_rows = ((rows * cycle, piece), BF16)
    (grad_all,) = call(
        collect_body, "collect", [grad_rows], [me], [r0, r1, r2, r3], flops=6 * 10**9,
    )
    far_block, cross_block, totals = call(
        backward_far_body, "backward_far", [grad_block, grad_block, sums],
        [me, lengths], [parts, slopes, grad_all], flops=10**10, vmem=16,
    )
    p2, p3 = hop(far_block, 2), hop(cross_block, 3)
    own_block, near_block = call(
        backward_rest_body, "backward_rest", [grad_block] * 2,
        [me, lengths], [parts, slopes, grad_all, totals], vmem=16,
        scratch=[pltpu.VMEM(*sums)],
    )
    p1 = hop(near_block, 1)
    grads = [own_block, near_block, far_block, cross_block]
    share = width // owners
    pairs = owners // 2
    columns = 5 * piece
    weight_parts = call(
        functools.partial(weight_body, cycle, pairs), "weights",
        [((pairs * share, columns), BF16)] * 2 if by_hops else [((width, columns), BF16)], [dp],
        [side_keep, side_last, normed, near, far, cross, *grads], vmem=16,
        scratch=[pltpu.VMEM((width, columns), F32)],
    )
    (partial_in,) = call(
        input_far_body, "input_far", [wide], [me], [p2, p3, gate_in, proj_weight], flops=6 * 10**9,
    )
    (grad_owned,) = call(
        input_body, "input_grad", [square], [me],
        [own_block, p1, partial_in, owned, cotangent, proj_weight], vmem=16,
    )
    if by_hops:
        kept, sent = weight_parts
        halves = call(
            pair_body, "pair_sum", [((share, columns), BF16)] * pairs, [], [kept, dp_hop(sent, 1)],
            far=[partial_in],
        )
        summed_parts = [halves[0]] + [dp_hop(halves[j], 2 * j) for j in range(1, pairs)]
    else:
        summed_parts = [swap_whole(weight_parts[0]).reshape(owners, share, columns)]
    (mine,) = call(sum_body, "sum", [((share, columns), BF16)], [], summed_parts)
    (back,) = call(
        functools.partial(spread_body, blocks), "spread", [((owners * capacity, width), BF16)],
        [mask], [grad_owned, landing], far=[mine],
    )
    returned = swap_whole(back)
    w1, w2, w3 = (hop(mine, step) for step in range(1, cycle))
    (grad_tokens,) = call(
        functools.partial(return_body, capacity), "give_back", [square], [mask], [owner_here, returned]
    )
    grad_proj, grad_outw = call(
        finish_body, "finish", [((share, 4 * width), F32), ((share, width), F32)],
        [me], [mine, w1, w2, w3],
    )
    return layer_out, grad_tokens, grad_proj, grad_outw


def solution(mesh):
    placed = (
        P(("dp", "ctx"), None),
        P(("dp", "ctx")),
        P(("dp", "ctx")),
        P("dp", None),
        P(),
        P(),
        P(("dp", "ctx"), None),
    )
    return jax.shard_map(
        on_device,
        mesh=mesh,
        in_specs=placed,
        out_specs=(P(("dp", "ctx"), None), P(("dp", "ctx"), None), P("dp", None), P("dp", None)),
        check_vma=False,
    )
```

```python
import functools

import jax
import jax.numpy as jnp
from jax import lax
from jax.experimental import pallas as pl
from jax.experimental.pallas import tpu as pltpu
from jax.sharding import PartitionSpec as P

HEADS = 8
EPSILON = 1e-05
LANES = 128
F32 = jnp.float32
BF16 = jnp.bfloat16

WHOLE = pl.BlockSpec(memory_space=pltpu.VMEM)
SCALARS = pl.BlockSpec(memory_space=pltpu.SMEM)
ANYWHERE = pl.BlockSpec(memory_space=pl.ANY)


def call(body, name, outs, scalars, arrays, scratch=(), flops=10**8, vmem=8, far=()):
    return pl.pallas_call(
        body,
        name=name,
        out_shape=[jax.ShapeDtypeStruct(s, d) for s, d in outs],
        in_specs=[SCALARS] * len(scalars) + [WHOLE] * len(arrays) + [ANYWHERE] * len(far),
        out_specs=[WHOLE] * len(outs),
        scratch_shapes=list(scratch),
        compiler_params=pltpu.CompilerParams(vmem_limit_bytes=vmem * 2**20),
        cost_estimate=pl.CostEstimate(flops=flops, bytes_accessed=2**20, transcendentals=0),
    )(*scalars, *arrays, *far)


def iota(shape, dim):
    return lax.broadcasted_iota(jnp.int32, shape, dim)


def mm(a, b):
    return jnp.dot(a, b, preferred_element_type=F32)


def mm_t(a, b):
    return lax.dot_general(a, b, (((1,), (1,)), ((), ())), preferred_element_type=F32)


def t_mm(a, b):
    return lax.dot_general(a, b, (((0,), (0,)), ((), ())), preferred_element_type=F32)


def hot(condition):
    return jnp.where(condition, 1.0, 0.0).astype(BF16)


def normalize(value):
    middle = jnp.mean(value, axis=-1, keepdims=True)
    centred = value - middle
    inv_dev = lax.rsqrt(jnp.mean(centred * centred, axis=-1, keepdims=True) + EPSILON)
    return centred * inv_dev, inv_dev


def norm_back(grad, normed, inv_dev):
    return inv_dev * (
        grad
        - jnp.mean(grad, axis=-1, keepdims=True)
        - normed * jnp.mean(grad * normed, axis=-1, keepdims=True)
    )


def silu_both(value):
    squashed = 0.5 * jnp.tanh(0.5 * value) + 0.5
    return value * squashed, squashed * (1.0 + value * (1.0 - squashed))


def rank_rows(owner):
    rows = owner.shape[1]
    down, across = iota((rows, rows), 0), iota((rows, rows), 1)
    spread = jnp.broadcast_to(owner, (rows, rows))
    owner_col = jnp.sum(jnp.where(down == across, spread, 0).astype(F32), axis=1, keepdims=True)
    same = owner_col.astype(jnp.int32) == spread
    rank_row = jnp.sum(jnp.where(same & (down < across), 1.0, 0.0), axis=0, keepdims=True)
    rank_col = jnp.sum(jnp.where(same & (across < down), 1.0, 0.0), axis=1, keepdims=True)
    return rank_row.astype(jnp.int32), rank_col.astype(jnp.int32)


def fetch(sources, targets, sems):
    copies = [pltpu.make_async_copy(a, b, sems.at[i]) for i, (a, b) in enumerate(zip(sources, targets))]
    for copy in copies:
        copy.start()
    for copy in copies:
        copy.wait()


def store_blocks(refs, value):
    size = refs[0].shape[0]
    for i, ref in enumerate(refs):
        ref[...] = value[i * size : (i + 1) * size].astype(ref.dtype)


def hop_order(count):
    return sorted(range(count), key=lambda k: (0 < k < count // 2, k))


def load_blocks(refs):
    order = hop_order(len(refs))
    return jnp.concatenate(
        [refs[order.index(k)][...].astype(F32) for k in range(len(refs))], axis=0
    ).astype(BF16)


def pack_blocks(steps, capacity, stride, owner, slot, tokens, out_refs):
    rows, width = tokens.shape
    rank_row, rank_col = rank_rows(owner)
    place = iota((len(steps) * stride, rows), 0)
    for i, (before, k) in enumerate(zip((-1, *steps), steps)):
        if k != before + 1:
            place = jnp.where(iota(place.shape, 0) >= i * stride, place + (k - before - 1) * stride, place)
    chosen = hot(place == owner * stride + rank_row)
    slots = jnp.where(place == owner * stride + capacity, slot + 1, 0)
    by_rank = hot(rank_col == iota((rows, width), 1))
    store_blocks(out_refs, mm(chosen, tokens) + mm(slots.astype(F32).astype(BF16), by_rank))


def pack_body(steps, capacity, stride, mask_ref, owner_hbm, slot_hbm, tokens_hbm, *refs):
    *out_refs, owner_ref, slot_ref, tokens_ref, sems = refs
    fetch((owner_hbm, slot_hbm, tokens_hbm), (owner_ref, slot_ref, tokens_ref), sems)
    owner = owner_ref[...] ^ mask_ref[0]
    owner_ref[...] = owner
    if len(steps) == 1:
        steps = range(out_refs[0].shape[0] // stride)
    pack_blocks(tuple(steps), capacity, stride, owner, slot_ref[...], tokens_ref[...], out_refs)


def pack_rest_body(steps, capacity, stride, owner_ref, slot_ref, tokens_ref, _, *out_refs):
    pack_blocks(steps, capacity, stride, owner_ref[...], slot_ref[...], tokens_ref[...], out_refs)


def block_rem(owners, stride):
    col, first = iota((owners, owners * stride), 1), iota((owners, owners * stride), 0)
    above = jnp.sum(jnp.where(col >= stride * (first + 1), 1.0, 0.0), axis=0, keepdims=True)
    rem = iota((1, owners * stride), 1) - stride * above.astype(jnp.int32)
    inside = (col >= stride * first) & (col < stride * (first + 1))
    return rem, inside


def landing_row(table, owners, capacity, stride):
    rem, inside = block_rem(owners, stride)
    lanes = iota((table.shape[1], owners * stride), 0)
    spread = mm(table, hot((lanes == rem) & (lanes < capacity)))
    return jnp.sum(jnp.where(inside, spread, 0.0), axis=0, keepdims=True)


def place_body(owners, capacity, stride, *refs):
    owned_ref, normed_ref, landing_ref = refs[-3:]
    rows = owned_ref.shape[0]
    arrived = load_blocks(refs[:-3])
    total = arrived.shape[0]
    pick = hot(iota((owners, total), 1) == iota((owners, total), 0) * stride + capacity)
    table = mm(pick, arrived).astype(BF16)
    landing = landing_row(table, owners, capacity, stride).astype(jnp.int32)
    owned = mm(hot(iota((rows, total), 0) + 1 == landing), arrived)
    owned_ref[...] = owned.astype(BF16)
    normed_ref[...] = normalize(owned)[0].astype(BF16)
    landing_ref[...] = landing_row(table, owners, capacity, capacity).astype(jnp.int32)


def early_body(cot_ref, outw_ref, proj_ref, grad_ref):
    grad_ref[...] = mm_t(cot_ref[...], outw_ref[...])


def history_start(pos, lengths_ref):
    first = lengths_ref[0, 0]
    second = lengths_ref[0, 1]
    return jnp.where(pos >= first + second, first + second, jnp.where(pos >= first, first, 0))


def attend(query_ref, key, value, shared, acc_ref):
    width = query_ref.shape[1]
    left = iota((1, LANES), 1) < LANES // 2
    for pair in range(width // LANES):
        cols = slice(pair * LANES, (pair + 1) * LANES)
        query, key_pair, value_pair = query_ref[:, cols], key[:, cols], value[:, cols]
        total = acc_ref[:, cols]
        for mine in (left, ~left):
            half = mm_t(jnp.where(mine, query, 0).astype(BF16), key_pair) * 0.0625
            weights = (half * (1.0 + jnp.tanh(half)) * shared).astype(BF16)
            total += mm(weights, jnp.where(mine, value_pair, 0).astype(BF16))
        acc_ref[:, cols] = total


def shared_factor(block, me, rows, lengths_ref):
    query_pos = me * rows + iota((rows, 1), 0)
    start = history_start(query_pos, lengths_ref)
    inverse = 1.0 / (query_pos - start + 1).astype(F32)
    key_pos = block * rows + iota((1, rows), 1)
    return jnp.where((key_pos >= start) & (key_pos <= query_pos), inverse, 0.0)


def attend_other(step, me, lengths_ref, other_ref, proj_ref, query_ref, acc_ref):
    rows, width = query_ref.shape
    block = me ^ step
    reach = history_start(me * rows, lengths_ref)

    @pl.when((block < me) & ((block + 1) * rows > reach))
    def _():
        normed = other_ref[...]
        value = silu_both(mm(normed, proj_ref[:, width : 2 * width]))[0].astype(BF16)
        key = silu_both(mm(normed, proj_ref[:, 3 * width :]))[0].astype(BF16)
        attend(query_ref, key, value, shared_factor(block, me, rows, lengths_ref), acc_ref)


def own_body(
    me_ref, lengths_ref, normed_ref, proj_ref, gate_ref, slope_ref, query_ref, acc_ref, copy_ref
):
    rows, width = normed_ref.shape
    copy_ref[...] = normed_ref[...]
    me = me_ref[0]
    preact = mm(normed_ref[...], proj_ref[...])
    gate, slope = silu_both(preact[:, :width])
    gate_ref[...] = gate.astype(BF16)
    slope_ref[...] = slope
    value = silu_both(preact[:, width : 2 * width])[0].astype(BF16)
    query_ref[...] = silu_both(preact[:, 2 * width : 3 * width])[0].astype(BF16)
    key = silu_both(preact[:, 3 * width :])[0].astype(BF16)
    acc_ref[...] = jnp.zeros_like(acc_ref)
    attend(query_ref, key, value, shared_factor(me, me, rows, lengths_ref), acc_ref)


def middle_body(me_ref, lengths_ref, near_ref, far_ref, proj_ref, query_ref, partial_ref, acc_ref):
    me = me_ref[0]
    acc_ref[...] = partial_ref[...]
    attend_other(1, me, lengths_ref, near_ref, proj_ref, query_ref, acc_ref)
    attend_other(2, me, lengths_ref, far_ref, proj_ref, query_ref, acc_ref)


def forward_body(
    me_ref, lengths_ref, cross_ref, proj_ref, gate_ref, query_ref, partial_ref, grad_ref,
    normed_ref, *rest,
):
    grads, acc_ref = rest[:-1], rest[-1]
    width = query_ref.shape[1]
    me = me_ref[0]
    acc_ref[...] = partial_ref[...]
    attend_other(3, me, lengths_ref, cross_ref, proj_ref, query_ref, acc_ref)
    normed, inv_dev = normalize(acc_ref[...])
    normed_ref[...] = normed
    acc_ref[...] = norm_back(grad_ref[...] * gate_ref[...].astype(F32), normed, inv_dev)
    piece = width // len(grads)
    for step, ref in enumerate(grads):
        ref[...] = acc_ref[:, pl.ds(pl.multiple_of((me ^ step) * piece, LANES), piece)].astype(BF16)


def side_body(
    me_ref, own_ref, normed_ref, gate_ref, slope_ref, grad_ref, cot_ref, proj_ref, outw_ref, owned_ref,
    kept_ref, sent_ref, gate_in_ref, out_ref, part_ref,
):
    width = own_ref.shape[1]
    me = me_ref[0]
    normed = normed_ref[...]
    gated = (normed * gate_ref[...].astype(F32)).astype(BF16)
    gate_grad = (grad_ref[...] * normed * slope_ref[...]).astype(BF16)
    out_ref[...] = (mm(gated, outw_ref[...]) + owned_ref[...].astype(F32)).astype(BF16)
    part_ref[:, :width] = t_mm(own_ref[...], gate_grad)
    part_ref[:, width:] = t_mm(gated, cot_ref[...])
    gate_in_ref[...] = mm_t(gate_grad, proj_ref[:, :width])
    for ref, steps in ((kept_ref, (0, 2)), (sent_ref, (1, 3))):
        place = 0
        for step in steps:
            for base in (0, width):
                source = pl.ds(pl.multiple_of(base + (me ^ step) * LANES, LANES), LANES)
                ref[:, place : place + LANES] = part_ref[:, source].astype(BF16)
                place += LANES


def side_sum_body(kept_ref, came_ref, keep_ref, send_ref):
    total = kept_ref[...].astype(F32) + came_ref[...].astype(F32)
    half = total.shape[1] // 2
    keep_ref[...] = total[:, :half].astype(BF16)
    send_ref[...] = total[:, half:].astype(BF16)


def heads_body(me_ref, n0_ref, n1_ref, n2_ref, n3_ref, proj_ref, part_ref, slope_ref):
    rows, width = n0_ref.shape
    me = me_ref[0]
    piece = width // 4
    cols = [proj_ref[:, pl.ds(pl.multiple_of(b * width + me * piece, LANES), piece)] for b in (1, 2, 3)]
    weight = jnp.concatenate(cols, axis=1)
    for step, ref in enumerate((n0_ref, n1_ref, n2_ref, n3_ref)):
        act, slope = silu_both(mm(ref[...], weight))
        at = pl.ds(pl.multiple_of((me ^ step) * rows, rows), rows)
        part_ref[at, :] = act.astype(BF16)
        slope_ref[at, :] = slope


def block_at(block, rows):
    return pl.ds(pl.multiple_of(block * rows, rows), rows)


def visit(first, second, same, lengths_ref, part_ref, grad_ref, total_ref):
    rows, piece = grad_ref.shape[0] // 4, grad_ref.shape[1]
    q_block, k_block = jnp.maximum(first, second), jnp.minimum(first, second)

    def work():
        q_at, k_at = block_at(q_block, rows), block_at(k_block, rows)
        left = iota((1, LANES), 1) < LANES // 2
        query_pos = q_block * rows + iota((1, rows), 1)
        start = history_start(query_pos, lengths_ref)
        key_pos = k_block * rows + iota((rows, 1), 0)
        inverse = 1.0 / (query_pos - start + 1).astype(F32)
        allowed = key_pos >= start
        if same:
            allowed &= key_pos <= query_pos
        shared = jnp.where(allowed, inverse, 0.0)
        value = part_ref[k_at, :piece]
        query = part_ref[q_at, piece : 2 * piece]
        key = part_ref[k_at, 2 * piece :]
        grad = grad_ref[q_at, :]
        small = value * jnp.asarray(0.0625, BF16)
        d_value, d_query, d_key = 0.0, 0.0, 0.0
        for mine in (left, ~left):
            query_h = jnp.where(mine, query, 0).astype(BF16)
            key_h = jnp.where(mine, key, 0).astype(BF16)
            grad_h = jnp.where(mine, grad, 0).astype(BF16)
            half = mm_t(key_h, query) * 0.0625
            up = 1.0 + jnp.tanh(half)
            act = half * up
            weights = (act * shared).astype(BF16)
            slope = (up + act * (2.0 - up)) * shared
            d_scores = (mm_t(small, grad_h) * slope).astype(BF16)
            d_value += mm(weights, grad_h)
            d_key += mm(d_scores, query_h)
            d_query += t_mm(d_scores, key_h)
        total_ref[k_at, :piece] += d_value
        total_ref[q_at, piece : 2 * piece] += d_query
        total_ref[k_at, 2 * piece :] += d_key

    if same:
        work()
    else:
        pl.when((k_block + 1) * rows > history_start(q_block * rows, lengths_ref))(work)


def backward_rows(steps, finished, me, lengths_ref, part_ref, slope_ref, grad_ref, total_ref, refs):
    done = list(finished)
    for step, ref in zip(steps, refs):
        for other in range(4):
            if other not in done:
                visit(me ^ step, me ^ other, other == step, lengths_ref, part_ref, grad_ref, total_ref)
        done.append(step)
        at = block_at(me ^ step, ref.shape[0])
        ref[...] = (total_ref[at, :] * slope_ref[at, :]).astype(BF16)


def collect_body(me_ref, g0_ref, g1_ref, g2_ref, g3_ref, grad_ref):
    rows = g0_ref.shape[0]
    for step, ref in enumerate((g0_ref, g1_ref, g2_ref, g3_ref)):
        grad_ref[block_at(me_ref[0] ^ step, rows), :] = ref[...]


def backward_far_body(me_ref, lengths_ref, part_ref, slope_ref, grad_ref, o2_ref, o3_ref, total_ref):
    total_ref[...] = jnp.zeros_like(total_ref)
    backward_rows(
        (2, 3), (), me_ref[0], lengths_ref, part_ref, slope_ref, grad_ref, total_ref, (o2_ref, o3_ref)
    )


def backward_rest_body(
    me_ref, lengths_ref, part_ref, slope_ref, grad_ref, sums_ref, o0_ref, o1_ref, total_ref
):
    total_ref[...] = sums_ref[...]
    backward_rows(
        (1, 0), (2, 3), me_ref[0], lengths_ref, part_ref, slope_ref, grad_ref, total_ref, (o1_ref, o0_ref)
    )


def weight_body(sources, pairs, dp_ref, kept_side_ref, came_side_ref, *refs):
    normed, grads = refs[:sources], refs[sources : 2 * sources]
    outs, total_ref = refs[2 * sources : -1], refs[-1]
    side = kept_side_ref.shape[1]
    total = 0.0
    for n_ref, g_ref in zip(normed, grads):
        total += t_mm(n_ref[...], g_ref[...])
    total_ref[:, :side] = kept_side_ref[...].astype(F32) + came_side_ref[...].astype(F32)
    total_ref[:, side:] = total
    if len(outs) == 1:
        outs[0][...] = total_ref[...].astype(BF16)
        return
    kept_ref, sent_ref = outs
    share = kept_ref.shape[0] // pairs
    for j in range(pairs):
        at = slice(j * share, (j + 1) * share)
        for ref, k in ((kept_ref, 2 * j), (sent_ref, 2 * j + 1)):
            source = pl.ds(pl.multiple_of((dp_ref[0] ^ k) * share, share), share)
            ref[at, :] = total_ref[source, :].astype(BF16)


def pair_body(kept_ref, came_ref, _, *outs):
    store_blocks(outs, kept_ref[...].astype(F32) + came_ref[...].astype(F32))


def head_columns(owner, proj_ref):
    width = proj_ref.shape[0]
    cols = [proj_ref[:, pl.ds(pl.multiple_of(b * width + owner * LANES, LANES), LANES)] for b in (1, 2, 3)]
    return jnp.concatenate(cols, axis=1)


def input_far_body(me_ref, far_ref, cross_ref, gate_in_ref, proj_ref, out_ref):
    me = me_ref[0]
    total = gate_in_ref[...] + mm_t(far_ref[...], head_columns(me ^ 2, proj_ref))
    out_ref[...] = total + mm_t(cross_ref[...], head_columns(me ^ 3, proj_ref))


def input_body(me_ref, own_ref, near_ref, partial_ref, owned_ref, cot_ref, proj_ref, out_ref):
    me = me_ref[0]
    total = partial_ref[...] + mm_t(own_ref[...], head_columns(me, proj_ref))
    total += mm_t(near_ref[...], head_columns(me ^ 1, proj_ref))
    centred, inv_scale = normalize(owned_ref[...].astype(F32))
    grad = (norm_back(total, centred, inv_scale) + cot_ref[...].astype(F32)).astype(BF16)
    out_ref[...] = grad


def spread_body(blocks, mask_ref, grad_ref, landing_ref, _, out_ref):
    select = hot(iota((grad_ref.shape[0], landing_ref.shape[1]), 0) + 1 == landing_ref[...])
    value = t_mm(select, grad_ref[...])
    size = value.shape[0] // blocks
    for k in range(blocks):
        at = pl.ds(pl.multiple_of((mask_ref[0] ^ k) * size, size), size)
        out_ref[at, :] = value[k * size : (k + 1) * size].astype(BF16)


def return_body(capacity, mask_ref, owner_ref, back_ref, out_ref):
    owner = owner_ref[...] ^ mask_ref[0]
    rank_row, _ = rank_rows(owner)
    chosen = hot(iota((back_ref.shape[0], owner.shape[1]), 0) == owner * capacity + rank_row)
    out_ref[...] = t_mm(chosen, back_ref[...]).astype(BF16)


def sum_body(*refs):
    total = 0.0
    for ref in refs[:-1]:
        parts = ref[...].astype(F32)
        total += parts if ref.ndim == 2 else jnp.sum(parts, axis=0)
    refs[-1][...] = total.astype(BF16)


def finish_body(me_ref, w0_ref, w1_ref, w2_ref, w3_ref, proj_ref, outw_ref):
    me = me_ref[0]
    width = outw_ref.shape[1]
    for step, ref in enumerate((w0_ref, w1_ref, w2_ref, w3_ref)):
        at = pl.ds(pl.multiple_of((me ^ step) * LANES, LANES), LANES)
        outw_ref[:, at] = ref[:, LANES : 2 * LANES].astype(F32)
        for b, source in enumerate((0, 2, 3, 4)):
            at = pl.ds(pl.multiple_of(b * width + (me ^ step) * LANES, LANES), LANES)
            proj_ref[:, at] = ref[:, source * LANES : (source + 1) * LANES].astype(F32)


def on_device(tokens, dest_owner, dest_slot, lengths, proj_weight, out_weight, cotangent):
    rows, width = tokens.shape
    owners = lax.axis_size("dp")
    cycle = lax.axis_size("ctx")
    assert cycle == 4 and width == cycle * LANES
    capacity = 2 * rows // owners
    stride = capacity + 8
    piece = width // cycle
    me = lax.axis_index("ctx").astype(jnp.int32).reshape(1)
    owner_row = dest_owner.reshape(1, rows)
    slot_row = dest_slot.reshape(1, rows)
    square = ((rows, width), BF16)

    def hop(value, step):
        return lax.ppermute(value, "ctx", [(i, i ^ step) for i in range(cycle)])

    def exchange(values):
        return [values[0]] + [hop(values[step], step) for step in (2, 3, 1)]

    by_hops = owners <= 8
    blocks = owners if by_hops else 1
    dp = lax.axis_index("dp").astype(jnp.int32).reshape(1)
    mask = dp if by_hops else jnp.zeros_like(dp)

    def dp_hop(value, step):
        return lax.ppermute(value, "dp", [(i, i ^ step) for i in range(owners)])

    def swap_whole(value):
        split = value.reshape(owners, value.shape[0] // owners, value.shape[1])
        return lax.all_to_all(split, "dp", split_axis=0, concat_axis=0, tiled=True).reshape(value.shape)

    def swap(values):
        if by_hops:
            return [dp_hop(values[k], k) if k else values[k] for k in hop_order(owners)]
        return [swap_whole(values[0])]

    def block_shapes(height, columns, dtype):
        return [((owners * height // blocks, columns), dtype)] * blocks

    wide = ((rows, width), F32)
    steps = tuple(range(blocks))
    later = steps[owners // 4 : owners // 2] if by_hops else ()
    first = tuple(k for k in steps if k not in later)
    *outgoing, owner_here, slot_here, tokens_here = call(
        functools.partial(pack_body, first, capacity, stride),
        "pack",
        block_shapes(stride, width, BF16)[: len(first)] + [((1, rows), jnp.int32)] * 2 + [square],
        [mask], [], far=[owner_row, slot_row, tokens], scratch=[pltpu.SemaphoreType.DMA((3,))],
    )
    (grad_gated,) = call(early_body, "early", [wide], [], [cotangent, out_weight, proj_weight])
    outgoing = dict(zip(first, outgoing))
    if later:
        rest = call(
            functools.partial(pack_rest_body, later, capacity, stride),
            "pack_rest", block_shapes(stride, width, BF16)[: len(later)], [],
            [owner_here, slot_here, tokens_here], far=[grad_gated],
        )
        outgoing.update(zip(later, rest))
    arrived = swap([outgoing[k] for k in steps])
    owned, normed, landing = call(
        functools.partial(place_body, owners, capacity, stride),
        "place", [square, square, ((1, owners * capacity), jnp.int32)], [], arrived,
    )
    far = hop(normed, 2)
    cross = hop(far, 1)
    gate, slope, query, partial, normed_copy = call(
        own_body, "own_rows", [square, wide, square, wide, square],
        [me, lengths], [normed, proj_weight], flops=10**10, vmem=16,
    )
    near = hop(normed_copy, 1)
    (partial,) = call(
        middle_body, "middle", [wide], [me, lengths], [near, far, proj_weight, query, partial],
        flops=10**10, vmem=16,
    )
    normed_out, *grad_pieces = call(
        forward_body, "forward", [wide] + [((rows, piece), BF16)] * cycle,
        [me, lengths], [cross, proj_weight, gate, query, partial, grad_gated],
        scratch=[pltpu.VMEM((rows, width), F32)], vmem=16,
    )
    r0, r2, r3, r1 = exchange(grad_pieces)
    side_half = ((width, 4 * piece), BF16)
    side_piece = ((width, 2 * piece), BF16)
    side_kept, side_sent, gate_in, layer_out = call(
        side_body, "side", [side_half, side_half, wide, square],
        [me], [normed, normed_out, gate, slope, grad_gated, cotangent, proj_weight, out_weight, owned],
        scratch=[pltpu.VMEM((width, 2 * width), F32)], vmem=16,
    )
    side_came = hop(side_sent, 1)
    parts, slopes = call(
        heads_body, "heads",
        [((rows * cycle, 3 * piece), BF16), ((rows * cycle, 3 * piece), F32)],
        [me], [normed, near, far, cross, proj_weight], vmem=16,
    )
    side_keep, side_send = call(
        side_sum_body, "side_sum", [side_piece, side_piece], [], [side_kept, side_came]
    )
    side_last = hop(side_send, 2)
    grad_block = ((rows, 3 * piece), BF16)
    sums = ((rows * cycle, 3 * piece), F32)
    grad_rows = ((rows * cycle, piece), BF16)
    (grad_all,) = call(
        collect_body, "collect", [grad_rows], [me], [r0, r1, r2, r3], flops=6 * 10**9,
    )
    far_block, cross_block, totals = call(
        backward_far_body, "backward_far", [grad_block, grad_block, sums],
        [me, lengths], [parts, slopes, grad_all], flops=10**10, vmem=16,
    )
    p2, p3 = hop(far_block, 2), hop(cross_block, 3)
    own_block, near_block = call(
        backward_rest_body, "backward_rest", [grad_block] * 2,
        [me, lengths], [parts, slopes, grad_all, totals], vmem=16,
        scratch=[pltpu.VMEM(*sums)],
    )
    p1 = hop(near_block, 1)
    grads = [own_block, near_block, far_block, cross_block]
    share = width // owners
    pairs = owners // 2
    columns = 5 * piece
    weight_parts = call(
        functools.partial(weight_body, cycle, pairs), "weights",
        [((pairs * share, columns), BF16)] * 2 if by_hops else [((width, columns), BF16)], [dp],
        [side_keep, side_last, normed, near, far, cross, *grads], vmem=16,
        scratch=[pltpu.VMEM((width, columns), F32)],
    )
    (partial_in,) = call(
        input_far_body, "input_far", [wide], [me], [p2, p3, gate_in, proj_weight], flops=6 * 10**9,
    )
    (grad_owned,) = call(
        input_body, "input_grad", [square], [me],
        [own_block, p1, partial_in, owned, cotangent, proj_weight], vmem=16,
    )
    if by_hops:
        kept, sent = weight_parts
        halves = call(
            pair_body, "pair_sum", [((share, columns), BF16)] * pairs, [], [kept, dp_hop(sent, 1)],
            far=[partial_in],
        )
        summed_parts = [halves[0]] + [dp_hop(halves[j], 2 * j) for j in range(1, pairs)]
    else:
        halves = weight_parts
        summed_parts = [swap_whole(weight_parts[0]).reshape(owners, share, columns)]
    (mine,) = call(sum_body, "sum", [((share, columns), BF16)], [], summed_parts, flops=10**11)
    (back,) = call(
        functools.partial(spread_body, blocks), "spread", [((owners * capacity, width), BF16)],
        [mask], [grad_owned, landing], far=halves[:1],
    )
    returned = swap_whole(back)
    w1, w2, w3 = (hop(mine, step) for step in range(1, cycle))
    (grad_tokens,) = call(
        functools.partial(return_body, capacity), "give_back", [square], [mask], [owner_here, returned]
    )
    grad_proj, grad_outw = call(
        finish_body, "finish", [((share, 4 * width), F32), ((share, width), F32)],
        [me], [mine, w1, w2, w3],
    )
    return layer_out, grad_tokens, grad_proj, grad_outw


def solution(mesh):
    placed = (
        P(("dp", "ctx"), None),
        P(("dp", "ctx")),
        P(("dp", "ctx")),
        P("dp", None),
        P(),
        P(),
        P(("dp", "ctx"), None),
    )
    return jax.shard_map(
        on_device,
        mesh=mesh,
        in_specs=placed,
        out_specs=(P(("dp", "ctx"), None), P(("dp", "ctx"), None), P("dp", None), P("dp", None)),
        check_vma=False,
    )
```

```python
import functools

import jax
import jax.numpy as jnp
from jax import lax
from jax.experimental import pallas as pl
from jax.experimental.pallas import tpu as pltpu
from jax.sharding import PartitionSpec as P

HEADS = 8
EPSILON = 1e-05
LANES = 128
F32 = jnp.float32
BF16 = jnp.bfloat16

WHOLE = pl.BlockSpec(memory_space=pltpu.VMEM)
SCALARS = pl.BlockSpec(memory_space=pltpu.SMEM)
ANYWHERE = pl.BlockSpec(memory_space=pl.ANY)


def call(body, name, outs, scalars, arrays, scratch=(), flops=10**8, vmem=8, far=()):
    return pl.pallas_call(
        body,
        name=name,
        out_shape=[jax.ShapeDtypeStruct(s, d) for s, d in outs],
        in_specs=[SCALARS] * len(scalars) + [WHOLE] * len(arrays) + [ANYWHERE] * len(far),
        out_specs=[WHOLE] * len(outs),
        scratch_shapes=list(scratch),
        compiler_params=pltpu.CompilerParams(vmem_limit_bytes=vmem * 2**20),
        cost_estimate=pl.CostEstimate(flops=flops, bytes_accessed=2**20, transcendentals=0),
    )(*scalars, *arrays, *far)


def iota(shape, dim):
    return lax.broadcasted_iota(jnp.int32, shape, dim)


def mm(a, b):
    return jnp.dot(a, b, preferred_element_type=F32)


def mm_t(a, b):
    return lax.dot_general(a, b, (((1,), (1,)), ((), ())), preferred_element_type=F32)


def t_mm(a, b):
    return lax.dot_general(a, b, (((0,), (0,)), ((), ())), preferred_element_type=F32)


def hot(condition):
    return jnp.where(condition, 1.0, 0.0).astype(BF16)


def normalize(value):
    middle = jnp.mean(value, axis=-1, keepdims=True)
    centred = value - middle
    inv_dev = lax.rsqrt(jnp.mean(centred * centred, axis=-1, keepdims=True) + EPSILON)
    return centred * inv_dev, inv_dev


def norm_back(grad, normed, inv_dev):
    return inv_dev * (
        grad
        - jnp.mean(grad, axis=-1, keepdims=True)
        - normed * jnp.mean(grad * normed, axis=-1, keepdims=True)
    )


def silu_both(value):
    squashed = 0.5 * jnp.tanh(0.5 * value) + 0.5
    return value * squashed, squashed * (1.0 + value * (1.0 - squashed))


def rank_rows(owner):
    rows = owner.shape[1]
    down, across = iota((rows, rows), 0), iota((rows, rows), 1)
    spread = jnp.broadcast_to(owner, (rows, rows))
    owner_col = jnp.sum(jnp.where(down == across, spread, 0).astype(F32), axis=1, keepdims=True)
    same = owner_col.astype(jnp.int32) == spread
    rank_row = jnp.sum(jnp.where(same & (down < across), 1.0, 0.0), axis=0, keepdims=True)
    rank_col = jnp.sum(jnp.where(same & (across < down), 1.0, 0.0), axis=1, keepdims=True)
    return rank_row.astype(jnp.int32), rank_col.astype(jnp.int32)


def fetch(sources, targets, sems):
    copies = [pltpu.make_async_copy(a, b, sems.at[i]) for i, (a, b) in enumerate(zip(sources, targets))]
    for copy in copies:
        copy.start()
    for copy in copies:
        copy.wait()


def store_blocks(refs, value):
    size = refs[0].shape[0]
    for i, ref in enumerate(refs):
        ref[...] = value[i * size : (i + 1) * size].astype(ref.dtype)


def hop_order(count):
    return sorted(range(count), key=lambda k: (0 < k < count // 2, k))


def load_blocks(refs):
    order = hop_order(len(refs))
    return jnp.concatenate(
        [refs[order.index(k)][...].astype(F32) for k in range(len(refs))], axis=0
    ).astype(BF16)


def pack_blocks(steps, capacity, stride, owner, slot, tokens, out_refs):
    rows, width = tokens.shape
    rank_row, rank_col = rank_rows(owner)
    place = iota((len(steps) * stride, rows), 0)
    for i, (before, k) in enumerate(zip((-1, *steps), steps)):
        if k != before + 1:
            place = jnp.where(iota(place.shape, 0) >= i * stride, place + (k - before - 1) * stride, place)
    chosen = hot(place == owner * stride + rank_row)
    slots = jnp.where(place == owner * stride + capacity, slot + 1, 0)
    by_rank = hot(rank_col == iota((rows, width), 1))
    store_blocks(out_refs, mm(chosen, tokens) + mm(slots.astype(F32).astype(BF16), by_rank))


def pack_body(steps, capacity, stride, mask_ref, owner_hbm, slot_hbm, tokens_hbm, *refs):
    *out_refs, owner_ref, slot_ref, tokens_ref, sems = refs
    fetch((owner_hbm, slot_hbm, tokens_hbm), (owner_ref, slot_ref, tokens_ref), sems)
    owner = owner_ref[...] ^ mask_ref[0]
    owner_ref[...] = owner
    if len(steps) == 1:
        steps = range(out_refs[0].shape[0] // stride)
    pack_blocks(tuple(steps), capacity, stride, owner, slot_ref[...], tokens_ref[...], out_refs)


def pack_rest_body(steps, capacity, stride, owner_ref, slot_ref, tokens_ref, _, *out_refs):
    pack_blocks(steps, capacity, stride, owner_ref[...], slot_ref[...], tokens_ref[...], out_refs)


def block_rem(owners, stride):
    col, first = iota((owners, owners * stride), 1), iota((owners, owners * stride), 0)
    above = jnp.sum(jnp.where(col >= stride * (first + 1), 1.0, 0.0), axis=0, keepdims=True)
    rem = iota((1, owners * stride), 1) - stride * above.astype(jnp.int32)
    inside = (col >= stride * first) & (col < stride * (first + 1))
    return rem, inside


def landing_row(table, owners, capacity, stride):
    rem, inside = block_rem(owners, stride)
    lanes = iota((table.shape[1], owners * stride), 0)
    spread = mm(table, hot((lanes == rem) & (lanes < capacity)))
    return jnp.sum(jnp.where(inside, spread, 0.0), axis=0, keepdims=True)


def place_body(owners, capacity, stride, *refs):
    owned_ref, normed_ref, landing_ref = refs[-3:]
    rows = owned_ref.shape[0]
    arrived = load_blocks(refs[:-3])
    total = arrived.shape[0]
    pick = hot(iota((owners, total), 1) == iota((owners, total), 0) * stride + capacity)
    table = mm(pick, arrived).astype(BF16)
    landing = landing_row(table, owners, capacity, stride).astype(jnp.int32)
    owned = mm(hot(iota((rows, total), 0) + 1 == landing), arrived)
    owned_ref[...] = owned.astype(BF16)
    normed_ref[...] = normalize(owned)[0].astype(BF16)
    landing_ref[...] = landing_row(table, owners, capacity, capacity).astype(jnp.int32)


def early_body(cot_ref, outw_ref, proj_ref, grad_ref):
    grad_ref[...] = mm_t(cot_ref[...], outw_ref[...])


def history_start(pos, lengths_ref):
    first = lengths_ref[0, 0]
    second = lengths_ref[0, 1]
    return jnp.where(pos >= first + second, first + second, jnp.where(pos >= first, first, 0))


def attend(query_ref, key, value, shared, acc_ref):
    width = query_ref.shape[1]
    left = iota((1, LANES), 1) < LANES // 2
    for pair in range(width // LANES):
        cols = slice(pair * LANES, (pair + 1) * LANES)
        query, key_pair, value_pair = query_ref[:, cols], key[:, cols], value[:, cols]
        total = acc_ref[:, cols]
        for mine in (left, ~left):
            half = mm_t(jnp.where(mine, query, 0).astype(BF16), key_pair) * 0.0625
            weights = (half * (1.0 + jnp.tanh(half)) * shared).astype(BF16)
            total += mm(weights, jnp.where(mine, value_pair, 0).astype(BF16))
        acc_ref[:, cols] = total


def shared_factor(block, me, rows, lengths_ref):
    query_pos = me * rows + iota((rows, 1), 0)
    start = history_start(query_pos, lengths_ref)
    inverse = 1.0 / (query_pos - start + 1).astype(F32)
    key_pos = block * rows + iota((1, rows), 1)
    return jnp.where((key_pos >= start) & (key_pos <= query_pos), inverse, 0.0)


def attend_other(step, me, lengths_ref, other_ref, proj_ref, query_ref, acc_ref):
    rows, width = query_ref.shape
    block = me ^ step
    reach = history_start(me * rows, lengths_ref)

    @pl.when((block < me) & ((block + 1) * rows > reach))
    def _():
        normed = other_ref[...]
        value = silu_both(mm(normed, proj_ref[:, width : 2 * width]))[0].astype(BF16)
        key = silu_both(mm(normed, proj_ref[:, 3 * width :]))[0].astype(BF16)
        attend(query_ref, key, value, shared_factor(block, me, rows, lengths_ref), acc_ref)


def own_body(
    me_ref, lengths_ref, normed_ref, proj_ref, gate_ref, slope_ref, query_ref, acc_ref, copy_ref
):
    rows, width = normed_ref.shape
    copy_ref[...] = normed_ref[...]
    me = me_ref[0]
    preact = mm(normed_ref[...], proj_ref[...])
    gate, slope = silu_both(preact[:, :width])
    gate_ref[...] = gate.astype(BF16)
    slope_ref[...] = slope
    value = silu_both(preact[:, width : 2 * width])[0].astype(BF16)
    query_ref[...] = silu_both(preact[:, 2 * width : 3 * width])[0].astype(BF16)
    key = silu_both(preact[:, 3 * width :])[0].astype(BF16)
    acc_ref[...] = jnp.zeros_like(acc_ref)
    attend(query_ref, key, value, shared_factor(me, me, rows, lengths_ref), acc_ref)


def middle_body(me_ref, lengths_ref, near_ref, far_ref, proj_ref, query_ref, partial_ref, acc_ref):
    me = me_ref[0]
    acc_ref[...] = partial_ref[...]
    attend_other(1, me, lengths_ref, near_ref, proj_ref, query_ref, acc_ref)
    attend_other(2, me, lengths_ref, far_ref, proj_ref, query_ref, acc_ref)


def forward_body(
    me_ref, lengths_ref, cross_ref, proj_ref, gate_ref, query_ref, partial_ref, grad_ref,
    normed_ref, *rest,
):
    grads, acc_ref = rest[:-1], rest[-1]
    width = query_ref.shape[1]
    me = me_ref[0]
    acc_ref[...] = partial_ref[...]
    attend_other(3, me, lengths_ref, cross_ref, proj_ref, query_ref, acc_ref)
    normed, inv_dev = normalize(acc_ref[...])
    normed_ref[...] = normed
    acc_ref[...] = norm_back(grad_ref[...] * gate_ref[...].astype(F32), normed, inv_dev)
    piece = width // len(grads)
    for step, ref in enumerate(grads):
        ref[...] = acc_ref[:, pl.ds(pl.multiple_of((me ^ step) * piece, LANES), piece)].astype(BF16)


def side_body(
    me_ref, own_ref, normed_ref, gate_ref, slope_ref, grad_ref, cot_ref, proj_ref, outw_ref, owned_ref,
    kept_ref, sent_ref, gate_in_ref, out_ref, part_ref,
):
    width = own_ref.shape[1]
    me = me_ref[0]
    normed = normed_ref[...]
    gated = (normed * gate_ref[...].astype(F32)).astype(BF16)
    gate_grad = (grad_ref[...] * normed * slope_ref[...]).astype(BF16)
    out_ref[...] = (mm(gated, outw_ref[...]) + owned_ref[...].astype(F32)).astype(BF16)
    part_ref[:, :width] = t_mm(own_ref[...], gate_grad)
    part_ref[:, width:] = t_mm(gated, cot_ref[...])
    gate_in_ref[...] = mm_t(gate_grad, proj_ref[:, :width])
    for ref, steps in ((kept_ref, (0, 2)), (sent_ref, (1, 3))):
        place = 0
        for step in steps:
            for base in (0, width):
                source = pl.ds(pl.multiple_of(base + (me ^ step) * LANES, LANES), LANES)
                ref[:, place : place + LANES] = part_ref[:, source].astype(BF16)
                place += LANES


def side_sum_body(kept_ref, came_ref, keep_ref, send_ref):
    total = kept_ref[...].astype(F32) + came_ref[...].astype(F32)
    half = total.shape[1] // 2
    keep_ref[...] = total[:, :half].astype(BF16)
    send_ref[...] = total[:, half:].astype(BF16)


def heads_body(me_ref, n0_ref, n1_ref, n2_ref, n3_ref, proj_ref, part_ref, slope_ref):
    rows, width = n0_ref.shape
    me = me_ref[0]
    piece = width // 4
    cols = [proj_ref[:, pl.ds(pl.multiple_of(b * width + me * piece, LANES), piece)] for b in (1, 2, 3)]
    weight = jnp.concatenate(cols, axis=1)
    for step, ref in enumerate((n0_ref, n1_ref, n2_ref, n3_ref)):
        act, slope = silu_both(mm(ref[...], weight))
        at = pl.ds(pl.multiple_of((me ^ step) * rows, rows), rows)
        part_ref[at, :] = act.astype(BF16)
        slope_ref[at, :] = slope


def block_at(block, rows):
    return pl.ds(pl.multiple_of(block * rows, rows), rows)


def visit(first, second, same, lengths_ref, part_ref, grad_ref, total_ref):
    rows, piece = grad_ref.shape[0] // 4, grad_ref.shape[1]
    q_block, k_block = jnp.maximum(first, second), jnp.minimum(first, second)

    def work():
        q_at, k_at = block_at(q_block, rows), block_at(k_block, rows)
        left = iota((1, LANES), 1) < LANES // 2
        query_pos = q_block * rows + iota((1, rows), 1)
        start = history_start(query_pos, lengths_ref)
        key_pos = k_block * rows + iota((rows, 1), 0)
        inverse = 1.0 / (query_pos - start + 1).astype(F32)
        allowed = key_pos >= start
        if same:
            allowed &= key_pos <= query_pos
        shared = jnp.where(allowed, inverse, 0.0)
        value = part_ref[k_at, :piece]
        query = part_ref[q_at, piece : 2 * piece]
        key = part_ref[k_at, 2 * piece :]
        grad = grad_ref[q_at, :]
        small = value * jnp.asarray(0.0625, BF16)
        d_value, d_query, d_key = 0.0, 0.0, 0.0
        for mine in (left, ~left):
            query_h = jnp.where(mine, query, 0).astype(BF16)
            key_h = jnp.where(mine, key, 0).astype(BF16)
            grad_h = jnp.where(mine, grad, 0).astype(BF16)
            half = mm_t(key_h, query) * 0.0625
            up = 1.0 + jnp.tanh(half)
            act = half * up
            weights = (act * shared).astype(BF16)
            slope = (up + act * (2.0 - up)) * shared
            d_scores = (mm_t(small, grad_h) * slope).astype(BF16)
            d_value += mm(weights, grad_h)
            d_key += mm(d_scores, query_h)
            d_query += t_mm(d_scores, key_h)
        total_ref[k_at, :piece] += d_value
        total_ref[q_at, piece : 2 * piece] += d_query
        total_ref[k_at, 2 * piece :] += d_key

    if same:
        work()
    else:
        pl.when((k_block + 1) * rows > history_start(q_block * rows, lengths_ref))(work)


def backward_rows(steps, finished, me, lengths_ref, part_ref, slope_ref, grad_ref, total_ref, refs):
    done = list(finished)
    for step, ref in zip(steps, refs):
        for other in range(4):
            if other not in done:
                visit(me ^ step, me ^ other, other == step, lengths_ref, part_ref, grad_ref, total_ref)
        done.append(step)
        at = block_at(me ^ step, ref.shape[0])
        ref[...] = (total_ref[at, :] * slope_ref[at, :]).astype(BF16)


def collect_body(me_ref, g0_ref, g1_ref, g2_ref, g3_ref, grad_ref):
    rows = g0_ref.shape[0]
    for step, ref in enumerate((g0_ref, g1_ref, g2_ref, g3_ref)):
        grad_ref[block_at(me_ref[0] ^ step, rows), :] = ref[...]


def backward_far_body(me_ref, lengths_ref, part_ref, slope_ref, grad_ref, o2_ref, o3_ref, total_ref):
    total_ref[...] = jnp.zeros_like(total_ref)
    backward_rows(
        (2, 3), (), me_ref[0], lengths_ref, part_ref, slope_ref, grad_ref, total_ref, (o2_ref, o3_ref)
    )


def backward_rest_body(
    me_ref, lengths_ref, part_ref, slope_ref, grad_ref, sums_ref, o0_ref, o1_ref, total_ref
):
    total_ref[...] = sums_ref[...]
    backward_rows(
        (1, 0), (2, 3), me_ref[0], lengths_ref, part_ref, slope_ref, grad_ref, total_ref, (o1_ref, o0_ref)
    )


def weight_body(sources, pairs, dp_ref, kept_side_ref, came_side_ref, *refs):
    normed, grads = refs[:sources], refs[sources : 2 * sources]
    outs, total_ref = refs[2 * sources : -1], refs[-1]
    side = kept_side_ref.shape[1]
    total = 0.0
    for n_ref, g_ref in zip(normed, grads):
        total += t_mm(n_ref[...], g_ref[...])
    total_ref[:, :side] = kept_side_ref[...].astype(F32) + came_side_ref[...].astype(F32)
    total_ref[:, side:] = total
    if len(outs) == 1:
        outs[0][...] = total_ref[...].astype(BF16)
        return
    kept_ref, sent_ref = outs
    share = kept_ref.shape[0] // pairs
    for j in range(pairs):
        at = slice(j * share, (j + 1) * share)
        for ref, k in ((kept_ref, 2 * j), (sent_ref, 2 * j + 1)):
            source = pl.ds(pl.multiple_of((dp_ref[0] ^ k) * share, share), share)
            ref[at, :] = total_ref[source, :].astype(BF16)


def pair_body(kept_ref, came_ref, _, *outs):
    store_blocks(outs, kept_ref[...].astype(F32) + came_ref[...].astype(F32))


def head_columns(owner, proj_ref):
    width = proj_ref.shape[0]
    cols = [proj_ref[:, pl.ds(pl.multiple_of(b * width + owner * LANES, LANES), LANES)] for b in (1, 2, 3)]
    return jnp.concatenate(cols, axis=1)


def input_far_body(me_ref, far_ref, cross_ref, gate_in_ref, proj_ref, out_ref):
    me = me_ref[0]
    total = gate_in_ref[...] + mm_t(far_ref[...], head_columns(me ^ 2, proj_ref))
    out_ref[...] = total + mm_t(cross_ref[...], head_columns(me ^ 3, proj_ref))


def input_body(me_ref, own_ref, near_ref, partial_ref, owned_ref, cot_ref, proj_ref, out_ref):
    me = me_ref[0]
    total = partial_ref[...] + mm_t(own_ref[...], head_columns(me, proj_ref))
    total += mm_t(near_ref[...], head_columns(me ^ 1, proj_ref))
    centred, inv_scale = normalize(owned_ref[...].astype(F32))
    grad = (norm_back(total, centred, inv_scale) + cot_ref[...].astype(F32)).astype(BF16)
    out_ref[...] = grad


def spread_body(blocks, mask_ref, grad_ref, landing_ref, out_ref):
    select = hot(iota((grad_ref.shape[0], landing_ref.shape[1]), 0) + 1 == landing_ref[...])
    value = t_mm(select, grad_ref[...])
    size = value.shape[0] // blocks
    for k in range(blocks):
        at = pl.ds(pl.multiple_of((mask_ref[0] ^ k) * size, size), size)
        out_ref[at, :] = value[k * size : (k + 1) * size].astype(BF16)


def return_body(capacity, mask_ref, owner_ref, back_ref, out_ref):
    owner = owner_ref[...] ^ mask_ref[0]
    rank_row, _ = rank_rows(owner)
    chosen = hot(iota((back_ref.shape[0], owner.shape[1]), 0) == owner * capacity + rank_row)
    out_ref[...] = t_mm(chosen, back_ref[...]).astype(BF16)


def sum_body(*refs):
    total = 0.0
    for ref in refs[:-1]:
        parts = ref[...].astype(F32)
        total += parts if ref.ndim == 2 else jnp.sum(parts, axis=0)
    refs[-1][...] = total.astype(BF16)


def finish_body(me_ref, w0_ref, w1_ref, w2_ref, w3_ref, proj_ref, outw_ref):
    me = me_ref[0]
    width = outw_ref.shape[1]
    for step, ref in enumerate((w0_ref, w1_ref, w2_ref, w3_ref)):
        at = pl.ds(pl.multiple_of((me ^ step) * LANES, LANES), LANES)
        outw_ref[:, at] = ref[:, LANES : 2 * LANES].astype(F32)
        for b, source in enumerate((0, 2, 3, 4)):
            at = pl.ds(pl.multiple_of(b * width + (me ^ step) * LANES, LANES), LANES)
            proj_ref[:, at] = ref[:, source * LANES : (source + 1) * LANES].astype(F32)


def on_device(tokens, dest_owner, dest_slot, lengths, proj_weight, out_weight, cotangent):
    rows, width = tokens.shape
    owners = lax.axis_size("dp")
    cycle = lax.axis_size("ctx")
    assert cycle == 4 and width == cycle * LANES
    capacity = 2 * rows // owners
    stride = capacity + 8
    piece = width // cycle
    me = lax.axis_index("ctx").astype(jnp.int32).reshape(1)
    owner_row = dest_owner.reshape(1, rows)
    slot_row = dest_slot.reshape(1, rows)
    square = ((rows, width), BF16)

    def hop(value, step):
        return lax.ppermute(value, "ctx", [(i, i ^ step) for i in range(cycle)])

    def exchange(values):
        return [values[0]] + [hop(values[step], step) for step in (2, 3, 1)]

    by_hops = owners <= 8
    blocks = owners if by_hops else 1
    dp = lax.axis_index("dp").astype(jnp.int32).reshape(1)
    mask = dp if by_hops else jnp.zeros_like(dp)

    def dp_hop(value, step):
        return lax.ppermute(value, "dp", [(i, i ^ step) for i in range(owners)])

    def swap_whole(value):
        split = value.reshape(owners, value.shape[0] // owners, value.shape[1])
        return lax.all_to_all(split, "dp", split_axis=0, concat_axis=0, tiled=True).reshape(value.shape)

    def swap(values):
        if by_hops:
            return [dp_hop(values[k], k) if k else values[k] for k in hop_order(owners)]
        return [swap_whole(values[0])]

    def block_shapes(height, columns, dtype):
        return [((owners * height // blocks, columns), dtype)] * blocks

    wide = ((rows, width), F32)
    steps = tuple(range(blocks))
    later = steps[owners // 4 : owners // 2] if by_hops else ()
    first = tuple(k for k in steps if k not in later)
    *outgoing, owner_here, slot_here, tokens_here = call(
        functools.partial(pack_body, first, capacity, stride),
        "pack",
        block_shapes(stride, width, BF16)[: len(first)] + [((1, rows), jnp.int32)] * 2 + [square],
        [mask], [], far=[owner_row, slot_row, tokens], scratch=[pltpu.SemaphoreType.DMA((3,))], vmem=60,
    )
    (grad_gated,) = call(early_body, "early", [wide], [], [cotangent, out_weight, proj_weight])
    outgoing = dict(zip(first, outgoing))
    if later:
        rest = call(
            functools.partial(pack_rest_body, later, capacity, stride),
            "pack_rest", block_shapes(stride, width, BF16)[: len(later)], [],
            [owner_here, slot_here, tokens_here], far=[grad_gated],
        )
        outgoing.update(zip(later, rest))
    arrived = swap([outgoing[k] for k in steps])
    owned, normed, landing = call(
        functools.partial(place_body, owners, capacity, stride),
        "place", [square, square, ((1, owners * capacity), jnp.int32)], [], arrived,
    )
    far = hop(normed, 2)
    cross = hop(far, 1)
    gate, slope, query, partial, normed_copy = call(
        own_body, "own_rows", [square, wide, square, wide, square],
        [me, lengths], [normed, proj_weight], flops=10**10, vmem=16,
    )
    near = hop(normed_copy, 1)
    (partial,) = call(
        middle_body, "middle", [wide], [me, lengths], [near, far, proj_weight, query, partial],
        flops=10**10, vmem=16,
    )
    normed_out, *grad_pieces = call(
        forward_body, "forward", [wide] + [((rows, piece), BF16)] * cycle,
        [me, lengths], [cross, proj_weight, gate, query, partial, grad_gated],
        scratch=[pltpu.VMEM((rows, width), F32)], vmem=16,
    )
    r0, r2, r3, r1 = exchange(grad_pieces)
    side_half = ((width, 4 * piece), BF16)
    side_piece = ((width, 2 * piece), BF16)
    side_kept, side_sent, gate_in, layer_out = call(
        side_body, "side", [side_half, side_half, wide, square],
        [me], [normed, normed_out, gate, slope, grad_gated, cotangent, proj_weight, out_weight, owned],
        scratch=[pltpu.VMEM((width, 2 * width), F32)], vmem=16,
    )
    side_came = hop(side_sent, 1)
    parts, slopes = call(
        heads_body, "heads",
        [((rows * cycle, 3 * piece), BF16), ((rows * cycle, 3 * piece), F32)],
        [me], [normed, near, far, cross, proj_weight], vmem=16,
    )
    side_keep, side_send = call(
        side_sum_body, "side_sum", [side_piece, side_piece], [], [side_kept, side_came]
    )
    side_last = hop(side_send, 2)
    grad_block = ((rows, 3 * piece), BF16)
    sums = ((rows * cycle, 3 * piece), F32)
    grad_rows = ((rows * cycle, piece), BF16)
    (grad_all,) = call(
        collect_body, "collect", [grad_rows], [me], [r0, r1, r2, r3], flops=6 * 10**9,
    )
    far_block, cross_block, totals = call(
        backward_far_body, "backward_far", [grad_block, grad_block, sums],
        [me, lengths], [parts, slopes, grad_all], flops=10**10, vmem=16,
    )
    p2, p3 = hop(far_block, 2), hop(cross_block, 3)
    own_block, near_block = call(
        backward_rest_body, "backward_rest", [grad_block] * 2,
        [me, lengths], [parts, slopes, grad_all, totals], vmem=16,
        scratch=[pltpu.VMEM(*sums)],
    )
    p1 = hop(near_block, 1)
    grads = [own_block, near_block, far_block, cross_block]
    share = width // owners
    pairs = owners // 2
    columns = 5 * piece
    weight_parts = call(
        functools.partial(weight_body, cycle, pairs), "weights",
        [((pairs * share, columns), BF16)] * 2 if by_hops else [((width, columns), BF16)], [dp],
        [side_keep, side_last, normed, near, far, cross, *grads], vmem=16,
        scratch=[pltpu.VMEM((width, columns), F32)],
    )
    (partial_in,) = call(
        input_far_body, "input_far", [wide], [me], [p2, p3, gate_in, proj_weight], flops=6 * 10**9,
    )
    (grad_owned,) = call(
        input_body, "input_grad", [square], [me],
        [own_block, p1, partial_in, owned, cotangent, proj_weight], vmem=16,
    )
    (back,) = call(
        functools.partial(spread_body, blocks), "spread", [((owners * capacity, width), BF16)],
        [mask], [grad_owned, landing],
    )
    if by_hops:
        kept, sent = weight_parts
        halves = call(
            pair_body, "pair_sum", [((share, columns), BF16)] * pairs, [], [kept, dp_hop(sent, 1)],
            far=[back],
        )
        summed_parts = [halves[0]] + [dp_hop(halves[j], 2 * j) for j in range(1, pairs)]
    else:
        summed_parts = [swap_whole(weight_parts[0]).reshape(owners, share, columns)]
    (mine,) = call(sum_body, "sum", [((share, columns), BF16)], [], summed_parts, flops=10**11)
    returned = swap_whole(back)
    w1, w2, w3 = (hop(mine, step) for step in range(1, cycle))
    (grad_tokens,) = call(
        functools.partial(return_body, capacity), "give_back", [square], [mask], [owner_here, returned]
    )
    grad_proj, grad_outw = call(
        finish_body, "finish", [((share, 4 * width), F32), ((share, width), F32)],
        [me], [mine, w1, w2, w3],
    )
    return layer_out, grad_tokens, grad_proj, grad_outw


def solution(mesh):
    placed = (
        P(("dp", "ctx"), None),
        P(("dp", "ctx")),
        P(("dp", "ctx")),
        P("dp", None),
        P(),
        P(),
        P(("dp", "ctx"), None),
    )
    return jax.shard_map(
        on_device,
        mesh=mesh,
        in_specs=placed,
        out_specs=(P(("dp", "ctx"), None), P(("dp", "ctx"), None), P("dp", None), P("dp", None)),
        check_vma=False,
    )
```

```python
import functools

import jax
import jax.numpy as jnp
from jax import lax
from jax.experimental import pallas as pl
from jax.experimental.pallas import tpu as pltpu
from jax.sharding import PartitionSpec as P

HEADS = 8
EPSILON = 1e-05
LANES = 128
F32 = jnp.float32
BF16 = jnp.bfloat16

WHOLE = pl.BlockSpec(memory_space=pltpu.VMEM)
SCALARS = pl.BlockSpec(memory_space=pltpu.SMEM)
ANYWHERE = pl.BlockSpec(memory_space=pl.ANY)


def call(body, name, outs, scalars, arrays, scratch=(), flops=10**8, vmem=8, far=()):
    return pl.pallas_call(
        body,
        name=name,
        out_shape=[jax.ShapeDtypeStruct(s, d) for s, d in outs],
        in_specs=[SCALARS] * len(scalars) + [WHOLE] * len(arrays) + [ANYWHERE] * len(far),
        out_specs=[WHOLE] * len(outs),
        scratch_shapes=list(scratch),
        compiler_params=pltpu.CompilerParams(vmem_limit_bytes=vmem * 2**20),
        cost_estimate=pl.CostEstimate(flops=flops, bytes_accessed=2**20, transcendentals=0),
    )(*scalars, *arrays, *far)


def iota(shape, dim):
    return lax.broadcasted_iota(jnp.int32, shape, dim)


def mm(a, b):
    return jnp.dot(a, b, preferred_element_type=F32)


def mm_t(a, b):
    return lax.dot_general(a, b, (((1,), (1,)), ((), ())), preferred_element_type=F32)


def t_mm(a, b):
    return lax.dot_general(a, b, (((0,), (0,)), ((), ())), preferred_element_type=F32)


def hot(condition):
    return jnp.where(condition, 1.0, 0.0).astype(BF16)


def normalize(value):
    middle = jnp.mean(value, axis=-1, keepdims=True)
    centred = value - middle
    inv_dev = lax.rsqrt(jnp.mean(centred * centred, axis=-1, keepdims=True) + EPSILON)
    return centred * inv_dev, inv_dev


def norm_back(grad, normed, inv_dev):
    return inv_dev * (
        grad
        - jnp.mean(grad, axis=-1, keepdims=True)
        - normed * jnp.mean(grad * normed, axis=-1, keepdims=True)
    )


def silu_both(value):
    squashed = 0.5 * jnp.tanh(0.5 * value) + 0.5
    return value * squashed, squashed * (1.0 + value * (1.0 - squashed))


def rank_rows(owner):
    rows = owner.shape[1]
    down, across = iota((rows, rows), 0), iota((rows, rows), 1)
    spread = jnp.broadcast_to(owner, (rows, rows))
    owner_col = jnp.sum(jnp.where(down == across, spread, 0).astype(F32), axis=1, keepdims=True)
    same = owner_col.astype(jnp.int32) == spread
    rank_row = jnp.sum(jnp.where(same & (down < across), 1.0, 0.0), axis=0, keepdims=True)
    rank_col = jnp.sum(jnp.where(same & (across < down), 1.0, 0.0), axis=1, keepdims=True)
    return rank_row.astype(jnp.int32), rank_col.astype(jnp.int32)


def fetch(sources, targets, sems):
    copies = [pltpu.make_async_copy(a, b, sems.at[i]) for i, (a, b) in enumerate(zip(sources, targets))]
    for copy in copies:
        copy.start()
    for copy in copies:
        copy.wait()


def store_blocks(refs, value):
    size = refs[0].shape[0]
    for i, ref in enumerate(refs):
        ref[...] = value[i * size : (i + 1) * size].astype(ref.dtype)


def hop_order(count):
    return sorted(range(count), key=lambda k: (0 < k < count // 2, k))


def load_blocks(refs):
    order = hop_order(len(refs))
    return jnp.concatenate(
        [refs[order.index(k)][...].astype(F32) for k in range(len(refs))], axis=0
    ).astype(BF16)


def pack_blocks(steps, capacity, stride, owner, slot, tokens, out_refs):
    rows, width = tokens.shape
    rank_row, rank_col = rank_rows(owner)
    place = iota((len(steps) * stride, rows), 0)
    for i, (before, k) in enumerate(zip((-1, *steps), steps)):
        if k != before + 1:
            place = jnp.where(iota(place.shape, 0) >= i * stride, place + (k - before - 1) * stride, place)
    chosen = hot(place == owner * stride + rank_row)
    slots = jnp.where(place == owner * stride + capacity, slot + 1, 0)
    by_rank = hot(rank_col == iota((rows, width), 1))
    store_blocks(out_refs, mm(chosen, tokens) + mm(slots.astype(F32).astype(BF16), by_rank))


def pack_body(steps, capacity, stride, mask_ref, owner_hbm, slot_hbm, tokens_hbm, *refs):
    *out_refs, owner_ref, slot_ref, tokens_ref, sems = refs
    fetch((owner_hbm, slot_hbm, tokens_hbm), (owner_ref, slot_ref, tokens_ref), sems)
    owner = owner_ref[...] ^ mask_ref[0]
    owner_ref[...] = owner
    if len(steps) == 1:
        steps = range(out_refs[0].shape[0] // stride)
    pack_blocks(tuple(steps), capacity, stride, owner, slot_ref[...], tokens_ref[...], out_refs)


def pack_rest_body(steps, capacity, stride, owner_ref, slot_ref, tokens_ref, _, *out_refs):
    pack_blocks(steps, capacity, stride, owner_ref[...], slot_ref[...], tokens_ref[...], out_refs)


def block_rem(owners, stride):
    col, first = iota((owners, owners * stride), 1), iota((owners, owners * stride), 0)
    above = jnp.sum(jnp.where(col >= stride * (first + 1), 1.0, 0.0), axis=0, keepdims=True)
    rem = iota((1, owners * stride), 1) - stride * above.astype(jnp.int32)
    inside = (col >= stride * first) & (col < stride * (first + 1))
    return rem, inside


def landing_row(table, owners, capacity, stride):
    rem, inside = block_rem(owners, stride)
    lanes = iota((table.shape[1], owners * stride), 0)
    spread = mm(table, hot((lanes == rem) & (lanes < capacity)))
    return jnp.sum(jnp.where(inside, spread, 0.0), axis=0, keepdims=True)


def place_body(owners, capacity, stride, *refs):
    owned_ref, normed_ref, landing_ref = refs[-3:]
    rows = owned_ref.shape[0]
    arrived = load_blocks(refs[:-3])
    total = arrived.shape[0]
    pick = hot(iota((owners, total), 1) == iota((owners, total), 0) * stride + capacity)
    table = mm(pick, arrived).astype(BF16)
    landing = landing_row(table, owners, capacity, stride).astype(jnp.int32)
    owned = mm(hot(iota((rows, total), 0) + 1 == landing), arrived)
    owned_ref[...] = owned.astype(BF16)
    normed_ref[...] = normalize(owned)[0].astype(BF16)
    landing_ref[...] = landing_row(table, owners, capacity, capacity).astype(jnp.int32)


def early_body(cot_ref, outw_ref, proj_ref, grad_ref):
    grad_ref[...] = mm_t(cot_ref[...], outw_ref[...])


def history_start(pos, lengths_ref):
    first = lengths_ref[0, 0]
    second = lengths_ref[0, 1]
    return jnp.where(pos >= first + second, first + second, jnp.where(pos >= first, first, 0))


def attend(query_ref, key, value, shared, acc_ref):
    width = query_ref.shape[1]
    left = iota((1, LANES), 1) < LANES // 2
    for pair in range(width // LANES):
        cols = slice(pair * LANES, (pair + 1) * LANES)
        query, key_pair, value_pair = query_ref[:, cols], key[:, cols], value[:, cols]
        total = acc_ref[:, cols]
        for mine in (left, ~left):
            half = mm_t(jnp.where(mine, query, 0).astype(BF16), key_pair) * 0.0625
            weights = (half * (1.0 + jnp.tanh(half)) * shared).astype(BF16)
            total += mm(weights, jnp.where(mine, value_pair, 0).astype(BF16))
        acc_ref[:, cols] = total


def shared_factor(block, me, rows, lengths_ref):
    query_pos = me * rows + iota((rows, 1), 0)
    start = history_start(query_pos, lengths_ref)
    inverse = 1.0 / (query_pos - start + 1).astype(F32)
    key_pos = block * rows + iota((1, rows), 1)
    return jnp.where((key_pos >= start) & (key_pos <= query_pos), inverse, 0.0)


def attend_other(step, me, lengths_ref, other_ref, proj_ref, query_ref, acc_ref):
    rows, width = query_ref.shape
    block = me ^ step
    reach = history_start(me * rows, lengths_ref)

    @pl.when((block < me) & ((block + 1) * rows > reach))
    def _():
        normed = other_ref[...]
        value = silu_both(mm(normed, proj_ref[:, width : 2 * width]))[0].astype(BF16)
        key = silu_both(mm(normed, proj_ref[:, 3 * width :]))[0].astype(BF16)
        attend(query_ref, key, value, shared_factor(block, me, rows, lengths_ref), acc_ref)


def own_body(
    me_ref, lengths_ref, normed_ref, proj_ref, gate_ref, slope_ref, query_ref, acc_ref, copy_ref
):
    rows, width = normed_ref.shape
    copy_ref[...] = normed_ref[...]
    me = me_ref[0]
    preact = mm(normed_ref[...], proj_ref[...])
    gate, slope = silu_both(preact[:, :width])
    gate_ref[...] = gate.astype(BF16)
    slope_ref[...] = slope
    value = silu_both(preact[:, width : 2 * width])[0].astype(BF16)
    query_ref[...] = silu_both(preact[:, 2 * width : 3 * width])[0].astype(BF16)
    key = silu_both(preact[:, 3 * width :])[0].astype(BF16)
    acc_ref[...] = jnp.zeros_like(acc_ref)
    attend(query_ref, key, value, shared_factor(me, me, rows, lengths_ref), acc_ref)


def middle_body(me_ref, lengths_ref, near_ref, far_ref, proj_ref, query_ref, partial_ref, acc_ref):
    me = me_ref[0]
    acc_ref[...] = partial_ref[...]
    attend_other(1, me, lengths_ref, near_ref, proj_ref, query_ref, acc_ref)
    attend_other(2, me, lengths_ref, far_ref, proj_ref, query_ref, acc_ref)


def forward_body(
    me_ref, lengths_ref, cross_ref, proj_ref, gate_ref, query_ref, partial_ref, grad_ref,
    normed_ref, *rest,
):
    grads, acc_ref = rest[:-1], rest[-1]
    width = query_ref.shape[1]
    me = me_ref[0]
    acc_ref[...] = partial_ref[...]
    attend_other(3, me, lengths_ref, cross_ref, proj_ref, query_ref, acc_ref)
    normed, inv_dev = normalize(acc_ref[...])
    normed_ref[...] = normed
    acc_ref[...] = norm_back(grad_ref[...] * gate_ref[...].astype(F32), normed, inv_dev)
    piece = width // len(grads)
    for step, ref in enumerate(grads):
        ref[...] = acc_ref[:, pl.ds(pl.multiple_of((me ^ step) * piece, LANES), piece)].astype(BF16)


def side_body(
    me_ref, own_ref, normed_ref, gate_ref, slope_ref, grad_ref, cot_ref, proj_ref, outw_ref, owned_ref,
    kept_ref, sent_ref, gate_in_ref, out_ref, part_ref,
):
    width = own_ref.shape[1]
    me = me_ref[0]
    normed = normed_ref[...]
    gated = (normed * gate_ref[...].astype(F32)).astype(BF16)
    gate_grad = (grad_ref[...] * normed * slope_ref[...]).astype(BF16)
    out_ref[...] = (mm(gated, outw_ref[...]) + owned_ref[...].astype(F32)).astype(BF16)
    part_ref[:, :width] = t_mm(own_ref[...], gate_grad)
    part_ref[:, width:] = t_mm(gated, cot_ref[...])
    gate_in_ref[...] = mm_t(gate_grad, proj_ref[:, :width])
    for ref, steps in ((kept_ref, (0, 2)), (sent_ref, (1, 3))):
        place = 0
        for step in steps:
            for base in (0, width):
                source = pl.ds(pl.multiple_of(base + (me ^ step) * LANES, LANES), LANES)
                ref[:, place : place + LANES] = part_ref[:, source].astype(BF16)
                place += LANES


def side_sum_body(kept_ref, came_ref, keep_ref, send_ref):
    total = kept_ref[...].astype(F32) + came_ref[...].astype(F32)
    half = total.shape[1] // 2
    keep_ref[...] = total[:, :half].astype(BF16)
    send_ref[...] = total[:, half:].astype(BF16)


def heads_body(me_ref, n0_ref, n1_ref, n2_ref, n3_ref, proj_ref, part_ref, slope_ref):
    rows, width = n0_ref.shape
    me = me_ref[0]
    piece = width // 4
    cols = [proj_ref[:, pl.ds(pl.multiple_of(b * width + me * piece, LANES), piece)] for b in (1, 2, 3)]
    weight = jnp.concatenate(cols, axis=1)
    for step, ref in enumerate((n0_ref, n1_ref, n2_ref, n3_ref)):
        act, slope = silu_both(mm(ref[...], weight))
        at = pl.ds(pl.multiple_of((me ^ step) * rows, rows), rows)
        part_ref[at, :] = act.astype(BF16)
        slope_ref[at, :] = slope


def block_at(block, rows):
    return pl.ds(pl.multiple_of(block * rows, rows), rows)


def visit(first, second, same, lengths_ref, part_ref, grad_ref, total_ref):
    rows, piece = grad_ref.shape[0] // 4, grad_ref.shape[1]
    q_block, k_block = jnp.maximum(first, second), jnp.minimum(first, second)

    def work():
        q_at, k_at = block_at(q_block, rows), block_at(k_block, rows)
        left = iota((1, LANES), 1) < LANES // 2
        query_pos = q_block * rows + iota((1, rows), 1)
        start = history_start(query_pos, lengths_ref)
        key_pos = k_block * rows + iota((rows, 1), 0)
        inverse = 1.0 / (query_pos - start + 1).astype(F32)
        allowed = key_pos >= start
        if same:
            allowed &= key_pos <= query_pos
        shared = jnp.where(allowed, inverse, 0.0)
        value = part_ref[k_at, :piece]
        query = part_ref[q_at, piece : 2 * piece]
        key = part_ref[k_at, 2 * piece :]
        grad = grad_ref[q_at, :]
        small = value * jnp.asarray(0.0625, BF16)
        d_value, d_query, d_key = 0.0, 0.0, 0.0
        for mine in (left, ~left):
            query_h = jnp.where(mine, query, 0).astype(BF16)
            key_h = jnp.where(mine, key, 0).astype(BF16)
            grad_h = jnp.where(mine, grad, 0).astype(BF16)
            half = mm_t(key_h, query) * 0.0625
            up = 1.0 + jnp.tanh(half)
            act = half * up
            weights = (act * shared).astype(BF16)
            slope = (up + act * (2.0 - up)) * shared
            d_scores = (mm_t(small, grad_h) * slope).astype(BF16)
            d_value += mm(weights, grad_h)
            d_key += mm(d_scores, query_h)
            d_query += t_mm(d_scores, key_h)
        total_ref[k_at, :piece] += d_value
        total_ref[q_at, piece : 2 * piece] += d_query
        total_ref[k_at, 2 * piece :] += d_key

    if same:
        work()
    else:
        pl.when((k_block + 1) * rows > history_start(q_block * rows, lengths_ref))(work)


def backward_rows(steps, finished, me, lengths_ref, part_ref, slope_ref, grad_ref, total_ref, refs):
    done = list(finished)
    for step, ref in zip(steps, refs):
        for other in range(4):
            if other not in done:
                visit(me ^ step, me ^ other, other == step, lengths_ref, part_ref, grad_ref, total_ref)
        done.append(step)
        at = block_at(me ^ step, ref.shape[0])
        ref[...] = (total_ref[at, :] * slope_ref[at, :]).astype(BF16)


def collect_body(me_ref, g0_ref, g1_ref, g2_ref, g3_ref, grad_ref):
    rows = g0_ref.shape[0]
    for step, ref in enumerate((g0_ref, g1_ref, g2_ref, g3_ref)):
        grad_ref[block_at(me_ref[0] ^ step, rows), :] = ref[...]


def backward_far_body(me_ref, lengths_ref, part_ref, slope_ref, grad_ref, o2_ref, o3_ref, total_ref):
    total_ref[...] = jnp.zeros_like(total_ref)
    backward_rows(
        (2, 3), (), me_ref[0], lengths_ref, part_ref, slope_ref, grad_ref, total_ref, (o2_ref, o3_ref)
    )


def backward_rest_body(
    me_ref, lengths_ref, part_ref, slope_ref, grad_ref, sums_ref, o0_ref, o1_ref, total_ref
):
    total_ref[...] = sums_ref[...]
    backward_rows(
        (1, 0), (2, 3), me_ref[0], lengths_ref, part_ref, slope_ref, grad_ref, total_ref, (o1_ref, o0_ref)
    )


def weight_body(sources, pairs, blocks, dp_ref, mask_ref, kept_side_ref, came_side_ref, landing_ref, *refs):
    normed, grads = refs[:sources], refs[sources : 2 * sources]
    outs, (select_ref, total_ref) = refs[2 * sources : -2], refs[-2:]
    select = jnp.where(iota((select_ref.shape[1], landing_ref.shape[1]), 0) + 1 == landing_ref[...], 1.0, 0.0)
    select = jnp.transpose(select)
    size = select.shape[0] // blocks
    for k in range(blocks):
        at = pl.ds(pl.multiple_of((mask_ref[0] ^ k) * size, size), size)
        select_ref[at, :] = select[k * size : (k + 1) * size].astype(BF16)
    side = kept_side_ref.shape[1]
    total = 0.0
    for n_ref, g_ref in zip(normed, grads):
        total += t_mm(n_ref[...], g_ref[...])
    total_ref[:, :side] = kept_side_ref[...].astype(F32) + came_side_ref[...].astype(F32)
    total_ref[:, side:] = total
    if len(outs) == 1:
        outs[0][...] = total_ref[...].astype(BF16)
        return
    kept_ref, sent_ref = outs
    share = kept_ref.shape[0] // pairs
    for j in range(pairs):
        at = slice(j * share, (j + 1) * share)
        for ref, k in ((kept_ref, 2 * j), (sent_ref, 2 * j + 1)):
            source = pl.ds(pl.multiple_of((dp_ref[0] ^ k) * share, share), share)
            ref[at, :] = total_ref[source, :].astype(BF16)


def pair_body(kept_ref, came_ref, _, *outs):
    store_blocks(outs, kept_ref[...].astype(F32) + came_ref[...].astype(F32))


def head_columns(owner, proj_ref):
    width = proj_ref.shape[0]
    cols = [proj_ref[:, pl.ds(pl.multiple_of(b * width + owner * LANES, LANES), LANES)] for b in (1, 2, 3)]
    return jnp.concatenate(cols, axis=1)


def input_far_body(me_ref, far_ref, cross_ref, gate_in_ref, proj_ref, out_ref):
    me = me_ref[0]
    total = gate_in_ref[...] + mm_t(far_ref[...], head_columns(me ^ 2, proj_ref))
    out_ref[...] = total + mm_t(cross_ref[...], head_columns(me ^ 3, proj_ref))


def input_body(me_ref, own_ref, near_ref, partial_ref, owned_ref, cot_ref, proj_ref, out_ref):
    me = me_ref[0]
    total = partial_ref[...] + mm_t(own_ref[...], head_columns(me, proj_ref))
    total += mm_t(near_ref[...], head_columns(me ^ 1, proj_ref))
    centred, inv_scale = normalize(owned_ref[...].astype(F32))
    grad = (norm_back(total, centred, inv_scale) + cot_ref[...].astype(F32)).astype(BF16)
    out_ref[...] = grad


def spread_body(select_ref, grad_ref, out_ref):
    out_ref[...] = mm(select_ref[...], grad_ref[...]).astype(BF16)


def return_body(chosen_ref, back_ref, out_ref):
    out_ref[...] = mm(chosen_ref[...], back_ref[...]).astype(BF16)


def sum_body(*refs):
    total = 0.0
    for ref in refs[:-1]:
        parts = ref[...].astype(F32)
        total += parts if ref.ndim == 2 else jnp.sum(parts, axis=0)
    refs[-1][...] = total.astype(BF16)


def finish_body(
    capacity, me_ref, mask_ref, w0_ref, w1_ref, w2_ref, w3_ref, owner_ref, proj_ref, outw_ref, chosen_ref
):
    owner = owner_ref[...] ^ mask_ref[0]
    rank_row, _ = rank_rows(owner)
    chosen = jnp.where(
        iota(chosen_ref.shape[::-1], 0) == owner * capacity + rank_row, 1.0, 0.0
    )
    chosen_ref[...] = jnp.transpose(chosen).astype(BF16)
    me = me_ref[0]
    width = outw_ref.shape[1]
    for step, ref in enumerate((w0_ref, w1_ref, w2_ref, w3_ref)):
        at = pl.ds(pl.multiple_of((me ^ step) * LANES, LANES), LANES)
        outw_ref[:, at] = ref[:, LANES : 2 * LANES].astype(F32)
        for b, source in enumerate((0, 2, 3, 4)):
            at = pl.ds(pl.multiple_of(b * width + (me ^ step) * LANES, LANES), LANES)
            proj_ref[:, at] = ref[:, source * LANES : (source + 1) * LANES].astype(F32)


def on_device(tokens, dest_owner, dest_slot, lengths, proj_weight, out_weight, cotangent):
    rows, width = tokens.shape
    owners = lax.axis_size("dp")
    cycle = lax.axis_size("ctx")
    assert cycle == 4 and width == cycle * LANES
    capacity = 2 * rows // owners
    stride = capacity + 8
    piece = width // cycle
    me = lax.axis_index("ctx").astype(jnp.int32).reshape(1)
    owner_row = dest_owner.reshape(1, rows)
    slot_row = dest_slot.reshape(1, rows)
    square = ((rows, width), BF16)

    def hop(value, step):
        return lax.ppermute(value, "ctx", [(i, i ^ step) for i in range(cycle)])

    def exchange(values):
        return [values[0]] + [hop(values[step], step) for step in (2, 3, 1)]

    by_hops = owners <= 8
    blocks = owners if by_hops else 1
    dp = lax.axis_index("dp").astype(jnp.int32).reshape(1)
    mask = dp if by_hops else jnp.zeros_like(dp)

    def dp_hop(value, step):
        return lax.ppermute(value, "dp", [(i, i ^ step) for i in range(owners)])

    def swap_whole(value):
        split = value.reshape(owners, value.shape[0] // owners, value.shape[1])
        return lax.all_to_all(split, "dp", split_axis=0, concat_axis=0, tiled=True).reshape(value.shape)

    def swap(values):
        if by_hops:
            return [dp_hop(values[k], k) if k else values[k] for k in hop_order(owners)]
        return [swap_whole(values[0])]

    def block_shapes(height, columns, dtype):
        return [((owners * height // blocks, columns), dtype)] * blocks

    wide = ((rows, width), F32)
    steps = tuple(range(blocks))
    later = steps[owners // 4 : owners // 2] if by_hops else ()
    first = tuple(k for k in steps if k not in later)
    *outgoing, owner_here, slot_here, tokens_here = call(
        functools.partial(pack_body, first, capacity, stride),
        "pack",
        block_shapes(stride, width, BF16)[: len(first)] + [((1, rows), jnp.int32)] * 2 + [square],
        [mask], [], far=[owner_row, slot_row, tokens], scratch=[pltpu.SemaphoreType.DMA((3,))], vmem=60,
    )
    (grad_gated,) = call(early_body, "early", [wide], [], [cotangent, out_weight, proj_weight])
    outgoing = dict(zip(first, outgoing))
    if later:
        rest = call(
            functools.partial(pack_rest_body, later, capacity, stride),
            "pack_rest", block_shapes(stride, width, BF16)[: len(later)], [],
            [owner_here, slot_here, tokens_here], far=[grad_gated],
        )
        outgoing.update(zip(later, rest))
    arrived = swap([outgoing[k] for k in steps])
    owned, normed, landing = call(
        functools.partial(place_body, owners, capacity, stride),
        "place", [square, square, ((1, owners * capacity), jnp.int32)], [], arrived,
    )
    far = hop(normed, 2)
    cross = hop(far, 1)
    gate, slope, query, partial, normed_copy = call(
        own_body, "own_rows", [square, wide, square, wide, square],
        [me, lengths], [normed, proj_weight], flops=10**10, vmem=16,
    )
    near = hop(normed_copy, 1)
    (partial,) = call(
        middle_body, "middle", [wide], [me, lengths], [near, far, proj_weight, query, partial],
        flops=10**10, vmem=16,
    )
    normed_out, *grad_pieces = call(
        forward_body, "forward", [wide] + [((rows, piece), BF16)] * cycle,
        [me, lengths], [cross, proj_weight, gate, query, partial, grad_gated],
        scratch=[pltpu.VMEM((rows, width), F32)], vmem=16,
    )
    r0, r2, r3, r1 = exchange(grad_pieces)
    side_half = ((width, 4 * piece), BF16)
    side_piece = ((width, 2 * piece), BF16)
    side_kept, side_sent, gate_in, layer_out = call(
        side_body, "side", [side_half, side_half, wide, square],
        [me], [normed, normed_out, gate, slope, grad_gated, cotangent, proj_weight, out_weight, owned],
        scratch=[pltpu.VMEM((width, 2 * width), F32)], vmem=16,
    )
    side_came = hop(side_sent, 1)
    parts, slopes = call(
        heads_body, "heads",
        [((rows * cycle, 3 * piece), BF16), ((rows * cycle, 3 * piece), F32)],
        [me], [normed, near, far, cross, proj_weight], vmem=16,
    )
    side_keep, side_send = call(
        side_sum_body, "side_sum", [side_piece, side_piece], [], [side_kept, side_came]
    )
    side_last = hop(side_send, 2)
    grad_block = ((rows, 3 * piece), BF16)
    sums = ((rows * cycle, 3 * piece), F32)
    grad_rows = ((rows * cycle, piece), BF16)
    (grad_all,) = call(
        collect_body, "collect", [grad_rows], [me], [r0, r1, r2, r3], flops=6 * 10**9,
    )
    far_block, cross_block, totals = call(
        backward_far_body, "backward_far", [grad_block, grad_block, sums],
        [me, lengths], [parts, slopes, grad_all], flops=10**10, vmem=16,
    )
    p2, p3 = hop(far_block, 2), hop(cross_block, 3)
    own_block, near_block = call(
        backward_rest_body, "backward_rest", [grad_block] * 2,
        [me, lengths], [parts, slopes, grad_all, totals], vmem=16,
        scratch=[pltpu.VMEM(*sums)],
    )
    p1 = hop(near_block, 1)
    grads = [own_block, near_block, far_block, cross_block]
    share = width // owners
    pairs = owners // 2
    columns = 5 * piece
    *weight_parts, select = call(
        functools.partial(weight_body, cycle, pairs, blocks), "weights",
        ([((pairs * share, columns), BF16)] * 2 if by_hops else [((width, columns), BF16)])
        + [((owners * capacity, rows), BF16)],
        [dp, mask],
        [side_keep, side_last, landing, normed, near, far, cross, *grads], vmem=16,
        scratch=[pltpu.VMEM((width, columns), F32)],
    )
    (partial_in,) = call(
        input_far_body, "input_far", [wide], [me], [p2, p3, gate_in, proj_weight], flops=6 * 10**9,
    )
    (grad_owned,) = call(
        input_body, "input_grad", [square], [me],
        [own_block, p1, partial_in, owned, cotangent, proj_weight], vmem=16,
    )
    (back,) = call(
        spread_body, "spread", [((owners * capacity, width), BF16)], [], [select, grad_owned],
    )
    if by_hops:
        kept, sent = weight_parts
        halves = call(
            pair_body, "pair_sum", [((share, columns), BF16)] * pairs, [], [kept, dp_hop(sent, 1)],
            far=[back],
        )
        summed_parts = [halves[0]] + [dp_hop(halves[j], 2 * j) for j in range(1, pairs)]
    else:
        summed_parts = [swap_whole(weight_parts[0]).reshape(owners, share, columns)]
    (mine,) = call(sum_body, "sum", [((share, columns), BF16)], [], summed_parts, flops=10**11)
    returned = swap_whole(back)
    w1, w2, w3 = (hop(mine, step) for step in range(1, cycle))
    grad_proj, grad_outw, chosen = call(
        functools.partial(finish_body, capacity), "finish",
        [((share, 4 * width), F32), ((share, width), F32), ((rows, owners * capacity), BF16)],
        [me, mask], [mine, w1, w2, w3, owner_here],
    )
    (grad_tokens,) = call(return_body, "give_back", [square], [], [chosen, returned])
    return layer_out, grad_tokens, grad_proj, grad_outw


def solution(mesh):
    placed = (
        P(("dp", "ctx"), None),
        P(("dp", "ctx")),
        P(("dp", "ctx")),
        P("dp", None),
        P(),
        P(),
        P(("dp", "ctx"), None),
    )
    return jax.shard_map(
        on_device,
        mesh=mesh,
        in_specs=placed,
        out_specs=(P(("dp", "ctx"), None), P(("dp", "ctx"), None), P("dp", None), P("dp", None)),
        check_vma=False,
    )
```

```python
import functools

import jax
import jax.numpy as jnp
from jax import lax
from jax.experimental import pallas as pl
from jax.experimental.pallas import tpu as pltpu
from jax.sharding import PartitionSpec as P

HEADS = 8
EPSILON = 1e-05
LANES = 128
F32 = jnp.float32
BF16 = jnp.bfloat16

WHOLE = pl.BlockSpec(memory_space=pltpu.VMEM)
SCALARS = pl.BlockSpec(memory_space=pltpu.SMEM)
ANYWHERE = pl.BlockSpec(memory_space=pl.ANY)


def call(body, name, outs, scalars, arrays, scratch=(), flops=10**8, vmem=8, far=()):
    return pl.pallas_call(
        body,
        name=name,
        out_shape=[jax.ShapeDtypeStruct(s, d) for s, d in outs],
        in_specs=[SCALARS] * len(scalars) + [WHOLE] * len(arrays) + [ANYWHERE] * len(far),
        out_specs=[WHOLE] * len(outs),
        scratch_shapes=list(scratch),
        compiler_params=pltpu.CompilerParams(vmem_limit_bytes=vmem * 2**20),
        cost_estimate=pl.CostEstimate(flops=flops, bytes_accessed=2**20, transcendentals=0),
    )(*scalars, *arrays, *far)


def iota(shape, dim):
    return lax.broadcasted_iota(jnp.int32, shape, dim)


def mm(a, b):
    return jnp.dot(a, b, preferred_element_type=F32)


def mm_t(a, b):
    return lax.dot_general(a, b, (((1,), (1,)), ((), ())), preferred_element_type=F32)


def t_mm(a, b):
    return lax.dot_general(a, b, (((0,), (0,)), ((), ())), preferred_element_type=F32)


def hot(condition):
    return jnp.where(condition, 1.0, 0.0).astype(BF16)


def normalize(value):
    middle = jnp.mean(value, axis=-1, keepdims=True)
    centred = value - middle
    inv_dev = lax.rsqrt(jnp.mean(centred * centred, axis=-1, keepdims=True) + EPSILON)
    return centred * inv_dev, inv_dev


def norm_back(grad, normed, inv_dev):
    return inv_dev * (
        grad
        - jnp.mean(grad, axis=-1, keepdims=True)
        - normed * jnp.mean(grad * normed, axis=-1, keepdims=True)
    )


def silu_both(value):
    squashed = 0.5 * jnp.tanh(0.5 * value) + 0.5
    return value * squashed, squashed * (1.0 + value * (1.0 - squashed))


def rank_rows(owner):
    rows = owner.shape[1]
    down, across = iota((rows, rows), 0), iota((rows, rows), 1)
    spread = jnp.broadcast_to(owner, (rows, rows))
    owner_col = jnp.sum(jnp.where(down == across, spread, 0).astype(F32), axis=1, keepdims=True)
    same = owner_col.astype(jnp.int32) == spread
    rank_row = jnp.sum(jnp.where(same & (down < across), 1.0, 0.0), axis=0, keepdims=True)
    rank_col = jnp.sum(jnp.where(same & (across < down), 1.0, 0.0), axis=1, keepdims=True)
    return rank_row.astype(jnp.int32), rank_col.astype(jnp.int32)


def fetch(sources, targets, sems):
    copies = [pltpu.make_async_copy(a, b, sems.at[i]) for i, (a, b) in enumerate(zip(sources, targets))]
    for copy in copies:
        copy.start()
    for copy in copies:
        copy.wait()


def store_blocks(refs, value):
    size = refs[0].shape[0]
    for i, ref in enumerate(refs):
        ref[...] = value[i * size : (i + 1) * size].astype(ref.dtype)


def hop_order(count):
    return sorted(range(count), key=lambda k: (0 < k < count // 2, k))


def load_blocks(refs):
    order = hop_order(len(refs))
    return jnp.concatenate(
        [refs[order.index(k)][...].astype(F32) for k in range(len(refs))], axis=0
    ).astype(BF16)


def pack_blocks(steps, capacity, stride, owner, slot, tokens, out_refs):
    rows, width = tokens.shape
    rank_row, rank_col = rank_rows(owner)
    place = iota((len(steps) * stride, rows), 0)
    for i, (before, k) in enumerate(zip((-1, *steps), steps)):
        if k != before + 1:
            place = jnp.where(iota(place.shape, 0) >= i * stride, place + (k - before - 1) * stride, place)
    chosen = hot(place == owner * stride + rank_row)
    slots = jnp.where(place == owner * stride + capacity, slot + 1, 0)
    by_rank = hot(rank_col == iota((rows, width), 1))
    store_blocks(out_refs, mm(chosen, tokens) + mm(slots.astype(F32).astype(BF16), by_rank))


def pack_body(steps, capacity, stride, mask_ref, owner_hbm, slot_hbm, tokens_hbm, *refs):
    *out_refs, owner_ref, slot_ref, tokens_ref, sems = refs
    fetch((owner_hbm, slot_hbm, tokens_hbm), (owner_ref, slot_ref, tokens_ref), sems)
    owner = owner_ref[...] ^ mask_ref[0]
    owner_ref[...] = owner
    if len(steps) == 1:
        steps = range(out_refs[0].shape[0] // stride)
    pack_blocks(tuple(steps), capacity, stride, owner, slot_ref[...], tokens_ref[...], out_refs)


def pack_rest_body(steps, capacity, stride, owner_ref, slot_ref, tokens_ref, _, *out_refs):
    pack_blocks(steps, capacity, stride, owner_ref[...], slot_ref[...], tokens_ref[...], out_refs)


def block_rem(owners, stride):
    col, first = iota((owners, owners * stride), 1), iota((owners, owners * stride), 0)
    above = jnp.sum(jnp.where(col >= stride * (first + 1), 1.0, 0.0), axis=0, keepdims=True)
    rem = iota((1, owners * stride), 1) - stride * above.astype(jnp.int32)
    inside = (col >= stride * first) & (col < stride * (first + 1))
    return rem, inside


def landing_row(table, owners, capacity, stride):
    rem, inside = block_rem(owners, stride)
    lanes = iota((table.shape[1], owners * stride), 0)
    spread = mm(table, hot((lanes == rem) & (lanes < capacity)))
    return jnp.sum(jnp.where(inside, spread, 0.0), axis=0, keepdims=True)


def place_body(owners, capacity, stride, *refs):
    owned_ref, normed_ref, landing_ref = refs[-3:]
    rows = owned_ref.shape[0]
    arrived = load_blocks(refs[:-3])
    total = arrived.shape[0]
    pick = hot(iota((owners, total), 1) == iota((owners, total), 0) * stride + capacity)
    table = mm(pick, arrived).astype(BF16)
    landing = landing_row(table, owners, capacity, stride).astype(jnp.int32)
    owned = mm(hot(iota((rows, total), 0) + 1 == landing), arrived)
    owned_ref[...] = owned.astype(BF16)
    normed_ref[...] = normalize(owned)[0].astype(BF16)
    landing_ref[...] = landing_row(table, owners, capacity, capacity).astype(jnp.int32)


def early_body(cot_ref, outw_ref, proj_ref, grad_ref):
    grad_ref[...] = mm_t(cot_ref[...], outw_ref[...])


def history_start(pos, lengths_ref):
    first = lengths_ref[0, 0]
    second = lengths_ref[0, 1]
    return jnp.where(pos >= first + second, first + second, jnp.where(pos >= first, first, 0))


def attend(query_ref, key, value, shared, acc_ref):
    width = query_ref.shape[1]
    left = iota((1, LANES), 1) < LANES // 2
    for pair in range(width // LANES):
        cols = slice(pair * LANES, (pair + 1) * LANES)
        query, key_pair, value_pair = query_ref[:, cols], key[:, cols], value[:, cols]
        total = acc_ref[:, cols]
        for mine in (left, ~left):
            half = mm_t(jnp.where(mine, query, 0).astype(BF16), key_pair) * 0.0625
            weights = (half * (1.0 + jnp.tanh(half)) * shared).astype(BF16)
            total += mm(weights, jnp.where(mine, value_pair, 0).astype(BF16))
        acc_ref[:, cols] = total


def shared_factor(block, me, rows, lengths_ref):
    query_pos = me * rows + iota((rows, 1), 0)
    start = history_start(query_pos, lengths_ref)
    inverse = 1.0 / (query_pos - start + 1).astype(F32)
    key_pos = block * rows + iota((1, rows), 1)
    return jnp.where((key_pos >= start) & (key_pos <= query_pos), inverse, 0.0)


def attend_other(step, me, lengths_ref, other_ref, proj_ref, query_ref, acc_ref):
    rows, width = query_ref.shape
    block = me ^ step
    reach = history_start(me * rows, lengths_ref)

    @pl.when((block < me) & ((block + 1) * rows > reach))
    def _():
        normed = other_ref[...]
        value = silu_both(mm(normed, proj_ref[:, width : 2 * width]))[0].astype(BF16)
        key = silu_both(mm(normed, proj_ref[:, 3 * width :]))[0].astype(BF16)
        attend(query_ref, key, value, shared_factor(block, me, rows, lengths_ref), acc_ref)


def own_body(
    me_ref, lengths_ref, normed_ref, proj_ref, gate_ref, slope_ref, query_ref, acc_ref, copy_ref
):
    rows, width = normed_ref.shape
    copy_ref[...] = normed_ref[...]
    me = me_ref[0]
    preact = mm(normed_ref[...], proj_ref[...])
    gate, slope = silu_both(preact[:, :width])
    gate_ref[...] = gate.astype(BF16)
    slope_ref[...] = slope
    value = silu_both(preact[:, width : 2 * width])[0].astype(BF16)
    query_ref[...] = silu_both(preact[:, 2 * width : 3 * width])[0].astype(BF16)
    key = silu_both(preact[:, 3 * width :])[0].astype(BF16)
    acc_ref[...] = jnp.zeros_like(acc_ref)
    attend(query_ref, key, value, shared_factor(me, me, rows, lengths_ref), acc_ref)


def middle_body(me_ref, lengths_ref, near_ref, far_ref, proj_ref, query_ref, partial_ref, acc_ref):
    me = me_ref[0]
    acc_ref[...] = partial_ref[...]
    attend_other(1, me, lengths_ref, near_ref, proj_ref, query_ref, acc_ref)
    attend_other(2, me, lengths_ref, far_ref, proj_ref, query_ref, acc_ref)


def forward_body(
    me_ref, lengths_ref, cross_ref, proj_ref, gate_ref, query_ref, partial_ref, grad_ref,
    normed_ref, *rest,
):
    grads, acc_ref = rest[:-1], rest[-1]
    width = query_ref.shape[1]
    me = me_ref[0]
    acc_ref[...] = partial_ref[...]
    attend_other(3, me, lengths_ref, cross_ref, proj_ref, query_ref, acc_ref)
    normed, inv_dev = normalize(acc_ref[...])
    normed_ref[...] = normed
    acc_ref[...] = norm_back(grad_ref[...] * gate_ref[...].astype(F32), normed, inv_dev)
    piece = width // len(grads)
    for step, ref in enumerate(grads):
        ref[...] = acc_ref[:, pl.ds(pl.multiple_of((me ^ step) * piece, LANES), piece)].astype(BF16)


def side_body(
    me_ref, own_ref, normed_ref, gate_ref, slope_ref, grad_ref, cot_ref, proj_ref, outw_ref, owned_ref,
    kept_ref, sent_ref, gate_in_ref, out_ref, part_ref,
):
    width = own_ref.shape[1]
    me = me_ref[0]
    normed = normed_ref[...]
    gated = (normed * gate_ref[...].astype(F32)).astype(BF16)
    gate_grad = (grad_ref[...] * normed * slope_ref[...]).astype(BF16)
    out_ref[...] = (mm(gated, outw_ref[...]) + owned_ref[...].astype(F32)).astype(BF16)
    part_ref[:, :width] = t_mm(own_ref[...], gate_grad)
    part_ref[:, width:] = t_mm(gated, cot_ref[...])
    gate_in_ref[...] = mm_t(gate_grad, proj_ref[:, :width])
    for ref, steps in ((kept_ref, (0, 2)), (sent_ref, (1, 3))):
        place = 0
        for step in steps:
            for base in (0, width):
                source = pl.ds(pl.multiple_of(base + (me ^ step) * LANES, LANES), LANES)
                ref[:, place : place + LANES] = part_ref[:, source].astype(BF16)
                place += LANES


def side_sum_body(kept_ref, came_ref, keep_ref, send_ref):
    total = kept_ref[...].astype(F32) + came_ref[...].astype(F32)
    half = total.shape[1] // 2
    keep_ref[...] = total[:, :half].astype(BF16)
    send_ref[...] = total[:, half:].astype(BF16)


def heads_body(me_ref, n0_ref, n1_ref, n2_ref, n3_ref, proj_ref, part_ref, slope_ref):
    rows, width = n0_ref.shape
    me = me_ref[0]
    piece = width // 4
    cols = [proj_ref[:, pl.ds(pl.multiple_of(b * width + me * piece, LANES), piece)] for b in (1, 2, 3)]
    weight = jnp.concatenate(cols, axis=1)
    for step, ref in enumerate((n0_ref, n1_ref, n2_ref, n3_ref)):
        act, slope = silu_both(mm(ref[...], weight))
        at = pl.ds(pl.multiple_of((me ^ step) * rows, rows), rows)
        part_ref[at, :] = act.astype(BF16)
        slope_ref[at, :] = slope


def block_at(block, rows):
    return pl.ds(pl.multiple_of(block * rows, rows), rows)


def visit(first, second, same, lengths_ref, part_ref, grad_ref, total_ref):
    rows, piece = grad_ref.shape[0] // 4, grad_ref.shape[1]
    q_block, k_block = jnp.maximum(first, second), jnp.minimum(first, second)

    def work():
        q_at, k_at = block_at(q_block, rows), block_at(k_block, rows)
        left = iota((1, LANES), 1) < LANES // 2
        query_pos = q_block * rows + iota((1, rows), 1)
        start = history_start(query_pos, lengths_ref)
        key_pos = k_block * rows + iota((rows, 1), 0)
        inverse = 1.0 / (query_pos - start + 1).astype(F32)
        allowed = key_pos >= start
        if same:
            allowed &= key_pos <= query_pos
        shared = jnp.where(allowed, inverse, 0.0)
        value = part_ref[k_at, :piece]
        query = part_ref[q_at, piece : 2 * piece]
        key = part_ref[k_at, 2 * piece :]
        grad = grad_ref[q_at, :]
        small = value * jnp.asarray(0.0625, BF16)
        d_value, d_query, d_key = 0.0, 0.0, 0.0
        for mine in (left, ~left):
            query_h = jnp.where(mine, query, 0).astype(BF16)
            key_h = jnp.where(mine, key, 0).astype(BF16)
            grad_h = jnp.where(mine, grad, 0).astype(BF16)
            half = mm_t(key_h, query) * 0.0625
            up = 1.0 + jnp.tanh(half)
            act = half * up
            weights = (act * shared).astype(BF16)
            slope = (up + act * (2.0 - up)) * shared
            d_scores = (mm_t(small, grad_h) * slope).astype(BF16)
            d_value += mm(weights, grad_h)
            d_key += mm(d_scores, query_h)
            d_query += t_mm(d_scores, key_h)
        total_ref[k_at, :piece] += d_value
        total_ref[q_at, piece : 2 * piece] += d_query
        total_ref[k_at, 2 * piece :] += d_key

    if same:
        work()
    else:
        pl.when((k_block + 1) * rows > history_start(q_block * rows, lengths_ref))(work)


def backward_rows(steps, finished, me, lengths_ref, part_ref, slope_ref, grad_ref, total_ref, refs):
    done = list(finished)
    for step, ref in zip(steps, refs):
        for other in range(4):
            if other not in done:
                visit(me ^ step, me ^ other, other == step, lengths_ref, part_ref, grad_ref, total_ref)
        done.append(step)
        at = block_at(me ^ step, ref.shape[0])
        ref[...] = (total_ref[at, :] * slope_ref[at, :]).astype(BF16)


def collect_body(me_ref, g0_ref, g1_ref, g2_ref, g3_ref, grad_ref):
    rows = g0_ref.shape[0]
    for step, ref in enumerate((g0_ref, g1_ref, g2_ref, g3_ref)):
        grad_ref[block_at(me_ref[0] ^ step, rows), :] = ref[...]


def backward_far_body(me_ref, lengths_ref, part_ref, slope_ref, grad_ref, o2_ref, o3_ref, total_ref):
    total_ref[...] = jnp.zeros_like(total_ref)
    backward_rows(
        (2, 3), (), me_ref[0], lengths_ref, part_ref, slope_ref, grad_ref, total_ref, (o2_ref, o3_ref)
    )


def backward_rest_body(
    me_ref, lengths_ref, part_ref, slope_ref, grad_ref, sums_ref, o0_ref, o1_ref, total_ref
):
    total_ref[...] = sums_ref[...]
    backward_rows(
        (1, 0), (2, 3), me_ref[0], lengths_ref, part_ref, slope_ref, grad_ref, total_ref, (o1_ref, o0_ref)
    )


def weight_body(sources, pairs, blocks, dp_ref, mask_ref, kept_side_ref, came_side_ref, landing_ref, *refs):
    normed, grads = refs[:sources], refs[sources : 2 * sources]
    outs, (select_ref, total_ref) = refs[2 * sources : -2], refs[-2:]
    select = jnp.where(iota((select_ref.shape[1], landing_ref.shape[1]), 0) + 1 == landing_ref[...], 1.0, 0.0)
    select = jnp.transpose(select)
    size = select.shape[0] // blocks
    for k in range(blocks):
        at = pl.ds(pl.multiple_of((mask_ref[0] ^ k) * size, size), size)
        select_ref[at, :] = select[k * size : (k + 1) * size].astype(BF16)
    side = kept_side_ref.shape[1]
    total = 0.0
    for n_ref, g_ref in zip(normed, grads):
        total += t_mm(n_ref[...], g_ref[...])
    total_ref[:, :side] = kept_side_ref[...].astype(F32) + came_side_ref[...].astype(F32)
    total_ref[:, side:] = total
    if len(outs) == 1:
        outs[0][...] = total_ref[...].astype(BF16)
        return
    kept_ref, sent_ref = outs
    share = kept_ref.shape[0] // pairs
    for j in range(pairs):
        at = slice(j * share, (j + 1) * share)
        for ref, k in ((kept_ref, 2 * j), (sent_ref, 2 * j + 1)):
            source = pl.ds(pl.multiple_of((dp_ref[0] ^ k) * share, share), share)
            ref[at, :] = total_ref[source, :].astype(BF16)


def pair_body(kept_ref, came_ref, _, *outs):
    store_blocks(outs, kept_ref[...].astype(F32) + came_ref[...].astype(F32))


def head_columns(owner, proj_ref):
    width = proj_ref.shape[0]
    cols = [proj_ref[:, pl.ds(pl.multiple_of(b * width + owner * LANES, LANES), LANES)] for b in (1, 2, 3)]
    return jnp.concatenate(cols, axis=1)


def input_far_body(me_ref, far_ref, cross_ref, gate_in_ref, proj_ref, out_ref):
    me = me_ref[0]
    total = gate_in_ref[...] + mm_t(far_ref[...], head_columns(me ^ 2, proj_ref))
    out_ref[...] = total + mm_t(cross_ref[...], head_columns(me ^ 3, proj_ref))


def input_body(me_ref, own_ref, near_ref, partial_ref, owned_ref, cot_ref, proj_ref, out_ref):
    me = me_ref[0]
    total = partial_ref[...] + mm_t(own_ref[...], head_columns(me, proj_ref))
    total += mm_t(near_ref[...], head_columns(me ^ 1, proj_ref))
    centred, inv_scale = normalize(owned_ref[...].astype(F32))
    grad = (norm_back(total, centred, inv_scale) + cot_ref[...].astype(F32)).astype(BF16)
    out_ref[...] = grad


def spread_body(select_ref, grad_ref, out_ref):
    out_ref[...] = mm(select_ref[...], grad_ref[...]).astype(BF16)


def return_body(chosen_ref, back_ref, out_ref):
    out_ref[...] = mm(chosen_ref[...], back_ref[...]).astype(BF16)


def sum_body(*refs):
    total = 0.0
    for ref in refs[:-1]:
        parts = ref[...].astype(F32)
        total += parts if ref.ndim == 2 else jnp.sum(parts, axis=0)
    refs[-1][...] = total.astype(BF16)


def finish_body(
    capacity, me_ref, mask_ref, w0_ref, w1_ref, w2_ref, w3_ref, owner_ref, proj_ref, outw_ref, chosen_ref
):
    owner = owner_ref[...] ^ mask_ref[0]
    rank_row, _ = rank_rows(owner)
    chosen = jnp.where(
        iota(chosen_ref.shape[::-1], 0) == owner * capacity + rank_row, 1.0, 0.0
    )
    chosen_ref[...] = jnp.transpose(chosen).astype(BF16)
    me = me_ref[0]
    width = outw_ref.shape[1]
    for step, ref in enumerate((w0_ref, w1_ref, w2_ref, w3_ref)):
        at = pl.ds(pl.multiple_of((me ^ step) * LANES, LANES), LANES)
        outw_ref[:, at] = ref[:, LANES : 2 * LANES].astype(F32)
        for b, source in enumerate((0, 2, 3, 4)):
            at = pl.ds(pl.multiple_of(b * width + (me ^ step) * LANES, LANES), LANES)
            proj_ref[:, at] = ref[:, source * LANES : (source + 1) * LANES].astype(F32)


def on_device(tokens, dest_owner, dest_slot, lengths, proj_weight, out_weight, cotangent):
    rows, width = tokens.shape
    owners = lax.axis_size("dp")
    cycle = lax.axis_size("ctx")
    assert cycle == 4 and width == cycle * LANES
    capacity = 2 * rows // owners
    stride = capacity + 8
    piece = width // cycle
    me = lax.axis_index("ctx").astype(jnp.int32).reshape(1)
    owner_row = dest_owner.reshape(1, rows)
    slot_row = dest_slot.reshape(1, rows)
    square = ((rows, width), BF16)

    def hop(value, step):
        return lax.ppermute(value, "ctx", [(i, i ^ step) for i in range(cycle)])

    def exchange(values):
        return [values[0]] + [hop(values[step], step) for step in (2, 3, 1)]

    by_hops = owners <= 8
    blocks = owners if by_hops else 1
    dp = lax.axis_index("dp").astype(jnp.int32).reshape(1)
    mask = dp if by_hops else jnp.zeros_like(dp)

    def dp_hop(value, step):
        return lax.ppermute(value, "dp", [(i, i ^ step) for i in range(owners)])

    def swap_whole(value):
        split = value.reshape(owners, value.shape[0] // owners, value.shape[1])
        return lax.all_to_all(split, "dp", split_axis=0, concat_axis=0, tiled=True).reshape(value.shape)

    def swap(values):
        if by_hops:
            return [dp_hop(values[k], k) if k else values[k] for k in hop_order(owners)]
        return [swap_whole(values[0])]

    def block_shapes(height, columns, dtype):
        return [((owners * height // blocks, columns), dtype)] * blocks

    wide = ((rows, width), F32)
    steps = tuple(range(blocks))
    later = steps[owners // 4 : owners // 2] if by_hops else ()
    first = tuple(k for k in steps if k not in later)
    *outgoing, owner_here, slot_here, tokens_here = call(
        functools.partial(pack_body, first, capacity, stride),
        "pack",
        block_shapes(stride, width, BF16)[: len(first)] + [((1, rows), jnp.int32)] * 2 + [square],
        [mask], [], far=[owner_row, slot_row, tokens], scratch=[pltpu.SemaphoreType.DMA((3,))], vmem=60,
    )
    (grad_gated,) = call(early_body, "early", [wide], [], [cotangent, out_weight, proj_weight])
    outgoing = dict(zip(first, outgoing))
    if later:
        rest = call(
            functools.partial(pack_rest_body, later, capacity, stride),
            "pack_rest", block_shapes(stride, width, BF16)[: len(later)], [],
            [owner_here, slot_here, tokens_here], far=[grad_gated],
        )
        outgoing.update(zip(later, rest))
    arrived = swap([outgoing[k] for k in steps])
    owned, normed, landing = call(
        functools.partial(place_body, owners, capacity, stride),
        "place", [square, square, ((1, owners * capacity), jnp.int32)], [], arrived,
    )
    far = hop(normed, 2)
    cross = hop(far, 1)
    gate, slope, query, partial, normed_copy = call(
        own_body, "own_rows", [square, wide, square, wide, square],
        [me, lengths], [normed, proj_weight], flops=10**10, vmem=16,
    )
    near = hop(normed_copy, 1)
    (partial,) = call(
        middle_body, "middle", [wide], [me, lengths], [near, far, proj_weight, query, partial],
        flops=10**10, vmem=16,
    )
    normed_out, *grad_pieces = call(
        forward_body, "forward", [wide] + [((rows, piece), BF16)] * cycle,
        [me, lengths], [cross, proj_weight, gate, query, partial, grad_gated],
        scratch=[pltpu.VMEM((rows, width), F32)], vmem=16,
    )
    r0, r2, r3, r1 = exchange(grad_pieces)
    side_half = ((width, 4 * piece), BF16)
    side_piece = ((width, 2 * piece), BF16)
    side_kept, side_sent, gate_in, layer_out = call(
        side_body, "side", [side_half, side_half, wide, square],
        [me], [normed, normed_out, gate, slope, grad_gated, cotangent, proj_weight, out_weight, owned],
        scratch=[pltpu.VMEM((width, 2 * width), F32)], vmem=16,
    )
    side_came = hop(side_sent, 1)
    parts, slopes = call(
        heads_body, "heads",
        [((rows * cycle, 3 * piece), BF16), ((rows * cycle, 3 * piece), F32)],
        [me], [normed, near, far, cross, proj_weight], vmem=16,
    )
    side_keep, side_send = call(
        side_sum_body, "side_sum", [side_piece, side_piece], [], [side_kept, side_came]
    )
    side_last = hop(side_send, 2)
    grad_block = ((rows, 3 * piece), BF16)
    sums = ((rows * cycle, 3 * piece), F32)
    grad_rows = ((rows * cycle, piece), BF16)
    (grad_all,) = call(
        collect_body, "collect", [grad_rows], [me], [r0, r1, r2, r3], flops=6 * 10**9,
    )
    far_block, cross_block, totals = call(
        backward_far_body, "backward_far", [grad_block, grad_block, sums],
        [me, lengths], [parts, slopes, grad_all], flops=10**10, vmem=16,
    )
    p2, p3 = hop(far_block, 2), hop(cross_block, 3)
    own_block, near_block = call(
        backward_rest_body, "backward_rest", [grad_block] * 2,
        [me, lengths], [parts, slopes, grad_all, totals], vmem=16,
        scratch=[pltpu.VMEM(*sums)],
    )
    p1 = hop(near_block, 1)
    grads = [own_block, near_block, far_block, cross_block]
    share = width // owners
    pairs = owners // 2
    columns = 5 * piece
    *weight_parts, select = call(
        functools.partial(weight_body, cycle, pairs, blocks), "weights",
        ([((pairs * share, columns), BF16)] * 2 if by_hops else [((width, columns), BF16)])
        + [((owners * capacity, rows), BF16)],
        [dp, mask],
        [side_keep, side_last, landing, normed, near, far, cross, *grads], vmem=16,
        scratch=[pltpu.VMEM((width, columns), F32)],
    )
    (partial_in,) = call(
        input_far_body, "input_far", [wide], [me], [p2, p3, gate_in, proj_weight], flops=6 * 10**9,
    )
    (grad_owned,) = call(
        input_body, "input_grad", [square], [me],
        [own_block, p1, partial_in, owned, cotangent, proj_weight], vmem=16,
    )
    (back,) = call(
        spread_body, "spread", [((owners * capacity, width), BF16)], [], [select, grad_owned],
    )
    if by_hops:
        kept, sent = weight_parts
        halves = call(
            pair_body, "pair_sum", [((share, columns), BF16)] * pairs, [], [kept, dp_hop(sent, 1)],
            far=[back],
        )
        order = sorted(range(1, pairs), key=lambda j: (j < pairs // 2, j))
        summed_parts = [halves[0]] + [dp_hop(halves[j], 2 * j) for j in order]
    else:
        summed_parts = [swap_whole(weight_parts[0]).reshape(owners, share, columns)]
    (mine,) = call(sum_body, "sum", [((share, columns), BF16)], [], summed_parts, flops=10**11)
    returned = swap_whole(back)
    w1, w2, w3 = (hop(mine, step) for step in range(1, cycle))
    grad_proj, grad_outw, chosen = call(
        functools.partial(finish_body, capacity), "finish",
        [((share, 4 * width), F32), ((share, width), F32), ((rows, owners * capacity), BF16)],
        [me, mask], [mine, w1, w2, w3, owner_here],
    )
    (grad_tokens,) = call(return_body, "give_back", [square], [], [chosen, returned])
    return layer_out, grad_tokens, grad_proj, grad_outw


def solution(mesh):
    placed = (
        P(("dp", "ctx"), None),
        P(("dp", "ctx")),
        P(("dp", "ctx")),
        P("dp", None),
        P(),
        P(),
        P(("dp", "ctx"), None),
    )
    return jax.shard_map(
        on_device,
        mesh=mesh,
        in_specs=placed,
        out_specs=(P(("dp", "ctx"), None), P(("dp", "ctx"), None), P("dp", None), P("dp", None)),
        check_vma=False,
    )
```
